32 devices in a mesh: side: 2 (over x), grp: 4 (over z), blk: 4 (over y, core).
Axes of the slice: x: 2, y: 2, z: 4, core: 2. Of those that a mesh axis runs over, the one named last changes fastest.
Arguments:
- embed_codes: bfloat16 [2, 8192, 128], P('side', ('grp', 'blk')), may hold values from -4 to 4
- embed_exps: int32 [2, 64], P('side', ('grp', 'blk')), may hold values from -1 to 1
- degrees: int32 [2, 8192], P('side', ('grp', 'blk')), may hold values from 16 to 128
- adjacency: bfloat16 [2, 1536, 128, 128], P('side', ('grp', 'blk')), may hold values from 0 to 1
- block_index: int32 [2, 2, 1536], P('side', None, ('grp', 'blk')), may hold values from 0 to 16, as said below
Outputs:
- layer_rows: bfloat16 [2, 8192, 128], P('side', ('grp', 'blk'))
The draws below stay inside these ranges and needn't reach their ends.
Inputs may be any that keep to these rules, and one draw needn't show every extreme that they name: `block_index`: each device's list of 96 slots: its used slots come first, in non-decreasing source tile (row 1 below 16), with distinct (destination, source) pairs and destination tiles below 16; the remaining slots have source 16 and destination 0. Every list uses 96 // 4 slots or more, and in each section one list uses all 96.
All inputs are finite; a program needn't handle non-finite values.
Results may differ from the reference program's by a relative error of at most 0.0048.
Values may be sent and summed in bfloat16 or wider, within the bound.
No kernel may reach another device: no remote copies, remote signals or barrier semaphores. Data moves between devices by JAX's collectives and lax.ppermute only.
A program may use at most 128 MiB of HBM per device.

```python
import jax
import jax.numpy as jnp
from jax import lax

W = 128
TILE = 128
TPS = 4
DEVS = 16
NODES = 8192
SRC_TILES = 16
DST_TILES = 16
MAXB = 96
N_GRP = 4
N_BLK = 4


def device_list(key, filled):
    key_heat, key_score, key_used = jax.random.split(key, 3)
    pair_count = DST_TILES * SRC_TILES
    pairs = jnp.arange(pair_count, dtype=jnp.int32)
    source_tile = pairs % SRC_TILES
    target_tile = pairs // SRC_TILES
    heat = jax.random.randint(key_heat, (SRC_TILES // TPS,), 0, 4)
    score = jax.random.randint(key_score, (pair_count,), 0, 1024) + heat[source_tile // TPS] * 1024
    score = score * pair_count + pairs
    used_count = jnp.where(filled, MAXB, MAXB - jax.random.randint(key_used, (), 0, MAXB - MAXB // 4 + 1))
    _, order = lax.top_k(score, MAXB)
    ranks = jnp.arange(MAXB, dtype=jnp.int32)
    keeping = ranks < used_count
    chosen_source = jnp.where(keeping, source_tile[order], SRC_TILES)
    chosen_target = jnp.where(keeping, target_tile[order], 0)
    arrange = jnp.argsort(chosen_source * MAXB + ranks, stable=True)
    return jnp.stack([chosen_target[arrange], chosen_source[arrange]])


def draw_block_index(key, part):
    full_device = jax.random.randint(jax.random.fold_in(key, 11), (2,), 0, DEVS)
    device_keys = jax.random.split(jax.random.fold_in(key, 12), 2 * DEVS)
    marks = (jnp.arange(DEVS)[None, :] == full_device[:, None]).reshape(2 * DEVS)
    lists = jax.vmap(device_list)(device_keys, marks)
    lists = lists.reshape(2, DEVS, 2, MAXB).transpose(0, 2, 1, 3)
    return lists.reshape(2, 2, DEVS * MAXB).astype(jnp.int32)


def touch_ends(entries, stream_key, low, largest):
    dims = entries.shape
    index_at = [jax.random.randint(jax.random.fold_in(stream_key, axis), (), 0, dims[axis]) for axis in range(len(dims))]
    entries = entries.at[tuple(index_at)].set(low)
    longest = dims.index(max(dims))
    index_at[longest] = (index_at[longest] + 1) % dims[longest]
    return entries.at[tuple(index_at)].set(largest)


def shard_levels(key, shape, cuts, smallest, largest):
    def one(axis_at, shards_of):
        steps = jax.random.uniform(jax.random.fold_in(jax.random.fold_in(key, 6), axis_at), (shards_of,), jnp.float32, smallest / len(cuts), largest / len(cuts))
        return jnp.repeat(jnp.exp(steps), shape[axis_at] // shards_of).reshape((-1,) + (1,) * (len(shape) - axis_at - 1))

    level = one(*cuts[0])
    for cut in cuts[1:]:
        level = level * one(*cut)
    return level


def noise(stream_key, shape, deviation, bound, shards=(), held_as=jnp.bfloat16):
    drawn = deviation * jax.random.normal(stream_key, shape, jnp.float32)
    if shards:
        drawn = drawn * shard_levels(stream_key, shape, shards, -0.22, 0.18)
    return jnp.clip(drawn, -bound, bound).astype(held_as)


def setup_inputs(seed: int = 0) -> dict:
    keys = jax.random.split(jax.random.key(seed), 6)
    return {
        "embed_codes": noise(keys[0], (2, NODES, W), 1.0, 4.0, ((0, 2), (1, 16))),
        "embed_exps": touch_ends(jax.random.randint(keys[1], (2, NODES // TILE), -1, 2), jax.random.fold_in(keys[1], 1), -1, 1).astype(jnp.int32),
        "degrees": touch_ends(jax.random.randint(keys[2], (2, NODES), 16, 129), jax.random.fold_in(keys[2], 1), 16, 128).astype(jnp.int32),
        "adjacency": jnp.clip(1.0 * jax.random.uniform(keys[3], (2, DEVS * MAXB, TILE, TILE), jnp.float32) ** shard_levels(keys[3], (2, DEVS * MAXB, TILE, TILE), ((0, 2), (1, 16)), -0.2, 0.2), 0.0, 1.0).astype(jnp.bfloat16),
        "block_index": draw_block_index(jax.random.fold_in(keys[5], 71), 0),
    }


def reference(embed_codes, embed_exps, degrees, adjacency, block_index):
    tile_rows = adjacency.shape[2]
    row_width = embed_codes.shape[2]
    scale = jnp.repeat(jnp.exp2(embed_exps.astype(jnp.float32)), tile_rows, axis=1)
    inverse = lax.rsqrt(degrees.astype(jnp.float32))
    source_rows = (embed_codes.astype(jnp.float32) * scale[..., None] * inverse[..., None]).astype(jnp.bfloat16)
    results = []
    for section in range(2):
        source = source_rows[1 - section].reshape(N_GRP, SRC_TILES, tile_rows, row_width)
        grid = adjacency[section].reshape(N_GRP, N_BLK, MAXB, tile_rows, tile_rows)
        listed = block_index[section].reshape(2, N_GRP, N_BLK, MAXB)

        def one_group(running, group):
            tiles, group_blocks, targets, sources = group

            def one_device(device):
                dev_blocks, dev_targets, dev_sources = device
                active = dev_sources < SRC_TILES
                picked = tiles[jnp.minimum(dev_sources, SRC_TILES - 1)].astype(jnp.float32)
                products = jnp.einsum('kij,kjw->kiw', dev_blocks.astype(jnp.float32), picked)
                products = jnp.where(active[:, None, None], products, jnp.zeros_like(products))
                return jax.ops.segment_sum(products, dev_targets, num_segments=DST_TILES)
            partial_sums = lax.map(one_device, (group_blocks, targets, sources))
            return (running + partial_sums, None)
        starting = jnp.zeros((N_BLK, DST_TILES, tile_rows, row_width), jnp.float32)
        running, _ = lax.scan(one_group, starting, (source, grid, listed[0], listed[1]))
        running = running.reshape(N_BLK, N_GRP, TPS * tile_rows, row_width)
        running = running.transpose(1, 0, 2, 3).reshape(NODES, row_width)
        results.append((running * inverse[section][:, None]).astype(jnp.bfloat16))
    return jnp.stack(results)
```

```python
import functools

import jax
import jax.numpy as jnp
from jax import lax
from jax.experimental import pallas as pl
from jax.experimental.pallas import tpu as pltpu
from jax.sharding import PartitionSpec as P


def scale_rows(codes_part, exps_part, degree_part, tile_rows):
    scale = jnp.repeat(jnp.exp2(exps_part.astype(jnp.float32)), tile_rows, axis=1)
    inverse = lax.rsqrt(degree_part.astype(jnp.float32))
    return (codes_part.astype(jnp.float32) * scale[..., None] * inverse[..., None]).astype(
        jnp.bfloat16
    )


def block_kernel(blks, groups, tiles_dev, unroll, index_ref, place_ref, *refs):
    panels = refs[:blks]
    blocks = refs[blks]
    outs = refs[blks + 1 : blks + 1 + groups]
    source, total = refs[blks + 1 + groups :]
    my_blk = place_ref[0]
    my_grp = place_ref[1]
    source_tiles = blks * tiles_dev
    dest_tiles = groups * tiles_dev
    capacity = blocks.shape[0]
    for hop in range(blks):
        source[pl.ds((my_blk ^ hop) * tiles_dev, tiles_dev)] = panels[hop][...]
    total[...] = jnp.zeros_like(total)

    def step(slot):
        target = index_ref[0, slot]
        origin = index_ref[1, slot]
        held = origin < source_tiles
        target = jnp.where(held, target, dest_tiles)
        origin = jnp.where(held, origin, 0)
        return target, jnp.dot(
            blocks[slot], source[origin], preferred_element_type=jnp.float32
        )

    @pl.loop(0, capacity // unroll)
    def _(batch):
        made = [step(batch * unroll + part) for part in range(unroll)]
        for target, product in made:
            total[target] += product

    for hop in range(groups):
        mine = total[pl.ds((my_grp ^ hop) * tiles_dev, tiles_dev)]
        outs[hop][...] = mine.astype(outs[hop].dtype)


def propagate(index, place, panels, blocks, groups):
    blks = len(panels)
    tiles_dev, tile_rows, row_width = panels[0].shape
    capacity = blocks.shape[0]
    unroll = next(size for size in (8, 4, 2, 1) if capacity % size == 0)
    vmem = pl.BlockSpec(memory_space=pltpu.VMEM)
    smem = pl.BlockSpec(memory_space=pltpu.SMEM)
    part = (tiles_dev, tile_rows, row_width)
    return pl.pallas_call(
        functools.partial(block_kernel, blks, groups, tiles_dev, unroll),
        out_shape=[
            jax.ShapeDtypeStruct(part, jnp.float32 if hop == 0 else jnp.bfloat16)
            for hop in range(groups)
        ],
        in_specs=[smem, smem] + [vmem] * (blks + 1),
        out_specs=[vmem] * groups,
        scratch_shapes=[
            pltpu.VMEM((blks * tiles_dev, tile_rows, row_width), jnp.bfloat16),
            pltpu.VMEM((groups * tiles_dev + 1, tile_rows, row_width), jnp.float32),
        ],
        compiler_params=pltpu.CompilerParams(vmem_limit_bytes=48 * 1024 * 1024),
        cost_estimate=pl.CostEstimate(
            flops=2 * capacity * tile_rows * tile_rows * row_width,
            bytes_accessed=2 * capacity * tile_rows * tile_rows,
            transcendentals=0,
        ),
    )(index, place, *panels, blocks)


def shards(embed_codes, embed_exps, degrees, adjacency, block_index):
    tile_rows = adjacency.shape[2]
    row_width = embed_codes.shape[2]
    row_count = embed_codes.shape[1]
    tiles_dev = row_count // tile_rows
    groups = lax.axis_size("grp")
    blks = lax.axis_size("blk")
    source = scale_rows(embed_codes, embed_exps, degrees, tile_rows)
    panel = lax.ppermute(
        source.reshape(tiles_dev, tile_rows, row_width), "side", [(0, 1), (1, 0)]
    )
    panels = [panel] + [
        lax.ppermute(panel, "blk", [(at, at ^ hop) for at in range(blks)])
        for hop in range(1, blks)
    ]
    place = jnp.stack([lax.axis_index("blk"), lax.axis_index("grp")]).astype(jnp.int32)
    parts = propagate(block_index[0], place, panels, adjacency[0], groups)
    summed = parts[0]
    for hop in range(1, groups):
        arrived = lax.ppermute(parts[hop], "grp", [(at, at ^ hop) for at in range(groups)])
        summed = summed + arrived.astype(jnp.float32)
    inverse = lax.rsqrt(degrees.astype(jnp.float32))
    return (summed.reshape(1, row_count, row_width) * inverse[..., None]).astype(jnp.bfloat16)


def solution(mesh):
    placed = (
        P("side", ("grp", "blk"), None),
        P("side", ("grp", "blk")),
        P("side", ("grp", "blk")),
        P("side", ("grp", "blk"), None, None),
        P("side", None, ("grp", "blk")),
    )
    return jax.shard_map(
        shards,
        mesh=mesh,
        in_specs=placed,
        out_specs=P("side", ("grp", "blk"), None),
        check_vma=False,
    )
```

```python
import functools

import jax
import jax.numpy as jnp
from jax import lax
from jax.experimental import pallas as pl
from jax.experimental.pallas import tpu as pltpu
from jax.sharding import PartitionSpec as P

UNROLL = 8
STAGES = 4
VMEM = pl.BlockSpec(memory_space=pltpu.VMEM)
SMEM = pl.BlockSpec(memory_space=pltpu.SMEM)
HBM = pl.BlockSpec(memory_space=pl.ANY)
LIMIT = pltpu.CompilerParams(vmem_limit_bytes=48 * 1024 * 1024)


def scale_rows(codes_part, exps_part, degree_part, tile_rows):
    scale = jnp.repeat(jnp.exp2(exps_part.astype(jnp.float32)), tile_rows, axis=1)
    inverse = lax.rsqrt(degree_part.astype(jnp.float32))
    return (codes_part.astype(jnp.float32) * scale[..., None] * inverse[..., None]).astype(
        jnp.bfloat16
    )


def stage_kernel(blks, groups, tiles_dev, index_ref, place_ref, blocks_hbm, order_ref, blocks, sem):
    copy = pltpu.make_async_copy(blocks_hbm, blocks, sem)
    copy.start()
    my_blk = place_ref[0]
    my_grp = place_ref[1]
    capacity = index_ref.shape[1]
    source_tiles = blks * tiles_dev
    dest_tiles = groups * tiles_dev

    def located(slot):
        target = index_ref[0, slot]
        origin = index_ref[1, slot]
        held = origin < source_tiles
        hop = (origin // tiles_dev) ^ my_blk
        chunk = (target // tiles_dev) ^ my_grp
        far = (chunk >= 2) & (chunk % 2 == 1)
        stage = jnp.where(hop % 2 == 0, jnp.where(hop == 0, 0, 1), jnp.where(far, 2, 3))
        stage = jnp.where(held, stage, STAGES)
        row = jnp.where(stage == 1, hop // 2 - 1, hop // 2) * tiles_dev + origin % tiles_dev
        return stage, row, chunk * tiles_dev + target % tiles_dev

    def count(slot, counts):
        stage, _, _ = located(slot)
        return tuple(seen + (stage == at).astype(jnp.int32) for at, seen in enumerate(counts))

    zero = jnp.int32(0)
    counts = lax.fori_loop(0, capacity, count, (zero,) * STAGES, unroll=8)
    begins = []
    begin = zero
    for at in range(STAGES):
        begins.append(begin)
        order_ref[3, 2 * at] = begin // UNROLL
        begin = begin + (counts[at] + (UNROLL - 1)) // UNROLL * UNROLL
        order_ref[3, 2 * at + 1] = begin // UNROLL
    for at in range(STAGES):
        for extra in range(UNROLL):
            where = begins[at] + counts[at] + extra
            order_ref[0, where] = 0
            order_ref[1, where] = 0
            order_ref[2, where] = dest_tiles

    def place(slot, nexts):
        stage, row, target = located(slot)
        where = jnp.int32(capacity + STAGES * UNROLL)
        for at, position in enumerate(nexts):
            where = jnp.where(stage == at, position, where)
        order_ref[0, where] = slot
        order_ref[1, where] = row
        order_ref[2, where] = target
        return tuple(
            position + (stage == at).astype(jnp.int32) for at, position in enumerate(nexts)
        )

    lax.fori_loop(0, capacity, place, tuple(begins), unroll=8)
    copy.wait()


def stage_blocks(index, place, blocks, blks, groups, tiles_dev):
    capacity = blocks.shape[0]
    width = capacity + STAGES * UNROLL + UNROLL
    return pl.pallas_call(
        functools.partial(stage_kernel, blks, groups, tiles_dev),
        out_shape=[
            jax.ShapeDtypeStruct((4, width), jnp.int32),
            jax.ShapeDtypeStruct(blocks.shape, blocks.dtype),
        ],
        in_specs=[SMEM, SMEM, HBM],
        out_specs=[SMEM, VMEM],
        scratch_shapes=[pltpu.SemaphoreType.DMA],
        compiler_params=LIMIT,
        cost_estimate=pl.CostEstimate(
            flops=0, bytes_accessed=0, transcendentals=0
        ),
    )(index, place, blocks)


def add_products(stage, order_ref, blocks, source, total):
    @pl.loop(order_ref[3, 2 * stage], order_ref[3, 2 * stage + 1])
    def _(batch):
        made = []
        for part in range(UNROLL):
            entry = batch * UNROLL + part
            made.append(
                jnp.dot(
                    blocks[order_ref[0, entry]],
                    source[order_ref[1, entry]],
                    preferred_element_type=jnp.float32,
                )
            )
        for part in range(UNROLL):
            total[order_ref[2, batch * UNROLL + part]] += made[part]


def gather_panels(panels, source):
    for at, panel in enumerate(panels):
        rows = panel.shape[0]
        source[at * rows : (at + 1) * rows] = panel[...]


def first_kernel(order_ref, panel, blocks, total):
    total[...] = jnp.zeros_like(total)
    add_products(0, order_ref, blocks, panel, total)


def second_kernel(order_ref, *refs):
    *panels, blocks, _, total, source = refs
    gather_panels(panels, source)
    add_products(1, order_ref, blocks, source, total)


def far_kernel(tiles_dev, chunks, order_ref, *refs):
    *panels, blocks, _, far, total, source = refs
    gather_panels(panels, source)
    add_products(2, order_ref, blocks, source, total)
    for at, chunk in enumerate(chunks):
        far[at] = total[chunk * tiles_dev : (chunk + 1) * tiles_dev].astype(far.dtype)


def near_kernel(tiles_dev, chunks, order_ref, *refs):
    *panels, blocks, total, own, near, mine, source = refs
    gather_panels(panels, source)
    add_products(3, order_ref, blocks, source, total)
    own[...] = total[:tiles_dev]
    near[...] = total[tiles_dev : 2 * tiles_dev].astype(near.dtype)
    for at, chunk in enumerate(chunks):
        mine[at] = total[chunk * tiles_dev : (chunk + 1) * tiles_dev]


def cost_of(slots, tile_rows, row_width):
    return pl.CostEstimate(
        flops=2 * slots * tile_rows * tile_rows * row_width,
        bytes_accessed=2 * slots * tile_rows * tile_rows,
        transcendentals=0,
    )


def shards(embed_codes, embed_exps, degrees, adjacency, block_index):
    tile_rows = adjacency.shape[2]
    row_width = embed_codes.shape[2]
    row_count = embed_codes.shape[1]
    capacity = adjacency.shape[1]
    tiles_dev = row_count // tile_rows
    groups = lax.axis_size("grp")
    blks = lax.axis_size("blk")
    part = (tiles_dev, tile_rows, row_width)
    dest_tiles = groups * tiles_dev
    source = scale_rows(embed_codes, embed_exps, degrees, tile_rows).reshape(part)

    def across(value, hop):
        pairs = [
            (side * blks + at, (1 - side) * blks + (at ^ hop))
            for side in range(2)
            for at in range(blks)
        ]
        return lax.ppermute(value, ("side", "blk"), pairs)

    def paired(value, axis, hop):
        return lax.ppermute(value, axis, [(at, at ^ hop) for at in range(lax.axis_size(axis))])

    place = jnp.stack([lax.axis_index("blk"), lax.axis_index("grp")]).astype(jnp.int32)
    straight, *diagonal = [across(source, hop) for hop in range(0, blks, 2)]
    order, blocks = stage_blocks(block_index[0], place, adjacency[0], blks, groups, tiles_dev)
    straight, order = lax.optimization_barrier((straight, order))
    total_shape = jax.ShapeDtypeStruct((dest_tiles + 1, tile_rows, row_width), jnp.float32)
    total = pl.pallas_call(
        first_kernel,
        out_shape=total_shape,
        in_specs=[SMEM] + [VMEM] * 2,
        out_specs=VMEM,
        compiler_params=LIMIT,
        cost_estimate=cost_of(capacity // 4, tile_rows, row_width),
    )(order, straight, blocks)
    *diagonal, total = lax.optimization_barrier((*diagonal, total))
    others = [paired(panel, "blk", 1) for panel in (straight, *diagonal)]
    total = pl.pallas_call(
        second_kernel,
        out_shape=total_shape,
        in_specs=[SMEM] + [VMEM] * (len(diagonal) + 2),
        out_specs=VMEM,
        input_output_aliases={len(diagonal) + 2: 0},
        scratch_shapes=[
            pltpu.VMEM((len(diagonal) * tiles_dev, tile_rows, row_width), jnp.bfloat16)
        ],
        compiler_params=LIMIT,
        cost_estimate=cost_of(capacity // 4, tile_rows, row_width),
    )(order, *diagonal, blocks, total)
    *others, total = lax.optimization_barrier((*others, total))
    others_scratch = [pltpu.VMEM((len(others) * tiles_dev, tile_rows, row_width), jnp.bfloat16)]
    far_chunks = range(3, groups, 2)
    far, total = pl.pallas_call(
        functools.partial(far_kernel, tiles_dev, far_chunks),
        out_shape=[
            jax.ShapeDtypeStruct((len(far_chunks),) + part, jnp.bfloat16),
            total_shape,
        ],
        in_specs=[SMEM] + [VMEM] * (len(others) + 2),
        out_specs=[VMEM, VMEM],
        input_output_aliases={len(others) + 2: 1},
        scratch_shapes=others_scratch,
        compiler_params=LIMIT,
        cost_estimate=cost_of(capacity // 8, tile_rows, row_width),
    )(order, *others, blocks, total)
    far_arrived = paired(far, "grp", 1)
    mine_chunks = range(2, groups, 2)
    own, near, mine = pl.pallas_call(
        functools.partial(near_kernel, tiles_dev, mine_chunks),
        out_shape=[
            jax.ShapeDtypeStruct(part, jnp.float32),
            jax.ShapeDtypeStruct(part, jnp.bfloat16),
            jax.ShapeDtypeStruct((len(mine_chunks),) + part, jnp.float32),
        ],
        in_specs=[SMEM] + [VMEM] * (len(others) + 2),
        out_specs=[VMEM] * 3,
        scratch_shapes=others_scratch,
        compiler_params=LIMIT,
        cost_estimate=cost_of(capacity // 2, tile_rows, row_width),
    )(order, *others, blocks, total)
    summed = own
    for at, hop in enumerate(mine_chunks):
        pair = (mine[at] + far_arrived[at].astype(jnp.float32)).astype(jnp.bfloat16)
        near, pair = lax.optimization_barrier((near, pair))
        summed = summed + paired(pair, "grp", hop).astype(jnp.float32)
    summed = summed + paired(near, "grp", 1).astype(jnp.float32)
    inverse = lax.rsqrt(degrees.astype(jnp.float32))
    return (summed.reshape(1, row_count, row_width) * inverse[..., None]).astype(jnp.bfloat16)


def solution(mesh):
    placed = (
        P("side", ("grp", "blk"), None),
        P("side", ("grp", "blk")),
        P("side", ("grp", "blk")),
        P("side", ("grp", "blk"), None, None),
        P("side", None, ("grp", "blk")),
    )
    return jax.shard_map(
        shards,
        mesh=mesh,
        in_specs=placed,
        out_specs=P("side", ("grp", "blk"), None),
        check_vma=False,
    )
```

```python
import functools

import jax
import jax.numpy as jnp
from jax import lax
from jax.experimental import pallas as pl
from jax.experimental.pallas import tpu as pltpu
from jax.sharding import PartitionSpec as P

UNROLL = 8
STAGES = 4
VMEM = pl.BlockSpec(memory_space=pltpu.VMEM)
SMEM = pl.BlockSpec(memory_space=pltpu.SMEM)
HBM = pl.BlockSpec(memory_space=pltpu.HBM)
LIMIT = pltpu.CompilerParams(vmem_limit_bytes=48 * 1024 * 1024)


def in_hbm(*arrays):
    return [pltpu.with_memory_space_constraint(array, pltpu.HBM) for array in arrays]


def split(value, size):
    if size & (size - 1) == 0:
        return value >> (size.bit_length() - 1), value & (size - 1)
    return value // size, value % size


def scale_kernel(exps_hbm, degrees_hbm, codes_hbm, rows, exps_ref, degrees, codes, sems):
    pairs = [(exps_hbm, exps_ref), (degrees_hbm, degrees), (codes_hbm, codes)]
    fetches = [
        pltpu.make_async_copy(held, wanted, sems.at[at])
        for at, (held, wanted) in enumerate(pairs)
    ]
    for fetch in fetches:
        fetch.start()
    fetches[0].wait()
    fetches[1].wait()
    tiles_dev, tile_rows, row_width = rows.shape
    inverse = lax.rsqrt(degrees[...].astype(jnp.float32))
    factors = []
    for tile in range(tiles_dev):
        lanes = inverse[:, tile * tile_rows : (tile + 1) * tile_rows]
        scale = jnp.exp2(jnp.full(lanes.shape, exps_ref[0, tile], jnp.int32).astype(jnp.float32))
        factors.append(jnp.broadcast_to(lanes * scale, (row_width, tile_rows)).T)
    fetches[2].wait()
    for tile, factor in enumerate(factors):
        rows[tile] = (codes[tile].astype(jnp.float32) * factor).astype(rows.dtype)


def scale_rows(codes, exps, degrees):
    return pl.pallas_call(
        scale_kernel,
        out_shape=jax.ShapeDtypeStruct(codes.shape, jnp.bfloat16),
        in_specs=[HBM] * 3,
        out_specs=VMEM,
        scratch_shapes=[
            pltpu.SMEM(exps.shape, exps.dtype),
            pltpu.VMEM(degrees.shape, degrees.dtype),
            pltpu.VMEM(codes.shape, codes.dtype),
            pltpu.SemaphoreType.DMA((3,)),
        ],
        compiler_params=LIMIT,
        cost_estimate=pl.CostEstimate(
            flops=codes.size, bytes_accessed=4 * codes.size, transcendentals=0
        ),
    )(*in_hbm(exps, degrees, codes))


def stage_kernel(
    blks, groups, tiles_dev, place_ref, index_hbm, blocks_hbm, order_ref, blocks, index_ref, sems
):
    fetch = pltpu.make_async_copy(index_hbm, index_ref, sems.at[0])
    fetch.start()
    copy = pltpu.make_async_copy(blocks_hbm, blocks, sems.at[1])
    copy.start()
    fetch.wait()
    my_blk = place_ref[0]
    my_grp = place_ref[1]
    capacity = index_ref.shape[1]
    source_tiles = blks * tiles_dev

    def enlist(slot, nexts):
        target = index_ref[0, slot]
        origin = index_ref[1, slot]
        hop, row = split(origin, tiles_dev)
        chunk, tile = split(target, tiles_dev)
        hop = hop ^ my_blk
        chunk = chunk ^ my_grp
        near = jnp.where((chunk >= 2) & ((chunk & 1) == 1), 2, 3)
        stage = jnp.where((hop & 1) == 1, near, jnp.where(hop == 0, 0, 1))
        stage = jnp.where(origin < source_tiles, stage, STAGES)
        panel = (hop >> 1) - (stage == 1).astype(jnp.int32)
        word = pack(slot, panel * tiles_dev + row, chunk * tiles_dev + tile)
        where = jnp.int32(0)
        for at, position in enumerate(nexts):
            where = jnp.where(stage == at, position, where)
        order_ref[stage, where] = word
        return tuple(
            position + (stage == at).astype(jnp.int32) for at, position in enumerate(nexts)
        )

    ends = lax.fori_loop(0, capacity, enlist, (jnp.int32(0),) * STAGES, unroll=8)
    spare = pack(0, 0, groups * tiles_dev)
    for at, end in enumerate(ends):
        for extra in range(UNROLL):
            order_ref[at, end + extra] = spare
        order_ref[at, capacity + UNROLL] = split(end + (UNROLL - 1), UNROLL)[0]
    copy.wait()


def pack(slot, row, target):
    return (slot << 16) | (row << 8) | target


def unpack(word):
    return word >> 16, (word >> 8) & 255, word & 255


def stage_blocks(index, place, blocks, blks, groups, tiles_dev):
    capacity = blocks.shape[0]
    assert blks * tiles_dev < 256 and groups * tiles_dev < 256 and capacity < 2**15
    return pl.pallas_call(
        functools.partial(stage_kernel, blks, groups, tiles_dev),
        out_shape=[
            jax.ShapeDtypeStruct((STAGES + 1, capacity + 2 * UNROLL), jnp.int32),
            jax.ShapeDtypeStruct(blocks.shape, blocks.dtype),
        ],
        in_specs=[SMEM, HBM, HBM],
        out_specs=[SMEM, VMEM],
        scratch_shapes=[
            pltpu.SMEM(index.shape, index.dtype),
            pltpu.SemaphoreType.DMA((2,)),
        ],
        compiler_params=LIMIT,
        cost_estimate=pl.CostEstimate(flops=0, bytes_accessed=0, transcendentals=0),
    )(place, *in_hbm(index, blocks))


def add_products(stage, order_ref, blocks, source, total):
    @pl.loop(0, order_ref[stage, order_ref.shape[1] - UNROLL])
    def _(batch):
        made = []
        for part in range(UNROLL):
            slot, row, target = unpack(order_ref[stage, batch * UNROLL + part])
            product = jnp.dot(blocks[slot], source[row], preferred_element_type=jnp.float32)
            made.append((target, product))
        for target, product in made:
            total[target] += product


def gather_panels(panels, source):
    for at, panel in enumerate(panels):
        rows = panel.shape[0]
        source[at * rows : (at + 1) * rows] = panel[...]


def first_kernel(order_ref, panel, blocks, total):
    total[...] = jnp.zeros_like(total)
    add_products(0, order_ref, blocks, panel, total)


def second_kernel(order_ref, *refs):
    *panels, blocks, _, total, source = refs
    gather_panels(panels, source)
    add_products(1, order_ref, blocks, source, total)


def far_kernel(tiles_dev, chunks, order_ref, *refs):
    *panels, blocks, _, far, total, source = refs
    gather_panels(panels, source)
    add_products(2, order_ref, blocks, source, total)
    for at, chunk in enumerate(chunks):
        far[at] = total[chunk * tiles_dev : (chunk + 1) * tiles_dev].astype(far.dtype)


def near_kernel(tiles_dev, chunks, order_ref, *refs):
    *panels, blocks, total, own, near, mine, source = refs
    gather_panels(panels, source)
    add_products(3, order_ref, blocks, source, total)
    own[...] = total[:tiles_dev]
    near[...] = total[tiles_dev : 2 * tiles_dev].astype(near.dtype)
    for at, chunk in enumerate(chunks):
        mine[at] = total[chunk * tiles_dev : (chunk + 1) * tiles_dev]


def cost_of(slots, tile_rows, row_width):
    return pl.CostEstimate(
        flops=2 * slots * tile_rows * tile_rows * row_width,
        bytes_accessed=2 * slots * tile_rows * tile_rows,
        transcendentals=0,
    )


def shards(embed_codes, embed_exps, degrees, adjacency, block_index):
    tile_rows = adjacency.shape[2]
    row_width = embed_codes.shape[2]
    row_count = embed_codes.shape[1]
    capacity = adjacency.shape[1]
    tiles_dev = row_count // tile_rows
    groups = lax.axis_size("grp")
    blks = lax.axis_size("blk")
    part = (tiles_dev, tile_rows, row_width)
    dest_tiles = groups * tiles_dev
    source = scale_rows(embed_codes.reshape(part), embed_exps, degrees)

    def across(value, hop):
        pairs = [
            (side * blks + at, (1 - side) * blks + (at ^ hop))
            for side in range(2)
            for at in range(blks)
        ]
        return lax.ppermute(value, ("side", "blk"), pairs)

    def paired(value, axis, hop):
        return lax.ppermute(value, axis, [(at, at ^ hop) for at in range(lax.axis_size(axis))])

    place = jnp.stack([lax.axis_index("blk"), lax.axis_index("grp")]).astype(jnp.int32)
    straight, *diagonal = [across(source, hop) for hop in range(0, blks, 2)]
    order, blocks = stage_blocks(block_index[0], place, adjacency[0], blks, groups, tiles_dev)
    straight, order = lax.optimization_barrier((straight, order))
    total_shape = jax.ShapeDtypeStruct((dest_tiles + 1, tile_rows, row_width), jnp.float32)
    total = pl.pallas_call(
        first_kernel,
        out_shape=total_shape,
        in_specs=[SMEM] + [VMEM] * 2,
        out_specs=VMEM,
        compiler_params=LIMIT,
        cost_estimate=cost_of(capacity // 4, tile_rows, row_width),
    )(order, straight, blocks)
    *diagonal, total = lax.optimization_barrier((*diagonal, total))
    others = [paired(panel, "blk", 1) for panel in (straight, *diagonal)]
    total = pl.pallas_call(
        second_kernel,
        out_shape=total_shape,
        in_specs=[SMEM] + [VMEM] * (len(diagonal) + 2),
        out_specs=VMEM,
        input_output_aliases={len(diagonal) + 2: 0},
        scratch_shapes=[
            pltpu.VMEM((len(diagonal) * tiles_dev, tile_rows, row_width), jnp.bfloat16)
        ],
        compiler_params=LIMIT,
        cost_estimate=cost_of(capacity // 4, tile_rows, row_width),
    )(order, *diagonal, blocks, total)
    *others, total = lax.optimization_barrier((*others, total))
    others_scratch = [pltpu.VMEM((len(others) * tiles_dev, tile_rows, row_width), jnp.bfloat16)]
    far_chunks = range(3, groups, 2)
    far, total = pl.pallas_call(
        functools.partial(far_kernel, tiles_dev, far_chunks),
        out_shape=[
            jax.ShapeDtypeStruct((len(far_chunks),) + part, jnp.bfloat16),
            total_shape,
        ],
        in_specs=[SMEM] + [VMEM] * (len(others) + 2),
        out_specs=[VMEM, VMEM],
        input_output_aliases={len(others) + 2: 1},
        scratch_shapes=others_scratch,
        compiler_params=LIMIT,
        cost_estimate=cost_of(capacity // 8, tile_rows, row_width),
    )(order, *others, blocks, total)
    far_arrived = paired(far, "grp", 1)
    mine_chunks = range(2, groups, 2)
    own, near, mine = pl.pallas_call(
        functools.partial(near_kernel, tiles_dev, mine_chunks),
        out_shape=[
            jax.ShapeDtypeStruct(part, jnp.float32),
            jax.ShapeDtypeStruct(part, jnp.bfloat16),
            jax.ShapeDtypeStruct((len(mine_chunks),) + part, jnp.float32),
        ],
        in_specs=[SMEM] + [VMEM] * (len(others) + 2),
        out_specs=[VMEM] * 3,
        scratch_shapes=others_scratch,
        compiler_params=LIMIT,
        cost_estimate=cost_of(capacity // 2, tile_rows, row_width),
    )(order, *others, blocks, total)
    summed = own
    for at, hop in enumerate(mine_chunks):
        pair = (mine[at] + far_arrived[at].astype(jnp.float32)).astype(jnp.bfloat16)
        near, pair = lax.optimization_barrier((near, pair))
        summed = summed + paired(pair, "grp", hop).astype(jnp.float32)
    summed = summed + paired(near, "grp", 1).astype(jnp.float32)
    inverse = lax.rsqrt(degrees.astype(jnp.float32))
    return (summed.reshape(1, row_count, row_width) * inverse[..., None]).astype(jnp.bfloat16)


def solution(mesh):
    placed = (
        P("side", ("grp", "blk"), None),
        P("side", ("grp", "blk")),
        P("side", ("grp", "blk")),
        P("side", ("grp", "blk"), None, None),
        P("side", None, ("grp", "blk")),
    )
    return jax.shard_map(
        shards,
        mesh=mesh,
        in_specs=placed,
        out_specs=P("side", ("grp", "blk"), None),
        check_vma=False,
    )
```

```python
import functools

import jax
import jax.numpy as jnp
from jax import lax
from jax.experimental import pallas as pl
from jax.experimental.pallas import tpu as pltpu
from jax.sharding import PartitionSpec as P

UNROLL = 8
STAGES = 4
VMEM = pl.BlockSpec(memory_space=pltpu.VMEM)
SMEM = pl.BlockSpec(memory_space=pltpu.SMEM)
HBM = pl.BlockSpec(memory_space=pltpu.HBM)
LIMIT = pltpu.CompilerParams(vmem_limit_bytes=48 * 1024 * 1024)


def in_hbm(*arrays):
    return [pltpu.with_memory_space_constraint(array, pltpu.HBM) for array in arrays]


def split(value, size):
    if size & (size - 1) == 0:
        return value >> (size.bit_length() - 1), value & (size - 1)
    return value // size, value % size


def scale_kernel(exps_hbm, degrees_hbm, codes_hbm, rows, exps_ref, degrees, codes, sems):
    pairs = [(exps_hbm, exps_ref), (degrees_hbm, degrees), (codes_hbm, codes)]
    fetches = [
        pltpu.make_async_copy(held, wanted, sems.at[at])
        for at, (held, wanted) in enumerate(pairs)
    ]
    for fetch in fetches:
        fetch.start()
    fetches[0].wait()
    fetches[1].wait()
    tiles_dev, tile_rows, row_width = rows.shape
    inverse = lax.rsqrt(degrees[...].astype(jnp.float32))
    factors = []
    for tile in range(tiles_dev):
        lanes = inverse[:, tile * tile_rows : (tile + 1) * tile_rows]
        scale = jnp.exp2(jnp.full(lanes.shape, exps_ref[0, tile], jnp.int32).astype(jnp.float32))
        factors.append(jnp.broadcast_to(lanes * scale, (row_width, tile_rows)).T)
    fetches[2].wait()
    for tile, factor in enumerate(factors):
        rows[tile] = (codes[tile].astype(jnp.float32) * factor).astype(rows.dtype)


def scale_rows(codes, exps, degrees):
    return pl.pallas_call(
        scale_kernel,
        out_shape=jax.ShapeDtypeStruct(codes.shape, jnp.bfloat16),
        in_specs=[HBM] * 3,
        out_specs=VMEM,
        scratch_shapes=[
            pltpu.SMEM(exps.shape, exps.dtype),
            pltpu.VMEM(degrees.shape, degrees.dtype),
            pltpu.VMEM(codes.shape, codes.dtype),
            pltpu.SemaphoreType.DMA((3,)),
        ],
        compiler_params=LIMIT,
        cost_estimate=pl.CostEstimate(
            flops=codes.size, bytes_accessed=4 * codes.size, transcendentals=0
        ),
    )(*in_hbm(exps, degrees, codes))


def stage_kernel(
    blks, groups, tiles_dev, place_ref, index_hbm, blocks_hbm, order_ref, blocks, index_ref, sems
):
    fetch = pltpu.make_async_copy(index_hbm, index_ref, sems.at[0])
    fetch.start()
    copy = pltpu.make_async_copy(blocks_hbm, blocks, sems.at[1])
    copy.start()
    fetch.wait()
    my_blk = place_ref[0]
    my_grp = place_ref[1]
    capacity = index_ref.shape[1]
    source_tiles = blks * tiles_dev
    late = blks // 2 - 1

    def enlist(slot, nexts):
        target = index_ref[0, slot]
        origin = index_ref[1, slot]
        hop, row = split(origin, tiles_dev)
        chunk, tile = split(target, tiles_dev)
        hop = hop ^ my_blk
        chunk = chunk ^ my_grp
        odd = hop & 1
        far = (chunk >= 2) & ((chunk & 1) == 1)
        stage = jnp.where(hop == 0, 0, jnp.where(far, 1 + odd, 3))
        stage = jnp.where(origin < source_tiles, stage, STAGES)
        panel = hop >> 1
        panel = jnp.where(odd == 1, panel, jnp.where(stage == 3, panel + late, jnp.maximum(panel - 1, 0)))
        word = pack(slot, panel * tiles_dev + row, chunk * tiles_dev + tile)
        where = jnp.int32(0)
        for at, position in enumerate(nexts):
            where = jnp.where(stage == at, position, where)
        order_ref[stage, where] = word
        return tuple(
            position + (stage == at).astype(jnp.int32) for at, position in enumerate(nexts)
        )

    ends = lax.fori_loop(0, capacity, enlist, (jnp.int32(0),) * STAGES, unroll=8)
    spare = pack(0, 0, groups * tiles_dev)
    for at, end in enumerate(ends):
        for extra in range(UNROLL):
            order_ref[at, end + extra] = spare
        order_ref[at, capacity + UNROLL] = split(end + (UNROLL - 1), UNROLL)[0]
    copy.wait()


def pack(slot, row, target):
    return (slot << 16) | (row << 8) | target


def unpack(word):
    return word >> 16, (word >> 8) & 255, word & 255


def stage_blocks(index, place, blocks, blks, groups, tiles_dev):
    capacity = blocks.shape[0]
    assert blks * tiles_dev < 256 and groups * tiles_dev < 256 and capacity < 2**15
    return pl.pallas_call(
        functools.partial(stage_kernel, blks, groups, tiles_dev),
        out_shape=[
            jax.ShapeDtypeStruct((STAGES + 1, capacity + 2 * UNROLL), jnp.int32),
            jax.ShapeDtypeStruct(blocks.shape, blocks.dtype),
        ],
        in_specs=[SMEM, HBM, HBM],
        out_specs=[SMEM, VMEM],
        scratch_shapes=[
            pltpu.SMEM(index.shape, index.dtype),
            pltpu.SemaphoreType.DMA((2,)),
        ],
        compiler_params=LIMIT,
        cost_estimate=pl.CostEstimate(flops=0, bytes_accessed=0, transcendentals=0),
    )(place, *in_hbm(index, blocks))


def add_products(stage, order_ref, blocks, source, total):
    @pl.loop(0, order_ref[stage, order_ref.shape[1] - UNROLL])
    def _(batch):
        made = []
        for part in range(UNROLL):
            slot, row, target = unpack(order_ref[stage, batch * UNROLL + part])
            product = jnp.dot(blocks[slot], source[row], preferred_element_type=jnp.float32)
            made.append((target, product))
        for target, product in made:
            total[target] += product


def gather_panels(panels, source):
    for at, panel in enumerate(panels):
        rows = panel.shape[0]
        source[at * rows : (at + 1) * rows] = panel[...]


def first_kernel(order_ref, panel, blocks, total):
    total[...] = jnp.zeros_like(total)
    add_products(0, order_ref, blocks, panel, total)


def second_kernel(order_ref, *refs):
    *panels, blocks, _, total, source = refs
    gather_panels(panels, source)
    add_products(1, order_ref, blocks, source, total)


def far_kernel(tiles_dev, chunks, order_ref, *refs):
    *panels, blocks, _, far, total, source = refs
    gather_panels(panels, source)
    add_products(2, order_ref, blocks, source, total)
    for at, chunk in enumerate(chunks):
        far[at] = total[chunk * tiles_dev : (chunk + 1) * tiles_dev].astype(far.dtype)


def near_kernel(tiles_dev, chunks, order_ref, *refs):
    *panels, blocks, total, own, near, mine, source = refs
    gather_panels(panels, source)
    add_products(3, order_ref, blocks, source, total)
    own[...] = total[:tiles_dev]
    near[...] = total[tiles_dev : 2 * tiles_dev].astype(near.dtype)
    for at, chunk in enumerate(chunks):
        mine[at] = total[chunk * tiles_dev : (chunk + 1) * tiles_dev]


def cost_of(slots, tile_rows, row_width):
    return pl.CostEstimate(
        flops=2 * slots * tile_rows * tile_rows * row_width,
        bytes_accessed=2 * slots * tile_rows * tile_rows,
        transcendentals=0,
    )


def shards(embed_codes, embed_exps, degrees, adjacency, block_index):
    tile_rows = adjacency.shape[2]
    row_width = embed_codes.shape[2]
    row_count = embed_codes.shape[1]
    capacity = adjacency.shape[1]
    tiles_dev = row_count // tile_rows
    groups = lax.axis_size("grp")
    blks = lax.axis_size("blk")
    part = (tiles_dev, tile_rows, row_width)
    dest_tiles = groups * tiles_dev
    source = scale_rows(embed_codes.reshape(part), embed_exps, degrees)

    def across(value, hop):
        pairs = [
            (side * blks + at, (1 - side) * blks + (at ^ hop))
            for side in range(2)
            for at in range(blks)
        ]
        return lax.ppermute(value, ("side", "blk"), pairs)

    def paired(value, axis, hop):
        return lax.ppermute(value, axis, [(at, at ^ hop) for at in range(lax.axis_size(axis))])

    place = jnp.stack([lax.axis_index("blk"), lax.axis_index("grp")]).astype(jnp.int32)
    straight, *diagonal = [across(source, hop) for hop in range(0, blks, 2)]
    order, blocks = stage_blocks(block_index[0], place, adjacency[0], blks, groups, tiles_dev)
    straight, order = lax.optimization_barrier((straight, order))
    total_shape = jax.ShapeDtypeStruct((dest_tiles + 1, tile_rows, row_width), jnp.float32)
    total = pl.pallas_call(
        first_kernel,
        out_shape=total_shape,
        in_specs=[SMEM] + [VMEM] * 2,
        out_specs=VMEM,
        compiler_params=LIMIT,
        cost_estimate=cost_of(capacity // 4, tile_rows, row_width),
    )(order, straight, blocks)
    *diagonal, total = lax.optimization_barrier((*diagonal, total))
    others = [paired(panel, "blk", 1) for panel in (straight, *diagonal)]
    total = pl.pallas_call(
        second_kernel,
        out_shape=total_shape,
        in_specs=[SMEM] + [VMEM] * (len(diagonal) + 2),
        out_specs=VMEM,
        input_output_aliases={len(diagonal) + 2: 0},
        scratch_shapes=[
            pltpu.VMEM((len(diagonal) * tiles_dev, tile_rows, row_width), jnp.bfloat16)
        ],
        compiler_params=LIMIT,
        cost_estimate=cost_of(capacity // 4, tile_rows, row_width),
    )(order, *diagonal, blocks, total)
    *others, total = lax.optimization_barrier((*others, total))
    others_scratch = [pltpu.VMEM((len(others) * tiles_dev, tile_rows, row_width), jnp.bfloat16)]
    far_chunks = range(3, groups, 2)
    far, total = pl.pallas_call(
        functools.partial(far_kernel, tiles_dev, far_chunks),
        out_shape=[
            jax.ShapeDtypeStruct((len(far_chunks),) + part, jnp.bfloat16),
            total_shape,
        ],
        in_specs=[SMEM] + [VMEM] * (len(others) + 2),
        out_specs=[VMEM, VMEM],
        input_output_aliases={len(others) + 2: 1},
        scratch_shapes=others_scratch,
        compiler_params=LIMIT,
        cost_estimate=cost_of(capacity // 8, tile_rows, row_width),
    )(order, *others, blocks, total)
    far_arrived = paired(far, "grp", 1)
    mine_chunks = range(2, groups, 2)
    own, near, mine = pl.pallas_call(
        functools.partial(near_kernel, tiles_dev, mine_chunks),
        out_shape=[
            jax.ShapeDtypeStruct(part, jnp.float32),
            jax.ShapeDtypeStruct(part, jnp.bfloat16),
            jax.ShapeDtypeStruct((len(mine_chunks),) + part, jnp.float32),
        ],
        in_specs=[SMEM] + [VMEM] * (len(others) + len(diagonal) + 2),
        out_specs=[VMEM] * 3,
        scratch_shapes=[
            pltpu.VMEM(((blks - 1) * tiles_dev, tile_rows, row_width), jnp.bfloat16)
        ],
        compiler_params=LIMIT,
        cost_estimate=cost_of(capacity // 2, tile_rows, row_width),
    )(order, *others, *diagonal, blocks, total)
    summed = own
    for at, hop in enumerate(mine_chunks):
        pair = (mine[at] + far_arrived[at].astype(jnp.float32)).astype(jnp.bfloat16)
        near, pair = lax.optimization_barrier((near, pair))
        summed = summed + paired(pair, "grp", hop).astype(jnp.float32)
    summed = summed + paired(near, "grp", 1).astype(jnp.float32)
    inverse = lax.rsqrt(degrees.astype(jnp.float32))
    return (summed.reshape(1, row_count, row_width) * inverse[..., None]).astype(jnp.bfloat16)


def solution(mesh):
    placed = (
        P("side", ("grp", "blk"), None),
        P("side", ("grp", "blk")),
        P("side", ("grp", "blk")),
        P("side", ("grp", "blk"), None, None),
        P("side", None, ("grp", "blk")),
    )
    return jax.shard_map(
        shards,
        mesh=mesh,
        in_specs=placed,
        out_specs=P("side", ("grp", "blk"), None),
        check_vma=False,
    )
```

```python
import functools

import jax
import jax.numpy as jnp
from jax import lax
from jax.experimental import pallas as pl
from jax.experimental.pallas import tpu as pltpu
from jax.sharding import PartitionSpec as P

UNROLL = 8
STAGES = 4
VMEM = pl.BlockSpec(memory_space=pltpu.VMEM)
SMEM = pl.BlockSpec(memory_space=pltpu.SMEM)
HBM = pl.BlockSpec(memory_space=pltpu.HBM)
LIMIT = pltpu.CompilerParams(vmem_limit_bytes=48 * 1024 * 1024)


def in_hbm(*arrays):
    return [pltpu.with_memory_space_constraint(array, pltpu.HBM) for array in arrays]


def split(value, size):
    if size & (size - 1) == 0:
        return value >> (size.bit_length() - 1), value & (size - 1)
    return value // size, value % size


def scale_kernel(exps_hbm, degrees_hbm, codes_hbm, rows, exps_ref, degrees, codes, sems):
    pairs = [(exps_hbm, exps_ref), (degrees_hbm, degrees), (codes_hbm, codes)]
    fetches = [
        pltpu.make_async_copy(held, wanted, sems.at[at])
        for at, (held, wanted) in enumerate(pairs)
    ]
    for fetch in fetches:
        fetch.start()
    fetches[0].wait()
    fetches[1].wait()
    tiles_dev, tile_rows, row_width = rows.shape
    inverse = lax.rsqrt(degrees[...].astype(jnp.float32))
    factors = []
    for tile in range(tiles_dev):
        lanes = inverse[:, tile * tile_rows : (tile + 1) * tile_rows]
        scale = jnp.exp2(jnp.full(lanes.shape, exps_ref[0, tile], jnp.int32).astype(jnp.float32))
        factors.append(jnp.broadcast_to(lanes * scale, (row_width, tile_rows)).T)
    fetches[2].wait()
    for tile, factor in enumerate(factors):
        rows[tile] = (codes[tile].astype(jnp.float32) * factor).astype(rows.dtype)


def scale_rows(codes, exps, degrees):
    return pl.pallas_call(
        scale_kernel,
        out_shape=jax.ShapeDtypeStruct(codes.shape, jnp.bfloat16),
        in_specs=[HBM] * 3,
        out_specs=VMEM,
        scratch_shapes=[
            pltpu.SMEM(exps.shape, exps.dtype),
            pltpu.VMEM(degrees.shape, degrees.dtype),
            pltpu.VMEM(codes.shape, codes.dtype),
            pltpu.SemaphoreType.DMA((3,)),
        ],
        compiler_params=LIMIT,
        cost_estimate=pl.CostEstimate(
            flops=codes.size, bytes_accessed=4 * codes.size, transcendentals=0
        ),
    )(*in_hbm(exps, degrees, codes))


def stage_kernel(
    blks, groups, tiles_dev, place_ref, index_hbm, blocks_hbm, order_ref, blocks, index_ref, sems
):
    fetch = pltpu.make_async_copy(index_hbm, index_ref, sems.at[0])
    fetch.start()
    copy = pltpu.make_async_copy(blocks_hbm, blocks, sems.at[1])
    copy.start()
    fetch.wait()
    my_blk = place_ref[0]
    my_grp = place_ref[1]
    capacity = index_ref.shape[1]
    source_tiles = blks * tiles_dev
    late = blks // 2 - 1

    def enlist(slot, nexts):
        target = index_ref[0, slot]
        origin = index_ref[1, slot]
        hop, row = split(origin, tiles_dev)
        chunk, tile = split(target, tiles_dev)
        hop = hop ^ my_blk
        chunk = chunk ^ my_grp
        odd = hop & 1
        far = (chunk >= 2) & ((chunk & 1) == 1)
        stage = jnp.where(hop == 0, 0, jnp.where(far, 1 + odd, 3))
        stage = jnp.where(origin < source_tiles, stage, STAGES)
        panel = hop >> 1
        panel = jnp.where(odd == 1, panel, jnp.where(stage == 3, panel + late, jnp.maximum(panel - 1, 0)))
        word = pack(slot, panel * tiles_dev + row, chunk * tiles_dev + tile)
        where = jnp.int32(0)
        for at, position in enumerate(nexts):
            where = jnp.where(stage == at, position, where)
        order_ref[stage, where] = word
        return tuple(
            position + (stage == at).astype(jnp.int32) for at, position in enumerate(nexts)
        )

    ends = lax.fori_loop(0, capacity, enlist, (jnp.int32(0),) * STAGES, unroll=8)
    spare = pack(0, 0, groups * tiles_dev)
    for at, end in enumerate(ends):
        for extra in range(UNROLL):
            order_ref[at, end + extra] = spare
        order_ref[at, capacity + UNROLL] = split(end + (UNROLL - 1), UNROLL)[0]
    copy.wait()


def pack(slot, row, target):
    return (slot << 16) | (row << 8) | target


def unpack(word):
    return word >> 16, (word >> 8) & 255, word & 255


def stage_blocks(index, place, blocks, blks, groups, tiles_dev):
    capacity = blocks.shape[0]
    assert blks * tiles_dev < 256 and groups * tiles_dev < 256 and capacity < 2**15
    return pl.pallas_call(
        functools.partial(stage_kernel, blks, groups, tiles_dev),
        out_shape=[
            jax.ShapeDtypeStruct((STAGES + 1, capacity + 2 * UNROLL), jnp.int32),
            jax.ShapeDtypeStruct(blocks.shape, blocks.dtype),
        ],
        in_specs=[SMEM, HBM, HBM],
        out_specs=[SMEM, VMEM],
        scratch_shapes=[
            pltpu.SMEM(index.shape, index.dtype),
            pltpu.SemaphoreType.DMA((2,)),
        ],
        compiler_params=LIMIT,
        cost_estimate=pl.CostEstimate(flops=0, bytes_accessed=0, transcendentals=0),
    )(place, *in_hbm(index, blocks))


def add_products(stage, order_ref, blocks, source, total):
    @pl.loop(0, order_ref[stage, order_ref.shape[1] - UNROLL])
    def _(batch):
        made = []
        for part in range(UNROLL):
            slot, row, target = unpack(order_ref[stage, batch * UNROLL + part])
            product = jnp.dot(blocks[slot], source[row], preferred_element_type=jnp.float32)
            made.append((target, product))
        for target, product in made:
            total[target] += product


def gather_panels(panels, source):
    for at, panel in enumerate(panels):
        rows = panel.shape[0]
        source[at * rows : (at + 1) * rows] = panel[...]


def first_kernel(order_ref, panel, blocks, total):
    total[...] = jnp.zeros_like(total)
    add_products(0, order_ref, blocks, panel, total)


def second_kernel(order_ref, *refs):
    *panels, blocks, _, total, source = refs
    gather_panels(panels, source)
    add_products(1, order_ref, blocks, source, total)


def far_kernel(tiles_dev, chunks, order_ref, *refs):
    *panels, blocks, _, far, total, source = refs
    gather_panels(panels, source)
    add_products(2, order_ref, blocks, source, total)
    for at, chunk in enumerate(chunks):
        far[at] = total[chunk * tiles_dev : (chunk + 1) * tiles_dev].astype(far.dtype)


def near_kernel(tiles_dev, chunks, order_ref, *refs):
    *panels, blocks, total, own, near, mine, source = refs
    gather_panels(panels, source)
    add_products(3, order_ref, blocks, source, total)
    own[...] = total[:tiles_dev]
    near[...] = total[tiles_dev : 2 * tiles_dev].astype(near.dtype)
    for at, chunk in enumerate(chunks):
        mine[at] = total[chunk * tiles_dev : (chunk + 1) * tiles_dev].astype(mine.dtype)


def cost_of(slots, tile_rows, row_width):
    return pl.CostEstimate(
        flops=2 * slots * tile_rows * tile_rows * row_width,
        bytes_accessed=2 * slots * tile_rows * tile_rows,
        transcendentals=0,
    )


def shards(embed_codes, embed_exps, degrees, adjacency, block_index):
    tile_rows = adjacency.shape[2]
    row_width = embed_codes.shape[2]
    row_count = embed_codes.shape[1]
    capacity = adjacency.shape[1]
    tiles_dev = row_count // tile_rows
    groups = lax.axis_size("grp")
    blks = lax.axis_size("blk")
    part = (tiles_dev, tile_rows, row_width)
    dest_tiles = groups * tiles_dev
    source = scale_rows(embed_codes.reshape(part), embed_exps, degrees)

    def across(value, hop):
        pairs = [
            (side * blks + at, (1 - side) * blks + (at ^ hop))
            for side in range(2)
            for at in range(blks)
        ]
        return lax.ppermute(value, ("side", "blk"), pairs)

    def paired(value, axis, hop):
        return lax.ppermute(value, axis, [(at, at ^ hop) for at in range(lax.axis_size(axis))])

    place = jnp.stack([lax.axis_index("blk"), lax.axis_index("grp")]).astype(jnp.int32)
    straight, *diagonal = [across(source, hop) for hop in range(0, blks, 2)]
    order, blocks = stage_blocks(block_index[0], place, adjacency[0], blks, groups, tiles_dev)
    straight, order = lax.optimization_barrier((straight, order))
    total_shape = jax.ShapeDtypeStruct((dest_tiles + 1, tile_rows, row_width), jnp.float32)
    total = pl.pallas_call(
        first_kernel,
        out_shape=total_shape,
        in_specs=[SMEM] + [VMEM] * 2,
        out_specs=VMEM,
        compiler_params=LIMIT,
        cost_estimate=cost_of(capacity // 4, tile_rows, row_width),
    )(order, straight, blocks)
    *diagonal, total = lax.optimization_barrier((*diagonal, total))
    others = [paired(panel, "blk", 1) for panel in (straight, *diagonal)]
    total = pl.pallas_call(
        second_kernel,
        out_shape=total_shape,
        in_specs=[SMEM] + [VMEM] * (len(diagonal) + 2),
        out_specs=VMEM,
        input_output_aliases={len(diagonal) + 2: 0},
        scratch_shapes=[
            pltpu.VMEM((len(diagonal) * tiles_dev, tile_rows, row_width), jnp.bfloat16)
        ],
        compiler_params=LIMIT,
        cost_estimate=cost_of(capacity // 4, tile_rows, row_width),
    )(order, *diagonal, blocks, total)
    *others, total = lax.optimization_barrier((*others, total))
    others_scratch = [pltpu.VMEM((len(others) * tiles_dev, tile_rows, row_width), jnp.bfloat16)]
    far_chunks = range(3, groups, 2)
    far, total = pl.pallas_call(
        functools.partial(far_kernel, tiles_dev, far_chunks),
        out_shape=[
            jax.ShapeDtypeStruct((len(far_chunks),) + part, jnp.bfloat16),
            total_shape,
        ],
        in_specs=[SMEM] + [VMEM] * (len(others) + 2),
        out_specs=[VMEM, VMEM],
        input_output_aliases={len(others) + 2: 1},
        scratch_shapes=others_scratch,
        compiler_params=LIMIT,
        cost_estimate=cost_of(capacity // 8, tile_rows, row_width),
    )(order, *others, blocks, total)
    arrived = [paired(far[at], "grp", hop) for at, hop in enumerate(far_chunks)]
    mine_chunks = range(2, groups, 2)
    own, near, mine = pl.pallas_call(
        functools.partial(near_kernel, tiles_dev, mine_chunks),
        out_shape=[
            jax.ShapeDtypeStruct(part, jnp.float32),
            jax.ShapeDtypeStruct(part, jnp.bfloat16),
            jax.ShapeDtypeStruct((len(mine_chunks),) + part, jnp.bfloat16),
        ],
        in_specs=[SMEM] + [VMEM] * (len(others) + len(diagonal) + 2),
        out_specs=[VMEM] * 3,
        scratch_shapes=[
            pltpu.VMEM(((blks - 1) * tiles_dev, tile_rows, row_width), jnp.bfloat16)
        ],
        compiler_params=LIMIT,
        cost_estimate=cost_of(capacity // 2, tile_rows, row_width),
    )(order, *others, *diagonal, blocks, total)
    arrived += [paired(mine[at], "grp", hop) for at, hop in enumerate(mine_chunks)]
    arrived += [paired(near, "grp", 1)]
    summed = own
    for at, piece in enumerate(arrived):
        summed = summed + piece.astype(jnp.float32)
        if at + 1 == len(far_chunks):
            summed, *arrived[at + 1 :] = lax.optimization_barrier((summed, *arrived[at + 1 :]))
    inverse = lax.rsqrt(degrees.astype(jnp.float32))
    return (summed.reshape(1, row_count, row_width) * inverse[..., None]).astype(jnp.bfloat16)


def solution(mesh):
    placed = (
        P("side", ("grp", "blk"), None),
        P("side", ("grp", "blk")),
        P("side", ("grp", "blk")),
        P("side", ("grp", "blk"), None, None),
        P("side", None, ("grp", "blk")),
    )
    return jax.shard_map(
        shards,
        mesh=mesh,
        in_specs=placed,
        out_specs=P("side", ("grp", "blk"), None),
        check_vma=False,
    )
```

```python
import functools

import jax
import jax.numpy as jnp
from jax import lax
from jax.experimental import pallas as pl
from jax.experimental.pallas import tpu as pltpu
from jax.sharding import PartitionSpec as P

UNROLL = 8
STAGES = 3
VMEM = pl.BlockSpec(memory_space=pltpu.VMEM)
SMEM = pl.BlockSpec(memory_space=pltpu.SMEM)
HBM = pl.BlockSpec(memory_space=pltpu.HBM)
LIMIT = pltpu.CompilerParams(vmem_limit_bytes=48 * 1024 * 1024)


def in_hbm(*arrays):
    return [pltpu.with_memory_space_constraint(array, pltpu.HBM) for array in arrays]


def split(value, size):
    if size & (size - 1) == 0:
        return value >> (size.bit_length() - 1), value & (size - 1)
    return value // size, value % size


def scale_kernel(exps_hbm, degrees_hbm, codes_hbm, rows, exps_ref, degrees, codes, sems):
    pairs = [(exps_hbm, exps_ref), (degrees_hbm, degrees), (codes_hbm, codes)]
    fetches = [
        pltpu.make_async_copy(held, wanted, sems.at[at])
        for at, (held, wanted) in enumerate(pairs)
    ]
    for fetch in fetches:
        fetch.start()
    fetches[0].wait()
    fetches[1].wait()
    tiles_dev, tile_rows, row_width = rows.shape
    inverse = lax.rsqrt(degrees[...].astype(jnp.float32))
    factors = []
    for tile in range(tiles_dev):
        lanes = inverse[:, tile * tile_rows : (tile + 1) * tile_rows]
        scale = jnp.exp2(jnp.full(lanes.shape, exps_ref[0, tile], jnp.int32).astype(jnp.float32))
        factors.append(jnp.broadcast_to(lanes * scale, (row_width, tile_rows)).T)
    fetches[2].wait()
    for tile, factor in enumerate(factors):
        rows[tile] = (codes[tile].astype(jnp.float32) * factor).astype(rows.dtype)


def scale_rows(codes, exps, degrees):
    return pl.pallas_call(
        scale_kernel,
        out_shape=jax.ShapeDtypeStruct(codes.shape, jnp.bfloat16),
        in_specs=[HBM] * 3,
        out_specs=VMEM,
        scratch_shapes=[
            pltpu.SMEM(exps.shape, exps.dtype),
            pltpu.VMEM(degrees.shape, degrees.dtype),
            pltpu.VMEM(codes.shape, codes.dtype),
            pltpu.SemaphoreType.DMA((3,)),
        ],
        compiler_params=LIMIT,
        cost_estimate=pl.CostEstimate(
            flops=codes.size, bytes_accessed=4 * codes.size, transcendentals=0
        ),
    )(*in_hbm(exps, degrees, codes))


def stage_kernel(
    blks, groups, tiles_dev, place_ref, index_hbm, blocks_hbm, order_ref, blocks, index_ref, sems
):
    fetch = pltpu.make_async_copy(index_hbm, index_ref, sems.at[0])
    fetch.start()
    copy = pltpu.make_async_copy(blocks_hbm, blocks, sems.at[1])
    copy.start()
    fetch.wait()
    my_blk = place_ref[0]
    capacity = index_ref.shape[1]
    source_tiles = blks * tiles_dev

    def enlist(slot, nexts):
        target = index_ref[0, slot]
        origin = index_ref[1, slot]
        hop, row = split(origin, tiles_dev)
        chunk, tile = split(target, tiles_dev)
        hop = hop ^ my_blk
        odd = hop & 1
        stage = jnp.where(hop == 0, 0, 1 + odd)
        stage = jnp.where(origin < source_tiles, stage, STAGES)
        panel = jnp.where(odd == 1, hop >> 1, jnp.maximum((hop >> 1) - 1, 0))
        word = pack(slot, panel * tiles_dev + row, chunk * tiles_dev + tile)
        where = jnp.int32(0)
        for at, position in enumerate(nexts):
            where = jnp.where(stage == at, position, where)
        order_ref[stage, where] = word
        return tuple(
            position + (stage == at).astype(jnp.int32) for at, position in enumerate(nexts)
        )

    ends = lax.fori_loop(0, capacity, enlist, (jnp.int32(0),) * STAGES, unroll=8)
    spare = pack(0, 0, groups * tiles_dev)
    for at, end in enumerate(ends):
        for extra in range(UNROLL):
            order_ref[at, end + extra] = spare
        order_ref[at, capacity + UNROLL] = split(end + (UNROLL - 1), UNROLL)[0]
    copy.wait()


def pack(slot, row, target):
    return (slot << 16) | (row << 8) | target


def unpack(word):
    return word >> 16, (word >> 8) & 255, word & 255


def stage_blocks(index, place, blocks, blks, groups, tiles_dev):
    capacity = blocks.shape[0]
    assert blks * tiles_dev < 256 and groups * tiles_dev < 256 and capacity < 2**15
    return pl.pallas_call(
        functools.partial(stage_kernel, blks, groups, tiles_dev),
        out_shape=[
            jax.ShapeDtypeStruct((STAGES + 1, capacity + 2 * UNROLL), jnp.int32),
            jax.ShapeDtypeStruct(blocks.shape, blocks.dtype),
        ],
        in_specs=[SMEM, HBM, HBM],
        out_specs=[SMEM, VMEM],
        scratch_shapes=[
            pltpu.SMEM(index.shape, index.dtype),
            pltpu.SemaphoreType.DMA((2,)),
        ],
        compiler_params=LIMIT,
        cost_estimate=pl.CostEstimate(flops=0, bytes_accessed=0, transcendentals=0),
    )(place, *in_hbm(index, blocks))


def add_products(stage, order_ref, blocks, source, total):
    @pl.loop(0, order_ref[stage, order_ref.shape[1] - UNROLL])
    def _(batch):
        made = []
        for part in range(UNROLL):
            slot, row, target = unpack(order_ref[stage, batch * UNROLL + part])
            product = jnp.dot(blocks[slot], source[row], preferred_element_type=jnp.float32)
            made.append((target, product))
        for target, product in made:
            total[target] += product


def gather_panels(panels, source):
    for at, panel in enumerate(panels):
        rows = panel.shape[0]
        source[at * rows : (at + 1) * rows] = panel[...]


def first_kernel(order_ref, panel, blocks, total):
    total[...] = jnp.zeros_like(total)
    add_products(0, order_ref, blocks, panel, total)


def second_kernel(order_ref, *refs):
    *panels, blocks, _, total, source = refs
    gather_panels(panels, source)
    add_products(1, order_ref, blocks, source, total)


def last_kernel(tiles_dev, place_ref, order_ref, *refs):
    *panels, blocks, total, own, sent, source = refs
    gather_panels(panels, source)
    add_products(2, order_ref, blocks, source, total)
    own[...] = total[pl.ds(place_ref[1] * tiles_dev, tiles_dev)]
    for chunk in range(sent.shape[0]):
        sent[chunk] = total[chunk * tiles_dev : (chunk + 1) * tiles_dev].astype(sent.dtype)


def cost_of(slots, tile_rows, row_width):
    return pl.CostEstimate(
        flops=2 * slots * tile_rows * tile_rows * row_width,
        bytes_accessed=2 * slots * tile_rows * tile_rows,
        transcendentals=0,
    )


def shards(embed_codes, embed_exps, degrees, adjacency, block_index):
    tile_rows = adjacency.shape[2]
    row_width = embed_codes.shape[2]
    row_count = embed_codes.shape[1]
    capacity = adjacency.shape[1]
    tiles_dev = row_count // tile_rows
    groups = lax.axis_size("grp")
    blks = lax.axis_size("blk")
    part = (tiles_dev, tile_rows, row_width)
    dest_tiles = groups * tiles_dev
    source = scale_rows(embed_codes.reshape(part), embed_exps, degrees)

    def across(value, hop):
        pairs = [
            (side * blks + at, (1 - side) * blks + (at ^ hop))
            for side in range(2)
            for at in range(blks)
        ]
        return lax.ppermute(value, ("side", "blk"), pairs)

    def paired(value, axis, hop):
        return lax.ppermute(value, axis, [(at, at ^ hop) for at in range(lax.axis_size(axis))])

    place = jnp.stack([lax.axis_index("blk"), lax.axis_index("grp")]).astype(jnp.int32)
    straight, *diagonal = [across(source, hop) for hop in range(0, blks, 2)]
    order, blocks = stage_blocks(block_index[0], place, adjacency[0], blks, groups, tiles_dev)
    straight, order = lax.optimization_barrier((straight, order))
    total_shape = jax.ShapeDtypeStruct((dest_tiles + 1, tile_rows, row_width), jnp.float32)
    total = pl.pallas_call(
        first_kernel,
        out_shape=total_shape,
        in_specs=[SMEM] + [VMEM] * 2,
        out_specs=VMEM,
        compiler_params=LIMIT,
        cost_estimate=cost_of(capacity // 4, tile_rows, row_width),
    )(order, straight, blocks)
    *diagonal, total = lax.optimization_barrier((*diagonal, total))
    others = [paired(panel, "blk", 1) for panel in (straight, *diagonal)]
    total = pl.pallas_call(
        second_kernel,
        out_shape=total_shape,
        in_specs=[SMEM] + [VMEM] * (len(diagonal) + 2),
        out_specs=VMEM,
        input_output_aliases={len(diagonal) + 2: 0},
        scratch_shapes=[
            pltpu.VMEM((len(diagonal) * tiles_dev, tile_rows, row_width), jnp.bfloat16)
        ],
        compiler_params=LIMIT,
        cost_estimate=cost_of(capacity // 4, tile_rows, row_width),
    )(order, *diagonal, blocks, total)
    *others, total = lax.optimization_barrier((*others, total))
    others_scratch = [pltpu.VMEM((len(others) * tiles_dev, tile_rows, row_width), jnp.bfloat16)]
    own, sent = pl.pallas_call(
        functools.partial(last_kernel, tiles_dev),
        out_shape=[
            jax.ShapeDtypeStruct(part, jnp.float32),
            jax.ShapeDtypeStruct((groups,) + part, jnp.bfloat16),
        ],
        in_specs=[SMEM, SMEM] + [VMEM] * (len(others) + 2),
        out_specs=[VMEM] * 2,
        scratch_shapes=others_scratch,
        compiler_params=LIMIT,
        cost_estimate=cost_of(capacity // 2, tile_rows, row_width),
    )(place, order, *others, blocks, total)
    arrived = lax.all_to_all(sent, "grp", split_axis=0, concat_axis=0)
    mine = jnp.arange(groups)[:, None, None, None] == lax.axis_index("grp")
    summed = own + jnp.sum(jnp.where(mine, 0.0, arrived.astype(jnp.float32)), axis=0)
    inverse = lax.rsqrt(degrees.astype(jnp.float32))
    return (summed.reshape(1, row_count, row_width) * inverse[..., None]).astype(jnp.bfloat16)


def solution(mesh):
    placed = (
        P("side", ("grp", "blk"), None),
        P("side", ("grp", "blk")),
        P("side", ("grp", "blk")),
        P("side", ("grp", "blk"), None, None),
        P("side", None, ("grp", "blk")),
    )
    return jax.shard_map(
        shards,
        mesh=mesh,
        in_specs=placed,
        out_specs=P("side", ("grp", "blk"), None),
        check_vma=False,
    )
```

```python
import functools

import jax
import jax.numpy as jnp
from jax import lax
from jax.experimental import pallas as pl
from jax.experimental.pallas import tpu as pltpu
from jax.sharding import PartitionSpec as P

UNROLL = 8
STAGES = 4
VMEM = pl.BlockSpec(memory_space=pltpu.VMEM)
SMEM = pl.BlockSpec(memory_space=pltpu.SMEM)
HBM = pl.BlockSpec(memory_space=pltpu.HBM)
LIMIT = pltpu.CompilerParams(vmem_limit_bytes=48 * 1024 * 1024)


def in_hbm(*arrays):
    return [pltpu.with_memory_space_constraint(array, pltpu.HBM) for array in arrays]


def split(value, size):
    if size & (size - 1) == 0:
        return value >> (size.bit_length() - 1), value & (size - 1)
    return value // size, value % size


def scale_kernel(exps_hbm, degrees_hbm, codes_hbm, rows, exps_ref, degrees, codes, sems):
    pairs = [(exps_hbm, exps_ref), (degrees_hbm, degrees), (codes_hbm, codes)]
    fetches = [
        pltpu.make_async_copy(held, wanted, sems.at[at])
        for at, (held, wanted) in enumerate(pairs)
    ]
    for fetch in fetches:
        fetch.start()
    fetches[0].wait()
    fetches[1].wait()
    tiles_dev, tile_rows, row_width = rows.shape
    inverse = lax.rsqrt(degrees[...].astype(jnp.float32))
    factors = []
    for tile in range(tiles_dev):
        lanes = inverse[:, tile * tile_rows : (tile + 1) * tile_rows]
        scale = jnp.exp2(jnp.full(lanes.shape, exps_ref[0, tile], jnp.int32).astype(jnp.float32))
        factors.append(jnp.broadcast_to(lanes * scale, (row_width, tile_rows)).T)
    fetches[2].wait()
    for tile, factor in enumerate(factors):
        rows[tile] = (codes[tile].astype(jnp.float32) * factor).astype(rows.dtype)


def scale_rows(codes, exps, degrees):
    return pl.pallas_call(
        scale_kernel,
        out_shape=jax.ShapeDtypeStruct(codes.shape, jnp.bfloat16),
        in_specs=[HBM] * 3,
        out_specs=VMEM,
        scratch_shapes=[
            pltpu.SMEM(exps.shape, exps.dtype),
            pltpu.VMEM(degrees.shape, degrees.dtype),
            pltpu.VMEM(codes.shape, codes.dtype),
            pltpu.SemaphoreType.DMA((3,)),
        ],
        compiler_params=LIMIT,
        cost_estimate=pl.CostEstimate(
            flops=codes.size, bytes_accessed=4 * codes.size, transcendentals=0
        ),
    )(*in_hbm(exps, degrees, codes))


def stage_kernel(
    blks, groups, tiles_dev, place_ref, index_hbm, blocks_hbm, order_ref, blocks, index_ref, sems
):
    fetch = pltpu.make_async_copy(index_hbm, index_ref, sems.at[0])
    fetch.start()
    copy = pltpu.make_async_copy(blocks_hbm, blocks, sems.at[1])
    copy.start()
    fetch.wait()
    my_blk = place_ref[0]
    my_grp = place_ref[1]
    capacity = index_ref.shape[1]
    source_tiles = blks * tiles_dev
    half = blks // 2

    def enlist(slot, nexts):
        target = index_ref[0, slot]
        origin = index_ref[1, slot]
        hop, row = split(origin, tiles_dev)
        chunk, tile = split(target, tiles_dev)
        hop = hop ^ my_blk
        chunk = chunk ^ my_grp
        rank = half - 1 - (hop >> 1)
        odd = hop & 1
        far = (chunk >= 2) & ((chunk & 1) == 1)
        first = (odd == 0) & (rank == 0)
        last = (odd == 1) & (rank > 0)
        stage = jnp.where(first, 0, jnp.where(far, jnp.where(last, 2, 1), 3))
        stage = jnp.where(origin < source_tiles, stage, STAGES)
        panel = jnp.where(odd == 1, jnp.where(rank == 0, half - 1, rank - 1), rank - 1)
        panel = jnp.where(last & (stage == 3), panel + half, jnp.maximum(panel, 0))
        word = pack(slot, panel * tiles_dev + row, chunk * tiles_dev + tile)
        where = jnp.int32(0)
        for at, position in enumerate(nexts):
            where = jnp.where(stage == at, position, where)
        order_ref[stage, where] = word
        return tuple(
            position + (stage == at).astype(jnp.int32) for at, position in enumerate(nexts)
        )

    ends = lax.fori_loop(0, capacity, enlist, (jnp.int32(0),) * STAGES, unroll=8)
    spare = pack(0, 0, groups * tiles_dev)
    for at, end in enumerate(ends):
        for extra in range(UNROLL):
            order_ref[at, end + extra] = spare
        order_ref[at, capacity + UNROLL] = split(end + (UNROLL - 1), UNROLL)[0]
    copy.wait()


def pack(slot, row, target):
    return (slot << 16) | (row << 8) | target


def unpack(word):
    return word >> 16, (word >> 8) & 255, word & 255


def stage_blocks(index, place, blocks, blks, groups, tiles_dev):
    capacity = blocks.shape[0]
    assert blks * tiles_dev < 256 and groups * tiles_dev < 256 and capacity < 2**15
    return pl.pallas_call(
        functools.partial(stage_kernel, blks, groups, tiles_dev),
        out_shape=[
            jax.ShapeDtypeStruct((STAGES + 1, capacity + 2 * UNROLL), jnp.int32),
            jax.ShapeDtypeStruct(blocks.shape, blocks.dtype),
        ],
        in_specs=[SMEM, HBM, HBM],
        out_specs=[SMEM, VMEM],
        scratch_shapes=[
            pltpu.SMEM(index.shape, index.dtype),
            pltpu.SemaphoreType.DMA((2,)),
        ],
        compiler_params=LIMIT,
        cost_estimate=pl.CostEstimate(flops=0, bytes_accessed=0, transcendentals=0),
    )(place, *in_hbm(index, blocks))


def add_products(stage, order_ref, blocks, source, total):
    @pl.loop(0, order_ref[stage, order_ref.shape[1] - UNROLL])
    def _(batch):
        made = []
        for part in range(UNROLL):
            slot, row, target = unpack(order_ref[stage, batch * UNROLL + part])
            product = jnp.dot(blocks[slot], source[row], preferred_element_type=jnp.float32)
            made.append((target, product))
        for target, product in made:
            total[target] += product


def gather_panels(panels, source):
    for at, panel in enumerate(panels):
        rows = panel.shape[0]
        source[at * rows : (at + 1) * rows] = panel[...]


def first_kernel(order_ref, panel, blocks, total):
    total[...] = jnp.zeros_like(total)
    add_products(0, order_ref, blocks, panel, total)


def second_kernel(order_ref, *refs):
    *panels, blocks, _, total, source = refs
    gather_panels(panels, source)
    add_products(1, order_ref, blocks, source, total)


def far_kernel(tiles_dev, chunks, order_ref, *refs):
    *panels, blocks, _, far, total, source = refs
    gather_panels(panels, source)
    add_products(2, order_ref, blocks, source, total)
    for at, chunk in enumerate(chunks):
        far[at] = total[chunk * tiles_dev : (chunk + 1) * tiles_dev].astype(far.dtype)


def near_kernel(tiles_dev, chunks, order_ref, *refs):
    *panels, blocks, total, own, near, mine, source = refs
    gather_panels(panels, source)
    add_products(3, order_ref, blocks, source, total)
    own[...] = total[:tiles_dev]
    near[...] = total[tiles_dev : 2 * tiles_dev].astype(near.dtype)
    for at, chunk in enumerate(chunks):
        mine[at] = total[chunk * tiles_dev : (chunk + 1) * tiles_dev]


def cost_of(slots, tile_rows, row_width):
    return pl.CostEstimate(
        flops=2 * slots * tile_rows * tile_rows * row_width,
        bytes_accessed=2 * slots * tile_rows * tile_rows,
        transcendentals=0,
    )


def shards(embed_codes, embed_exps, degrees, adjacency, block_index):
    tile_rows = adjacency.shape[2]
    row_width = embed_codes.shape[2]
    row_count = embed_codes.shape[1]
    capacity = adjacency.shape[1]
    tiles_dev = row_count // tile_rows
    groups = lax.axis_size("grp")
    blks = lax.axis_size("blk")
    part = (tiles_dev, tile_rows, row_width)
    dest_tiles = groups * tiles_dev
    source = scale_rows(embed_codes.reshape(part), embed_exps, degrees)

    def across(value, hop):
        pairs = [
            (side * blks + at, (1 - side) * blks + (at ^ hop))
            for side in range(2)
            for at in range(blks)
        ]
        return lax.ppermute(value, ("side", "blk"), pairs)

    def paired(value, axis, hop):
        return lax.ppermute(value, axis, [(at, at ^ hop) for at in range(lax.axis_size(axis))])

    place = jnp.stack([lax.axis_index("blk"), lax.axis_index("grp")]).astype(jnp.int32)
    early, *middle = [across(source, hop) for hop in reversed(range(0, blks, 2))]
    order, blocks = stage_blocks(block_index[0], place, adjacency[0], blks, groups, tiles_dev)
    early, order = lax.optimization_barrier((early, order))
    total_shape = jax.ShapeDtypeStruct((dest_tiles + 1, tile_rows, row_width), jnp.float32)
    total = pl.pallas_call(
        first_kernel,
        out_shape=total_shape,
        in_specs=[SMEM] + [VMEM] * 2,
        out_specs=VMEM,
        compiler_params=LIMIT,
        cost_estimate=cost_of(capacity // 4, tile_rows, row_width),
    )(order, early, blocks)
    other = paired(early, "blk", 1)
    *middle, total = lax.optimization_barrier((*middle, total))
    last = [paired(panel, "blk", 1) for panel in middle]
    middle += [other]
    total = pl.pallas_call(
        second_kernel,
        out_shape=total_shape,
        in_specs=[SMEM] + [VMEM] * (len(middle) + 2),
        out_specs=VMEM,
        input_output_aliases={len(middle) + 2: 0},
        scratch_shapes=[
            pltpu.VMEM((len(middle) * tiles_dev, tile_rows, row_width), jnp.bfloat16)
        ],
        compiler_params=LIMIT,
        cost_estimate=cost_of(capacity // 4, tile_rows, row_width),
    )(order, *middle, blocks, total)
    *last, total = lax.optimization_barrier((*last, total))
    far_chunks = range(3, groups, 2)
    far, total = pl.pallas_call(
        functools.partial(far_kernel, tiles_dev, far_chunks),
        out_shape=[
            jax.ShapeDtypeStruct((len(far_chunks),) + part, jnp.bfloat16),
            total_shape,
        ],
        in_specs=[SMEM] + [VMEM] * (len(last) + 2),
        out_specs=[VMEM, VMEM],
        input_output_aliases={len(last) + 2: 1},
        scratch_shapes=[
            pltpu.VMEM((len(last) * tiles_dev, tile_rows, row_width), jnp.bfloat16)
        ],
        compiler_params=LIMIT,
        cost_estimate=cost_of(capacity // 8, tile_rows, row_width),
    )(order, *last, blocks, total)
    far_arrived = paired(far, "grp", 1)
    mine_chunks = range(2, groups, 2)
    own, near, mine = pl.pallas_call(
        functools.partial(near_kernel, tiles_dev, mine_chunks),
        out_shape=[
            jax.ShapeDtypeStruct(part, jnp.float32),
            jax.ShapeDtypeStruct(part, jnp.bfloat16),
            jax.ShapeDtypeStruct((len(mine_chunks),) + part, jnp.float32),
        ],
        in_specs=[SMEM] + [VMEM] * (len(middle) + len(last) + 2),
        out_specs=[VMEM] * 3,
        scratch_shapes=[
            pltpu.VMEM(((blks - 1) * tiles_dev, tile_rows, row_width), jnp.bfloat16)
        ],
        compiler_params=LIMIT,
        cost_estimate=cost_of(capacity // 2, tile_rows, row_width),
    )(order, *middle, *last, blocks, total)
    summed = own
    for at, hop in enumerate(mine_chunks):
        pair = (mine[at] + far_arrived[at].astype(jnp.float32)).astype(jnp.bfloat16)
        near, pair = lax.optimization_barrier((near, pair))
        summed = summed + paired(pair, "grp", hop).astype(jnp.float32)
    summed = summed + paired(near, "grp", 1).astype(jnp.float32)
    inverse = lax.rsqrt(degrees.astype(jnp.float32))
    return (summed.reshape(1, row_count, row_width) * inverse[..., None]).astype(jnp.bfloat16)


def solution(mesh):
    placed = (
        P("side", ("grp", "blk"), None),
        P("side", ("grp", "blk")),
        P("side", ("grp", "blk")),
        P("side", ("grp", "blk"), None, None),
        P("side", None, ("grp", "blk")),
    )
    return jax.shard_map(
        shards,
        mesh=mesh,
        in_specs=placed,
        out_specs=P("side", ("grp", "blk"), None),
        check_vma=False,
    )
```

```python
import functools

import jax
import jax.numpy as jnp
from jax import lax
from jax.experimental import pallas as pl
from jax.experimental.pallas import tpu as pltpu
from jax.sharding import PartitionSpec as P

UNROLL = 8
STAGES = 3
VMEM = pl.BlockSpec(memory_space=pltpu.VMEM)
SMEM = pl.BlockSpec(memory_space=pltpu.SMEM)
HBM = pl.BlockSpec(memory_space=pltpu.HBM)
LIMIT = pltpu.CompilerParams(vmem_limit_bytes=48 * 1024 * 1024)


def in_hbm(*arrays):
    return [pltpu.with_memory_space_constraint(array, pltpu.HBM) for array in arrays]


def split(value, size):
    if size & (size - 1) == 0:
        return value >> (size.bit_length() - 1), value & (size - 1)
    return value // size, value % size


def scale_kernel(exps_hbm, degrees_hbm, codes_hbm, rows, exps_ref, degrees, codes, sems):
    pairs = [(exps_hbm, exps_ref), (degrees_hbm, degrees), (codes_hbm, codes)]
    fetches = [
        pltpu.make_async_copy(held, wanted, sems.at[at])
        for at, (held, wanted) in enumerate(pairs)
    ]
    for fetch in fetches:
        fetch.start()
    fetches[0].wait()
    fetches[1].wait()
    tiles_dev, tile_rows, row_width = rows.shape
    inverse = lax.rsqrt(degrees[...].astype(jnp.float32))
    factors = []
    for tile in range(tiles_dev):
        lanes = inverse[:, tile * tile_rows : (tile + 1) * tile_rows]
        scale = jnp.exp2(jnp.full(lanes.shape, exps_ref[0, tile], jnp.int32).astype(jnp.float32))
        factors.append(jnp.broadcast_to(lanes * scale, (row_width, tile_rows)).T)
    fetches[2].wait()
    for tile, factor in enumerate(factors):
        rows[tile] = (codes[tile].astype(jnp.float32) * factor).astype(rows.dtype)


def scale_rows(codes, exps, degrees):
    return pl.pallas_call(
        scale_kernel,
        out_shape=jax.ShapeDtypeStruct(codes.shape, jnp.bfloat16),
        in_specs=[HBM] * 3,
        out_specs=VMEM,
        scratch_shapes=[
            pltpu.SMEM(exps.shape, exps.dtype),
            pltpu.VMEM(degrees.shape, degrees.dtype),
            pltpu.VMEM(codes.shape, codes.dtype),
            pltpu.SemaphoreType.DMA((3,)),
        ],
        compiler_params=LIMIT,
        cost_estimate=pl.CostEstimate(
            flops=codes.size, bytes_accessed=4 * codes.size, transcendentals=0
        ),
    )(*in_hbm(exps, degrees, codes))


def stage_kernel(
    blks, groups, tiles_dev, place_ref, index_hbm, blocks_hbm, order_ref, blocks, index_ref, sems
):
    fetch = pltpu.make_async_copy(index_hbm, index_ref, sems.at[0])
    fetch.start()
    copy = pltpu.make_async_copy(blocks_hbm, blocks, sems.at[1])
    copy.start()
    fetch.wait()
    my_blk = place_ref[0]
    my_grp = place_ref[1]
    capacity = index_ref.shape[1]
    source_tiles = blks * tiles_dev
    half = blks // 2

    def enlist(slot, nexts):
        target = index_ref[0, slot]
        origin = index_ref[1, slot]
        hop, row = split(origin, tiles_dev)
        chunk, tile = split(target, tiles_dev)
        hop = hop ^ my_blk
        chunk = chunk ^ my_grp
        rank = half - 1 - (hop >> 1)
        odd = hop & 1
        far = (chunk >= 2) & ((chunk & 1) == 1)
        stage = jnp.where(far, jnp.minimum(rank + odd, 1), 2)
        stage = jnp.where(origin < source_tiles, stage, STAGES)
        panel = rank + odd * half - (stage == 1).astype(jnp.int32)
        kept = jnp.where(far, (chunk - 3) >> 1, chunk)
        word = pack(slot, panel * tiles_dev + row, kept * tiles_dev + tile)
        where = jnp.int32(0)
        for at, position in enumerate(nexts):
            where = jnp.where(stage == at, position, where)
        order_ref[stage, where] = word
        return tuple(
            position + (stage == at).astype(jnp.int32) for at, position in enumerate(nexts)
        )

    ends = lax.fori_loop(0, capacity, enlist, (jnp.int32(0),) * STAGES, unroll=8)
    far_tiles = (groups // 2 - 1) * tiles_dev
    spares = [pack(0, 0, far_tiles)] * 2 + [pack(0, 0, groups * tiles_dev)]
    for at, (end, spare) in enumerate(zip(ends, spares)):
        for extra in range(UNROLL):
            order_ref[at, end + extra] = spare
        order_ref[at, capacity + UNROLL] = split(end + (UNROLL - 1), UNROLL)[0]
    copy.wait()


def pack(slot, row, target):
    return (slot << 16) | (row << 8) | target


def unpack(word):
    return word >> 16, (word >> 8) & 255, word & 255


def stage_blocks(index, place, blocks, blks, groups, tiles_dev):
    capacity = blocks.shape[0]
    assert blks * tiles_dev < 256 and groups * tiles_dev < 256 and capacity < 2**15
    return pl.pallas_call(
        functools.partial(stage_kernel, blks, groups, tiles_dev),
        out_shape=[
            jax.ShapeDtypeStruct((STAGES + 1, capacity + 2 * UNROLL), jnp.int32),
            jax.ShapeDtypeStruct(blocks.shape, blocks.dtype),
        ],
        in_specs=[SMEM, HBM, HBM],
        out_specs=[SMEM, VMEM],
        scratch_shapes=[
            pltpu.SMEM(index.shape, index.dtype),
            pltpu.SemaphoreType.DMA((2,)),
        ],
        compiler_params=LIMIT,
        cost_estimate=pl.CostEstimate(flops=0, bytes_accessed=0, transcendentals=0),
    )(place, *in_hbm(index, blocks))


def add_products(stage, order_ref, blocks, source, total):
    @pl.loop(0, order_ref[stage, order_ref.shape[1] - UNROLL])
    def _(batch):
        made = []
        for part in range(UNROLL):
            slot, row, target = unpack(order_ref[stage, batch * UNROLL + part])
            product = jnp.dot(blocks[slot], source[row], preferred_element_type=jnp.float32)
            made.append((target, product))
        for target, product in made:
            total[target] += product


def gather_panels(panels, source):
    for at, panel in enumerate(panels):
        rows = panel.shape[0]
        source[at * rows : (at + 1) * rows] = panel[...]


def early_kernel(order_ref, panel, blocks, total):
    total[...] = jnp.zeros_like(total)
    add_products(0, order_ref, blocks, panel, total)


def far_kernel(order_ref, *refs):
    *panels, blocks, total, far, source = refs
    gather_panels(panels, source)
    add_products(1, order_ref, blocks, source, total)
    far[...] = total[: far.shape[0]].astype(far.dtype)


def rest_kernel(tiles_dev, chunks, order_ref, *refs):
    *panels, blocks, own, near, mine, source, total = refs
    gather_panels(panels, source)
    total[...] = jnp.zeros_like(total)
    add_products(2, order_ref, blocks, source, total)
    own[...] = total[:tiles_dev]
    near[...] = total[tiles_dev : 2 * tiles_dev].astype(near.dtype)
    for at, chunk in enumerate(chunks):
        mine[at] = total[chunk * tiles_dev : (chunk + 1) * tiles_dev]


def cost_of(slots, tile_rows, row_width):
    return pl.CostEstimate(
        flops=2 * slots * tile_rows * tile_rows * row_width,
        bytes_accessed=2 * slots * tile_rows * tile_rows,
        transcendentals=0,
    )


def shards(embed_codes, embed_exps, degrees, adjacency, block_index):
    tile_rows = adjacency.shape[2]
    row_width = embed_codes.shape[2]
    row_count = embed_codes.shape[1]
    capacity = adjacency.shape[1]
    tiles_dev = row_count // tile_rows
    groups = lax.axis_size("grp")
    blks = lax.axis_size("blk")
    part = (tiles_dev, tile_rows, row_width)
    dest_tiles = groups * tiles_dev
    source = scale_rows(embed_codes.reshape(part), embed_exps, degrees)

    def across(value, hop):
        pairs = [
            (side * blks + at, (1 - side) * blks + (at ^ hop))
            for side in range(2)
            for at in range(blks)
        ]
        return lax.ppermute(value, ("side", "blk"), pairs)

    def paired(value, axis, hop):
        return lax.ppermute(value, axis, [(at, at ^ hop) for at in range(lax.axis_size(axis))])

    place = jnp.stack([lax.axis_index("blk"), lax.axis_index("grp")]).astype(jnp.int32)
    early, *middle = [across(source, hop) for hop in reversed(range(0, blks, 2))]
    order, blocks = stage_blocks(block_index[0], place, adjacency[0], blks, groups, tiles_dev)
    early, order = lax.optimization_barrier((early, order))
    other = paired(early, "blk", 1)
    far_chunks, mine_chunks = range(3, groups, 2), range(2, groups, 2)
    far_tiles = len(far_chunks) * tiles_dev

    def held(count, dtype):
        return pltpu.VMEM((count, tile_rows, row_width), dtype)

    total = pl.pallas_call(
        early_kernel,
        out_shape=jax.ShapeDtypeStruct((far_tiles + 1, tile_rows, row_width), jnp.float32),
        in_specs=[SMEM] + [VMEM] * 2,
        out_specs=VMEM,
        compiler_params=LIMIT,
        cost_estimate=cost_of(capacity // 8, tile_rows, row_width),
    )(order, early, blocks)
    *middle, total = lax.optimization_barrier((*middle, total))
    panels = middle + [other] + [paired(panel, "blk", 1) for panel in middle]
    far = pl.pallas_call(
        far_kernel,
        out_shape=jax.ShapeDtypeStruct((far_tiles, tile_rows, row_width), jnp.bfloat16),
        in_specs=[SMEM] + [VMEM] * (len(panels) + 2),
        out_specs=VMEM,
        scratch_shapes=[held(len(panels) * tiles_dev, jnp.bfloat16)],
        compiler_params=LIMIT,
        cost_estimate=cost_of(capacity // 8, tile_rows, row_width),
    )(order, *panels, blocks, total)
    far, order = lax.optimization_barrier((far, order))
    far_arrived = paired(far, "grp", 1).reshape((len(far_chunks),) + part)
    panels = [early] + panels
    own, near, mine = pl.pallas_call(
        functools.partial(rest_kernel, tiles_dev, mine_chunks),
        out_shape=[
            jax.ShapeDtypeStruct(part, jnp.float32),
            jax.ShapeDtypeStruct(part, jnp.bfloat16),
            jax.ShapeDtypeStruct((len(mine_chunks),) + part, jnp.float32),
        ],
        in_specs=[SMEM] + [VMEM] * (len(panels) + 1),
        out_specs=[VMEM] * 3,
        scratch_shapes=[
            held(len(panels) * tiles_dev, jnp.bfloat16),
            held(dest_tiles + 1, jnp.float32),
        ],
        compiler_params=LIMIT,
        cost_estimate=cost_of(capacity, tile_rows, row_width),
    )(order, *panels, blocks)
    summed = own
    for at, hop in enumerate(mine_chunks):
        pair = (mine[at] + far_arrived[at].astype(jnp.float32)).astype(jnp.bfloat16)
        near, pair = lax.optimization_barrier((near, pair))
        summed = summed + paired(pair, "grp", hop).astype(jnp.float32)
    summed = summed + paired(near, "grp", 1).astype(jnp.float32)
    inverse = lax.rsqrt(degrees.astype(jnp.float32))
    return (summed.reshape(1, row_count, row_width) * inverse[..., None]).astype(jnp.bfloat16)


def solution(mesh):
    placed = (
        P("side", ("grp", "blk"), None),
        P("side", ("grp", "blk")),
        P("side", ("grp", "blk")),
        P("side", ("grp", "blk"), None, None),
        P("side", None, ("grp", "blk")),
    )
    return jax.shard_map(
        shards,
        mesh=mesh,
        in_specs=placed,
        out_specs=P("side", ("grp", "blk"), None),
        check_vma=False,
    )
```

```python
import functools

import jax
import jax.numpy as jnp
from jax import lax
from jax.experimental import pallas as pl
from jax.experimental.pallas import tpu as pltpu
from jax.sharding import PartitionSpec as P

UNROLL = 8
STAGES = 3
VMEM = pl.BlockSpec(memory_space=pltpu.VMEM)
SMEM = pl.BlockSpec(memory_space=pltpu.SMEM)
HBM = pl.BlockSpec(memory_space=pltpu.HBM)
LIMIT = pltpu.CompilerParams(vmem_limit_bytes=48 * 1024 * 1024)


def in_hbm(*arrays):
    return [pltpu.with_memory_space_constraint(array, pltpu.HBM) for array in arrays]


def split(value, size):
    if size & (size - 1) == 0:
        return value >> (size.bit_length() - 1), value & (size - 1)
    return value // size, value % size


def scale_kernel(exps_hbm, degrees_hbm, codes_hbm, rows, factors, exps_ref, degrees, codes, sems):
    pairs = [(exps_hbm, exps_ref), (degrees_hbm, degrees), (codes_hbm, codes)]
    fetches = [
        pltpu.make_async_copy(held, wanted, sems.at[at])
        for at, (held, wanted) in enumerate(pairs)
    ]
    for fetch in fetches:
        fetch.start()
    fetches[0].wait()
    fetches[1].wait()
    tiles_dev, tile_rows, row_width = rows.shape
    inverse = lax.rsqrt(degrees[...].astype(jnp.float32))
    for tile in range(tiles_dev):
        lanes = inverse[:, tile * tile_rows : (tile + 1) * tile_rows]
        factors[tile] = jnp.broadcast_to(lanes, (row_width, tile_rows)).T
    fetches[2].wait()
    for tile in range(tiles_dev):
        scale = jnp.exp2(jnp.full((1, 1), exps_ref[0, tile], jnp.int32).astype(jnp.float32))
        scaled = codes[tile].astype(jnp.float32) * scale * factors[tile]
        rows[tile] = scaled.astype(rows.dtype)


def scale_rows(codes, exps, degrees):
    return pl.pallas_call(
        scale_kernel,
        out_shape=[
            jax.ShapeDtypeStruct(codes.shape, jnp.bfloat16),
            jax.ShapeDtypeStruct(codes.shape, jnp.float32),
        ],
        in_specs=[HBM] * 3,
        out_specs=[VMEM] * 2,
        scratch_shapes=[
            pltpu.SMEM(exps.shape, exps.dtype),
            pltpu.VMEM(degrees.shape, degrees.dtype),
            pltpu.VMEM(codes.shape, codes.dtype),
            pltpu.SemaphoreType.DMA((3,)),
        ],
        compiler_params=LIMIT,
        cost_estimate=pl.CostEstimate(
            flops=codes.size, bytes_accessed=4 * codes.size, transcendentals=0
        ),
    )(*in_hbm(exps, degrees, codes))


def stage_kernel(
    blks, groups, tiles_dev, place_ref, index_hbm, blocks_hbm, order_ref, blocks, index_ref, sems
):
    fetch = pltpu.make_async_copy(index_hbm, index_ref, sems.at[0])
    fetch.start()
    copy = pltpu.make_async_copy(blocks_hbm, blocks, sems.at[1])
    copy.start()
    fetch.wait()
    my_blk = place_ref[0]
    my_grp = place_ref[1]
    capacity = index_ref.shape[1]
    source_tiles = blks * tiles_dev
    half = blks // 2

    def enlist(slot, nexts):
        target = index_ref[0, slot]
        origin = index_ref[1, slot]
        hop, row = split(origin, tiles_dev)
        chunk, tile = split(target, tiles_dev)
        hop = hop ^ my_blk
        chunk = chunk ^ my_grp
        rank = half - 1 - (hop >> 1)
        odd = hop & 1
        far = (chunk >= 2) & ((chunk & 1) == 1)
        stage = jnp.where(far, jnp.minimum(rank + odd, 1), 2)
        stage = jnp.where(origin < source_tiles, stage, STAGES)
        panel = rank + odd * half - (stage == 1).astype(jnp.int32)
        kept = jnp.where(far, (chunk - 3) >> 1, chunk)
        word = pack(slot, panel * tiles_dev + row, kept * tiles_dev + tile)
        where = jnp.int32(0)
        for at, position in enumerate(nexts):
            where = jnp.where(stage == at, position, where)
        order_ref[stage, where] = word
        return tuple(
            position + (stage == at).astype(jnp.int32) for at, position in enumerate(nexts)
        )

    ends = lax.fori_loop(0, capacity, enlist, (jnp.int32(0),) * STAGES, unroll=8)
    far_tiles = (groups // 2 - 1) * tiles_dev
    spares = [pack(0, 0, far_tiles)] * 2 + [pack(0, 0, groups * tiles_dev)]
    for at, (end, spare) in enumerate(zip(ends, spares)):
        for extra in range(UNROLL):
            order_ref[at, end + extra] = spare
        order_ref[at, capacity + UNROLL] = split(end + (UNROLL - 1), UNROLL)[0]
    copy.wait()


def pack(slot, row, target):
    return (slot << 16) | (row << 8) | target


def unpack(word):
    return word >> 16, (word >> 8) & 255, word & 255


def stage_blocks(index, place, blocks, blks, groups, tiles_dev):
    capacity = blocks.shape[0]
    assert blks * tiles_dev < 256 and groups * tiles_dev < 256 and capacity < 2**15
    return pl.pallas_call(
        functools.partial(stage_kernel, blks, groups, tiles_dev),
        out_shape=[
            jax.ShapeDtypeStruct((STAGES + 1, capacity + 2 * UNROLL), jnp.int32),
            jax.ShapeDtypeStruct(blocks.shape, blocks.dtype),
        ],
        in_specs=[SMEM, HBM, HBM],
        out_specs=[SMEM, VMEM],
        scratch_shapes=[
            pltpu.SMEM(index.shape, index.dtype),
            pltpu.SemaphoreType.DMA((2,)),
        ],
        compiler_params=LIMIT,
        cost_estimate=pl.CostEstimate(flops=0, bytes_accessed=0, transcendentals=0),
    )(place, *in_hbm(index, blocks))


def add_products(stage, order_ref, blocks, source, total):
    @pl.loop(0, order_ref[stage, order_ref.shape[1] - UNROLL])
    def _(batch):
        made = []
        for part in range(UNROLL):
            slot, row, target = unpack(order_ref[stage, batch * UNROLL + part])
            product = jnp.dot(blocks[slot], source[row], preferred_element_type=jnp.float32)
            made.append((target, product))
        for target, product in made:
            total[target] += product


def gather_panels(panels, source):
    for at, panel in enumerate(panels):
        rows = panel.shape[0]
        source[at * rows : (at + 1) * rows] = panel[...]


def early_kernel(order_ref, panel, blocks, total):
    total[...] = jnp.zeros_like(total)
    add_products(0, order_ref, blocks, panel, total)


def far_kernel(half, order_ref, *refs):
    *panels, blocks, total, far, straight, source = refs
    gather_panels(panels, source)
    add_products(1, order_ref, blocks, source, total)
    tiles_dev = half + straight.shape[1]
    for at in range(far.shape[0]):
        chunk = total.at[pl.ds(at * tiles_dev, tiles_dev)]
        far[at] = chunk[:half].astype(far.dtype)
        straight[at] = chunk[half:].astype(straight.dtype)


def rest_kernel(half, chunks, order_ref, *refs):
    *panels, blocks, own_low, own_high, near, mine, straight, source, total = refs
    gather_panels(panels, source)
    total[...] = jnp.zeros_like(total)
    add_products(2, order_ref, blocks, source, total)
    tiles_dev = near.shape[0]
    own_low[...] = total[:half]
    own_high[...] = total[half:tiles_dev]
    near[...] = total[tiles_dev : 2 * tiles_dev].astype(near.dtype)
    for at, chunk in enumerate(chunks):
        begin = chunk * tiles_dev
        mine[at] = total[begin : begin + half]
        straight[at] = total[begin + half : begin + tiles_dev].astype(straight.dtype)


def final_kernel(factors, near, own_low, own_high, *refs):
    *arrived, out_hbm, out, sems = refs
    half = own_low.shape[0]
    lows, highs = arrived[: len(arrived) // 2], arrived[len(arrived) // 2 :]
    copies = []
    for tile in range(out.shape[0]):
        own, pieces, at = (own_low, lows, tile) if tile < half else (own_high, highs, tile - half)
        value = own[at] + near[tile].astype(jnp.float32)
        for piece in pieces:
            value = value + piece[at].astype(jnp.float32)
        out[tile] = (value * factors[tile]).astype(out.dtype)
        copies.append(pltpu.make_async_copy(out.at[tile], out_hbm.at[tile], sems.at[tile]))
        copies[-1].start()
    for copy in copies:
        copy.wait()


def cost_of(slots, tile_rows, row_width):
    return pl.CostEstimate(
        flops=2 * slots * tile_rows * tile_rows * row_width,
        bytes_accessed=2 * slots * tile_rows * tile_rows,
        transcendentals=0,
    )


def shards(embed_codes, embed_exps, degrees, adjacency, block_index):
    tile_rows = adjacency.shape[2]
    row_width = embed_codes.shape[2]
    row_count = embed_codes.shape[1]
    capacity = adjacency.shape[1]
    tiles_dev = row_count // tile_rows
    groups = lax.axis_size("grp")
    blks = lax.axis_size("blk")
    part = (tiles_dev, tile_rows, row_width)
    dest_tiles = groups * tiles_dev
    source, factors = scale_rows(embed_codes.reshape(part), embed_exps, degrees)

    def across(value, hop):
        pairs = [
            (side * blks + at, (1 - side) * blks + (at ^ hop))
            for side in range(2)
            for at in range(blks)
        ]
        return lax.ppermute(value, ("side", "blk"), pairs)

    def paired(value, axis, hop):
        return lax.ppermute(value, axis, [(at, at ^ hop) for at in range(lax.axis_size(axis))])

    place = jnp.stack([lax.axis_index("blk"), lax.axis_index("grp")]).astype(jnp.int32)
    early, *middle = [across(source, hop) for hop in reversed(range(0, blks, 2))]
    order, blocks = stage_blocks(block_index[0], place, adjacency[0], blks, groups, tiles_dev)
    early, order = lax.optimization_barrier((early, order))
    other = paired(early, "blk", 1)
    far_chunks, mine_chunks = range(3, groups, 2), range(2, groups, 2)
    far_tiles = len(far_chunks) * tiles_dev

    def held(count, dtype):
        return pltpu.VMEM((count, tile_rows, row_width), dtype)

    total = pl.pallas_call(
        early_kernel,
        out_shape=jax.ShapeDtypeStruct((far_tiles + 1, tile_rows, row_width), jnp.float32),
        in_specs=[SMEM] + [VMEM] * 2,
        out_specs=VMEM,
        compiler_params=LIMIT,
        cost_estimate=cost_of(capacity // 8, tile_rows, row_width),
    )(order, early, blocks)
    *middle, total = lax.optimization_barrier((*middle, total))
    panels = middle + [other] + [paired(panel, "blk", 1) for panel in middle]
    half = tiles_dev // 2
    low, high = (half, tile_rows, row_width), (tiles_dev - half, tile_rows, row_width)
    far, far_high = pl.pallas_call(
        functools.partial(far_kernel, half),
        out_shape=[
            jax.ShapeDtypeStruct((len(far_chunks),) + low, jnp.bfloat16),
            jax.ShapeDtypeStruct((len(far_chunks),) + high, jnp.bfloat16),
        ],
        in_specs=[SMEM] + [VMEM] * (len(panels) + 2),
        out_specs=[VMEM] * 2,
        scratch_shapes=[held(len(panels) * tiles_dev, jnp.bfloat16)],
        compiler_params=LIMIT,
        cost_estimate=cost_of(capacity // 8, tile_rows, row_width),
    )(order, *panels, blocks, total)
    far, far_high, order = lax.optimization_barrier((far, far_high, order))
    far_arrived = paired(far, "grp", 1)
    highs = [paired(far_high[at], "grp", hop) for at, hop in enumerate(far_chunks)]
    panels = [early] + panels
    own_low, own_high, near, mine, mine_high = pl.pallas_call(
        functools.partial(rest_kernel, half, mine_chunks),
        out_shape=[
            jax.ShapeDtypeStruct(low, jnp.float32),
            jax.ShapeDtypeStruct(high, jnp.float32),
            jax.ShapeDtypeStruct(part, jnp.bfloat16),
            jax.ShapeDtypeStruct((len(mine_chunks),) + low, jnp.float32),
            jax.ShapeDtypeStruct((len(mine_chunks),) + high, jnp.bfloat16),
        ],
        in_specs=[SMEM] + [VMEM] * (len(panels) + 1),
        out_specs=[VMEM] * 5,
        scratch_shapes=[
            held(len(panels) * tiles_dev, jnp.bfloat16),
            held(dest_tiles + 1, jnp.float32),
        ],
        compiler_params=LIMIT,
        cost_estimate=cost_of(capacity, tile_rows, row_width),
    )(order, *panels, blocks)
    mine_arrived = [paired(mine_high[at], "grp", hop) for at, hop in enumerate(mine_chunks)]
    lows = []
    for at, hop in enumerate(mine_chunks):
        pair = (mine[at] + far_arrived[at].astype(jnp.float32)).astype(jnp.bfloat16)
        near, pair = lax.optimization_barrier((near, pair))
        lows.append(paired(pair, "grp", hop))
    near_arrived = paired(near, "grp", 1)
    own_high = own_high + sum(piece.astype(jnp.float32) for piece in highs)
    own_high, near_arrived, *tails = lax.optimization_barrier(
        (own_high, near_arrived, *lows, *mine_arrived)
    )
    out = pl.pallas_call(
        final_kernel,
        out_shape=jax.ShapeDtypeStruct(part, jnp.bfloat16),
        in_specs=[VMEM] * (4 + len(tails)),
        out_specs=HBM,
        scratch_shapes=[
            held(tiles_dev, jnp.bfloat16),
            pltpu.SemaphoreType.DMA((tiles_dev,)),
        ],
        compiler_params=LIMIT,
        cost_estimate=cost_of(0, tile_rows, row_width),
    )(factors, near_arrived, own_low, own_high, *tails)
    return out.reshape(1, row_count, row_width)


def solution(mesh):
    placed = (
        P("side", ("grp", "blk"), None),
        P("side", ("grp", "blk")),
        P("side", ("grp", "blk")),
        P("side", ("grp", "blk"), None, None),
        P("side", None, ("grp", "blk")),
    )
    return jax.shard_map(
        shards,
        mesh=mesh,
        in_specs=placed,
        out_specs=P("side", ("grp", "blk"), None),
        check_vma=False,
    )
```

```python
import functools

import jax
import jax.numpy as jnp
from jax import lax
from jax.experimental import pallas as pl
from jax.experimental.pallas import tpu as pltpu
from jax.sharding import PartitionSpec as P

UNROLL = 8
STAGES = 4
VMEM = pl.BlockSpec(memory_space=pltpu.VMEM)
SMEM = pl.BlockSpec(memory_space=pltpu.SMEM)
HBM = pl.BlockSpec(memory_space=pltpu.HBM)
LIMIT = pltpu.CompilerParams(vmem_limit_bytes=48 * 1024 * 1024)


def in_hbm(*arrays):
    return [pltpu.with_memory_space_constraint(array, pltpu.HBM) for array in arrays]


def split(value, size):
    if size & (size - 1) == 0:
        return value >> (size.bit_length() - 1), value & (size - 1)
    return value // size, value % size


def scale_kernel(exps_hbm, degrees_hbm, codes_hbm, rows, factors, exps_ref, degrees, codes, sems):
    pairs = [(exps_hbm, exps_ref), (degrees_hbm, degrees), (codes_hbm, codes)]
    fetches = [
        pltpu.make_async_copy(held, wanted, sems.at[at])
        for at, (held, wanted) in enumerate(pairs)
    ]
    for fetch in fetches:
        fetch.start()
    fetches[0].wait()
    fetches[1].wait()
    tiles_dev, tile_rows, row_width = rows.shape
    inverse = lax.rsqrt(degrees[...].astype(jnp.float32))
    for tile in range(tiles_dev):
        lanes = inverse[:, tile * tile_rows : (tile + 1) * tile_rows]
        factors[tile] = jnp.broadcast_to(lanes, (row_width, tile_rows)).T
    fetches[2].wait()
    for tile in range(tiles_dev):
        scale = jnp.exp2(jnp.full((1, 1), exps_ref[0, tile], jnp.int32).astype(jnp.float32))
        scaled = codes[tile].astype(jnp.float32) * scale * factors[tile]
        rows[tile] = scaled.astype(rows.dtype)


def scale_rows(codes, exps, degrees):
    return pl.pallas_call(
        scale_kernel,
        out_shape=[
            jax.ShapeDtypeStruct(codes.shape, jnp.bfloat16),
            jax.ShapeDtypeStruct(codes.shape, jnp.float32),
        ],
        in_specs=[HBM] * 3,
        out_specs=[VMEM] * 2,
        scratch_shapes=[
            pltpu.SMEM(exps.shape, exps.dtype),
            pltpu.VMEM(degrees.shape, degrees.dtype),
            pltpu.VMEM(codes.shape, codes.dtype),
            pltpu.SemaphoreType.DMA((3,)),
        ],
        compiler_params=LIMIT,
        cost_estimate=pl.CostEstimate(
            flops=codes.size, bytes_accessed=4 * codes.size, transcendentals=0
        ),
    )(*in_hbm(exps, degrees, codes))


def stage_kernel(
    blks, groups, tiles_dev, place_ref, index_hbm, blocks_hbm, order_ref, blocks, index_ref, sems
):
    fetch = pltpu.make_async_copy(index_hbm, index_ref, sems.at[0])
    fetch.start()
    copy = pltpu.make_async_copy(blocks_hbm, blocks, sems.at[1])
    copy.start()
    fetch.wait()
    my_blk = place_ref[0]
    my_grp = place_ref[1]
    capacity = index_ref.shape[1]
    source_tiles = blks * tiles_dev
    half = blks // 2

    def enlist(slot, nexts):
        target = index_ref[0, slot]
        origin = index_ref[1, slot]
        hop, row = split(origin, tiles_dev)
        chunk, tile = split(target, tiles_dev)
        hop = hop ^ my_blk
        chunk = chunk ^ my_grp
        rank = half - 1 - (hop >> 1)
        odd = hop & 1
        far = (chunk >= 2) & ((chunk & 1) == 1)
        stage = jnp.where(far, jnp.minimum(rank + odd, 1), jnp.where(chunk >= 2, 2, 3))
        stage = jnp.where(origin < source_tiles, stage, STAGES)
        panel = rank + odd * half - (stage == 1).astype(jnp.int32)
        kept = jnp.where(chunk >= 2, (chunk >> 1) - 1, chunk)
        word = pack(slot, panel * tiles_dev + row, kept * tiles_dev + tile)
        where = jnp.int32(0)
        for at, position in enumerate(nexts):
            where = jnp.where(stage == at, position, where)
        order_ref[stage, where] = word
        return tuple(
            position + (stage == at).astype(jnp.int32) for at, position in enumerate(nexts)
        )

    ends = lax.fori_loop(0, capacity, enlist, (jnp.int32(0),) * STAGES, unroll=8)
    far_tiles = (groups // 2 - 1) * tiles_dev
    spares = [pack(0, 0, far_tiles)] * 3 + [pack(0, 0, 2 * tiles_dev)]
    for at, (end, spare) in enumerate(zip(ends, spares)):
        for extra in range(UNROLL):
            order_ref[at, end + extra] = spare
        order_ref[at, capacity + UNROLL] = split(end + (UNROLL - 1), UNROLL)[0]
    copy.wait()


def pack(slot, row, target):
    return (slot << 16) | (row << 8) | target


def unpack(word):
    return word >> 16, (word >> 8) & 255, word & 255


def stage_blocks(index, place, blocks, blks, groups, tiles_dev):
    capacity = blocks.shape[0]
    assert blks * tiles_dev < 256 and groups * tiles_dev < 256 and capacity < 2**15
    return pl.pallas_call(
        functools.partial(stage_kernel, blks, groups, tiles_dev),
        out_shape=[
            jax.ShapeDtypeStruct((STAGES + 1, capacity + 2 * UNROLL), jnp.int32),
            jax.ShapeDtypeStruct(blocks.shape, blocks.dtype),
        ],
        in_specs=[SMEM, HBM, HBM],
        out_specs=[SMEM, VMEM],
        scratch_shapes=[
            pltpu.SMEM(index.shape, index.dtype),
            pltpu.SemaphoreType.DMA((2,)),
        ],
        compiler_params=LIMIT,
        cost_estimate=pl.CostEstimate(flops=0, bytes_accessed=0, transcendentals=0),
    )(place, *in_hbm(index, blocks))


def add_products(stage, order_ref, blocks, source, total):
    @pl.loop(0, order_ref[stage, order_ref.shape[1] - UNROLL])
    def _(batch):
        made = []
        for part in range(UNROLL):
            slot, row, target = unpack(order_ref[stage, batch * UNROLL + part])
            product = jnp.dot(blocks[slot], source[row], preferred_element_type=jnp.float32)
            made.append((target, product))
        for target, product in made:
            total[target] += product


def gather_panels(panels, source):
    for at, panel in enumerate(panels):
        rows = panel.shape[0]
        source[at * rows : (at + 1) * rows] = panel[...]


def early_kernel(order_ref, panel, blocks, total):
    total[...] = jnp.zeros_like(total)
    add_products(0, order_ref, blocks, panel, total)


def far_kernel(order_ref, *refs):
    *panels, blocks, total, far, source = refs
    gather_panels(panels, source)
    add_products(1, order_ref, blocks, source, total)
    far[...] = total[: far.shape[0]].astype(far.dtype)


def mine_kernel(order_ref, *refs):
    *panels, blocks, total, mine, source = refs
    gather_panels(panels, source)
    total[...] = jnp.zeros_like(total)
    add_products(2, order_ref, blocks, source, total)
    mine[...] = total[: mine.shape[0]].astype(mine.dtype)


def near_kernel(order_ref, *refs):
    *panels, blocks, own, near, source, total = refs
    gather_panels(panels, source)
    total[...] = jnp.zeros_like(total)
    add_products(3, order_ref, blocks, source, total)
    own[...] = total[: own.shape[0]]
    near[...] = total[own.shape[0] : 2 * own.shape[0]].astype(near.dtype)


def final_kernel(factors, own, *refs):
    *arrived, out_hbm, out, sems = refs
    copies = []
    for tile in range(out.shape[0]):
        value = own[tile]
        for piece in arrived:
            value = value + piece[tile].astype(jnp.float32)
        out[tile] = (value * factors[tile]).astype(out.dtype)
        copies.append(pltpu.make_async_copy(out.at[tile], out_hbm.at[tile], sems.at[tile]))
        copies[-1].start()
    for copy in copies:
        copy.wait()


def cost_of(slots, tile_rows, row_width):
    return pl.CostEstimate(
        flops=2 * slots * tile_rows * tile_rows * row_width,
        bytes_accessed=2 * slots * tile_rows * tile_rows,
        transcendentals=0,
    )


def shards(embed_codes, embed_exps, degrees, adjacency, block_index):
    tile_rows = adjacency.shape[2]
    row_width = embed_codes.shape[2]
    row_count = embed_codes.shape[1]
    capacity = adjacency.shape[1]
    tiles_dev = row_count // tile_rows
    groups = lax.axis_size("grp")
    blks = lax.axis_size("blk")
    part = (tiles_dev, tile_rows, row_width)
    source, factors = scale_rows(embed_codes.reshape(part), embed_exps, degrees)

    def across(value, hop):
        pairs = [
            (side * blks + at, (1 - side) * blks + (at ^ hop))
            for side in range(2)
            for at in range(blks)
        ]
        return lax.ppermute(value, ("side", "blk"), pairs)

    def paired(value, axis, hop):
        return lax.ppermute(value, axis, [(at, at ^ hop) for at in range(lax.axis_size(axis))])

    place = jnp.stack([lax.axis_index("blk"), lax.axis_index("grp")]).astype(jnp.int32)
    early, *middle = [across(source, hop) for hop in reversed(range(0, blks, 2))]
    order, blocks = stage_blocks(block_index[0], place, adjacency[0], blks, groups, tiles_dev)
    early, order = lax.optimization_barrier((early, order))
    other = paired(early, "blk", 1)
    far_chunks, mine_chunks = range(3, groups, 2), range(2, groups, 2)
    far_tiles = len(far_chunks) * tiles_dev

    def held(count, dtype):
        return pltpu.VMEM((count, tile_rows, row_width), dtype)

    total = pl.pallas_call(
        early_kernel,
        out_shape=jax.ShapeDtypeStruct((far_tiles + 1, tile_rows, row_width), jnp.float32),
        in_specs=[SMEM] + [VMEM] * 2,
        out_specs=VMEM,
        compiler_params=LIMIT,
        cost_estimate=cost_of(capacity // 8, tile_rows, row_width),
    )(order, early, blocks)
    *middle, total = lax.optimization_barrier((*middle, total))
    panels = middle + [other] + [paired(panel, "blk", 1) for panel in middle]
    far = pl.pallas_call(
        far_kernel,
        out_shape=jax.ShapeDtypeStruct((far_tiles, tile_rows, row_width), jnp.bfloat16),
        in_specs=[SMEM] + [VMEM] * (len(panels) + 2),
        out_specs=VMEM,
        scratch_shapes=[held(len(panels) * tiles_dev, jnp.bfloat16)],
        compiler_params=LIMIT,
        cost_estimate=cost_of(capacity // 8, tile_rows, row_width),
    )(order, *panels, blocks, total)
    far, order = lax.optimization_barrier((far, order))
    panels = [early] + panels
    mine_total, mine = pl.pallas_call(
        mine_kernel,
        out_shape=[
            jax.ShapeDtypeStruct((far_tiles + 1, tile_rows, row_width), jnp.float32),
            jax.ShapeDtypeStruct((far_tiles, tile_rows, row_width), jnp.bfloat16),
        ],
        in_specs=[SMEM] + [VMEM] * (len(panels) + 1),
        out_specs=[VMEM] * 2,
        scratch_shapes=[held(len(panels) * tiles_dev, jnp.bfloat16)],
        compiler_params=LIMIT,
        cost_estimate=cost_of(capacity // 4, tile_rows, row_width),
    )(order, *panels, blocks)
    mine, order = lax.optimization_barrier((mine, order))
    own, near = pl.pallas_call(
        near_kernel,
        out_shape=[
            jax.ShapeDtypeStruct(part, jnp.float32),
            jax.ShapeDtypeStruct(part, jnp.bfloat16),
        ],
        in_specs=[SMEM] + [VMEM] * (len(panels) + 1),
        out_specs=[VMEM] * 2,
        scratch_shapes=[
            held(len(panels) * tiles_dev, jnp.bfloat16),
            held(2 * tiles_dev + 1, jnp.float32),
        ],
        compiler_params=LIMIT,
        cost_estimate=cost_of(capacity // 2, tile_rows, row_width),
    )(order, *panels, blocks)

    def outer(at, owner):
        return abs(at - owner) > abs((at ^ 1) - owner)

    def sent(value, way, hop, wanted):
        pairs = [(at, at ^ way) for at in range(groups) if outer(at, at ^ hop) == wanted]
        return lax.ppermute(value, "grp", pairs)

    straight, sums = [], []
    for at, hop in enumerate(mine_chunks):
        piece = slice(at * tiles_dev, (at + 1) * tiles_dev)
        handed = sent(far[piece], 1, hop + 1, True)
        straight.append(sent(far[piece], hop + 1, hop + 1, False))
        straight.append(sent(mine[piece], hop, hop, True))
        pair = (mine_total[piece] + handed.astype(jnp.float32)).astype(jnp.bfloat16)
        near, pair = lax.optimization_barrier((near, pair))
        sums.append(sent(pair, hop, hop, False))
    near_arrived = paired(near, "grp", 1)
    own = own + sum(piece.astype(jnp.float32) for piece in straight)
    own, near_arrived, *sums = lax.optimization_barrier((own, near_arrived, *sums))
    out = pl.pallas_call(
        final_kernel,
        out_shape=jax.ShapeDtypeStruct(part, jnp.bfloat16),
        in_specs=[VMEM] * (3 + len(sums)),
        out_specs=HBM,
        scratch_shapes=[
            held(tiles_dev, jnp.bfloat16),
            pltpu.SemaphoreType.DMA((tiles_dev,)),
        ],
        compiler_params=LIMIT,
        cost_estimate=cost_of(0, tile_rows, row_width),
    )(factors, own, near_arrived, *sums)
    return out.reshape(1, row_count, row_width)


def solution(mesh):
    placed = (
        P("side", ("grp", "blk"), None),
        P("side", ("grp", "blk")),
        P("side", ("grp", "blk")),
        P("side", ("grp", "blk"), None, None),
        P("side", None, ("grp", "blk")),
    )
    return jax.shard_map(
        shards,
        mesh=mesh,
        in_specs=placed,
        out_specs=P("side", ("grp", "blk"), None),
        check_vma=False,
    )
```

```python
import functools

import jax
import jax.numpy as jnp
from jax import lax
from jax.experimental import pallas as pl
from jax.experimental.pallas import tpu as pltpu
from jax.sharding import PartitionSpec as P

UNROLL = 8
STAGES = 3
VMEM = pl.BlockSpec(memory_space=pltpu.VMEM)
SMEM = pl.BlockSpec(memory_space=pltpu.SMEM)
HBM = pl.BlockSpec(memory_space=pltpu.HBM)
LIMIT = pltpu.CompilerParams(vmem_limit_bytes=48 * 1024 * 1024)


def in_hbm(*arrays):
    return [pltpu.with_memory_space_constraint(array, pltpu.HBM) for array in arrays]


def split(value, size):
    if size & (size - 1) == 0:
        return value >> (size.bit_length() - 1), value & (size - 1)
    return value // size, value % size


def scale_kernel(exps_hbm, degrees_hbm, codes_hbm, rows, factors, exps_ref, degrees, codes, sems):
    pairs = [(exps_hbm, exps_ref), (degrees_hbm, degrees), (codes_hbm, codes)]
    fetches = [
        pltpu.make_async_copy(held, wanted, sems.at[at])
        for at, (held, wanted) in enumerate(pairs)
    ]
    for fetch in fetches:
        fetch.start()
    fetches[0].wait()
    fetches[1].wait()
    tiles_dev, tile_rows, row_width = rows.shape
    inverse = lax.rsqrt(degrees[...].astype(jnp.float32))
    for tile in range(tiles_dev):
        lanes = inverse[:, tile * tile_rows : (tile + 1) * tile_rows]
        factors[tile] = jnp.broadcast_to(lanes, (row_width, tile_rows)).T
    fetches[2].wait()
    for tile in range(tiles_dev):
        scale = jnp.exp2(jnp.full((1, 1), exps_ref[0, tile], jnp.int32).astype(jnp.float32))
        scaled = codes[tile].astype(jnp.float32) * scale * factors[tile]
        rows[tile] = scaled.astype(rows.dtype)


def scale_rows(codes, exps, degrees):
    return pl.pallas_call(
        scale_kernel,
        out_shape=[
            jax.ShapeDtypeStruct(codes.shape, jnp.bfloat16),
            jax.ShapeDtypeStruct(codes.shape, jnp.float32),
        ],
        in_specs=[HBM] * 3,
        out_specs=[VMEM] * 2,
        scratch_shapes=[
            pltpu.SMEM(exps.shape, exps.dtype),
            pltpu.VMEM(degrees.shape, degrees.dtype),
            pltpu.VMEM(codes.shape, codes.dtype),
            pltpu.SemaphoreType.DMA((3,)),
        ],
        compiler_params=LIMIT,
        cost_estimate=pl.CostEstimate(
            flops=codes.size, bytes_accessed=4 * codes.size, transcendentals=0
        ),
    )(*in_hbm(exps, degrees, codes))


def stage_kernel(
    blks, groups, tiles_dev, place_ref, index_hbm, blocks_hbm, order_ref, blocks, index_ref, sems
):
    fetch = pltpu.make_async_copy(index_hbm, index_ref, sems.at[0])
    fetch.start()
    copy = pltpu.make_async_copy(blocks_hbm, blocks, sems.at[1])
    copy.start()
    fetch.wait()
    my_blk = place_ref[0]
    my_grp = place_ref[1]
    capacity = index_ref.shape[1]
    source_tiles = blks * tiles_dev
    half = blks // 2
    role = my_blk & 1

    def enlist(slot, nexts):
        target = index_ref[0, slot]
        origin = index_ref[1, slot]
        hop, row = split(origin, tiles_dev)
        chunk, tile = split(target, tiles_dev)
        hop = hop ^ my_blk
        chunk = chunk ^ my_grp
        rank = half - 1 - (hop >> 1)
        odd = hop & 1
        far = (chunk >= 2) & ((chunk & 1) == 1)
        stage = jnp.where(far, jnp.minimum(rank + odd, 1), 2)
        stage = jnp.where(origin < source_tiles, stage, STAGES)
        panel = rank + odd * half - (stage == 1).astype(jnp.int32)
        kept = jnp.where(chunk == 1, 1 + role * (groups // 2 - 1), (chunk >> 1) + 1 - role)
        kept = jnp.where(chunk == 0, 0, jnp.where(far, (chunk >> 1) - 1, kept))
        word = pack(slot, panel * tiles_dev + row, kept * tiles_dev + tile)
        where = jnp.int32(0)
        for at, position in enumerate(nexts):
            where = jnp.where(stage == at, position, where)
        order_ref[stage, where] = word
        return tuple(
            position + (stage == at).astype(jnp.int32) for at, position in enumerate(nexts)
        )

    ends = lax.fori_loop(0, capacity, enlist, (jnp.int32(0),) * STAGES, unroll=8)
    far_tiles = (groups // 2 - 1) * tiles_dev
    spares = [pack(0, 0, far_tiles)] * 2 + [pack(0, 0, (groups // 2 + 1) * tiles_dev)]
    for at, (end, spare) in enumerate(zip(ends, spares)):
        for extra in range(UNROLL):
            order_ref[at, end + extra] = spare
        order_ref[at, capacity + UNROLL] = split(end + (UNROLL - 1), UNROLL)[0]
    copy.wait()


def pack(slot, row, target):
    return (slot << 16) | (row << 8) | target


def unpack(word):
    return word >> 16, (word >> 8) & 255, word & 255


def stage_blocks(index, place, blocks, blks, groups, tiles_dev):
    capacity = blocks.shape[0]
    assert blks * tiles_dev < 256 and groups * tiles_dev < 256 and capacity < 2**15
    return pl.pallas_call(
        functools.partial(stage_kernel, blks, groups, tiles_dev),
        out_shape=[
            jax.ShapeDtypeStruct((STAGES + 1, capacity + 2 * UNROLL), jnp.int32),
            jax.ShapeDtypeStruct(blocks.shape, blocks.dtype),
        ],
        in_specs=[SMEM, HBM, HBM],
        out_specs=[SMEM, VMEM],
        scratch_shapes=[
            pltpu.SMEM(index.shape, index.dtype),
            pltpu.SemaphoreType.DMA((2,)),
        ],
        compiler_params=LIMIT,
        cost_estimate=pl.CostEstimate(flops=0, bytes_accessed=0, transcendentals=0),
    )(place, *in_hbm(index, blocks))


def add_products(stage, order_ref, blocks, source, total):
    @pl.loop(0, order_ref[stage, order_ref.shape[1] - UNROLL])
    def _(batch):
        made = []
        for part in range(UNROLL):
            slot, row, target = unpack(order_ref[stage, batch * UNROLL + part])
            product = jnp.dot(blocks[slot], source[row], preferred_element_type=jnp.float32)
            made.append((target, product))
        for target, product in made:
            total[target] += product


def gather_panels(panels, source):
    for at, panel in enumerate(panels):
        rows = panel.shape[0]
        source[at * rows : (at + 1) * rows] = panel[...]


def early_kernel(order_ref, panel, blocks, total):
    total[...] = jnp.zeros_like(total)
    add_products(0, order_ref, blocks, panel, total)


def far_kernel(order_ref, *refs):
    *panels, blocks, total, far, source = refs
    gather_panels(panels, source)
    add_products(1, order_ref, blocks, source, total)
    far[...] = total[: far.shape[0]].astype(far.dtype)


def rest_kernel(order_ref, *refs):
    *panels, blocks, own, first, later, source, total = refs
    gather_panels(panels, source)
    total[...] = jnp.zeros_like(total)
    add_products(2, order_ref, blocks, source, total)
    tiles_dev = own.shape[0]
    own[...] = total[:tiles_dev]
    first[...] = total[tiles_dev : 2 * tiles_dev].astype(first.dtype)
    later[...] = total[2 * tiles_dev : 2 * tiles_dev + later.shape[0]]


def final_kernel(factors, own, *refs):
    *arrived, out_hbm, out, sems = refs
    copies = []
    for tile in range(out.shape[0]):
        value = own[tile]
        for piece in arrived:
            value = value + piece[tile].astype(jnp.float32)
        out[tile] = (value * factors[tile]).astype(out.dtype)
        copies.append(pltpu.make_async_copy(out.at[tile], out_hbm.at[tile], sems.at[tile]))
        copies[-1].start()
    for copy in copies:
        copy.wait()


def cost_of(slots, tile_rows, row_width):
    return pl.CostEstimate(
        flops=2 * slots * tile_rows * tile_rows * row_width,
        bytes_accessed=2 * slots * tile_rows * tile_rows,
        transcendentals=0,
    )


def shards(embed_codes, embed_exps, degrees, adjacency, block_index):
    tile_rows = adjacency.shape[2]
    row_width = embed_codes.shape[2]
    row_count = embed_codes.shape[1]
    capacity = adjacency.shape[1]
    tiles_dev = row_count // tile_rows
    groups = lax.axis_size("grp")
    blks = lax.axis_size("blk")
    part = (tiles_dev, tile_rows, row_width)
    source, factors = scale_rows(embed_codes.reshape(part), embed_exps, degrees)

    def across(value, hop):
        pairs = [
            (side * blks + at, (1 - side) * blks + (at ^ hop))
            for side in range(2)
            for at in range(blks)
        ]
        return lax.ppermute(value, ("side", "blk"), pairs)

    def paired(value, axis, hop):
        return lax.ppermute(value, axis, [(at, at ^ hop) for at in range(lax.axis_size(axis))])

    place = jnp.stack([lax.axis_index("blk"), lax.axis_index("grp")]).astype(jnp.int32)
    early, *middle = [across(source, hop) for hop in reversed(range(0, blks, 2))]
    order, blocks = stage_blocks(block_index[0], place, adjacency[0], blks, groups, tiles_dev)
    early, order = lax.optimization_barrier((early, order))
    other = paired(early, "blk", 1)
    far_tiles = (groups // 2 - 1) * tiles_dev

    def held(count, dtype):
        return pltpu.VMEM((count, tile_rows, row_width), dtype)

    total = pl.pallas_call(
        early_kernel,
        out_shape=jax.ShapeDtypeStruct((far_tiles + 1, tile_rows, row_width), jnp.float32),
        in_specs=[SMEM] + [VMEM] * 2,
        out_specs=VMEM,
        compiler_params=LIMIT,
        cost_estimate=cost_of(capacity // 8, tile_rows, row_width),
    )(order, early, blocks)
    *middle, total = lax.optimization_barrier((*middle, total))
    panels = middle + [other] + [paired(panel, "blk", 1) for panel in middle]
    far = pl.pallas_call(
        far_kernel,
        out_shape=jax.ShapeDtypeStruct((far_tiles, tile_rows, row_width), jnp.bfloat16),
        in_specs=[SMEM] + [VMEM] * (len(panels) + 2),
        out_specs=VMEM,
        scratch_shapes=[held(len(panels) * tiles_dev, jnp.bfloat16)],
        compiler_params=LIMIT,
        cost_estimate=cost_of(capacity // 8, tile_rows, row_width),
    )(order, *panels, blocks, total)
    far, order = lax.optimization_barrier((far, order))
    panels = [early] + panels
    own, first, later = pl.pallas_call(
        rest_kernel,
        out_shape=[
            jax.ShapeDtypeStruct(part, jnp.float32),
            jax.ShapeDtypeStruct(part, jnp.bfloat16),
            jax.ShapeDtypeStruct((far_tiles, tile_rows, row_width), jnp.float32),
        ],
        in_specs=[SMEM] + [VMEM] * (len(panels) + 1),
        out_specs=[VMEM] * 3,
        scratch_shapes=[
            held(len(panels) * tiles_dev, jnp.bfloat16),
            held((groups // 2 + 1) * tiles_dev + 1, jnp.float32),
        ],
        compiler_params=LIMIT,
        cost_estimate=cost_of(capacity, tile_rows, row_width),
    )(order, *panels, blocks)

    def turned(value, even_hop, odd_hop):
        hops = (even_hop, odd_hop)
        pairs = [
            (at * blks + blk, (at ^ hops[blk & 1]) * blks + blk)
            for at in range(groups)
            for blk in range(blks)
        ]
        return lax.ppermute(value, ("grp", "blk"), pairs)

    steps = groups // 2 - 1
    even_core = lax.axis_index("blk") % 2 == 0
    pieces = [slice(at * tiles_dev, (at + 1) * tiles_dev) for at in range(steps)]
    handed = [turned(far[pieces[at]], 1, 2 * at + 2).astype(jnp.float32) for at in range(steps)]
    arrived = [turned(first, 1, 2)]
    for at in range(steps):
        value = later[pieces[at]]
        for step, extra in enumerate(handed):
            if step == at == steps - 1:
                value = value + extra
            elif step == at:
                value = value + jnp.where(even_core, extra, 0.0)
            elif at == steps - 1:
                value = value + jnp.where(even_core, 0.0, extra)
        odd_hop = 1 if at == steps - 1 else 2 * at + 4
        arrived.append(turned(value.astype(jnp.bfloat16), 2 * at + 2, odd_hop))
    own = own + arrived[0].astype(jnp.float32)
    own, *sums = lax.optimization_barrier((own, *arrived[1:]))
    out = pl.pallas_call(
        final_kernel,
        out_shape=jax.ShapeDtypeStruct(part, jnp.bfloat16),
        in_specs=[VMEM] * (2 + len(sums)),
        out_specs=HBM,
        scratch_shapes=[
            held(tiles_dev, jnp.bfloat16),
            pltpu.SemaphoreType.DMA((tiles_dev,)),
        ],
        compiler_params=LIMIT,
        cost_estimate=cost_of(0, tile_rows, row_width),
    )(factors, own, *sums)
    return out.reshape(1, row_count, row_width)


def solution(mesh):
    placed = (
        P("side", ("grp", "blk"), None),
        P("side", ("grp", "blk")),
        P("side", ("grp", "blk")),
        P("side", ("grp", "blk"), None, None),
        P("side", None, ("grp", "blk")),
    )
    return jax.shard_map(
        shards,
        mesh=mesh,
        in_specs=placed,
        out_specs=P("side", ("grp", "blk"), None),
        check_vma=False,
    )
```

```python
import functools

import jax
import jax.numpy as jnp
from jax import lax
from jax.experimental import pallas as pl
from jax.experimental.pallas import tpu as pltpu
from jax.sharding import PartitionSpec as P

UNROLL = 8
STAGES = 5
VMEM = pl.BlockSpec(memory_space=pltpu.VMEM)
SMEM = pl.BlockSpec(memory_space=pltpu.SMEM)
HBM = pl.BlockSpec(memory_space=pltpu.HBM)
LIMIT = pltpu.CompilerParams(vmem_limit_bytes=48 * 1024 * 1024)


def in_hbm(*arrays):
    return [pltpu.with_memory_space_constraint(array, pltpu.HBM) for array in arrays]


def split(value, size):
    if size & (size - 1) == 0:
        return value >> (size.bit_length() - 1), value & (size - 1)
    return value // size, value % size


def scale_kernel(exps_hbm, degrees_hbm, codes_hbm, rows, factors, exps_ref, degrees, codes, sems):
    pairs = [(exps_hbm, exps_ref), (degrees_hbm, degrees), (codes_hbm, codes)]
    fetches = [
        pltpu.make_async_copy(held, wanted, sems.at[at])
        for at, (held, wanted) in enumerate(pairs)
    ]
    for fetch in fetches:
        fetch.start()
    fetches[0].wait()
    fetches[1].wait()
    tiles_dev, tile_rows, row_width = rows.shape
    inverse = lax.rsqrt(degrees[...].astype(jnp.float32))
    for tile in range(tiles_dev):
        lanes = inverse[:, tile * tile_rows : (tile + 1) * tile_rows]
        factors[tile] = jnp.broadcast_to(lanes, (row_width, tile_rows)).T
    fetches[2].wait()
    for tile in range(tiles_dev):
        scale = jnp.exp2(jnp.full((1, 1), exps_ref[0, tile], jnp.int32).astype(jnp.float32))
        scaled = codes[tile].astype(jnp.float32) * scale * factors[tile]
        rows[tile] = scaled.astype(rows.dtype)


def scale_rows(codes, exps, degrees):
    return pl.pallas_call(
        scale_kernel,
        out_shape=[
            jax.ShapeDtypeStruct(codes.shape, jnp.bfloat16),
            jax.ShapeDtypeStruct(codes.shape, jnp.float32),
        ],
        in_specs=[HBM] * 3,
        out_specs=[VMEM] * 2,
        scratch_shapes=[
            pltpu.SMEM(exps.shape, exps.dtype),
            pltpu.VMEM(degrees.shape, degrees.dtype),
            pltpu.VMEM(codes.shape, codes.dtype),
            pltpu.SemaphoreType.DMA((3,)),
        ],
        compiler_params=LIMIT,
        cost_estimate=pl.CostEstimate(
            flops=codes.size, bytes_accessed=4 * codes.size, transcendentals=0
        ),
    )(*in_hbm(exps, degrees, codes))


def stage_kernel(
    blks, groups, tiles_dev, place_ref, index_hbm, blocks_hbm, order_ref, blocks, index_ref, sems
):
    fetch = pltpu.make_async_copy(index_hbm, index_ref, sems.at[0])
    fetch.start()
    copy = pltpu.make_async_copy(blocks_hbm, blocks, sems.at[1])
    copy.start()
    fetch.wait()
    my_blk = place_ref[0]
    my_grp = place_ref[1]
    capacity = index_ref.shape[1]
    source_tiles = blks * tiles_dev
    half = blks // 2
    role = my_blk & 1

    def enlist(slot, nexts):
        target = index_ref[0, slot]
        origin = index_ref[1, slot]
        hop, row = split(origin, tiles_dev)
        chunk, tile = split(target, tiles_dev)
        hop = hop ^ my_blk
        chunk = chunk ^ my_grp
        rank = half - 1 - (hop >> 1)
        odd = hop & 1
        far = (chunk >= 2) & ((chunk & 1) == 1)
        kept = jnp.where(chunk == 1, 1 + role * (groups // 2 - 1), (chunk >> 1) + 1 - role)
        kept = jnp.where(chunk == 0, 0, jnp.where(far, (chunk >> 1) - 1, kept))
        stage = jnp.where(far, jnp.where(odd == 1, 2, jnp.minimum(rank, 1)), 4)
        stage = jnp.where(far | (kept != 1), stage, 3)
        kept = jnp.where(far, kept, jnp.where(stage == 3, 0, kept - (kept > 1).astype(jnp.int32)))
        stage = jnp.where(origin < source_tiles, stage, STAGES)
        panel = jnp.where(stage == 1, rank - 1, jnp.where(stage == 2, rank, rank + odd * half))
        word = pack(slot, panel * tiles_dev + row, kept * tiles_dev + tile)
        where = jnp.int32(0)
        for at, position in enumerate(nexts):
            where = jnp.where(stage == at, position, where)
        order_ref[stage, where] = word
        return tuple(
            position + (stage == at).astype(jnp.int32) for at, position in enumerate(nexts)
        )

    ends = lax.fori_loop(0, capacity, enlist, (jnp.int32(0),) * STAGES, unroll=8)
    far_tiles = (groups // 2 - 1) * tiles_dev
    tops = [far_tiles] * 3 + [tiles_dev, groups // 2 * tiles_dev]
    for at, (end, top) in enumerate(zip(ends, tops)):
        spare = pack(0, 0, top)
        for extra in range(UNROLL):
            order_ref[at, end + extra] = spare
        order_ref[at, capacity + UNROLL] = split(end + (UNROLL - 1), UNROLL)[0]
    copy.wait()


def pack(slot, row, target):
    return (slot << 16) | (row << 8) | target


def unpack(word):
    return word >> 16, (word >> 8) & 255, word & 255


def stage_blocks(index, place, blocks, blks, groups, tiles_dev):
    capacity = blocks.shape[0]
    assert blks * tiles_dev < 256 and groups * tiles_dev < 256 and capacity < 2**15
    return pl.pallas_call(
        functools.partial(stage_kernel, blks, groups, tiles_dev),
        out_shape=[
            jax.ShapeDtypeStruct((STAGES + 1, capacity + 2 * UNROLL), jnp.int32),
            jax.ShapeDtypeStruct(blocks.shape, blocks.dtype),
        ],
        in_specs=[SMEM, HBM, HBM],
        out_specs=[SMEM, VMEM],
        scratch_shapes=[
            pltpu.SMEM(index.shape, index.dtype),
            pltpu.SemaphoreType.DMA((2,)),
        ],
        compiler_params=LIMIT,
        cost_estimate=pl.CostEstimate(flops=0, bytes_accessed=0, transcendentals=0),
    )(place, *in_hbm(index, blocks))


def add_products(stage, order_ref, blocks, source, total):
    @pl.loop(0, order_ref[stage, order_ref.shape[1] - UNROLL])
    def _(batch):
        made = []
        for part in range(UNROLL):
            slot, row, target = unpack(order_ref[stage, batch * UNROLL + part])
            product = jnp.dot(blocks[slot], source[row], preferred_element_type=jnp.float32)
            made.append((target, product))
        for target, product in made:
            total[target] += product


def gather_panels(panels, source):
    for at, panel in enumerate(panels):
        rows = panel.shape[0]
        source[at * rows : (at + 1) * rows] = panel[...]


def early_kernel(order_ref, panel, blocks, total):
    total[...] = jnp.zeros_like(total)
    add_products(0, order_ref, blocks, panel, total)


def middle_kernel(order_ref, *refs):
    *panels, blocks, _, total, source = refs
    gather_panels(panels, source)
    add_products(1, order_ref, blocks, source, total)


def far_kernel(order_ref, *refs):
    *panels, blocks, total, far, source = refs
    gather_panels(panels, source)
    add_products(2, order_ref, blocks, source, total)
    far[...] = total[: far.shape[0]].astype(far.dtype)


def first_kernel(order_ref, *refs):
    *panels, blocks, first, source, total = refs
    gather_panels(panels, source)
    total[...] = jnp.zeros_like(total)
    add_products(3, order_ref, blocks, source, total)
    first[...] = total[: first.shape[0]].astype(first.dtype)


def rest_kernel(order_ref, *refs):
    *panels, blocks, own, later, source, total = refs
    gather_panels(panels, source)
    total[...] = jnp.zeros_like(total)
    add_products(4, order_ref, blocks, source, total)
    tiles_dev = own.shape[0]
    own[...] = total[:tiles_dev]
    later[...] = total[tiles_dev : tiles_dev + later.shape[0]]


def final_kernel(factors, own, *refs):
    *arrived, out_hbm, out, sems = refs
    copies = []
    for tile in range(out.shape[0]):
        value = own[tile]
        for piece in arrived:
            value = value + piece[tile].astype(jnp.float32)
        out[tile] = (value * factors[tile]).astype(out.dtype)
        copies.append(pltpu.make_async_copy(out.at[tile], out_hbm.at[tile], sems.at[tile]))
        copies[-1].start()
    for copy in copies:
        copy.wait()


def cost_of(slots, tile_rows, row_width):
    return pl.CostEstimate(
        flops=2 * slots * tile_rows * tile_rows * row_width,
        bytes_accessed=2 * slots * tile_rows * tile_rows,
        transcendentals=0,
    )


def shards(embed_codes, embed_exps, degrees, adjacency, block_index):
    tile_rows = adjacency.shape[2]
    row_width = embed_codes.shape[2]
    row_count = embed_codes.shape[1]
    capacity = adjacency.shape[1]
    tiles_dev = row_count // tile_rows
    groups = lax.axis_size("grp")
    blks = lax.axis_size("blk")
    part = (tiles_dev, tile_rows, row_width)
    source, factors = scale_rows(embed_codes.reshape(part), embed_exps, degrees)

    def across(value, hop):
        pairs = [
            (side * blks + at, (1 - side) * blks + (at ^ hop))
            for side in range(2)
            for at in range(blks)
        ]
        return lax.ppermute(value, ("side", "blk"), pairs)

    def paired(value, axis, hop):
        return lax.ppermute(value, axis, [(at, at ^ hop) for at in range(lax.axis_size(axis))])

    place = jnp.stack([lax.axis_index("blk"), lax.axis_index("grp")]).astype(jnp.int32)
    early, *middle = [across(source, hop) for hop in reversed(range(0, blks, 2))]
    order, blocks = stage_blocks(block_index[0], place, adjacency[0], blks, groups, tiles_dev)
    early, order = lax.optimization_barrier((early, order))
    other = paired(early, "blk", 1)
    far_tiles = (groups // 2 - 1) * tiles_dev

    def held(count, dtype):
        return pltpu.VMEM((count, tile_rows, row_width), dtype)

    total = pl.pallas_call(
        early_kernel,
        out_shape=jax.ShapeDtypeStruct((far_tiles + 1, tile_rows, row_width), jnp.float32),
        in_specs=[SMEM] + [VMEM] * 2,
        out_specs=VMEM,
        compiler_params=LIMIT,
        cost_estimate=cost_of(capacity // 8, tile_rows, row_width),
    )(order, early, blocks)
    *middle, total = lax.optimization_barrier((*middle, total))
    others = [other] + [paired(panel, "blk", 1) for panel in middle]
    total = pl.pallas_call(
        middle_kernel,
        out_shape=jax.ShapeDtypeStruct(total.shape, total.dtype),
        in_specs=[SMEM] + [VMEM] * (len(middle) + 2),
        out_specs=VMEM,
        input_output_aliases={len(middle) + 2: 0},
        scratch_shapes=[held(len(middle) * tiles_dev, jnp.bfloat16)],
        compiler_params=LIMIT,
        cost_estimate=cost_of(capacity // 8, tile_rows, row_width),
    )(order, *middle, blocks, total)
    *others, total = lax.optimization_barrier((*others, total))
    far = pl.pallas_call(
        far_kernel,
        out_shape=jax.ShapeDtypeStruct((far_tiles, tile_rows, row_width), jnp.bfloat16),
        in_specs=[SMEM] + [VMEM] * (len(others) + 2),
        out_specs=VMEM,
        scratch_shapes=[held(len(others) * tiles_dev, jnp.bfloat16)],
        compiler_params=LIMIT,
        cost_estimate=cost_of(capacity // 8, tile_rows, row_width),
    )(order, *others, blocks, total)
    far, order = lax.optimization_barrier((far, order))
    panels = [early] + middle + others
    first = pl.pallas_call(
        first_kernel,
        out_shape=jax.ShapeDtypeStruct(part, jnp.bfloat16),
        in_specs=[SMEM] + [VMEM] * (len(panels) + 1),
        out_specs=VMEM,
        scratch_shapes=[
            held(len(panels) * tiles_dev, jnp.bfloat16),
            held(tiles_dev + 1, jnp.float32),
        ],
        compiler_params=LIMIT,
        cost_estimate=cost_of(capacity // 4, tile_rows, row_width),
    )(order, *panels, blocks)
    first, order = lax.optimization_barrier((first, order))
    own, later = pl.pallas_call(
        rest_kernel,
        out_shape=[
            jax.ShapeDtypeStruct(part, jnp.float32),
            jax.ShapeDtypeStruct((far_tiles, tile_rows, row_width), jnp.float32),
        ],
        in_specs=[SMEM] + [VMEM] * (len(panels) + 1),
        out_specs=[VMEM] * 2,
        scratch_shapes=[
            held(len(panels) * tiles_dev, jnp.bfloat16),
            held(groups // 2 * tiles_dev + 1, jnp.float32),
        ],
        compiler_params=LIMIT,
        cost_estimate=cost_of(capacity // 2, tile_rows, row_width),
    )(order, *panels, blocks)

    def turned(value, even_hop, odd_hop):
        hops = (even_hop, odd_hop)
        pairs = [
            (at * blks + blk, (at ^ hops[blk & 1]) * blks + blk)
            for at in range(groups)
            for blk in range(blks)
        ]
        return lax.ppermute(value, ("grp", "blk"), pairs)

    steps = groups // 2 - 1
    even_core = lax.axis_index("blk") % 2 == 0
    pieces = [slice(at * tiles_dev, (at + 1) * tiles_dev) for at in range(steps)]
    handed = [turned(far[pieces[at]], 1, 2 * at + 2).astype(jnp.float32) for at in range(steps)]
    arrived = [turned(first, 1, 2)]
    for at in range(steps):
        value = later[pieces[at]]
        for step, extra in enumerate(handed):
            if step == at == steps - 1:
                value = value + extra
            elif step == at:
                value = value + jnp.where(even_core, extra, 0.0)
            elif at == steps - 1:
                value = value + jnp.where(even_core, 0.0, extra)
        odd_hop = 1 if at == steps - 1 else 2 * at + 4
        arrived.append(turned(value.astype(jnp.bfloat16), 2 * at + 2, odd_hop))
    own = own + arrived[0].astype(jnp.float32)
    own, *sums = lax.optimization_barrier((own, *arrived[1:]))
    out = pl.pallas_call(
        final_kernel,
        out_shape=jax.ShapeDtypeStruct(part, jnp.bfloat16),
        in_specs=[VMEM] * (2 + len(sums)),
        out_specs=HBM,
        scratch_shapes=[
            held(tiles_dev, jnp.bfloat16),
            pltpu.SemaphoreType.DMA((tiles_dev,)),
        ],
        compiler_params=LIMIT,
        cost_estimate=cost_of(0, tile_rows, row_width),
    )(factors, own, *sums)
    return out.reshape(1, row_count, row_width)


def solution(mesh):
    placed = (
        P("side", ("grp", "blk"), None),
        P("side", ("grp", "blk")),
        P("side", ("grp", "blk")),
        P("side", ("grp", "blk"), None, None),
        P("side", None, ("grp", "blk")),
    )
    return jax.shard_map(
        shards,
        mesh=mesh,
        in_specs=placed,
        out_specs=P("side", ("grp", "blk"), None),
        check_vma=False,
    )
```

```python
import functools

import jax
import jax.numpy as jnp
from jax import lax
from jax.experimental import pallas as pl
from jax.experimental.pallas import tpu as pltpu
from jax.sharding import PartitionSpec as P

UNROLL = 8
STAGES = 5
VMEM = pl.BlockSpec(memory_space=pltpu.VMEM)
SMEM = pl.BlockSpec(memory_space=pltpu.SMEM)
HBM = pl.BlockSpec(memory_space=pltpu.HBM)
LIMIT = pltpu.CompilerParams(vmem_limit_bytes=48 * 1024 * 1024)


def in_hbm(*arrays):
    return [pltpu.with_memory_space_constraint(array, pltpu.HBM) for array in arrays]


def split(value, size):
    if size & (size - 1) == 0:
        return value >> (size.bit_length() - 1), value & (size - 1)
    return value // size, value % size


def scale_kernel(exps_hbm, degrees_hbm, codes_hbm, rows, factors, exps_ref, degrees, codes, sems):
    pairs = [(exps_hbm, exps_ref), (degrees_hbm, degrees), (codes_hbm, codes)]
    fetches = [
        pltpu.make_async_copy(held, wanted, sems.at[at])
        for at, (held, wanted) in enumerate(pairs)
    ]
    for fetch in fetches:
        fetch.start()
    fetches[0].wait()
    fetches[1].wait()
    tiles_dev, tile_rows, row_width = rows.shape
    inverse = lax.rsqrt(degrees[...].astype(jnp.float32))
    for tile in range(tiles_dev):
        lanes = inverse[:, tile * tile_rows : (tile + 1) * tile_rows]
        factors[tile] = jnp.broadcast_to(lanes, (row_width, tile_rows)).T
    fetches[2].wait()
    for tile in range(tiles_dev):
        scale = jnp.exp2(jnp.full((1, 1), exps_ref[0, tile], jnp.int32).astype(jnp.float32))
        scaled = codes[tile].astype(jnp.float32) * scale * factors[tile]
        rows[tile] = scaled.astype(rows.dtype)


def scale_rows(codes, exps, degrees):
    return pl.pallas_call(
        scale_kernel,
        out_shape=[
            jax.ShapeDtypeStruct(codes.shape, jnp.bfloat16),
            jax.ShapeDtypeStruct(codes.shape, jnp.float32),
        ],
        in_specs=[HBM] * 3,
        out_specs=[VMEM] * 2,
        scratch_shapes=[
            pltpu.SMEM(exps.shape, exps.dtype),
            pltpu.VMEM(degrees.shape, degrees.dtype),
            pltpu.VMEM(codes.shape, codes.dtype),
            pltpu.SemaphoreType.DMA((3,)),
        ],
        compiler_params=LIMIT,
        cost_estimate=pl.CostEstimate(
            flops=codes.size, bytes_accessed=4 * codes.size, transcendentals=0
        ),
    )(*in_hbm(exps, degrees, codes))


def stage_kernel(
    blks, groups, tiles_dev, place_ref, index_hbm, blocks_hbm, order_ref, blocks, index_ref, sems
):
    fetch = pltpu.make_async_copy(index_hbm, index_ref, sems.at[0])
    fetch.start()
    copy = pltpu.make_async_copy(blocks_hbm, blocks, sems.at[1])
    copy.start()
    fetch.wait()
    my_blk = place_ref[0]
    my_grp = place_ref[1]
    capacity = index_ref.shape[1]
    source_tiles = blks * tiles_dev
    half = blks // 2
    role = my_blk & 1

    def enlist(slot, nexts):
        target = index_ref[0, slot]
        origin = index_ref[1, slot]
        hop, row = split(origin, tiles_dev)
        chunk, tile = split(target, tiles_dev)
        hop = hop ^ my_blk
        chunk = chunk ^ my_grp
        odd = hop & 1
        rank = jnp.where(role == odd, half - 1 - (hop >> 1), hop >> 1)
        far = (chunk >= 2) & ((chunk & 1) == 1)
        kept = jnp.where(chunk == 1, 1 + role * (groups // 2 - 1), (chunk >> 1) + 1 - role)
        kept = jnp.where(chunk == 0, 0, jnp.where(far, (chunk >> 1) - 1, kept))
        stage = jnp.where(far, jnp.where(odd == 1, 2, jnp.minimum(rank, 1)), 4)
        stage = jnp.where(far | (kept != 1), stage, 3)
        kept = jnp.where(far, kept, jnp.where(stage == 3, 0, kept - (kept > 1).astype(jnp.int32)))
        stage = jnp.where(origin < source_tiles, stage, STAGES)
        panel = jnp.where(stage == 1, rank - 1, jnp.where(stage == 2, rank, rank + odd * half))
        word = pack(slot, panel * tiles_dev + row, kept * tiles_dev + tile)
        where = jnp.int32(0)
        for at, position in enumerate(nexts):
            where = jnp.where(stage == at, position, where)
        order_ref[stage, where] = word
        return tuple(
            position + (stage == at).astype(jnp.int32) for at, position in enumerate(nexts)
        )

    ends = lax.fori_loop(0, capacity, enlist, (jnp.int32(0),) * STAGES, unroll=8)
    far_tiles = (groups // 2 - 1) * tiles_dev
    tops = [far_tiles] * 3 + [tiles_dev, groups // 2 * tiles_dev]
    for at, (end, top) in enumerate(zip(ends, tops)):
        spare = pack(0, 0, top)
        for extra in range(UNROLL):
            order_ref[at, end + extra] = spare
        order_ref[at, capacity + UNROLL] = split(end + (UNROLL - 1), UNROLL)[0]
    copy.wait()


def pack(slot, row, target):
    return (slot << 16) | (row << 8) | target


def unpack(word):
    return word >> 16, (word >> 8) & 255, word & 255


def stage_blocks(index, place, blocks, blks, groups, tiles_dev):
    capacity = blocks.shape[0]
    assert blks * tiles_dev < 256 and groups * tiles_dev < 256 and capacity < 2**15
    return pl.pallas_call(
        functools.partial(stage_kernel, blks, groups, tiles_dev),
        out_shape=[
            jax.ShapeDtypeStruct((STAGES + 1, capacity + 2 * UNROLL), jnp.int32),
            jax.ShapeDtypeStruct(blocks.shape, blocks.dtype),
        ],
        in_specs=[SMEM, HBM, HBM],
        out_specs=[SMEM, VMEM],
        scratch_shapes=[
            pltpu.SMEM(index.shape, index.dtype),
            pltpu.SemaphoreType.DMA((2,)),
        ],
        compiler_params=LIMIT,
        cost_estimate=pl.CostEstimate(flops=0, bytes_accessed=0, transcendentals=0),
    )(place, *in_hbm(index, blocks))


def add_products(stage, order_ref, blocks, source, total):
    @pl.loop(0, order_ref[stage, order_ref.shape[1] - UNROLL])
    def _(batch):
        made = []
        for part in range(UNROLL):
            slot, row, target = unpack(order_ref[stage, batch * UNROLL + part])
            product = jnp.dot(blocks[slot], source[row], preferred_element_type=jnp.float32)
            made.append((target, product))
        for target, product in made:
            total[target] += product


def gather_panels(panels, source):
    for at, panel in enumerate(panels):
        rows = panel.shape[0]
        source[at * rows : (at + 1) * rows] = panel[...]


def early_kernel(order_ref, panel, blocks, total):
    total[...] = jnp.zeros_like(total)
    add_products(0, order_ref, blocks, panel, total)


def middle_kernel(order_ref, *refs):
    *panels, blocks, _, total, source = refs
    gather_panels(panels, source)
    add_products(1, order_ref, blocks, source, total)


def far_kernel(order_ref, *refs):
    *panels, blocks, total, far, source = refs
    gather_panels(panels, source)
    add_products(2, order_ref, blocks, source, total)
    far[...] = total[: far.shape[0]].astype(far.dtype)


def first_kernel(order_ref, *refs):
    *panels, blocks, first, source, total = refs
    gather_panels(panels, source)
    total[...] = jnp.zeros_like(total)
    add_products(3, order_ref, blocks, source, total)
    first[...] = total[: first.shape[0]].astype(first.dtype)


def rest_kernel(order_ref, *refs):
    *panels, blocks, own, later, source, total = refs
    gather_panels(panels, source)
    total[...] = jnp.zeros_like(total)
    add_products(4, order_ref, blocks, source, total)
    tiles_dev = own.shape[0]
    own[...] = total[:tiles_dev]
    later[...] = total[tiles_dev : tiles_dev + later.shape[0]]


def final_kernel(factors, own, *refs):
    *arrived, out_hbm, out, sems = refs
    copies = []
    for tile in range(out.shape[0]):
        value = own[tile]
        for piece in arrived:
            value = value + piece[tile].astype(jnp.float32)
        out[tile] = (value * factors[tile]).astype(out.dtype)
        copies.append(pltpu.make_async_copy(out.at[tile], out_hbm.at[tile], sems.at[tile]))
        copies[-1].start()
    for copy in copies:
        copy.wait()


def cost_of(slots, tile_rows, row_width):
    return pl.CostEstimate(
        flops=2 * slots * tile_rows * tile_rows * row_width,
        bytes_accessed=2 * slots * tile_rows * tile_rows,
        transcendentals=0,
    )


def shards(embed_codes, embed_exps, degrees, adjacency, block_index):
    tile_rows = adjacency.shape[2]
    row_width = embed_codes.shape[2]
    row_count = embed_codes.shape[1]
    capacity = adjacency.shape[1]
    tiles_dev = row_count // tile_rows
    groups = lax.axis_size("grp")
    blks = lax.axis_size("blk")
    part = (tiles_dev, tile_rows, row_width)
    source, factors = scale_rows(embed_codes.reshape(part), embed_exps, degrees)

    def across(value, step):
        pairs = [
            (side * blks + at, (1 - side) * blks + (at ^ (2 * step if at & 1 else blks - 2 - 2 * step)))
            for side in range(2)
            for at in range(blks)
        ]
        return lax.ppermute(value, ("side", "blk"), pairs)

    def paired(value, axis, hop):
        return lax.ppermute(value, axis, [(at, at ^ hop) for at in range(lax.axis_size(axis))])

    place = jnp.stack([lax.axis_index("blk"), lax.axis_index("grp")]).astype(jnp.int32)
    early, *middle = [across(source, step) for step in range(blks // 2)]
    order, blocks = stage_blocks(block_index[0], place, adjacency[0], blks, groups, tiles_dev)
    early, order = lax.optimization_barrier((early, order))
    other = paired(early, "blk", 1)
    far_tiles = (groups // 2 - 1) * tiles_dev

    def held(count, dtype):
        return pltpu.VMEM((count, tile_rows, row_width), dtype)

    total = pl.pallas_call(
        early_kernel,
        out_shape=jax.ShapeDtypeStruct((far_tiles + 1, tile_rows, row_width), jnp.float32),
        in_specs=[SMEM] + [VMEM] * 2,
        out_specs=VMEM,
        compiler_params=LIMIT,
        cost_estimate=cost_of(capacity // 8, tile_rows, row_width),
    )(order, early, blocks)
    *middle, total = lax.optimization_barrier((*middle, total))
    others = [other] + [paired(panel, "blk", 1) for panel in middle]
    total = pl.pallas_call(
        middle_kernel,
        out_shape=jax.ShapeDtypeStruct(total.shape, total.dtype),
        in_specs=[SMEM] + [VMEM] * (len(middle) + 2),
        out_specs=VMEM,
        input_output_aliases={len(middle) + 2: 0},
        scratch_shapes=[held(len(middle) * tiles_dev, jnp.bfloat16)],
        compiler_params=LIMIT,
        cost_estimate=cost_of(capacity // 8, tile_rows, row_width),
    )(order, *middle, blocks, total)
    *others, total = lax.optimization_barrier((*others, total))
    far = pl.pallas_call(
        far_kernel,
        out_shape=jax.ShapeDtypeStruct((far_tiles, tile_rows, row_width), jnp.bfloat16),
        in_specs=[SMEM] + [VMEM] * (len(others) + 2),
        out_specs=VMEM,
        scratch_shapes=[held(len(others) * tiles_dev, jnp.bfloat16)],
        compiler_params=LIMIT,
        cost_estimate=cost_of(capacity // 8, tile_rows, row_width),
    )(order, *others, blocks, total)
    far, order = lax.optimization_barrier((far, order))
    panels = [early] + middle + others
    first = pl.pallas_call(
        first_kernel,
        out_shape=jax.ShapeDtypeStruct(part, jnp.bfloat16),
        in_specs=[SMEM] + [VMEM] * (len(panels) + 1),
        out_specs=VMEM,
        scratch_shapes=[
            held(len(panels) * tiles_dev, jnp.bfloat16),
            held(tiles_dev + 1, jnp.float32),
        ],
        compiler_params=LIMIT,
        cost_estimate=cost_of(capacity // 4, tile_rows, row_width),
    )(order, *panels, blocks)
    first, order = lax.optimization_barrier((first, order))
    own, later = pl.pallas_call(
        rest_kernel,
        out_shape=[
            jax.ShapeDtypeStruct(part, jnp.float32),
            jax.ShapeDtypeStruct((far_tiles, tile_rows, row_width), jnp.float32),
        ],
        in_specs=[SMEM] + [VMEM] * (len(panels) + 1),
        out_specs=[VMEM] * 2,
        scratch_shapes=[
            held(len(panels) * tiles_dev, jnp.bfloat16),
            held(groups // 2 * tiles_dev + 1, jnp.float32),
        ],
        compiler_params=LIMIT,
        cost_estimate=cost_of(capacity // 2, tile_rows, row_width),
    )(order, *panels, blocks)

    def turned(value, even_hop, odd_hop):
        hops = (even_hop, odd_hop)
        pairs = [
            (at * blks + blk, (at ^ hops[blk & 1]) * blks + blk)
            for at in range(groups)
            for blk in range(blks)
        ]
        return lax.ppermute(value, ("grp", "blk"), pairs)

    steps = groups // 2 - 1
    even_core = lax.axis_index("blk") % 2 == 0
    pieces = [slice(at * tiles_dev, (at + 1) * tiles_dev) for at in range(steps)]
    handed = [turned(far[pieces[at]], 1, 2 * at + 2).astype(jnp.float32) for at in range(steps)]
    arrived = [turned(first, 1, 2)]
    for at in range(steps):
        value = later[pieces[at]]
        for step, extra in enumerate(handed):
            if step == at == steps - 1:
                value = value + extra
            elif step == at:
                value = value + jnp.where(even_core, extra, 0.0)
            elif at == steps - 1:
                value = value + jnp.where(even_core, 0.0, extra)
        odd_hop = 1 if at == steps - 1 else 2 * at + 4
        arrived.append(turned(value.astype(jnp.bfloat16), 2 * at + 2, odd_hop))
    own = own + arrived[0].astype(jnp.float32)
    own, *sums = lax.optimization_barrier((own, *arrived[1:]))
    out = pl.pallas_call(
        final_kernel,
        out_shape=jax.ShapeDtypeStruct(part, jnp.bfloat16),
        in_specs=[VMEM] * (2 + len(sums)),
        out_specs=HBM,
        scratch_shapes=[
            held(tiles_dev, jnp.bfloat16),
            pltpu.SemaphoreType.DMA((tiles_dev,)),
        ],
        compiler_params=LIMIT,
        cost_estimate=cost_of(0, tile_rows, row_width),
    )(factors, own, *sums)
    return out.reshape(1, row_count, row_width)


def solution(mesh):
    placed = (
        P("side", ("grp", "blk"), None),
        P("side", ("grp", "blk")),
        P("side", ("grp", "blk")),
        P("side", ("grp", "blk"), None, None),
        P("side", None, ("grp", "blk")),
    )
    return jax.shard_map(
        shards,
        mesh=mesh,
        in_specs=placed,
        out_specs=P("side", ("grp", "blk"), None),
        check_vma=False,
    )
```

```python
import functools

import jax
import jax.numpy as jnp
from jax import lax
from jax.experimental import pallas as pl
from jax.experimental.pallas import tpu as pltpu
from jax.sharding import PartitionSpec as P

UNROLL = 8
STAGES = 5
VMEM = pl.BlockSpec(memory_space=pltpu.VMEM)
SMEM = pl.BlockSpec(memory_space=pltpu.SMEM)
HBM = pl.BlockSpec(memory_space=pltpu.HBM)
LIMIT = pltpu.CompilerParams(vmem_limit_bytes=48 * 1024 * 1024)


def in_hbm(*arrays):
    return [pltpu.with_memory_space_constraint(array, pltpu.HBM) for array in arrays]


def split(value, size):
    if size & (size - 1) == 0:
        return value >> (size.bit_length() - 1), value & (size - 1)
    return value // size, value % size


def scale_kernel(exps_hbm, degrees_hbm, codes_hbm, rows, factors, exps_ref, degrees, codes, sems):
    pairs = [(exps_hbm, exps_ref), (degrees_hbm, degrees), (codes_hbm, codes)]
    fetches = [
        pltpu.make_async_copy(held, wanted, sems.at[at])
        for at, (held, wanted) in enumerate(pairs)
    ]
    for fetch in fetches:
        fetch.start()
    fetches[0].wait()
    fetches[1].wait()
    tiles_dev, tile_rows, row_width = rows.shape
    inverse = lax.rsqrt(degrees[...].astype(jnp.float32))
    for tile in range(tiles_dev):
        lanes = inverse[:, tile * tile_rows : (tile + 1) * tile_rows]
        factors[tile] = jnp.broadcast_to(lanes, (row_width, tile_rows)).T
    fetches[2].wait()
    for tile in range(tiles_dev):
        scale = jnp.exp2(jnp.full((1, 1), exps_ref[0, tile], jnp.int32).astype(jnp.float32))
        scaled = codes[tile].astype(jnp.float32) * scale * factors[tile]
        rows[tile] = scaled.astype(rows.dtype)


def scale_rows(codes, exps, degrees):
    return pl.pallas_call(
        scale_kernel,
        out_shape=[
            jax.ShapeDtypeStruct(codes.shape, jnp.bfloat16),
            jax.ShapeDtypeStruct(codes.shape, jnp.float32),
        ],
        in_specs=[HBM] * 3,
        out_specs=[VMEM] * 2,
        scratch_shapes=[
            pltpu.SMEM(exps.shape, exps.dtype),
            pltpu.VMEM(degrees.shape, degrees.dtype),
            pltpu.VMEM(codes.shape, codes.dtype),
            pltpu.SemaphoreType.DMA((3,)),
        ],
        compiler_params=LIMIT,
        cost_estimate=pl.CostEstimate(
            flops=codes.size, bytes_accessed=4 * codes.size, transcendentals=0
        ),
    )(*in_hbm(exps, degrees, codes))


def stage_kernel(
    blks, groups, tiles_dev, place_ref, index_hbm, blocks_hbm, order_ref, blocks, index_ref, sems
):
    fetch = pltpu.make_async_copy(index_hbm, index_ref, sems.at[0])
    fetch.start()
    copy = pltpu.make_async_copy(blocks_hbm, blocks, sems.at[1])
    copy.start()
    fetch.wait()
    my_blk = place_ref[0]
    my_grp = place_ref[1]
    capacity = index_ref.shape[1]
    source_tiles = blks * tiles_dev
    half = blks // 2
    role = my_blk & 1

    def enlist(slot, nexts):
        target = index_ref[0, slot]
        origin = index_ref[1, slot]
        hop, row = split(origin, tiles_dev)
        chunk, tile = split(target, tiles_dev)
        hop = hop ^ my_blk
        chunk = chunk ^ my_grp
        odd = hop & 1
        rank = jnp.where(role == odd, half - 1 - (hop >> 1), hop >> 1)
        far = (chunk >= 2) & ((chunk & 1) == 1)
        kept = jnp.where(chunk == 1, 1 + (1 - role) * (groups // 2 - 1), (chunk >> 1) + role)
        kept = jnp.where(chunk == 0, 0, jnp.where(far, (chunk >> 1) - 1, kept))
        stage = jnp.where(far, jnp.where(odd == 1, 2, jnp.minimum(rank, 1)), 4)
        stage = jnp.where(far | (kept != 1), stage, 3)
        kept = jnp.where(far, kept, jnp.where(stage == 3, 0, kept - (kept > 1).astype(jnp.int32)))
        stage = jnp.where(origin < source_tiles, stage, STAGES)
        panel = jnp.where(stage == 1, rank - 1, jnp.where(stage == 2, rank, rank + odd * half))
        word = pack(slot, panel * tiles_dev + row, kept * tiles_dev + tile)
        where = jnp.int32(0)
        for at, position in enumerate(nexts):
            where = jnp.where(stage == at, position, where)
        order_ref[stage, where] = word
        return tuple(
            position + (stage == at).astype(jnp.int32) for at, position in enumerate(nexts)
        )

    ends = lax.fori_loop(0, capacity, enlist, (jnp.int32(0),) * STAGES, unroll=8)
    far_tiles = (groups // 2 - 1) * tiles_dev
    tops = [far_tiles] * 3 + [tiles_dev, groups // 2 * tiles_dev]
    for at, (end, top) in enumerate(zip(ends, tops)):
        spare = pack(0, 0, top)
        for extra in range(UNROLL):
            order_ref[at, end + extra] = spare
        order_ref[at, capacity + UNROLL] = split(end + (UNROLL - 1), UNROLL)[0]
    copy.wait()


def pack(slot, row, target):
    return (slot << 16) | (row << 8) | target


def unpack(word):
    return word >> 16, (word >> 8) & 255, word & 255


def stage_blocks(index, place, blocks, blks, groups, tiles_dev):
    capacity = blocks.shape[0]
    assert blks * tiles_dev < 256 and groups * tiles_dev < 256 and capacity < 2**15
    return pl.pallas_call(
        functools.partial(stage_kernel, blks, groups, tiles_dev),
        out_shape=[
            jax.ShapeDtypeStruct((STAGES + 1, capacity + 2 * UNROLL), jnp.int32),
            jax.ShapeDtypeStruct(blocks.shape, blocks.dtype),
        ],
        in_specs=[SMEM, HBM, HBM],
        out_specs=[SMEM, VMEM],
        scratch_shapes=[
            pltpu.SMEM(index.shape, index.dtype),
            pltpu.SemaphoreType.DMA((2,)),
        ],
        compiler_params=LIMIT,
        cost_estimate=pl.CostEstimate(flops=0, bytes_accessed=0, transcendentals=0),
    )(place, *in_hbm(index, blocks))


def add_products(stage, order_ref, blocks, source, total):
    @pl.loop(0, order_ref[stage, order_ref.shape[1] - UNROLL])
    def _(batch):
        made = []
        for part in range(UNROLL):
            slot, row, target = unpack(order_ref[stage, batch * UNROLL + part])
            product = jnp.dot(blocks[slot], source[row], preferred_element_type=jnp.float32)
            made.append((target, product))
        for target, product in made:
            total[target] += product


def gather_panels(panels, source):
    for at, panel in enumerate(panels):
        rows = panel.shape[0]
        source[at * rows : (at + 1) * rows] = panel[...]


def early_kernel(order_ref, panel, blocks, total):
    total[...] = jnp.zeros_like(total)
    add_products(0, order_ref, blocks, panel, total)


def middle_kernel(order_ref, *refs):
    *panels, blocks, _, total, source = refs
    gather_panels(panels, source)
    add_products(1, order_ref, blocks, source, total)


def far_kernel(order_ref, *refs):
    *panels, blocks, total, far, source = refs
    gather_panels(panels, source)
    add_products(2, order_ref, blocks, source, total)
    far[...] = total[: far.shape[0]].astype(far.dtype)


def first_kernel(order_ref, *refs):
    *panels, blocks, first, source, total = refs
    gather_panels(panels, source)
    total[...] = jnp.zeros_like(total)
    add_products(3, order_ref, blocks, source, total)
    first[...] = total[: first.shape[0]].astype(first.dtype)


def rest_kernel(order_ref, *refs):
    *panels, blocks, own, later, source, total = refs
    gather_panels(panels, source)
    total[...] = jnp.zeros_like(total)
    add_products(4, order_ref, blocks, source, total)
    tiles_dev = own.shape[0]
    own[...] = total[:tiles_dev]
    later[...] = total[tiles_dev : tiles_dev + later.shape[0]]


def final_kernel(factors, own, *refs):
    *arrived, out_hbm, out, sems = refs
    copies = []
    for tile in range(out.shape[0]):
        value = own[tile]
        for piece in arrived:
            value = value + piece[tile].astype(jnp.float32)
        out[tile] = (value * factors[tile]).astype(out.dtype)
        copies.append(pltpu.make_async_copy(out.at[tile], out_hbm.at[tile], sems.at[tile]))
        copies[-1].start()
    for copy in copies:
        copy.wait()


def cost_of(slots, tile_rows, row_width):
    return pl.CostEstimate(
        flops=2 * slots * tile_rows * tile_rows * row_width,
        bytes_accessed=2 * slots * tile_rows * tile_rows,
        transcendentals=0,
    )


def shards(embed_codes, embed_exps, degrees, adjacency, block_index):
    tile_rows = adjacency.shape[2]
    row_width = embed_codes.shape[2]
    row_count = embed_codes.shape[1]
    capacity = adjacency.shape[1]
    tiles_dev = row_count // tile_rows
    groups = lax.axis_size("grp")
    blks = lax.axis_size("blk")
    part = (tiles_dev, tile_rows, row_width)
    source, factors = scale_rows(embed_codes.reshape(part), embed_exps, degrees)

    def across(value, step):
        pairs = [
            (side * blks + at, (1 - side) * blks + (at ^ (2 * step if at & 1 else blks - 2 - 2 * step)))
            for side in range(2)
            for at in range(blks)
        ]
        return lax.ppermute(value, ("side", "blk"), pairs)

    def paired(value, axis, hop):
        return lax.ppermute(value, axis, [(at, at ^ hop) for at in range(lax.axis_size(axis))])

    place = jnp.stack([lax.axis_index("blk"), lax.axis_index("grp")]).astype(jnp.int32)
    early, *middle = [across(source, step) for step in range(blks // 2)]
    order, blocks = stage_blocks(block_index[0], place, adjacency[0], blks, groups, tiles_dev)
    early, order = lax.optimization_barrier((early, order))
    other = paired(early, "blk", 1)
    far_tiles = (groups // 2 - 1) * tiles_dev

    def held(count, dtype):
        return pltpu.VMEM((count, tile_rows, row_width), dtype)

    total = pl.pallas_call(
        early_kernel,
        out_shape=jax.ShapeDtypeStruct((far_tiles + 1, tile_rows, row_width), jnp.float32),
        in_specs=[SMEM] + [VMEM] * 2,
        out_specs=VMEM,
        compiler_params=LIMIT,
        cost_estimate=cost_of(capacity // 8, tile_rows, row_width),
    )(order, early, blocks)
    *middle, total = lax.optimization_barrier((*middle, total))
    others = [other] + [paired(panel, "blk", 1) for panel in middle]
    total = pl.pallas_call(
        middle_kernel,
        out_shape=jax.ShapeDtypeStruct(total.shape, total.dtype),
        in_specs=[SMEM] + [VMEM] * (len(middle) + 2),
        out_specs=VMEM,
        input_output_aliases={len(middle) + 2: 0},
        scratch_shapes=[held(len(middle) * tiles_dev, jnp.bfloat16)],
        compiler_params=LIMIT,
        cost_estimate=cost_of(capacity // 8, tile_rows, row_width),
    )(order, *middle, blocks, total)
    *others, total = lax.optimization_barrier((*others, total))
    far = pl.pallas_call(
        far_kernel,
        out_shape=jax.ShapeDtypeStruct((far_tiles, tile_rows, row_width), jnp.bfloat16),
        in_specs=[SMEM] + [VMEM] * (len(others) + 2),
        out_specs=VMEM,
        scratch_shapes=[held(len(others) * tiles_dev, jnp.bfloat16)],
        compiler_params=LIMIT,
        cost_estimate=cost_of(capacity // 8, tile_rows, row_width),
    )(order, *others, blocks, total)
    far, order = lax.optimization_barrier((far, order))
    panels = [early] + middle + others
    first = pl.pallas_call(
        first_kernel,
        out_shape=jax.ShapeDtypeStruct(part, jnp.bfloat16),
        in_specs=[SMEM] + [VMEM] * (len(panels) + 1),
        out_specs=VMEM,
        scratch_shapes=[
            held(len(panels) * tiles_dev, jnp.bfloat16),
            held(tiles_dev + 1, jnp.float32),
        ],
        compiler_params=LIMIT,
        cost_estimate=cost_of(capacity // 4, tile_rows, row_width),
    )(order, *panels, blocks)
    first, order = lax.optimization_barrier((first, order))
    own, later = pl.pallas_call(
        rest_kernel,
        out_shape=[
            jax.ShapeDtypeStruct(part, jnp.float32),
            jax.ShapeDtypeStruct((far_tiles, tile_rows, row_width), jnp.float32),
        ],
        in_specs=[SMEM] + [VMEM] * (len(panels) + 1),
        out_specs=[VMEM] * 2,
        scratch_shapes=[
            held(len(panels) * tiles_dev, jnp.bfloat16),
            held(groups // 2 * tiles_dev + 1, jnp.float32),
        ],
        compiler_params=LIMIT,
        cost_estimate=cost_of(capacity // 2, tile_rows, row_width),
    )(order, *panels, blocks)

    def turned(value, odd_hop, even_hop):
        hops = (even_hop, odd_hop)
        pairs = [
            (at * blks + blk, (at ^ hops[blk & 1]) * blks + blk)
            for at in range(groups)
            for blk in range(blks)
        ]
        return lax.ppermute(value, ("grp", "blk"), pairs)

    steps = groups // 2 - 1
    odd_core = lax.axis_index("blk") % 2 == 1
    pieces = [slice(at * tiles_dev, (at + 1) * tiles_dev) for at in range(steps)]
    handed = [turned(far[pieces[at]], 1, 2 * at + 2).astype(jnp.float32) for at in range(steps)]
    arrived = [turned(first, 1, 2)]
    for at in range(steps):
        value = later[pieces[at]]
        for step, extra in enumerate(handed):
            if step == at == steps - 1:
                value = value + extra
            elif step == at:
                value = value + jnp.where(odd_core, extra, 0.0)
            elif at == steps - 1:
                value = value + jnp.where(odd_core, 0.0, extra)
        even_hop = 1 if at == steps - 1 else 2 * at + 4
        arrived.append(turned(value.astype(jnp.bfloat16), 2 * at + 2, even_hop))
    own = own + arrived[0].astype(jnp.float32)
    own, *sums = lax.optimization_barrier((own, *arrived[1:]))
    out = pl.pallas_call(
        final_kernel,
        out_shape=jax.ShapeDtypeStruct(part, jnp.bfloat16),
        in_specs=[VMEM] * (2 + len(sums)),
        out_specs=HBM,
        scratch_shapes=[
            held(tiles_dev, jnp.bfloat16),
            pltpu.SemaphoreType.DMA((tiles_dev,)),
        ],
        compiler_params=LIMIT,
        cost_estimate=cost_of(0, tile_rows, row_width),
    )(factors, own, *sums)
    return out.reshape(1, row_count, row_width)


def solution(mesh):
    placed = (
        P("side", ("grp", "blk"), None),
        P("side", ("grp", "blk")),
        P("side", ("grp", "blk")),
        P("side", ("grp", "blk"), None, None),
        P("side", None, ("grp", "blk")),
    )
    return jax.shard_map(
        shards,
        mesh=mesh,
        in_specs=placed,
        out_specs=P("side", ("grp", "blk"), None),
        check_vma=False,
    )
```

```python
import functools

import jax
import jax.numpy as jnp
from jax import lax
from jax.experimental import pallas as pl
from jax.experimental.pallas import tpu as pltpu
from jax.sharding import PartitionSpec as P

UNROLL = 8
STAGES = 5
VMEM = pl.BlockSpec(memory_space=pltpu.VMEM)
SMEM = pl.BlockSpec(memory_space=pltpu.SMEM)
HBM = pl.BlockSpec(memory_space=pltpu.HBM)
LIMIT = pltpu.CompilerParams(vmem_limit_bytes=48 * 1024 * 1024)


def in_hbm(*arrays):
    return [pltpu.with_memory_space_constraint(array, pltpu.HBM) for array in arrays]


def split(value, size):
    if size & (size - 1) == 0:
        return value >> (size.bit_length() - 1), value & (size - 1)
    return value // size, value % size


def scale_kernel(exps_hbm, degrees_hbm, codes_hbm, rows, factors, exps_ref, degrees, codes, sems):
    pairs = [(exps_hbm, exps_ref), (degrees_hbm, degrees), (codes_hbm, codes)]
    fetches = [
        pltpu.make_async_copy(held, wanted, sems.at[at])
        for at, (held, wanted) in enumerate(pairs)
    ]
    for fetch in fetches:
        fetch.start()
    fetches[0].wait()
    fetches[1].wait()
    tiles_dev, tile_rows, row_width = rows.shape
    inverse = lax.rsqrt(degrees[...].astype(jnp.float32))
    for tile in range(tiles_dev):
        lanes = inverse[:, tile * tile_rows : (tile + 1) * tile_rows]
        factors[tile] = jnp.broadcast_to(lanes, (row_width, tile_rows)).T
    fetches[2].wait()
    for tile in range(tiles_dev):
        scale = jnp.exp2(jnp.full((1, 1), exps_ref[0, tile], jnp.int32).astype(jnp.float32))
        scaled = codes[tile].astype(jnp.float32) * scale * factors[tile]
        rows[tile] = scaled.astype(rows.dtype)


def scale_rows(codes, exps, degrees):
    return pl.pallas_call(
        scale_kernel,
        out_shape=[
            jax.ShapeDtypeStruct(codes.shape, jnp.bfloat16),
            jax.ShapeDtypeStruct(codes.shape, jnp.float32),
        ],
        in_specs=[HBM] * 3,
        out_specs=[VMEM] * 2,
        scratch_shapes=[
            pltpu.SMEM(exps.shape, exps.dtype),
            pltpu.VMEM(degrees.shape, degrees.dtype),
            pltpu.VMEM(codes.shape, codes.dtype),
            pltpu.SemaphoreType.DMA((3,)),
        ],
        compiler_params=LIMIT,
        cost_estimate=pl.CostEstimate(
            flops=codes.size, bytes_accessed=4 * codes.size, transcendentals=0
        ),
    )(*in_hbm(exps, degrees, codes))


def count_up(shape, axis):
    return lax.broadcasted_iota(jnp.int32, shape, axis)


def stage_kernel(
    blks, groups, tiles_dev, place_ref, index_hbm, blocks_hbm, order_ref, blocks, index_ref, sems
):
    fetch = pltpu.make_async_copy(index_hbm, index_ref, sems.at[0])
    fetch.start()
    copy = pltpu.make_async_copy(blocks_hbm, blocks, sems.at[1])
    copy.start()
    fetch.wait()
    my_blk = place_ref[0]
    my_grp = place_ref[1]
    capacity = index_ref.shape[1]
    width = order_ref.shape[1]
    source_tiles = blks * tiles_dev
    half = blks // 2
    role = my_blk & 1

    target = index_ref[0:1, :]
    origin = index_ref[1:2, :]
    hop, row = split(origin, tiles_dev)
    chunk, tile = split(target, tiles_dev)
    hop = hop ^ my_blk
    chunk = chunk ^ my_grp
    odd = hop & 1
    rank = jnp.where(odd == role, half - 1 - (hop >> 1), hop >> 1)
    far = (chunk >= 2) & ((chunk & 1) == 1)
    kept = jnp.where(chunk == 1, 1 + role * (groups // 2 - 1), (chunk >> 1) + 1 - role)
    kept = jnp.where(chunk == 0, 0, jnp.where(far, (chunk >> 1) - 1, kept))
    stage = jnp.where(far, jnp.where(odd == 1, 2, jnp.minimum(rank, 1)), 4)
    stage = jnp.where(far | (kept != 1), stage, 3)
    kept = jnp.where(far, kept, jnp.where(stage == 3, 0, kept - (kept > 1).astype(jnp.int32)))
    stage = jnp.where(origin < source_tiles, stage, STAGES)
    panel = jnp.where(stage == 1, rank - 1, jnp.where(stage == 2, rank, rank + odd * half))
    slot = count_up((1, capacity), 1)

    stages = (count_up((8, capacity), 0) == stage).astype(jnp.float32)
    earlier = count_up((capacity, capacity), 0) < count_up((capacity, capacity), 1)
    before = jnp.dot(
        stages.astype(jnp.bfloat16), earlier.astype(jnp.bfloat16), preferred_element_type=jnp.float32
    )
    position = jnp.sum(stages * before, axis=0, keepdims=True).astype(jnp.int32)
    parts = (slot & 127, slot >> 7, panel * tiles_dev + row, kept * tiles_dev + tile)
    values = sum(
        jnp.where(count_up((8, capacity), 0) == at, part, 0) for at, part in enumerate(parts)
    ).astype(jnp.bfloat16)
    far_tiles = (groups // 2 - 1) * tiles_dev
    tops = [far_tiles] * 3 + [tiles_dev, groups // 2 * tiles_dev]
    lanes = count_up((1, width), 1)
    for at, top in enumerate(tops):
        where = jnp.where(stage == at, position, -1)
        chosen = (count_up((width, capacity), 0) == where).astype(jnp.bfloat16)
        listed = lax.dot_general(
            values, chosen, (((1,), (1,)), ((), ())), preferred_element_type=jnp.float32
        ).astype(jnp.int32)
        word = pack(listed[0:1] + (listed[1:2] << 7), listed[2:3], listed[3:4])
        count = jnp.sum((stage == at).astype(jnp.int32), axis=1, keepdims=True)
        word = jnp.where(lanes < count, word, pack(0, 0, top))
        batches = split(count + (UNROLL - 1), UNROLL)[0]
        order_ref[at : at + 1, :] = jnp.where(lanes == width - UNROLL, batches, word)
    copy.wait()


def pack(slot, row, target):
    return (slot << 16) | (row << 8) | target


def unpack(word):
    return word >> 16, (word >> 8) & 255, word & 255


def stage_blocks(index, place, blocks, blks, groups, tiles_dev):
    capacity = blocks.shape[0]
    assert blks * tiles_dev < 256 and groups * tiles_dev < 256 and capacity < 2**15
    width = -(-(capacity + 2 * UNROLL) // 128) * 128
    return pl.pallas_call(
        functools.partial(stage_kernel, blks, groups, tiles_dev),
        out_shape=[
            jax.ShapeDtypeStruct((8, width), jnp.int32),
            jax.ShapeDtypeStruct(blocks.shape, blocks.dtype),
        ],
        in_specs=[SMEM, HBM, HBM],
        out_specs=[VMEM, VMEM],
        scratch_shapes=[
            pltpu.VMEM(index.shape, index.dtype),
            pltpu.SemaphoreType.DMA((2,)),
        ],
        compiler_params=LIMIT,
        cost_estimate=pl.CostEstimate(flops=0, bytes_accessed=0, transcendentals=0),
    )(place, *in_hbm(index, blocks))


def add_products(stage, order_ref, blocks, source, total):
    @pl.loop(0, order_ref[stage, order_ref.shape[1] - UNROLL])
    def _(batch):
        made = []
        for part in range(UNROLL):
            slot, row, target = unpack(order_ref[stage, batch * UNROLL + part])
            product = jnp.dot(blocks[slot], source[row], preferred_element_type=jnp.float32)
            made.append((target, product))
        for target, product in made:
            total[target] += product


def gather_panels(panels, source):
    for at, panel in enumerate(panels):
        rows = panel.shape[0]
        source[at * rows : (at + 1) * rows] = panel[...]


def early_kernel(order_ref, panel, blocks, total):
    total[...] = jnp.zeros_like(total)
    add_products(0, order_ref, blocks, panel, total)


def middle_kernel(order_ref, *refs):
    *panels, blocks, _, total, source = refs
    gather_panels(panels, source)
    add_products(1, order_ref, blocks, source, total)


def far_kernel(order_ref, *refs):
    *panels, blocks, total, far, source = refs
    gather_panels(panels, source)
    add_products(2, order_ref, blocks, source, total)
    far[...] = total[: far.shape[0]].astype(far.dtype)


def first_kernel(order_ref, *refs):
    *panels, blocks, first, source, total = refs
    gather_panels(panels, source)
    total[...] = jnp.zeros_like(total)
    add_products(3, order_ref, blocks, source, total)
    first[...] = total[: first.shape[0]].astype(first.dtype)


def rest_kernel(order_ref, *refs):
    *panels, blocks, own, later, source, total = refs
    gather_panels(panels, source)
    total[...] = jnp.zeros_like(total)
    add_products(4, order_ref, blocks, source, total)
    tiles_dev = own.shape[0]
    own[...] = total[:tiles_dev]
    later[...] = total[tiles_dev : tiles_dev + later.shape[0]]


def final_kernel(factors, own, *refs):
    *arrived, out_hbm, out, sems = refs
    copies = []
    for tile in range(out.shape[0]):
        value = own[tile]
        for piece in arrived:
            value = value + piece[tile].astype(jnp.float32)
        out[tile] = (value * factors[tile]).astype(out.dtype)
        copies.append(pltpu.make_async_copy(out.at[tile], out_hbm.at[tile], sems.at[tile]))
        copies[-1].start()
    for copy in copies:
        copy.wait()


def cost_of(slots, tile_rows, row_width):
    return pl.CostEstimate(
        flops=2 * slots * tile_rows * tile_rows * row_width,
        bytes_accessed=2 * slots * tile_rows * tile_rows,
        transcendentals=0,
    )


def shards(embed_codes, embed_exps, degrees, adjacency, block_index):
    tile_rows = adjacency.shape[2]
    row_width = embed_codes.shape[2]
    row_count = embed_codes.shape[1]
    capacity = adjacency.shape[1]
    tiles_dev = row_count // tile_rows
    groups = lax.axis_size("grp")
    blks = lax.axis_size("blk")
    part = (tiles_dev, tile_rows, row_width)
    source, factors = scale_rows(embed_codes.reshape(part), embed_exps, degrees)

    def across(value, step):
        pairs = [
            (side * blks + at, (1 - side) * blks + (at ^ (2 * step if at & 1 else blks - 2 - 2 * step)))
            for side in range(2)
            for at in range(blks)
        ]
        return lax.ppermute(value, ("side", "blk"), pairs)

    def paired(value, axis, hop):
        return lax.ppermute(value, axis, [(at, at ^ hop) for at in range(lax.axis_size(axis))])

    place = jnp.stack([lax.axis_index("blk"), lax.axis_index("grp")]).astype(jnp.int32)
    early, *middle = [across(source, step) for step in range(blks // 2)]
    order, blocks = stage_blocks(block_index[0], place, adjacency[0], blks, groups, tiles_dev)
    early, order = lax.optimization_barrier((early, order))
    other = paired(early, "blk", 1)
    far_tiles = (groups // 2 - 1) * tiles_dev

    def held(count, dtype):
        return pltpu.VMEM((count, tile_rows, row_width), dtype)

    total = pl.pallas_call(
        early_kernel,
        out_shape=jax.ShapeDtypeStruct((far_tiles + 1, tile_rows, row_width), jnp.float32),
        in_specs=[SMEM] + [VMEM] * 2,
        out_specs=VMEM,
        compiler_params=LIMIT,
        cost_estimate=cost_of(capacity // 8, tile_rows, row_width),
    )(order, early, blocks)
    *middle, total = lax.optimization_barrier((*middle, total))
    others = [other] + [paired(panel, "blk", 1) for panel in middle]
    total = pl.pallas_call(
        middle_kernel,
        out_shape=jax.ShapeDtypeStruct(total.shape, total.dtype),
        in_specs=[SMEM] + [VMEM] * (len(middle) + 2),
        out_specs=VMEM,
        input_output_aliases={len(middle) + 2: 0},
        scratch_shapes=[held(len(middle) * tiles_dev, jnp.bfloat16)],
        compiler_params=LIMIT,
        cost_estimate=cost_of(capacity // 8, tile_rows, row_width),
    )(order, *middle, blocks, total)
    *others, total = lax.optimization_barrier((*others, total))
    far = pl.pallas_call(
        far_kernel,
        out_shape=jax.ShapeDtypeStruct((far_tiles, tile_rows, row_width), jnp.bfloat16),
        in_specs=[SMEM] + [VMEM] * (len(others) + 2),
        out_specs=VMEM,
        scratch_shapes=[held(len(others) * tiles_dev, jnp.bfloat16)],
        compiler_params=LIMIT,
        cost_estimate=cost_of(capacity // 8, tile_rows, row_width),
    )(order, *others, blocks, total)
    far, order = lax.optimization_barrier((far, order))
    panels = [early] + middle + others
    first = pl.pallas_call(
        first_kernel,
        out_shape=jax.ShapeDtypeStruct(part, jnp.bfloat16),
        in_specs=[SMEM] + [VMEM] * (len(panels) + 1),
        out_specs=VMEM,
        scratch_shapes=[
            held(len(panels) * tiles_dev, jnp.bfloat16),
            held(tiles_dev + 1, jnp.float32),
        ],
        compiler_params=LIMIT,
        cost_estimate=cost_of(capacity // 4, tile_rows, row_width),
    )(order, *panels, blocks)
    first, order = lax.optimization_barrier((first, order))
    own, later = pl.pallas_call(
        rest_kernel,
        out_shape=[
            jax.ShapeDtypeStruct(part, jnp.float32),
            jax.ShapeDtypeStruct((far_tiles, tile_rows, row_width), jnp.float32),
        ],
        in_specs=[SMEM] + [VMEM] * (len(panels) + 1),
        out_specs=[VMEM] * 2,
        scratch_shapes=[
            held(len(panels) * tiles_dev, jnp.bfloat16),
            held(groups // 2 * tiles_dev + 1, jnp.float32),
        ],
        compiler_params=LIMIT,
        cost_estimate=cost_of(capacity // 2, tile_rows, row_width),
    )(order, *panels, blocks)

    def turned(value, even_hop, odd_hop):
        hops = (even_hop, odd_hop)
        pairs = [
            (at * blks + blk, (at ^ hops[blk & 1]) * blks + blk)
            for at in range(groups)
            for blk in range(blks)
        ]
        return lax.ppermute(value, ("grp", "blk"), pairs)

    steps = groups // 2 - 1
    even_core = lax.axis_index("blk") % 2 == 0
    pieces = [slice(at * tiles_dev, (at + 1) * tiles_dev) for at in range(steps)]
    handed = [turned(far[pieces[at]], 1, 2 * at + 2).astype(jnp.float32) for at in range(steps)]
    arrived = [turned(first, 1, 2)]
    for at in range(steps):
        value = later[pieces[at]]
        for step, extra in enumerate(handed):
            if step == at == steps - 1:
                value = value + extra
            elif step == at:
                value = value + jnp.where(even_core, extra, 0.0)
            elif at == steps - 1:
                value = value + jnp.where(even_core, 0.0, extra)
        odd_hop = 1 if at == steps - 1 else 2 * at + 4
        arrived.append(turned(value.astype(jnp.bfloat16), 2 * at + 2, odd_hop))
    own = own + arrived[0].astype(jnp.float32)
    own, *sums = lax.optimization_barrier((own, *arrived[1:]))
    out = pl.pallas_call(
        final_kernel,
        out_shape=jax.ShapeDtypeStruct(part, jnp.bfloat16),
        in_specs=[VMEM] * (2 + len(sums)),
        out_specs=HBM,
        scratch_shapes=[
            held(tiles_dev, jnp.bfloat16),
            pltpu.SemaphoreType.DMA((tiles_dev,)),
        ],
        compiler_params=LIMIT,
        cost_estimate=cost_of(0, tile_rows, row_width),
    )(factors, own, *sums)
    return out.reshape(1, row_count, row_width)


def solution(mesh):
    placed = (
        P("side", ("grp", "blk"), None),
        P("side", ("grp", "blk")),
        P("side", ("grp", "blk")),
        P("side", ("grp", "blk"), None, None),
        P("side", None, ("grp", "blk")),
    )
    return jax.shard_map(
        shards,
        mesh=mesh,
        in_specs=placed,
        out_specs=P("side", ("grp", "blk"), None),
        check_vma=False,
    )
```

```python
import functools

import jax
import jax.numpy as jnp
from jax import lax
from jax.experimental import pallas as pl
from jax.experimental.pallas import tpu as pltpu
from jax.sharding import PartitionSpec as P

UNROLL = 8
STAGES = 4
VMEM = pl.BlockSpec(memory_space=pltpu.VMEM)
SMEM = pl.BlockSpec(memory_space=pltpu.SMEM)
HBM = pl.BlockSpec(memory_space=pltpu.HBM)
LIMIT = pltpu.CompilerParams(vmem_limit_bytes=48 * 1024 * 1024)


def in_hbm(*arrays):
    return [pltpu.with_memory_space_constraint(array, pltpu.HBM) for array in arrays]


def split(value, size):
    if size & (size - 1) == 0:
        return value >> (size.bit_length() - 1), value & (size - 1)
    return value // size, value % size


def scale_kernel(exps_hbm, degrees_hbm, codes_hbm, rows, factors, exps_ref, degrees, codes, sems):
    pairs = [(exps_hbm, exps_ref), (degrees_hbm, degrees), (codes_hbm, codes)]
    fetches = [
        pltpu.make_async_copy(held, wanted, sems.at[at])
        for at, (held, wanted) in enumerate(pairs)
    ]
    for fetch in fetches:
        fetch.start()
    fetches[0].wait()
    fetches[1].wait()
    tiles_dev, tile_rows, row_width = rows.shape
    inverse = lax.rsqrt(degrees[...].astype(jnp.float32))
    for tile in range(tiles_dev):
        lanes = inverse[:, tile * tile_rows : (tile + 1) * tile_rows]
        factors[tile] = jnp.broadcast_to(lanes, (row_width, tile_rows)).T
    fetches[2].wait()
    for tile in range(tiles_dev):
        scale = jnp.exp2(jnp.full((1, 1), exps_ref[0, tile], jnp.int32).astype(jnp.float32))
        scaled = codes[tile].astype(jnp.float32) * scale * factors[tile]
        rows[tile] = scaled.astype(rows.dtype)


def scale_rows(codes, exps, degrees):
    return pl.pallas_call(
        scale_kernel,
        out_shape=[
            jax.ShapeDtypeStruct(codes.shape, jnp.bfloat16),
            jax.ShapeDtypeStruct(codes.shape, jnp.float32),
        ],
        in_specs=[HBM] * 3,
        out_specs=[VMEM] * 2,
        scratch_shapes=[
            pltpu.SMEM(exps.shape, exps.dtype),
            pltpu.VMEM(degrees.shape, degrees.dtype),
            pltpu.VMEM(codes.shape, codes.dtype),
            pltpu.SemaphoreType.DMA((3,)),
        ],
        compiler_params=LIMIT,
        cost_estimate=pl.CostEstimate(
            flops=codes.size, bytes_accessed=4 * codes.size, transcendentals=0
        ),
    )(*in_hbm(exps, degrees, codes))


def count_up(shape, axis):
    return lax.broadcasted_iota(jnp.int32, shape, axis)


def stage_kernel(
    blks, groups, tiles_dev, place_ref, index_hbm, blocks_hbm, order_ref, blocks, index_ref, sems
):
    fetch = pltpu.make_async_copy(index_hbm, index_ref, sems.at[0])
    fetch.start()
    copy = pltpu.make_async_copy(blocks_hbm, blocks, sems.at[1])
    copy.start()
    fetch.wait()
    my_blk = place_ref[0]
    my_grp = place_ref[1]
    capacity = index_ref.shape[1]
    width = order_ref.shape[1]
    source_tiles = blks * tiles_dev
    half = blks // 2
    role = my_blk & 1

    target = index_ref[0:1, :]
    origin = index_ref[1:2, :]
    hop, row = split(origin, tiles_dev)
    chunk, tile = split(target, tiles_dev)
    hop = hop ^ my_blk
    chunk = chunk ^ my_grp
    odd = hop & 1
    rank = jnp.where(odd == role, half - 1 - (hop >> 1), hop >> 1)
    far = (chunk >= 2) & ((chunk & 1) == 1)
    kept = jnp.where(chunk == 1, 1 + role * (groups // 2 - 1), (chunk >> 1) + 1 - role)
    kept = jnp.where(chunk == 0, 0, jnp.where(far, (chunk >> 1) - 1, kept))
    stage = jnp.where(far, jnp.where(odd == 1, 2, jnp.minimum(rank, 1)), 3)
    stage = jnp.where(origin < source_tiles, stage, STAGES)
    panel = jnp.where(stage == 1, rank - 1, jnp.where(stage == 2, rank, rank + odd * half))
    slot = count_up((1, capacity), 1)

    stages = (count_up((8, capacity), 0) == stage).astype(jnp.float32)
    earlier = count_up((capacity, capacity), 0) < count_up((capacity, capacity), 1)
    before = jnp.dot(
        stages.astype(jnp.bfloat16), earlier.astype(jnp.bfloat16), preferred_element_type=jnp.float32
    )
    position = jnp.sum(stages * before, axis=0, keepdims=True).astype(jnp.int32)
    parts = (slot & 127, slot >> 7, panel * tiles_dev + row, kept * tiles_dev + tile)
    values = sum(
        jnp.where(count_up((8, capacity), 0) == at, part, 0) for at, part in enumerate(parts)
    ).astype(jnp.bfloat16)
    far_tiles = (groups // 2 - 1) * tiles_dev
    tops = [far_tiles] * 3 + [(groups // 2 + 1) * tiles_dev]
    lanes = count_up((1, width), 1)
    for at, top in enumerate(tops):
        where = jnp.where(stage == at, position, -1)
        chosen = (count_up((width, capacity), 0) == where).astype(jnp.bfloat16)
        listed = lax.dot_general(
            values, chosen, (((1,), (1,)), ((), ())), preferred_element_type=jnp.float32
        ).astype(jnp.int32)
        word = pack(listed[0:1] + (listed[1:2] << 7), listed[2:3], listed[3:4])
        count = jnp.sum((stage == at).astype(jnp.int32), axis=1, keepdims=True)
        word = jnp.where(lanes < count, word, pack(0, 0, top))
        batches = split(count + (UNROLL - 1), UNROLL)[0]
        order_ref[at : at + 1, :] = jnp.where(lanes == width - UNROLL, batches, word)
    copy.wait()


def pack(slot, row, target):
    return (slot << 16) | (row << 8) | target


def unpack(word):
    return word >> 16, (word >> 8) & 255, word & 255


def stage_blocks(index, place, blocks, blks, groups, tiles_dev):
    capacity = blocks.shape[0]
    assert blks * tiles_dev < 256 and groups * tiles_dev < 256 and capacity < 2**15
    width = -(-(capacity + 2 * UNROLL) // 128) * 128
    return pl.pallas_call(
        functools.partial(stage_kernel, blks, groups, tiles_dev),
        out_shape=[
            jax.ShapeDtypeStruct((8, width), jnp.int32),
            jax.ShapeDtypeStruct(blocks.shape, blocks.dtype),
        ],
        in_specs=[SMEM, HBM, HBM],
        out_specs=[VMEM, VMEM],
        scratch_shapes=[
            pltpu.VMEM(index.shape, index.dtype),
            pltpu.SemaphoreType.DMA((2,)),
        ],
        compiler_params=LIMIT,
        cost_estimate=pl.CostEstimate(flops=0, bytes_accessed=0, transcendentals=0),
    )(place, *in_hbm(index, blocks))


def add_products(stage, order_ref, blocks, source, total):
    @pl.loop(0, order_ref[stage, order_ref.shape[1] - UNROLL])
    def _(batch):
        made = []
        for part in range(UNROLL):
            slot, row, target = unpack(order_ref[stage, batch * UNROLL + part])
            product = jnp.dot(blocks[slot], source[row], preferred_element_type=jnp.float32)
            made.append((target, product))
        for target, product in made:
            total[target] += product


def gather_panels(panels, source):
    for at, panel in enumerate(panels):
        rows = panel.shape[0]
        source[at * rows : (at + 1) * rows] = panel[...]


def early_kernel(order_ref, panel, blocks, total):
    total[...] = jnp.zeros_like(total)
    add_products(0, order_ref, blocks, panel, total)


def middle_kernel(order_ref, *refs):
    *panels, blocks, _, total, source = refs
    gather_panels(panels, source)
    add_products(1, order_ref, blocks, source, total)


def far_kernel(order_ref, *refs):
    *panels, blocks, total, far, source = refs
    gather_panels(panels, source)
    add_products(2, order_ref, blocks, source, total)
    far[...] = total[: far.shape[0]].astype(far.dtype)


def rest_kernel(order_ref, *refs):
    *panels, blocks, own, first, later, source, total = refs
    gather_panels(panels, source)
    total[...] = jnp.zeros_like(total)
    add_products(3, order_ref, blocks, source, total)
    tiles_dev = own.shape[0]
    own[...] = total[:tiles_dev]
    first[...] = total[tiles_dev : 2 * tiles_dev].astype(first.dtype)
    later[...] = total[2 * tiles_dev : 2 * tiles_dev + later.shape[0]]


def final_kernel(factors, own, *refs):
    *arrived, out_hbm, out, sems = refs
    copies = []
    for tile in range(out.shape[0]):
        value = own[tile]
        for piece in arrived:
            value = value + piece[tile].astype(jnp.float32)
        out[tile] = (value * factors[tile]).astype(out.dtype)
        copies.append(pltpu.make_async_copy(out.at[tile], out_hbm.at[tile], sems.at[tile]))
        copies[-1].start()
    for copy in copies:
        copy.wait()


def cost_of(slots, tile_rows, row_width):
    return pl.CostEstimate(
        flops=2 * slots * tile_rows * tile_rows * row_width,
        bytes_accessed=2 * slots * tile_rows * tile_rows,
        transcendentals=0,
    )


def shards(embed_codes, embed_exps, degrees, adjacency, block_index):
    tile_rows = adjacency.shape[2]
    row_width = embed_codes.shape[2]
    row_count = embed_codes.shape[1]
    capacity = adjacency.shape[1]
    tiles_dev = row_count // tile_rows
    groups = lax.axis_size("grp")
    blks = lax.axis_size("blk")
    part = (tiles_dev, tile_rows, row_width)
    source, factors = scale_rows(embed_codes.reshape(part), embed_exps, degrees)

    def across(value, step):
        pairs = [
            (side * blks + at, (1 - side) * blks + (at ^ (2 * step if at & 1 else blks - 2 - 2 * step)))
            for side in range(2)
            for at in range(blks)
        ]
        return lax.ppermute(value, ("side", "blk"), pairs)

    def paired(value, axis, hop):
        return lax.ppermute(value, axis, [(at, at ^ hop) for at in range(lax.axis_size(axis))])

    place = jnp.stack([lax.axis_index("blk"), lax.axis_index("grp")]).astype(jnp.int32)
    early, *middle = [across(source, step) for step in range(blks // 2)]
    order, blocks = stage_blocks(block_index[0], place, adjacency[0], blks, groups, tiles_dev)
    early, order = lax.optimization_barrier((early, order))
    other = paired(early, "blk", 1)
    far_tiles = (groups // 2 - 1) * tiles_dev

    def held(count, dtype):
        return pltpu.VMEM((count, tile_rows, row_width), dtype)

    total = pl.pallas_call(
        early_kernel,
        out_shape=jax.ShapeDtypeStruct((far_tiles + 1, tile_rows, row_width), jnp.float32),
        in_specs=[SMEM] + [VMEM] * 2,
        out_specs=VMEM,
        compiler_params=LIMIT,
        cost_estimate=cost_of(capacity // 8, tile_rows, row_width),
    )(order, early, blocks)
    *middle, total = lax.optimization_barrier((*middle, total))
    others = [other] + [paired(panel, "blk", 1) for panel in middle]
    total = pl.pallas_call(
        middle_kernel,
        out_shape=jax.ShapeDtypeStruct(total.shape, total.dtype),
        in_specs=[SMEM] + [VMEM] * (len(middle) + 2),
        out_specs=VMEM,
        input_output_aliases={len(middle) + 2: 0},
        scratch_shapes=[held(len(middle) * tiles_dev, jnp.bfloat16)],
        compiler_params=LIMIT,
        cost_estimate=cost_of(capacity // 8, tile_rows, row_width),
    )(order, *middle, blocks, total)
    *others, total = lax.optimization_barrier((*others, total))
    far = pl.pallas_call(
        far_kernel,
        out_shape=jax.ShapeDtypeStruct((far_tiles, tile_rows, row_width), jnp.bfloat16),
        in_specs=[SMEM] + [VMEM] * (len(others) + 2),
        out_specs=VMEM,
        scratch_shapes=[held(len(others) * tiles_dev, jnp.bfloat16)],
        compiler_params=LIMIT,
        cost_estimate=cost_of(capacity // 8, tile_rows, row_width),
    )(order, *others, blocks, total)
    far, order = lax.optimization_barrier((far, order))
    panels = [early] + middle + others
    own, first, later = pl.pallas_call(
        rest_kernel,
        out_shape=[
            jax.ShapeDtypeStruct(part, jnp.float32),
            jax.ShapeDtypeStruct(part, jnp.bfloat16),
            jax.ShapeDtypeStruct((far_tiles, tile_rows, row_width), jnp.float32),
        ],
        in_specs=[SMEM] + [VMEM] * (len(panels) + 1),
        out_specs=[VMEM] * 3,
        scratch_shapes=[
            held(len(panels) * tiles_dev, jnp.bfloat16),
            held((groups // 2 + 1) * tiles_dev + 1, jnp.float32),
        ],
        compiler_params=LIMIT,
        cost_estimate=cost_of(capacity, tile_rows, row_width),
    )(order, *panels, blocks)

    def turned(value, even_hop, odd_hop):
        hops = (even_hop, odd_hop)
        pairs = [
            (at * blks + blk, (at ^ hops[blk & 1]) * blks + blk)
            for at in range(groups)
            for blk in range(blks)
        ]
        return lax.ppermute(value, ("grp", "blk"), pairs)

    steps = groups // 2 - 1
    even_core = lax.axis_index("blk") % 2 == 0
    pieces = [slice(at * tiles_dev, (at + 1) * tiles_dev) for at in range(steps)]
    handed = [turned(far[pieces[at]], 1, 2 * at + 2).astype(jnp.float32) for at in range(steps)]
    arrived = [turned(first, 1, 2)]
    for at in range(steps):
        value = later[pieces[at]]
        for step, extra in enumerate(handed):
            if step == at == steps - 1:
                value = value + extra
            elif step == at:
                value = value + jnp.where(even_core, extra, 0.0)
            elif at == steps - 1:
                value = value + jnp.where(even_core, 0.0, extra)
        odd_hop = 1 if at == steps - 1 else 2 * at + 4
        arrived.append(turned(value.astype(jnp.bfloat16), 2 * at + 2, odd_hop))
    own = own + arrived[0].astype(jnp.float32)
    own, *sums = lax.optimization_barrier((own, *arrived[1:]))
    out = pl.pallas_call(
        final_kernel,
        out_shape=jax.ShapeDtypeStruct(part, jnp.bfloat16),
        in_specs=[VMEM] * (2 + len(sums)),
        out_specs=HBM,
        scratch_shapes=[
            held(tiles_dev, jnp.bfloat16),
            pltpu.SemaphoreType.DMA((tiles_dev,)),
        ],
        compiler_params=LIMIT,
        cost_estimate=cost_of(0, tile_rows, row_width),
    )(factors, own, *sums)
    return out.reshape(1, row_count, row_width)


def solution(mesh):
    placed = (
        P("side", ("grp", "blk"), None),
        P("side", ("grp", "blk")),
        P("side", ("grp", "blk")),
        P("side", ("grp", "blk"), None, None),
        P("side", None, ("grp", "blk")),
    )
    return jax.shard_map(
        shards,
        mesh=mesh,
        in_specs=placed,
        out_specs=P("side", ("grp", "blk"), None),
        check_vma=False,
    )
```

```python
import functools

import jax
import jax.numpy as jnp
from jax import lax
from jax.experimental import pallas as pl
from jax.experimental.pallas import tpu as pltpu
from jax.sharding import PartitionSpec as P

UNROLL = 8
STAGES = 5
VMEM = pl.BlockSpec(memory_space=pltpu.VMEM)
SMEM = pl.BlockSpec(memory_space=pltpu.SMEM)
HBM = pl.BlockSpec(memory_space=pltpu.HBM)
LIMIT = pltpu.CompilerParams(vmem_limit_bytes=48 * 1024 * 1024)


def in_hbm(*arrays):
    return [pltpu.with_memory_space_constraint(array, pltpu.HBM) for array in arrays]


def split(value, size):
    if size & (size - 1) == 0:
        return value >> (size.bit_length() - 1), value & (size - 1)
    return value // size, value % size


def scale_kernel(
    exps_hbm, degrees_hbm, codes_hbm, rows, factors, scales, exps_ref, degrees, codes, sems
):
    pairs = [(exps_hbm, exps_ref), (degrees_hbm, degrees), (codes_hbm, codes)]
    fetches = [
        pltpu.make_async_copy(held, wanted, sems.at[at])
        for at, (held, wanted) in enumerate(pairs)
    ]
    for fetch in fetches:
        fetch.start()
    fetches[0].wait()
    fetches[1].wait()
    tiles_dev, tile_rows, row_width = rows.shape
    inverse = lax.rsqrt(degrees[...].astype(jnp.float32))
    for tile in range(tiles_dev):
        lanes = inverse[:, tile * tile_rows : (tile + 1) * tile_rows]
        factors[tile] = jnp.broadcast_to(lanes, (row_width, tile_rows)).T
        scale = jnp.exp2(jnp.full((1, 1), exps_ref[0, tile], jnp.int32).astype(jnp.float32))
        scales[tile : tile + 1, :] = lanes * scale
    fetches[2].wait()
    for tile in range(tiles_dev):
        scale = jnp.exp2(jnp.full((1, 1), exps_ref[0, tile], jnp.int32).astype(jnp.float32))
        scaled = codes[tile].astype(jnp.float32) * scale * factors[tile]
        rows[tile] = scaled.astype(rows.dtype)


def scale_rows(codes, exps, degrees):
    return pl.pallas_call(
        scale_kernel,
        out_shape=[
            jax.ShapeDtypeStruct(codes.shape, jnp.bfloat16),
            jax.ShapeDtypeStruct(codes.shape, jnp.float32),
            jax.ShapeDtypeStruct(codes.shape[:2], jnp.float32),
        ],
        in_specs=[HBM] * 3,
        out_specs=[VMEM] * 3,
        scratch_shapes=[
            pltpu.SMEM(exps.shape, exps.dtype),
            pltpu.VMEM(degrees.shape, degrees.dtype),
            pltpu.VMEM(codes.shape, codes.dtype),
            pltpu.SemaphoreType.DMA((3,)),
        ],
        compiler_params=LIMIT,
        cost_estimate=pl.CostEstimate(
            flops=codes.size, bytes_accessed=4 * codes.size, transcendentals=0
        ),
    )(*in_hbm(exps, degrees, codes))


def count_up(shape, axis):
    return lax.broadcasted_iota(jnp.int32, shape, axis)


def stage_kernel(
    blks, groups, tiles_dev, place_ref, index_hbm, blocks_hbm, order_ref, blocks, index_ref, sems
):
    fetch = pltpu.make_async_copy(index_hbm, index_ref, sems.at[0])
    fetch.start()
    copy = pltpu.make_async_copy(blocks_hbm, blocks, sems.at[1])
    copy.start()
    fetch.wait()
    my_blk = place_ref[0]
    my_grp = place_ref[1]
    capacity = index_ref.shape[1]
    width = order_ref.shape[1]
    source_tiles = blks * tiles_dev
    half = blks // 2
    role = my_blk & 1

    target = index_ref[0:1, :]
    origin = index_ref[1:2, :]
    hop, row = split(origin, tiles_dev)
    chunk, tile = split(target, tiles_dev)
    hop = hop ^ my_blk
    chunk = chunk ^ my_grp
    odd = hop & 1
    rank = jnp.where(odd == role, half - 1 - (hop >> 1), hop >> 1)
    far = (chunk >= 2) & ((chunk & 1) == 1)
    kept = jnp.where(chunk == 1, 1 + role * (groups // 2 - 1), (chunk >> 1) + 1 - role)
    kept = jnp.where(chunk == 0, 0, jnp.where(far, (chunk >> 1) - 1, kept))
    stage = jnp.where(far, jnp.where(odd == 1, 2, jnp.minimum(rank, 1)), 4)
    stage = jnp.where(far | (kept != 1), stage, 3)
    kept = jnp.where(far, kept, jnp.where(stage == 3, 0, kept - (kept > 1).astype(jnp.int32)))
    stage = jnp.where(origin < source_tiles, stage, STAGES)
    panel = jnp.where(stage == 1, rank - 1, jnp.where(stage == 2, rank, rank + odd * half))
    slot = count_up((1, capacity), 1)

    stages = (count_up((8, capacity), 0) == stage).astype(jnp.float32)
    earlier = count_up((capacity, capacity), 0) < count_up((capacity, capacity), 1)
    before = jnp.dot(
        stages.astype(jnp.bfloat16), earlier.astype(jnp.bfloat16), preferred_element_type=jnp.float32
    )
    position = jnp.sum(stages * before, axis=0, keepdims=True).astype(jnp.int32)
    parts = (slot & 127, slot >> 7, panel * tiles_dev + row, kept * tiles_dev + tile)
    values = sum(
        jnp.where(count_up((8, capacity), 0) == at, part, 0) for at, part in enumerate(parts)
    ).astype(jnp.bfloat16)
    far_tiles = (groups // 2 - 1) * tiles_dev
    tops = [far_tiles] * 3 + [tiles_dev, groups // 2 * tiles_dev]
    lanes = count_up((1, width), 1)
    for at, top in enumerate(tops):
        where = jnp.where(stage == at, position, -1)
        chosen = (count_up((width, capacity), 0) == where).astype(jnp.bfloat16)
        listed = lax.dot_general(
            values, chosen, (((1,), (1,)), ((), ())), preferred_element_type=jnp.float32
        ).astype(jnp.int32)
        word = pack(listed[0:1] + (listed[1:2] << 7), listed[2:3], listed[3:4])
        count = jnp.sum((stage == at).astype(jnp.int32), axis=1, keepdims=True)
        word = jnp.where(lanes < count, word, pack(0, 0, top))
        batches = split(count + (UNROLL - 1), UNROLL)[0]
        order_ref[at : at + 1, :] = jnp.where(lanes == width - UNROLL, batches, word)
    copy.wait()


def pack(slot, row, target):
    return (slot << 16) | (row << 8) | target


def unpack(word):
    return word >> 16, (word >> 8) & 255, word & 255


def stage_blocks(index, place, blocks, blks, groups, tiles_dev):
    capacity = blocks.shape[0]
    assert blks * tiles_dev < 256 and groups * tiles_dev < 256 and capacity < 2**15
    width = -(-(capacity + 2 * UNROLL) // 128) * 128
    return pl.pallas_call(
        functools.partial(stage_kernel, blks, groups, tiles_dev),
        out_shape=[
            jax.ShapeDtypeStruct((8, width), jnp.int32),
            jax.ShapeDtypeStruct(blocks.shape, blocks.dtype),
        ],
        in_specs=[SMEM, HBM, HBM],
        out_specs=[VMEM, VMEM],
        scratch_shapes=[
            pltpu.VMEM(index.shape, index.dtype),
            pltpu.SemaphoreType.DMA((2,)),
        ],
        compiler_params=LIMIT,
        cost_estimate=pl.CostEstimate(flops=0, bytes_accessed=0, transcendentals=0),
    )(place, *in_hbm(index, blocks))


def add_products(stage, order_ref, blocks, source, total):
    @pl.loop(0, order_ref[stage, order_ref.shape[1] - UNROLL])
    def _(batch):
        made = []
        for part in range(UNROLL):
            slot, row, target = unpack(order_ref[stage, batch * UNROLL + part])
            product = jnp.dot(blocks[slot], source[row], preferred_element_type=jnp.float32)
            made.append((target, product))
        for target, product in made:
            total[target] += product


def gather_panels(panels, source):
    for at, panel in enumerate(panels):
        rows = panel.shape[0]
        source[at * rows : (at + 1) * rows] = panel[...]


def early_kernel(order_ref, panel, blocks, total):
    total[...] = jnp.zeros_like(total)
    add_products(0, order_ref, blocks, panel, total)


def middle_kernel(order_ref, *refs):
    *panels, blocks, _, total, source = refs
    gather_panels(panels, source)
    add_products(1, order_ref, blocks, source, total)


def far_kernel(order_ref, *refs):
    *panels, blocks, total, far, source = refs
    gather_panels(panels, source)
    add_products(2, order_ref, blocks, source, total)
    far[...] = total[: far.shape[0]].astype(far.dtype)


def first_kernel(order_ref, *refs):
    *panels, blocks, first, source, total = refs
    gather_panels(panels, source)
    total[...] = jnp.zeros_like(total)
    add_products(3, order_ref, blocks, source, total)
    first[...] = total[: first.shape[0]].astype(first.dtype)


def rest_kernel(order_ref, *refs):
    *panels, blocks, own, later, source, total = refs
    gather_panels(panels, source)
    total[...] = jnp.zeros_like(total)
    add_products(4, order_ref, blocks, source, total)
    tiles_dev = own.shape[0]
    own[...] = total[:tiles_dev]
    later[...] = total[tiles_dev : tiles_dev + later.shape[0]]


def final_kernel(factors, own, *refs):
    *arrived, out_hbm, out, sems = refs
    copies = []
    for tile in range(out.shape[0]):
        value = own[tile]
        for piece in arrived:
            value = value + piece[tile].astype(jnp.float32)
        out[tile] = (value * factors[tile]).astype(out.dtype)
        copies.append(pltpu.make_async_copy(out.at[tile], out_hbm.at[tile], sems.at[tile]))
        copies[-1].start()
    for copy in copies:
        copy.wait()


def cost_of(slots, tile_rows, row_width):
    return pl.CostEstimate(
        flops=2 * slots * tile_rows * tile_rows * row_width,
        bytes_accessed=2 * slots * tile_rows * tile_rows,
        transcendentals=0,
    )


def shards(embed_codes, embed_exps, degrees, adjacency, block_index):
    tile_rows = adjacency.shape[2]
    row_width = embed_codes.shape[2]
    row_count = embed_codes.shape[1]
    capacity = adjacency.shape[1]
    tiles_dev = row_count // tile_rows
    groups = lax.axis_size("grp")
    blks = lax.axis_size("blk")
    part = (tiles_dev, tile_rows, row_width)
    codes = embed_codes.reshape(part)
    source, factors, scales = scale_rows(codes, embed_exps, degrees)

    def across(value, step):
        pairs = [
            (side * blks + at, (1 - side) * blks + (at ^ (2 * step if at & 1 else blks - 2 - 2 * step)))
            for side in range(2)
            for at in range(blks)
        ]
        return lax.ppermute(value, ("side", "blk"), pairs)

    def paired(value, axis, hop):
        return lax.ppermute(value, axis, [(at, at ^ hop) for at in range(lax.axis_size(axis))])

    place = jnp.stack([lax.axis_index("blk"), lax.axis_index("grp")]).astype(jnp.int32)
    early = across(codes, 0)
    middle = [across(source, step) for step in range(1, blks // 2)]
    early_scales = across(scales, 0)
    order, blocks = stage_blocks(block_index[0], place, adjacency[0], blks, groups, tiles_dev)
    early, early_scales, order = lax.optimization_barrier((early, early_scales, order))
    early = (early.astype(jnp.float32) * early_scales[:, :, None]).astype(jnp.bfloat16)
    other = paired(early, "blk", 1)
    far_tiles = (groups // 2 - 1) * tiles_dev

    def held(count, dtype):
        return pltpu.VMEM((count, tile_rows, row_width), dtype)

    total = pl.pallas_call(
        early_kernel,
        out_shape=jax.ShapeDtypeStruct((far_tiles + 1, tile_rows, row_width), jnp.float32),
        in_specs=[SMEM] + [VMEM] * 2,
        out_specs=VMEM,
        compiler_params=LIMIT,
        cost_estimate=cost_of(capacity // 8, tile_rows, row_width),
    )(order, early, blocks)
    *middle, total = lax.optimization_barrier((*middle, total))
    others = [other] + [paired(panel, "blk", 1) for panel in middle]
    total = pl.pallas_call(
        middle_kernel,
        out_shape=jax.ShapeDtypeStruct(total.shape, total.dtype),
        in_specs=[SMEM] + [VMEM] * (len(middle) + 2),
        out_specs=VMEM,
        input_output_aliases={len(middle) + 2: 0},
        scratch_shapes=[held(len(middle) * tiles_dev, jnp.bfloat16)],
        compiler_params=LIMIT,
        cost_estimate=cost_of(capacity // 8, tile_rows, row_width),
    )(order, *middle, blocks, total)
    *others, total = lax.optimization_barrier((*others, total))
    far = pl.pallas_call(
        far_kernel,
        out_shape=jax.ShapeDtypeStruct((far_tiles, tile_rows, row_width), jnp.bfloat16),
        in_specs=[SMEM] + [VMEM] * (len(others) + 2),
        out_specs=VMEM,
        scratch_shapes=[held(len(others) * tiles_dev, jnp.bfloat16)],
        compiler_params=LIMIT,
        cost_estimate=cost_of(capacity // 8, tile_rows, row_width),
    )(order, *others, blocks, total)
    far, order = lax.optimization_barrier((far, order))
    panels = [early] + middle + others
    first = pl.pallas_call(
        first_kernel,
        out_shape=jax.ShapeDtypeStruct(part, jnp.bfloat16),
        in_specs=[SMEM] + [VMEM] * (len(panels) + 1),
        out_specs=VMEM,
        scratch_shapes=[
            held(len(panels) * tiles_dev, jnp.bfloat16),
            held(tiles_dev + 1, jnp.float32),
        ],
        compiler_params=LIMIT,
        cost_estimate=cost_of(capacity // 4, tile_rows, row_width),
    )(order, *panels, blocks)
    first, order = lax.optimization_barrier((first, order))
    own, later = pl.pallas_call(
        rest_kernel,
        out_shape=[
            jax.ShapeDtypeStruct(part, jnp.float32),
            jax.ShapeDtypeStruct((far_tiles, tile_rows, row_width), jnp.float32),
        ],
        in_specs=[SMEM] + [VMEM] * (len(panels) + 1),
        out_specs=[VMEM] * 2,
        scratch_shapes=[
            held(len(panels) * tiles_dev, jnp.bfloat16),
            held(groups // 2 * tiles_dev + 1, jnp.float32),
        ],
        compiler_params=LIMIT,
        cost_estimate=cost_of(capacity // 2, tile_rows, row_width),
    )(order, *panels, blocks)

    def turned(value, even_hop, odd_hop):
        hops = (even_hop, odd_hop)
        pairs = [
            (at * blks + blk, (at ^ hops[blk & 1]) * blks + blk)
            for at in range(groups)
            for blk in range(blks)
        ]
        return lax.ppermute(value, ("grp", "blk"), pairs)

    steps = groups // 2 - 1
    even_core = lax.axis_index("blk") % 2 == 0
    pieces = [slice(at * tiles_dev, (at + 1) * tiles_dev) for at in range(steps)]
    handed = [turned(far[pieces[at]], 1, 2 * at + 2).astype(jnp.float32) for at in range(steps)]
    arrived = [turned(first, 1, 2)]
    for at in range(steps):
        value = later[pieces[at]]
        for step, extra in enumerate(handed):
            if step == at == steps - 1:
                value = value + extra
            elif step == at:
                value = value + jnp.where(even_core, extra, 0.0)
            elif at == steps - 1:
                value = value + jnp.where(even_core, 0.0, extra)
        odd_hop = 1 if at == steps - 1 else 2 * at + 4
        arrived.append(turned(value.astype(jnp.bfloat16), 2 * at + 2, odd_hop))
    own = own + arrived[0].astype(jnp.float32)
    own, *sums = lax.optimization_barrier((own, *arrived[1:]))
    out = pl.pallas_call(
        final_kernel,
        out_shape=jax.ShapeDtypeStruct(part, jnp.bfloat16),
        in_specs=[VMEM] * (2 + len(sums)),
        out_specs=HBM,
        scratch_shapes=[
            held(tiles_dev, jnp.bfloat16),
            pltpu.SemaphoreType.DMA((tiles_dev,)),
        ],
        compiler_params=LIMIT,
        cost_estimate=cost_of(0, tile_rows, row_width),
    )(factors, own, *sums)
    return out.reshape(1, row_count, row_width)


def solution(mesh):
    placed = (
        P("side", ("grp", "blk"), None),
        P("side", ("grp", "blk")),
        P("side", ("grp", "blk")),
        P("side", ("grp", "blk"), None, None),
        P("side", None, ("grp", "blk")),
    )
    return jax.shard_map(
        shards,
        mesh=mesh,
        in_specs=placed,
        out_specs=P("side", ("grp", "blk"), None),
        check_vma=False,
    )
```

```python
import functools

import jax
import jax.numpy as jnp
from jax import lax
from jax.experimental import pallas as pl
from jax.experimental.pallas import tpu as pltpu
from jax.sharding import PartitionSpec as P

UNROLL = 8
STAGES = 5
VMEM = pl.BlockSpec(memory_space=pltpu.VMEM)
SMEM = pl.BlockSpec(memory_space=pltpu.SMEM)
HBM = pl.BlockSpec(memory_space=pltpu.HBM)
LIMIT = pltpu.CompilerParams(vmem_limit_bytes=48 * 1024 * 1024)


def in_hbm(*arrays):
    return [pltpu.with_memory_space_constraint(array, pltpu.HBM) for array in arrays]


def split(value, size):
    if size & (size - 1) == 0:
        return value >> (size.bit_length() - 1), value & (size - 1)
    return value // size, value % size


def scale_kernel(exps_hbm, degrees_hbm, factors, scales, exps_ref, degrees, sems):
    pairs = [(exps_hbm, exps_ref), (degrees_hbm, degrees)]
    fetches = [
        pltpu.make_async_copy(held, wanted, sems.at[at])
        for at, (held, wanted) in enumerate(pairs)
    ]
    for fetch in fetches:
        fetch.start()
    for fetch in fetches:
        fetch.wait()
    tiles_dev, tile_rows, row_width = factors.shape
    inverse = lax.rsqrt(degrees[...].astype(jnp.float32))
    for tile in range(tiles_dev):
        lanes = inverse[:, tile * tile_rows : (tile + 1) * tile_rows]
        factors[tile] = jnp.broadcast_to(lanes, (row_width, tile_rows)).T
        scale = jnp.exp2(jnp.full((1, 1), exps_ref[0, tile], jnp.int32).astype(jnp.float32))
        scales[tile : tile + 1, :] = lanes * scale


def scale_rows(exps, degrees, part):
    return pl.pallas_call(
        scale_kernel,
        out_shape=[
            jax.ShapeDtypeStruct(part, jnp.float32),
            jax.ShapeDtypeStruct(part[:2], jnp.float32),
        ],
        in_specs=[HBM] * 2,
        out_specs=[VMEM] * 2,
        scratch_shapes=[
            pltpu.SMEM(exps.shape, exps.dtype),
            pltpu.VMEM(degrees.shape, degrees.dtype),
            pltpu.SemaphoreType.DMA((2,)),
        ],
        compiler_params=LIMIT,
        cost_estimate=pl.CostEstimate(flops=0, bytes_accessed=0, transcendentals=0),
    )(*in_hbm(exps, degrees))


def count_up(shape, axis):
    return lax.broadcasted_iota(jnp.int32, shape, axis)


def stage_kernel(
    blks, groups, tiles_dev, place_ref, index_hbm, blocks_hbm, order_ref, blocks, index_ref, sems
):
    fetch = pltpu.make_async_copy(index_hbm, index_ref, sems.at[0])
    fetch.start()
    copy = pltpu.make_async_copy(blocks_hbm, blocks, sems.at[1])
    copy.start()
    fetch.wait()
    my_blk = place_ref[0]
    my_grp = place_ref[1]
    capacity = index_ref.shape[1]
    width = order_ref.shape[1]
    source_tiles = blks * tiles_dev
    half = blks // 2
    role = my_blk & 1

    target = index_ref[0:1, :]
    origin = index_ref[1:2, :]
    hop, row = split(origin, tiles_dev)
    chunk, tile = split(target, tiles_dev)
    hop = hop ^ my_blk
    chunk = chunk ^ my_grp
    odd = hop & 1
    rank = jnp.where(odd == role, half - 1 - (hop >> 1), hop >> 1)
    far = (chunk >= 2) & ((chunk & 1) == 1)
    kept = jnp.where(chunk == 1, 1 + role * (groups // 2 - 1), (chunk >> 1) + 1 - role)
    kept = jnp.where(chunk == 0, 0, jnp.where(far, (chunk >> 1) - 1, kept))
    stage = jnp.where(far, jnp.where(odd == 1, 2, jnp.minimum(rank, 1)), 4)
    stage = jnp.where(far | (kept != 1), stage, 3)
    kept = jnp.where(far, kept, jnp.where(stage == 3, 0, kept - (kept > 1).astype(jnp.int32)))
    stage = jnp.where(origin < source_tiles, stage, STAGES)
    panel = jnp.where(stage == 1, rank - 1, jnp.where(stage == 2, rank, rank + odd * half))
    slot = count_up((1, capacity), 1)

    stages = (count_up((8, capacity), 0) == stage).astype(jnp.float32)
    earlier = count_up((capacity, capacity), 0) < count_up((capacity, capacity), 1)
    before = jnp.dot(
        stages.astype(jnp.bfloat16), earlier.astype(jnp.bfloat16), preferred_element_type=jnp.float32
    )
    position = jnp.sum(stages * before, axis=0, keepdims=True).astype(jnp.int32)
    parts = (slot & 127, slot >> 7, panel * tiles_dev + row, kept * tiles_dev + tile)
    values = sum(
        jnp.where(count_up((8, capacity), 0) == at, part, 0) for at, part in enumerate(parts)
    ).astype(jnp.bfloat16)
    far_tiles = (groups // 2 - 1) * tiles_dev
    tops = [far_tiles] * 3 + [tiles_dev, groups // 2 * tiles_dev]
    lanes = count_up((1, width), 1)
    for at, top in enumerate(tops):
        where = jnp.where(stage == at, position, -1)
        chosen = (count_up((width, capacity), 0) == where).astype(jnp.bfloat16)
        listed = lax.dot_general(
            values, chosen, (((1,), (1,)), ((), ())), preferred_element_type=jnp.float32
        ).astype(jnp.int32)
        word = pack(listed[0:1] + (listed[1:2] << 7), listed[2:3], listed[3:4])
        count = jnp.sum((stage == at).astype(jnp.int32), axis=1, keepdims=True)
        word = jnp.where(lanes < count, word, pack(0, 0, top))
        batches = split(count + (UNROLL - 1), UNROLL)[0]
        order_ref[at : at + 1, :] = jnp.where(lanes == width - UNROLL, batches, word)
    copy.wait()


def pack(slot, row, target):
    return (slot << 16) | (row << 8) | target


def unpack(word):
    return word >> 16, (word >> 8) & 255, word & 255


def stage_blocks(index, place, blocks, blks, groups, tiles_dev):
    capacity = blocks.shape[0]
    assert blks * tiles_dev < 256 and groups * tiles_dev < 256 and capacity < 2**15
    width = -(-(capacity + 2 * UNROLL) // 128) * 128
    return pl.pallas_call(
        functools.partial(stage_kernel, blks, groups, tiles_dev),
        out_shape=[
            jax.ShapeDtypeStruct((8, width), jnp.int32),
            jax.ShapeDtypeStruct(blocks.shape, blocks.dtype),
        ],
        in_specs=[SMEM, HBM, HBM],
        out_specs=[VMEM, VMEM],
        scratch_shapes=[
            pltpu.VMEM(index.shape, index.dtype),
            pltpu.SemaphoreType.DMA((2,)),
        ],
        compiler_params=LIMIT,
        cost_estimate=pl.CostEstimate(flops=0, bytes_accessed=0, transcendentals=0),
    )(place, *in_hbm(index, blocks))


def add_products(stage, order_ref, blocks, source, total):
    @pl.loop(0, order_ref[stage, order_ref.shape[1] - UNROLL])
    def _(batch):
        made = []
        for part in range(UNROLL):
            slot, row, target = unpack(order_ref[stage, batch * UNROLL + part])
            product = jnp.dot(blocks[slot], source[row], preferred_element_type=jnp.float32)
            made.append((target, product))
        for target, product in made:
            total[target] += product


def gather_panels(panels, source):
    for at, panel in enumerate(panels):
        rows = panel.shape[0]
        source[at * rows : (at + 1) * rows] = panel[...]


def early_kernel(order_ref, panel, blocks, total):
    total[...] = jnp.zeros_like(total)
    add_products(0, order_ref, blocks, panel, total)


def middle_kernel(order_ref, *refs):
    *panels, blocks, _, total, source = refs
    gather_panels(panels, source)
    add_products(1, order_ref, blocks, source, total)


def far_kernel(order_ref, *refs):
    *panels, blocks, total, far, source = refs
    gather_panels(panels, source)
    add_products(2, order_ref, blocks, source, total)
    far[...] = total[: far.shape[0]].astype(far.dtype)


def first_kernel(order_ref, *refs):
    *panels, blocks, first, source, total = refs
    gather_panels(panels, source)
    total[...] = jnp.zeros_like(total)
    add_products(3, order_ref, blocks, source, total)
    first[...] = total[: first.shape[0]].astype(first.dtype)


def rest_kernel(order_ref, *refs):
    *panels, blocks, own, later, source, total = refs
    gather_panels(panels, source)
    total[...] = jnp.zeros_like(total)
    add_products(4, order_ref, blocks, source, total)
    tiles_dev = own.shape[0]
    own[...] = total[:tiles_dev]
    later[...] = total[tiles_dev : tiles_dev + later.shape[0]]


def final_kernel(factors, own, *refs):
    *arrived, out_hbm, out, sems = refs
    copies = []
    for tile in range(out.shape[0]):
        value = own[tile]
        for piece in arrived:
            value = value + piece[tile].astype(jnp.float32)
        out[tile] = (value * factors[tile]).astype(out.dtype)
        copies.append(pltpu.make_async_copy(out.at[tile], out_hbm.at[tile], sems.at[tile]))
        copies[-1].start()
    for copy in copies:
        copy.wait()


def cost_of(slots, tile_rows, row_width):
    return pl.CostEstimate(
        flops=2 * slots * tile_rows * tile_rows * row_width,
        bytes_accessed=2 * slots * tile_rows * tile_rows,
        transcendentals=0,
    )


def shards(embed_codes, embed_exps, degrees, adjacency, block_index):
    tile_rows = adjacency.shape[2]
    row_width = embed_codes.shape[2]
    row_count = embed_codes.shape[1]
    capacity = adjacency.shape[1]
    tiles_dev = row_count // tile_rows
    groups = lax.axis_size("grp")
    blks = lax.axis_size("blk")
    part = (tiles_dev, tile_rows, row_width)
    codes = embed_codes.reshape(part)
    factors, scales = scale_rows(embed_exps, degrees, part)

    def across(value, step):
        pairs = [
            (side * blks + at, (1 - side) * blks + (at ^ (2 * step if at & 1 else blks - 2 - 2 * step)))
            for side in range(2)
            for at in range(blks)
        ]
        return lax.ppermute(value, ("side", "blk"), pairs)

    def paired(value, axis, hop):
        return lax.ppermute(value, axis, [(at, at ^ hop) for at in range(lax.axis_size(axis))])

    place = jnp.stack([lax.axis_index("blk"), lax.axis_index("grp")]).astype(jnp.int32)
    def scaled(value, row_scales):
        return (value.astype(jnp.float32) * row_scales[:, :, None]).astype(jnp.bfloat16)

    early, *middle = [across(codes, step) for step in range(blks // 2)]
    early_scales, *middle_scales = [across(scales, step) for step in range(blks // 2)]
    order, blocks = stage_blocks(block_index[0], place, adjacency[0], blks, groups, tiles_dev)
    early, early_scales, order = lax.optimization_barrier((early, early_scales, order))
    early = scaled(early, early_scales)
    other = paired(early, "blk", 1)
    far_tiles = (groups // 2 - 1) * tiles_dev

    def held(count, dtype):
        return pltpu.VMEM((count, tile_rows, row_width), dtype)

    total = pl.pallas_call(
        early_kernel,
        out_shape=jax.ShapeDtypeStruct((far_tiles + 1, tile_rows, row_width), jnp.float32),
        in_specs=[SMEM] + [VMEM] * 2,
        out_specs=VMEM,
        compiler_params=LIMIT,
        cost_estimate=cost_of(capacity // 8, tile_rows, row_width),
    )(order, early, blocks)
    *middle, total = lax.optimization_barrier((*middle, total))
    middle = [scaled(*pair) for pair in zip(middle, middle_scales)]
    others = [other] + [paired(panel, "blk", 1) for panel in middle]
    total = pl.pallas_call(
        middle_kernel,
        out_shape=jax.ShapeDtypeStruct(total.shape, total.dtype),
        in_specs=[SMEM] + [VMEM] * (len(middle) + 2),
        out_specs=VMEM,
        input_output_aliases={len(middle) + 2: 0},
        scratch_shapes=[held(len(middle) * tiles_dev, jnp.bfloat16)],
        compiler_params=LIMIT,
        cost_estimate=cost_of(capacity // 8, tile_rows, row_width),
    )(order, *middle, blocks, total)
    *others, total = lax.optimization_barrier((*others, total))
    far = pl.pallas_call(
        far_kernel,
        out_shape=jax.ShapeDtypeStruct((far_tiles, tile_rows, row_width), jnp.bfloat16),
        in_specs=[SMEM] + [VMEM] * (len(others) + 2),
        out_specs=VMEM,
        scratch_shapes=[held(len(others) * tiles_dev, jnp.bfloat16)],
        compiler_params=LIMIT,
        cost_estimate=cost_of(capacity // 8, tile_rows, row_width),
    )(order, *others, blocks, total)
    far, order = lax.optimization_barrier((far, order))
    panels = [early] + middle + others
    first = pl.pallas_call(
        first_kernel,
        out_shape=jax.ShapeDtypeStruct(part, jnp.bfloat16),
        in_specs=[SMEM] + [VMEM] * (len(panels) + 1),
        out_specs=VMEM,
        scratch_shapes=[
            held(len(panels) * tiles_dev, jnp.bfloat16),
            held(tiles_dev + 1, jnp.float32),
        ],
        compiler_params=LIMIT,
        cost_estimate=cost_of(capacity // 4, tile_rows, row_width),
    )(order, *panels, blocks)
    first, order = lax.optimization_barrier((first, order))
    own, later = pl.pallas_call(
        rest_kernel,
        out_shape=[
            jax.ShapeDtypeStruct(part, jnp.float32),
            jax.ShapeDtypeStruct((far_tiles, tile_rows, row_width), jnp.float32),
        ],
        in_specs=[SMEM] + [VMEM] * (len(panels) + 1),
        out_specs=[VMEM] * 2,
        scratch_shapes=[
            held(len(panels) * tiles_dev, jnp.bfloat16),
            held(groups // 2 * tiles_dev + 1, jnp.float32),
        ],
        compiler_params=LIMIT,
        cost_estimate=cost_of(capacity // 2, tile_rows, row_width),
    )(order, *panels, blocks)

    def turned(value, even_hop, odd_hop):
        hops = (even_hop, odd_hop)
        pairs = [
            (at * blks + blk, (at ^ hops[blk & 1]) * blks + blk)
            for at in range(groups)
            for blk in range(blks)
        ]
        return lax.ppermute(value, ("grp", "blk"), pairs)

    steps = groups // 2 - 1
    even_core = lax.axis_index("blk") % 2 == 0
    pieces = [slice(at * tiles_dev, (at + 1) * tiles_dev) for at in range(steps)]
    handed = [turned(far[pieces[at]], 1, 2 * at + 2).astype(jnp.float32) for at in range(steps)]
    arrived = [turned(first, 1, 2)]
    for at in range(steps):
        value = later[pieces[at]]
        for step, extra in enumerate(handed):
            if step == at == steps - 1:
                value = value + extra
            elif step == at:
                value = value + jnp.where(even_core, extra, 0.0)
            elif at == steps - 1:
                value = value + jnp.where(even_core, 0.0, extra)
        odd_hop = 1 if at == steps - 1 else 2 * at + 4
        arrived.append(turned(value.astype(jnp.bfloat16), 2 * at + 2, odd_hop))
    own = own + arrived[0].astype(jnp.float32)
    own, *sums = lax.optimization_barrier((own, *arrived[1:]))
    out = pl.pallas_call(
        final_kernel,
        out_shape=jax.ShapeDtypeStruct(part, jnp.bfloat16),
        in_specs=[VMEM] * (2 + len(sums)),
        out_specs=HBM,
        scratch_shapes=[
            held(tiles_dev, jnp.bfloat16),
            pltpu.SemaphoreType.DMA((tiles_dev,)),
        ],
        compiler_params=LIMIT,
        cost_estimate=cost_of(0, tile_rows, row_width),
    )(factors, own, *sums)
    return out.reshape(1, row_count, row_width)


def solution(mesh):
    placed = (
        P("side", ("grp", "blk"), None),
        P("side", ("grp", "blk")),
        P("side", ("grp", "blk")),
        P("side", ("grp", "blk"), None, None),
        P("side", None, ("grp", "blk")),
    )
    return jax.shard_map(
        shards,
        mesh=mesh,
        in_specs=placed,
        out_specs=P("side", ("grp", "blk"), None),
        check_vma=False,
    )
```

```python
import functools

import jax
import jax.numpy as jnp
from jax import lax
from jax.experimental import pallas as pl
from jax.experimental.pallas import tpu as pltpu
from jax.sharding import PartitionSpec as P

UNROLL = 8
BATCHES = (4, 4, 4, 8, 8)
STAGES = len(BATCHES)
VMEM = pl.BlockSpec(memory_space=pltpu.VMEM)
SMEM = pl.BlockSpec(memory_space=pltpu.SMEM)
HBM = pl.BlockSpec(memory_space=pltpu.HBM)
LIMIT = pltpu.CompilerParams(vmem_limit_bytes=48 * 1024 * 1024)


def in_hbm(*arrays):
    return [pltpu.with_memory_space_constraint(array, pltpu.HBM) for array in arrays]


def split(value, size):
    if size & (size - 1) == 0:
        return value >> (size.bit_length() - 1), value & (size - 1)
    return value // size, value % size


def scale_kernel(
    exps_hbm, degrees_hbm, codes_hbm, rows, factors, scales, exps_ref, degrees, codes, sems
):
    pairs = [(exps_hbm, exps_ref), (degrees_hbm, degrees), (codes_hbm, codes)]
    fetches = [
        pltpu.make_async_copy(held, wanted, sems.at[at])
        for at, (held, wanted) in enumerate(pairs)
    ]
    for fetch in fetches:
        fetch.start()
    fetches[0].wait()
    fetches[1].wait()
    tiles_dev, tile_rows, row_width = rows.shape
    inverse = lax.rsqrt(degrees[...].astype(jnp.float32))
    for tile in range(tiles_dev):
        lanes = inverse[:, tile * tile_rows : (tile + 1) * tile_rows]
        factors[tile] = jnp.broadcast_to(lanes, (row_width, tile_rows)).T
        scale = jnp.exp2(jnp.full((1, 1), exps_ref[0, tile], jnp.int32).astype(jnp.float32))
        scales[tile : tile + 1, :] = lanes * scale
    fetches[2].wait()
    for tile in range(tiles_dev):
        scale = jnp.exp2(jnp.full((1, 1), exps_ref[0, tile], jnp.int32).astype(jnp.float32))
        scaled = codes[tile].astype(jnp.float32) * scale * factors[tile]
        rows[tile] = scaled.astype(rows.dtype)


def scale_rows(codes, exps, degrees):
    return pl.pallas_call(
        scale_kernel,
        out_shape=[
            jax.ShapeDtypeStruct(codes.shape, jnp.bfloat16),
            jax.ShapeDtypeStruct(codes.shape, jnp.float32),
            jax.ShapeDtypeStruct(codes.shape[:2], jnp.float32),
        ],
        in_specs=[HBM] * 3,
        out_specs=[VMEM] * 3,
        scratch_shapes=[
            pltpu.SMEM(exps.shape, exps.dtype),
            pltpu.VMEM(degrees.shape, degrees.dtype),
            pltpu.VMEM(codes.shape, codes.dtype),
            pltpu.SemaphoreType.DMA((3,)),
        ],
        compiler_params=LIMIT,
        cost_estimate=pl.CostEstimate(
            flops=codes.size, bytes_accessed=4 * codes.size, transcendentals=0
        ),
    )(*in_hbm(exps, degrees, codes))


def count_up(shape, axis):
    return lax.broadcasted_iota(jnp.int32, shape, axis)


def stage_kernel(
    blks, groups, tiles_dev, place_ref, index_hbm, blocks_hbm, order_ref, blocks, index_ref, sems
):
    fetch = pltpu.make_async_copy(index_hbm, index_ref, sems.at[0])
    fetch.start()
    copy = pltpu.make_async_copy(blocks_hbm, blocks, sems.at[1])
    copy.start()
    fetch.wait()
    my_blk = place_ref[0]
    my_grp = place_ref[1]
    capacity = index_ref.shape[1]
    width = order_ref.shape[1]
    source_tiles = blks * tiles_dev
    half = blks // 2
    role = my_blk & 1

    target = index_ref[0:1, :]
    origin = index_ref[1:2, :]
    hop, row = split(origin, tiles_dev)
    chunk, tile = split(target, tiles_dev)
    hop = hop ^ my_blk
    chunk = chunk ^ my_grp
    odd = hop & 1
    rank = jnp.where(odd == role, half - 1 - (hop >> 1), hop >> 1)
    far = (chunk >= 2) & ((chunk & 1) == 1)
    kept = jnp.where(chunk == 1, 1 + role * (groups // 2 - 1), (chunk >> 1) + 1 - role)
    kept = jnp.where(chunk == 0, 0, jnp.where(far, (chunk >> 1) - 1, kept))
    stage = jnp.where(far, jnp.where(odd == 1, 2, jnp.minimum(rank, 1)), 4)
    stage = jnp.where(far | (kept != 1), stage, 3)
    kept = jnp.where(far, kept, jnp.where(stage == 3, 0, kept - (kept > 1).astype(jnp.int32)))
    stage = jnp.where(origin < source_tiles, stage, STAGES)
    panel = jnp.where(stage == 1, rank - 1, jnp.where(stage == 2, rank, rank + odd * half))
    slot = count_up((1, capacity), 1)

    stages = (count_up((8, capacity), 0) == stage).astype(jnp.float32)
    earlier = count_up((capacity, capacity), 0) < count_up((capacity, capacity), 1)
    before = jnp.dot(
        stages.astype(jnp.bfloat16), earlier.astype(jnp.bfloat16), preferred_element_type=jnp.float32
    )
    position = jnp.sum(stages * before, axis=0, keepdims=True).astype(jnp.int32)
    parts = (slot & 127, slot >> 7, panel * tiles_dev + row, kept * tiles_dev + tile)
    values = sum(
        jnp.where(count_up((8, capacity), 0) == at, part, 0) for at, part in enumerate(parts)
    ).astype(jnp.bfloat16)
    far_tiles = (groups // 2 - 1) * tiles_dev
    tops = [far_tiles] * 3 + [tiles_dev, groups // 2 * tiles_dev]
    lanes = count_up((1, width), 1)
    for at, top in enumerate(tops):
        where = jnp.where(stage == at, position, -1)
        chosen = (count_up((width, capacity), 0) == where).astype(jnp.bfloat16)
        listed = lax.dot_general(
            values, chosen, (((1,), (1,)), ((), ())), preferred_element_type=jnp.float32
        ).astype(jnp.int32)
        word = pack(listed[0:1] + (listed[1:2] << 7), listed[2:3], listed[3:4])
        count = jnp.sum((stage == at).astype(jnp.int32), axis=1, keepdims=True)
        word = jnp.where(lanes < count, word, pack(0, 0, top))
        batches = split(count + (BATCHES[at] - 1), BATCHES[at])[0]
        order_ref[at : at + 1, :] = jnp.where(lanes == width - UNROLL, batches, word)
    copy.wait()


def pack(slot, row, target):
    return (slot << 16) | (row << 8) | target


def unpack(word):
    return word >> 16, (word >> 8) & 255, word & 255


def stage_blocks(index, place, blocks, blks, groups, tiles_dev):
    capacity = blocks.shape[0]
    assert blks * tiles_dev < 256 and groups * tiles_dev < 256 and capacity < 2**15
    width = -(-(capacity + 2 * UNROLL) // 128) * 128
    return pl.pallas_call(
        functools.partial(stage_kernel, blks, groups, tiles_dev),
        out_shape=[
            jax.ShapeDtypeStruct((8, width), jnp.int32),
            jax.ShapeDtypeStruct(blocks.shape, blocks.dtype),
        ],
        in_specs=[SMEM, HBM, HBM],
        out_specs=[VMEM, VMEM],
        scratch_shapes=[
            pltpu.VMEM(index.shape, index.dtype),
            pltpu.SemaphoreType.DMA((2,)),
        ],
        compiler_params=LIMIT,
        cost_estimate=pl.CostEstimate(flops=0, bytes_accessed=0, transcendentals=0),
    )(place, *in_hbm(index, blocks))


def add_products(stage, order_ref, blocks, source, total):
    @pl.loop(0, order_ref[stage, order_ref.shape[1] - UNROLL])
    def _(batch):
        made = []
        for part in range(BATCHES[stage]):
            slot, row, target = unpack(order_ref[stage, batch * BATCHES[stage] + part])
            product = jnp.dot(blocks[slot], source[row], preferred_element_type=jnp.float32)
            made.append((target, product))
        for target, product in made:
            total[target] += product


def gather_panels(panels, source):
    for at, panel in enumerate(panels):
        rows = panel.shape[0]
        source[at * rows : (at + 1) * rows] = panel[...]


def early_kernel(order_ref, panel, blocks, total):
    total[...] = jnp.zeros_like(total)
    add_products(0, order_ref, blocks, panel, total)


def middle_kernel(order_ref, *refs):
    *panels, blocks, _, total, source = refs
    gather_panels(panels, source)
    add_products(1, order_ref, blocks, source, total)


def far_kernel(order_ref, *refs):
    *panels, blocks, total, far, source = refs
    gather_panels(panels, source)
    add_products(2, order_ref, blocks, source, total)
    far[...] = total[: far.shape[0]].astype(far.dtype)


def first_kernel(order_ref, *refs):
    *panels, blocks, first, source, total = refs
    gather_panels(panels, source)
    total[...] = jnp.zeros_like(total)
    add_products(3, order_ref, blocks, source, total)
    first[...] = total[: first.shape[0]].astype(first.dtype)


def rest_kernel(order_ref, *refs):
    *panels, blocks, own, later, source, total = refs
    gather_panels(panels, source)
    total[...] = jnp.zeros_like(total)
    add_products(4, order_ref, blocks, source, total)
    tiles_dev = own.shape[0]
    own[...] = total[:tiles_dev]
    later[...] = total[tiles_dev : tiles_dev + later.shape[0]]


def final_kernel(factors, own, *refs):
    *arrived, out_hbm, out, sems = refs
    copies = []
    for tile in range(out.shape[0]):
        value = own[tile]
        for piece in arrived:
            value = value + piece[tile].astype(jnp.float32)
        out[tile] = (value * factors[tile]).astype(out.dtype)
        copies.append(pltpu.make_async_copy(out.at[tile], out_hbm.at[tile], sems.at[tile]))
        copies[-1].start()
    for copy in copies:
        copy.wait()


def cost_of(slots, tile_rows, row_width):
    return pl.CostEstimate(
        flops=2 * slots * tile_rows * tile_rows * row_width,
        bytes_accessed=2 * slots * tile_rows * tile_rows,
        transcendentals=0,
    )


def shards(embed_codes, embed_exps, degrees, adjacency, block_index):
    tile_rows = adjacency.shape[2]
    row_width = embed_codes.shape[2]
    row_count = embed_codes.shape[1]
    capacity = adjacency.shape[1]
    tiles_dev = row_count // tile_rows
    groups = lax.axis_size("grp")
    blks = lax.axis_size("blk")
    part = (tiles_dev, tile_rows, row_width)
    codes = embed_codes.reshape(part)
    source, factors, scales = scale_rows(codes, embed_exps, degrees)

    def across(value, step):
        pairs = [
            (side * blks + at, (1 - side) * blks + (at ^ (2 * step if at & 1 else blks - 2 - 2 * step)))
            for side in range(2)
            for at in range(blks)
        ]
        return lax.ppermute(value, ("side", "blk"), pairs)

    def paired(value, axis, hop):
        return lax.ppermute(value, axis, [(at, at ^ hop) for at in range(lax.axis_size(axis))])

    place = jnp.stack([lax.axis_index("blk"), lax.axis_index("grp")]).astype(jnp.int32)
    early = across(codes, 0)
    middle = [across(source, step) for step in range(1, blks // 2)]
    early_scales = across(scales, 0)
    order, blocks = stage_blocks(block_index[0], place, adjacency[0], blks, groups, tiles_dev)
    early, early_scales, order = lax.optimization_barrier((early, early_scales, order))
    early = (early.astype(jnp.float32) * early_scales[:, :, None]).astype(jnp.bfloat16)
    other = paired(early, "blk", 1)
    far_tiles = (groups // 2 - 1) * tiles_dev

    def held(count, dtype):
        return pltpu.VMEM((count, tile_rows, row_width), dtype)

    total = pl.pallas_call(
        early_kernel,
        out_shape=jax.ShapeDtypeStruct((far_tiles + 1, tile_rows, row_width), jnp.float32),
        in_specs=[SMEM] + [VMEM] * 2,
        out_specs=VMEM,
        compiler_params=LIMIT,
        cost_estimate=cost_of(capacity // 8, tile_rows, row_width),
    )(order, early, blocks)
    *middle, total = lax.optimization_barrier((*middle, total))
    others = [other] + [paired(panel, "blk", 1) for panel in middle]
    total = pl.pallas_call(
        middle_kernel,
        out_shape=jax.ShapeDtypeStruct(total.shape, total.dtype),
        in_specs=[SMEM] + [VMEM] * (len(middle) + 2),
        out_specs=VMEM,
        input_output_aliases={len(middle) + 2: 0},
        scratch_shapes=[held(len(middle) * tiles_dev, jnp.bfloat16)],
        compiler_params=LIMIT,
        cost_estimate=cost_of(capacity // 8, tile_rows, row_width),
    )(order, *middle, blocks, total)
    *others, total = lax.optimization_barrier((*others, total))
    far = pl.pallas_call(
        far_kernel,
        out_shape=jax.ShapeDtypeStruct((far_tiles, tile_rows, row_width), jnp.bfloat16),
        in_specs=[SMEM] + [VMEM] * (len(others) + 2),
        out_specs=VMEM,
        scratch_shapes=[held(len(others) * tiles_dev, jnp.bfloat16)],
        compiler_params=LIMIT,
        cost_estimate=cost_of(capacity // 8, tile_rows, row_width),
    )(order, *others, blocks, total)
    far, order = lax.optimization_barrier((far, order))
    panels = [early] + middle + others
    first = pl.pallas_call(
        first_kernel,
        out_shape=jax.ShapeDtypeStruct(part, jnp.bfloat16),
        in_specs=[SMEM] + [VMEM] * (len(panels) + 1),
        out_specs=VMEM,
        scratch_shapes=[
            held(len(panels) * tiles_dev, jnp.bfloat16),
            held(tiles_dev + 1, jnp.float32),
        ],
        compiler_params=LIMIT,
        cost_estimate=cost_of(capacity // 4, tile_rows, row_width),
    )(order, *panels, blocks)
    first, order = lax.optimization_barrier((first, order))
    own, later = pl.pallas_call(
        rest_kernel,
        out_shape=[
            jax.ShapeDtypeStruct(part, jnp.float32),
            jax.ShapeDtypeStruct((far_tiles, tile_rows, row_width), jnp.float32),
        ],
        in_specs=[SMEM] + [VMEM] * (len(panels) + 1),
        out_specs=[VMEM] * 2,
        scratch_shapes=[
            held(len(panels) * tiles_dev, jnp.bfloat16),
            held(groups // 2 * tiles_dev + 1, jnp.float32),
        ],
        compiler_params=LIMIT,
        cost_estimate=cost_of(capacity // 2, tile_rows, row_width),
    )(order, *panels, blocks)

    def turned(value, even_hop, odd_hop):
        hops = (even_hop, odd_hop)
        pairs = [
            (at * blks + blk, (at ^ hops[blk & 1]) * blks + blk)
            for at in range(groups)
            for blk in range(blks)
        ]
        return lax.ppermute(value, ("grp", "blk"), pairs)

    steps = groups // 2 - 1
    even_core = lax.axis_index("blk") % 2 == 0
    pieces = [slice(at * tiles_dev, (at + 1) * tiles_dev) for at in range(steps)]
    handed = [turned(far[pieces[at]], 1, 2 * at + 2).astype(jnp.float32) for at in range(steps)]
    arrived = [turned(first, 1, 2)]
    for at in range(steps):
        value = later[pieces[at]]
        for step, extra in enumerate(handed):
            if step == at == steps - 1:
                value = value + extra
            elif step == at:
                value = value + jnp.where(even_core, extra, 0.0)
            elif at == steps - 1:
                value = value + jnp.where(even_core, 0.0, extra)
        odd_hop = 1 if at == steps - 1 else 2 * at + 4
        arrived.append(turned(value.astype(jnp.bfloat16), 2 * at + 2, odd_hop))
    own = own + arrived[0].astype(jnp.float32)
    own, *sums = lax.optimization_barrier((own, *arrived[1:]))
    out = pl.pallas_call(
        final_kernel,
        out_shape=jax.ShapeDtypeStruct(part, jnp.bfloat16),
        in_specs=[VMEM] * (2 + len(sums)),
        out_specs=HBM,
        scratch_shapes=[
            held(tiles_dev, jnp.bfloat16),
            pltpu.SemaphoreType.DMA((tiles_dev,)),
        ],
        compiler_params=LIMIT,
        cost_estimate=cost_of(0, tile_rows, row_width),
    )(factors, own, *sums)
    return out.reshape(1, row_count, row_width)


def solution(mesh):
    placed = (
        P("side", ("grp", "blk"), None),
        P("side", ("grp", "blk")),
        P("side", ("grp", "blk")),
        P("side", ("grp", "blk"), None, None),
        P("side", None, ("grp", "blk")),
    )
    return jax.shard_map(
        shards,
        mesh=mesh,
        in_specs=placed,
        out_specs=P("side", ("grp", "blk"), None),
        check_vma=False,
    )
```

```python
import functools

import jax
import jax.numpy as jnp
from jax import lax
from jax.experimental import pallas as pl
from jax.experimental.pallas import tpu as pltpu
from jax.sharding import PartitionSpec as P

UNROLL = 8
BATCHES = (4, 4, 4, 8, 8, 8)
STAGES = len(BATCHES)
VMEM = pl.BlockSpec(memory_space=pltpu.VMEM)
SMEM = pl.BlockSpec(memory_space=pltpu.SMEM)
HBM = pl.BlockSpec(memory_space=pltpu.HBM)
LIMIT = pltpu.CompilerParams(vmem_limit_bytes=48 * 1024 * 1024)


def in_hbm(*arrays):
    return [pltpu.with_memory_space_constraint(array, pltpu.HBM) for array in arrays]


def split(value, size):
    if size & (size - 1) == 0:
        return value >> (size.bit_length() - 1), value & (size - 1)
    return value // size, value % size


def scale_kernel(
    exps_hbm, degrees_hbm, codes_hbm, rows, factors, scales, exps_ref, degrees, codes, sems
):
    pairs = [(exps_hbm, exps_ref), (degrees_hbm, degrees), (codes_hbm, codes)]
    fetches = [
        pltpu.make_async_copy(held, wanted, sems.at[at])
        for at, (held, wanted) in enumerate(pairs)
    ]
    for fetch in fetches:
        fetch.start()
    fetches[0].wait()
    fetches[1].wait()
    tiles_dev, tile_rows, row_width = rows.shape
    inverse = lax.rsqrt(degrees[...].astype(jnp.float32))
    for tile in range(tiles_dev):
        lanes = inverse[:, tile * tile_rows : (tile + 1) * tile_rows]
        factors[tile] = jnp.broadcast_to(lanes, (row_width, tile_rows)).T
        scale = jnp.exp2(jnp.full((1, 1), exps_ref[0, tile], jnp.int32).astype(jnp.float32))
        scales[tile : tile + 1, :] = lanes * scale
    fetches[2].wait()
    for tile in range(tiles_dev):
        scale = jnp.exp2(jnp.full((1, 1), exps_ref[0, tile], jnp.int32).astype(jnp.float32))
        scaled = codes[tile].astype(jnp.float32) * scale * factors[tile]
        rows[tile] = scaled.astype(rows.dtype)


def scale_rows(codes, exps, degrees):
    return pl.pallas_call(
        scale_kernel,
        out_shape=[
            jax.ShapeDtypeStruct(codes.shape, jnp.bfloat16),
            jax.ShapeDtypeStruct(codes.shape, jnp.float32),
            jax.ShapeDtypeStruct(codes.shape[:2], jnp.float32),
        ],
        in_specs=[HBM] * 3,
        out_specs=[VMEM] * 3,
        scratch_shapes=[
            pltpu.SMEM(exps.shape, exps.dtype),
            pltpu.VMEM(degrees.shape, degrees.dtype),
            pltpu.VMEM(codes.shape, codes.dtype),
            pltpu.SemaphoreType.DMA((3,)),
        ],
        compiler_params=LIMIT,
        cost_estimate=pl.CostEstimate(
            flops=codes.size, bytes_accessed=4 * codes.size, transcendentals=0
        ),
    )(*in_hbm(exps, degrees, codes))


def count_up(shape, axis):
    return lax.broadcasted_iota(jnp.int32, shape, axis)


def stage_kernel(
    blks, groups, tiles_dev, place_ref, index_hbm, blocks_hbm, order_ref, blocks, index_ref, sems
):
    fetch = pltpu.make_async_copy(index_hbm, index_ref, sems.at[0])
    fetch.start()
    copy = pltpu.make_async_copy(blocks_hbm, blocks, sems.at[1])
    copy.start()
    fetch.wait()
    my_blk = place_ref[0]
    my_grp = place_ref[1]
    capacity = index_ref.shape[1]
    width = order_ref.shape[1]
    source_tiles = blks * tiles_dev
    half = blks // 2
    role = my_blk & 1

    target = index_ref[0:1, :]
    origin = index_ref[1:2, :]
    hop, row = split(origin, tiles_dev)
    chunk, tile = split(target, tiles_dev)
    hop = hop ^ my_blk
    chunk = chunk ^ my_grp
    odd = hop & 1
    rank = jnp.where(odd == role, half - 1 - (hop >> 1), hop >> 1)
    far = (chunk >= 2) & ((chunk & 1) == 1)
    kept = jnp.where(chunk == 1, 1 + role * (groups // 2 - 1), (chunk >> 1) + 1 - role)
    kept = jnp.where(chunk == 0, 0, jnp.where(far, (chunk >> 1) - 1, kept))
    stage = jnp.where(far, jnp.where(odd == 1, 2, jnp.minimum(rank, 1)), 5)
    stage = jnp.where(far | (kept != 1), stage, 4 - role)
    kept = jnp.where(far | (kept == 0), kept, kept - 1)
    stage = jnp.where(origin < source_tiles, stage, STAGES)
    panel = jnp.where(stage == 1, rank - 1, jnp.where(stage == 2, rank, rank + odd * half))
    slot = count_up((1, capacity), 1)

    stages = (count_up((8, capacity), 0) == stage).astype(jnp.float32)
    earlier = count_up((capacity, capacity), 0) < count_up((capacity, capacity), 1)
    before = jnp.dot(
        stages.astype(jnp.bfloat16), earlier.astype(jnp.bfloat16), preferred_element_type=jnp.float32
    )
    position = jnp.sum(stages * before, axis=0, keepdims=True).astype(jnp.int32)
    parts = (slot & 127, slot >> 7, panel * tiles_dev + row, kept * tiles_dev + tile)
    values = sum(
        jnp.where(count_up((8, capacity), 0) == at, part, 0) for at, part in enumerate(parts)
    ).astype(jnp.bfloat16)
    far_tiles = (groups // 2 - 1) * tiles_dev
    tops = [far_tiles] * 3 + [tiles_dev] * 2 + [groups // 2 * tiles_dev]
    lanes = count_up((1, width), 1)
    for at, top in enumerate(tops):
        where = jnp.where(stage == at, position, -1)
        chosen = (count_up((width, capacity), 0) == where).astype(jnp.bfloat16)
        listed = lax.dot_general(
            values, chosen, (((1,), (1,)), ((), ())), preferred_element_type=jnp.float32
        ).astype(jnp.int32)
        word = pack(listed[0:1] + (listed[1:2] << 7), listed[2:3], listed[3:4])
        count = jnp.sum((stage == at).astype(jnp.int32), axis=1, keepdims=True)
        word = jnp.where(lanes < count, word, pack(0, 0, top))
        batches = split(count + (BATCHES[at] - 1), BATCHES[at])[0]
        order_ref[at : at + 1, :] = jnp.where(lanes == width - UNROLL, batches, word)
    copy.wait()


def pack(slot, row, target):
    return (slot << 16) | (row << 8) | target


def unpack(word):
    return word >> 16, (word >> 8) & 255, word & 255


def stage_blocks(index, place, blocks, blks, groups, tiles_dev):
    capacity = blocks.shape[0]
    assert blks * tiles_dev < 256 and groups * tiles_dev < 256 and capacity < 2**15
    width = -(-(capacity + 2 * UNROLL) // 128) * 128
    return pl.pallas_call(
        functools.partial(stage_kernel, blks, groups, tiles_dev),
        out_shape=[
            jax.ShapeDtypeStruct((8, width), jnp.int32),
            jax.ShapeDtypeStruct(blocks.shape, blocks.dtype),
        ],
        in_specs=[SMEM, HBM, HBM],
        out_specs=[VMEM, VMEM],
        scratch_shapes=[
            pltpu.VMEM(index.shape, index.dtype),
            pltpu.SemaphoreType.DMA((2,)),
        ],
        compiler_params=LIMIT,
        cost_estimate=pl.CostEstimate(flops=0, bytes_accessed=0, transcendentals=0),
    )(place, *in_hbm(index, blocks))


def add_products(stage, order_ref, blocks, source, total):
    @pl.loop(0, order_ref[stage, order_ref.shape[1] - UNROLL])
    def _(batch):
        made = []
        for part in range(BATCHES[stage]):
            slot, row, target = unpack(order_ref[stage, batch * BATCHES[stage] + part])
            product = jnp.dot(blocks[slot], source[row], preferred_element_type=jnp.float32)
            made.append((target, product))
        for target, product in made:
            total[target] += product


def gather_panels(panels, source):
    for at, panel in enumerate(panels):
        rows = panel.shape[0]
        source[at * rows : (at + 1) * rows] = panel[...]


def early_kernel(order_ref, panel, blocks, total):
    total[...] = jnp.zeros_like(total)
    add_products(0, order_ref, blocks, panel, total)


def middle_kernel(order_ref, *refs):
    *panels, blocks, _, total, source = refs
    gather_panels(panels, source)
    add_products(1, order_ref, blocks, source, total)


def far_kernel(tiles_dev, order_ref, *refs):
    *panels, blocks, _, far, first, total, source = refs
    others = len(panels) // 2 * tiles_dev
    gather_panels(panels, source)
    first[...] = jnp.zeros_like(first)
    add_products(2, order_ref, blocks, source.at[others:], total)
    add_products(3, order_ref, blocks, source, first)
    far[...] = total[: far.shape[0]].astype(far.dtype)


def first_kernel(order_ref, *refs):
    *panels, blocks, _, first, total, source = refs
    gather_panels(panels, source)
    add_products(4, order_ref, blocks, source, total)
    first[...] = total[: first.shape[0]].astype(first.dtype)


def rest_kernel(order_ref, *refs):
    *panels, blocks, own, later, source, total = refs
    gather_panels(panels, source)
    total[...] = jnp.zeros_like(total)
    add_products(5, order_ref, blocks, source, total)
    tiles_dev = own.shape[0]
    own[...] = total[:tiles_dev]
    later[...] = total[tiles_dev : tiles_dev + later.shape[0]]


def final_kernel(factors, own, *refs):
    *arrived, out_hbm, out, sems = refs
    copies = []
    for tile in range(out.shape[0]):
        value = own[tile]
        for piece in arrived:
            value = value + piece[tile].astype(jnp.float32)
        out[tile] = (value * factors[tile]).astype(out.dtype)
        copies.append(pltpu.make_async_copy(out.at[tile], out_hbm.at[tile], sems.at[tile]))
        copies[-1].start()
    for copy in copies:
        copy.wait()


def cost_of(slots, tile_rows, row_width):
    return pl.CostEstimate(
        flops=2 * slots * tile_rows * tile_rows * row_width,
        bytes_accessed=2 * slots * tile_rows * tile_rows,
        transcendentals=0,
    )


def shards(embed_codes, embed_exps, degrees, adjacency, block_index):
    tile_rows = adjacency.shape[2]
    row_width = embed_codes.shape[2]
    row_count = embed_codes.shape[1]
    capacity = adjacency.shape[1]
    tiles_dev = row_count // tile_rows
    groups = lax.axis_size("grp")
    blks = lax.axis_size("blk")
    part = (tiles_dev, tile_rows, row_width)
    codes = embed_codes.reshape(part)
    source, factors, scales = scale_rows(codes, embed_exps, degrees)

    def across(value, step):
        pairs = [
            (side * blks + at, (1 - side) * blks + (at ^ (2 * step if at & 1 else blks - 2 - 2 * step)))
            for side in range(2)
            for at in range(blks)
        ]
        return lax.ppermute(value, ("side", "blk"), pairs)

    def paired(value, axis, hop):
        return lax.ppermute(value, axis, [(at, at ^ hop) for at in range(lax.axis_size(axis))])

    place = jnp.stack([lax.axis_index("blk"), lax.axis_index("grp")]).astype(jnp.int32)
    early = across(codes, 0)
    middle = [across(source, step) for step in range(1, blks // 2)]
    early_scales = across(scales, 0)
    order, blocks = stage_blocks(block_index[0], place, adjacency[0], blks, groups, tiles_dev)
    early, early_scales, order = lax.optimization_barrier((early, early_scales, order))
    early = (early.astype(jnp.float32) * early_scales[:, :, None]).astype(jnp.bfloat16)
    other = paired(early, "blk", 1)
    far_tiles = (groups // 2 - 1) * tiles_dev

    def held(count, dtype):
        return pltpu.VMEM((count, tile_rows, row_width), dtype)

    total = pl.pallas_call(
        early_kernel,
        out_shape=jax.ShapeDtypeStruct((far_tiles + 1, tile_rows, row_width), jnp.float32),
        in_specs=[SMEM] + [VMEM] * 2,
        out_specs=VMEM,
        compiler_params=LIMIT,
        cost_estimate=cost_of(capacity // 8, tile_rows, row_width),
    )(order, early, blocks)
    *middle, total = lax.optimization_barrier((*middle, total))
    others = [other] + [paired(panel, "blk", 1) for panel in middle]
    total = pl.pallas_call(
        middle_kernel,
        out_shape=jax.ShapeDtypeStruct(total.shape, total.dtype),
        in_specs=[SMEM] + [VMEM] * (len(middle) + 2),
        out_specs=VMEM,
        input_output_aliases={len(middle) + 2: 0},
        scratch_shapes=[held(len(middle) * tiles_dev, jnp.bfloat16)],
        compiler_params=LIMIT,
        cost_estimate=cost_of(capacity // 8, tile_rows, row_width),
    )(order, *middle, blocks, total)
    *others, total = lax.optimization_barrier((*others, total))
    panels = [early] + middle + others
    far, first, _ = pl.pallas_call(
        functools.partial(far_kernel, tiles_dev),
        out_shape=[
            jax.ShapeDtypeStruct((far_tiles, tile_rows, row_width), jnp.bfloat16),
            jax.ShapeDtypeStruct((tiles_dev + 1, tile_rows, row_width), jnp.float32),
            jax.ShapeDtypeStruct(total.shape, total.dtype),
        ],
        in_specs=[SMEM] + [VMEM] * (len(panels) + 2),
        out_specs=[VMEM] * 3,
        input_output_aliases={len(panels) + 2: 2},
        scratch_shapes=[held(len(panels) * tiles_dev, jnp.bfloat16)],
        compiler_params=LIMIT,
        cost_estimate=cost_of(capacity // 8, tile_rows, row_width),
    )(order, *panels, blocks, total)
    far, order = lax.optimization_barrier((far, order))
    first, _ = pl.pallas_call(
        first_kernel,
        out_shape=[
            jax.ShapeDtypeStruct(part, jnp.bfloat16),
            jax.ShapeDtypeStruct(first.shape, first.dtype),
        ],
        in_specs=[SMEM] + [VMEM] * (len(panels) + 2),
        out_specs=[VMEM] * 2,
        input_output_aliases={len(panels) + 2: 1},
        scratch_shapes=[held(len(panels) * tiles_dev, jnp.bfloat16)],
        compiler_params=LIMIT,
        cost_estimate=cost_of(capacity // 4, tile_rows, row_width),
    )(order, *panels, blocks, first)
    first, order = lax.optimization_barrier((first, order))
    own, later = pl.pallas_call(
        rest_kernel,
        out_shape=[
            jax.ShapeDtypeStruct(part, jnp.float32),
            jax.ShapeDtypeStruct((far_tiles, tile_rows, row_width), jnp.float32),
        ],
        in_specs=[SMEM] + [VMEM] * (len(panels) + 1),
        out_specs=[VMEM] * 2,
        scratch_shapes=[
            held(len(panels) * tiles_dev, jnp.bfloat16),
            held(groups // 2 * tiles_dev + 1, jnp.float32),
        ],
        compiler_params=LIMIT,
        cost_estimate=cost_of(capacity // 2, tile_rows, row_width),
    )(order, *panels, blocks)

    def turned(value, even_hop, odd_hop):
        hops = (even_hop, odd_hop)
        pairs = [
            (at * blks + blk, (at ^ hops[blk & 1]) * blks + blk)
            for at in range(groups)
            for blk in range(blks)
        ]
        return lax.ppermute(value, ("grp", "blk"), pairs)

    steps = groups // 2 - 1
    even_core = lax.axis_index("blk") % 2 == 0
    pieces = [slice(at * tiles_dev, (at + 1) * tiles_dev) for at in range(steps)]
    handed = [turned(far[pieces[at]], 1, 2 * at + 2).astype(jnp.float32) for at in range(steps)]
    arrived = [turned(first, 1, 2)]
    for at in range(steps):
        value = later[pieces[at]]
        for step, extra in enumerate(handed):
            if step == at == steps - 1:
                value = value + extra
            elif step == at:
                value = value + jnp.where(even_core, extra, 0.0)
            elif at == steps - 1:
                value = value + jnp.where(even_core, 0.0, extra)
        odd_hop = 1 if at == steps - 1 else 2 * at + 4
        arrived.append(turned(value.astype(jnp.bfloat16), 2 * at + 2, odd_hop))
    own = own + arrived[0].astype(jnp.float32)
    own, *sums = lax.optimization_barrier((own, *arrived[1:]))
    out = pl.pallas_call(
        final_kernel,
        out_shape=jax.ShapeDtypeStruct(part, jnp.bfloat16),
        in_specs=[VMEM] * (2 + len(sums)),
        out_specs=HBM,
        scratch_shapes=[
            held(tiles_dev, jnp.bfloat16),
            pltpu.SemaphoreType.DMA((tiles_dev,)),
        ],
        compiler_params=LIMIT,
        cost_estimate=cost_of(0, tile_rows, row_width),
    )(factors, own, *sums)
    return out.reshape(1, row_count, row_width)


def solution(mesh):
    placed = (
        P("side", ("grp", "blk"), None),
        P("side", ("grp", "blk")),
        P("side", ("grp", "blk")),
        P("side", ("grp", "blk"), None, None),
        P("side", None, ("grp", "blk")),
    )
    return jax.shard_map(
        shards,
        mesh=mesh,
        in_specs=placed,
        out_specs=P("side", ("grp", "blk"), None),
        check_vma=False,
    )
```

```python
import functools

import jax
import jax.numpy as jnp
from jax import lax
from jax.experimental import pallas as pl
from jax.experimental.pallas import tpu as pltpu
from jax.sharding import PartitionSpec as P

UNROLL = 8
BATCHES = (4, 4, 8, 8, 8)
STAGES = len(BATCHES)
VMEM = pl.BlockSpec(memory_space=pltpu.VMEM)
SMEM = pl.BlockSpec(memory_space=pltpu.SMEM)
HBM = pl.BlockSpec(memory_space=pltpu.HBM)
LIMIT = pltpu.CompilerParams(vmem_limit_bytes=48 * 1024 * 1024)


def in_hbm(*arrays):
    return [pltpu.with_memory_space_constraint(array, pltpu.HBM) for array in arrays]


def split(value, size):
    if size & (size - 1) == 0:
        return value >> (size.bit_length() - 1), value & (size - 1)
    return value // size, value % size


def scale_kernel(
    exps_hbm, degrees_hbm, codes_hbm, rows, factors, scales, exps_ref, degrees, codes, sems
):
    pairs = [(exps_hbm, exps_ref), (degrees_hbm, degrees), (codes_hbm, codes)]
    fetches = [
        pltpu.make_async_copy(held, wanted, sems.at[at])
        for at, (held, wanted) in enumerate(pairs)
    ]
    for fetch in fetches:
        fetch.start()
    fetches[0].wait()
    fetches[1].wait()
    tiles_dev, tile_rows, row_width = rows.shape
    inverse = lax.rsqrt(degrees[...].astype(jnp.float32))
    for tile in range(tiles_dev):
        lanes = inverse[:, tile * tile_rows : (tile + 1) * tile_rows]
        factors[tile] = jnp.broadcast_to(lanes, (row_width, tile_rows)).T
        scale = jnp.exp2(jnp.full((1, 1), exps_ref[0, tile], jnp.int32).astype(jnp.float32))
        scales[tile : tile + 1, :] = lanes * scale
    fetches[2].wait()
    for tile in range(tiles_dev):
        scale = jnp.exp2(jnp.full((1, 1), exps_ref[0, tile], jnp.int32).astype(jnp.float32))
        scaled = codes[tile].astype(jnp.float32) * scale * factors[tile]
        rows[tile] = scaled.astype(rows.dtype)


def scale_rows(codes, exps, degrees):
    return pl.pallas_call(
        scale_kernel,
        out_shape=[
            jax.ShapeDtypeStruct(codes.shape, jnp.bfloat16),
            jax.ShapeDtypeStruct(codes.shape, jnp.float32),
            jax.ShapeDtypeStruct(codes.shape[:2], jnp.float32),
        ],
        in_specs=[HBM] * 3,
        out_specs=[VMEM] * 3,
        scratch_shapes=[
            pltpu.SMEM(exps.shape, exps.dtype),
            pltpu.VMEM(degrees.shape, degrees.dtype),
            pltpu.VMEM(codes.shape, codes.dtype),
            pltpu.SemaphoreType.DMA((3,)),
        ],
        compiler_params=LIMIT,
        cost_estimate=pl.CostEstimate(
            flops=codes.size, bytes_accessed=4 * codes.size, transcendentals=0
        ),
    )(*in_hbm(exps, degrees, codes))


def count_up(shape, axis):
    return lax.broadcasted_iota(jnp.int32, shape, axis)


def stage_kernel(
    blks, groups, tiles_dev, place_ref, index_hbm, blocks_hbm, order_ref, blocks, index_ref, sems
):
    fetch = pltpu.make_async_copy(index_hbm, index_ref, sems.at[0])
    fetch.start()
    copy = pltpu.make_async_copy(blocks_hbm, blocks, sems.at[1])
    copy.start()
    fetch.wait()
    my_blk = place_ref[0]
    my_grp = place_ref[1]
    capacity = index_ref.shape[1]
    width = order_ref.shape[1]
    source_tiles = blks * tiles_dev
    half = blks // 2
    role = my_blk & 1

    target = index_ref[0:1, :]
    origin = index_ref[1:2, :]
    hop, row = split(origin, tiles_dev)
    chunk, tile = split(target, tiles_dev)
    hop = hop ^ my_blk
    chunk = chunk ^ my_grp
    odd = hop & 1
    rank = jnp.where(odd == role, half - 1 - (hop >> 1), hop >> 1)
    far = (chunk >= 2) & ((chunk & 1) == 1)
    kept = jnp.where(chunk == 1, 1 + role * (groups // 2 - 1), (chunk >> 1) + 1 - role)
    kept = jnp.where(chunk == 0, 0, jnp.where(far, (chunk >> 1) - 1, kept))
    stage = jnp.where(far, odd, 4)
    stage = jnp.where(far | (kept != 1), stage, 3 - role)
    kept = jnp.where(far | (kept == 0), kept, kept - 1)
    stage = jnp.where(origin < source_tiles, stage, STAGES)
    panel = jnp.where(stage == 1, rank, rank + odd * half)
    slot = count_up((1, capacity), 1)

    stages = (count_up((8, capacity), 0) == stage).astype(jnp.float32)
    earlier = count_up((capacity, capacity), 0) < count_up((capacity, capacity), 1)
    before = jnp.dot(
        stages.astype(jnp.bfloat16), earlier.astype(jnp.bfloat16), preferred_element_type=jnp.float32
    )
    position = jnp.sum(stages * before, axis=0, keepdims=True).astype(jnp.int32)
    parts = (slot & 127, slot >> 7, panel * tiles_dev + row, kept * tiles_dev + tile)
    values = sum(
        jnp.where(count_up((8, capacity), 0) == at, part, 0) for at, part in enumerate(parts)
    ).astype(jnp.bfloat16)
    far_tiles = (groups // 2 - 1) * tiles_dev
    tops = [far_tiles] * 2 + [tiles_dev] * 2 + [groups // 2 * tiles_dev]
    lanes = count_up((1, width), 1)
    for at, top in enumerate(tops):
        where = jnp.where(stage == at, position, -1)
        chosen = (count_up((width, capacity), 0) == where).astype(jnp.bfloat16)
        listed = lax.dot_general(
            values, chosen, (((1,), (1,)), ((), ())), preferred_element_type=jnp.float32
        ).astype(jnp.int32)
        word = pack(listed[0:1] + (listed[1:2] << 7), listed[2:3], listed[3:4])
        count = jnp.sum((stage == at).astype(jnp.int32), axis=1, keepdims=True)
        word = jnp.where(lanes < count, word, pack(0, 0, top))
        batches = split(count + (BATCHES[at] - 1), BATCHES[at])[0]
        order_ref[at : at + 1, :] = jnp.where(lanes == width - UNROLL, batches, word)
    copy.wait()


def pack(slot, row, target):
    return (slot << 16) | (row << 8) | target


def unpack(word):
    return word >> 16, (word >> 8) & 255, word & 255


def stage_blocks(index, place, blocks, blks, groups, tiles_dev):
    capacity = blocks.shape[0]
    assert blks * tiles_dev < 256 and groups * tiles_dev < 256 and capacity < 2**15
    width = -(-(capacity + 2 * UNROLL) // 128) * 128
    return pl.pallas_call(
        functools.partial(stage_kernel, blks, groups, tiles_dev),
        out_shape=[
            jax.ShapeDtypeStruct((8, width), jnp.int32),
            jax.ShapeDtypeStruct(blocks.shape, blocks.dtype),
        ],
        in_specs=[SMEM, HBM, HBM],
        out_specs=[VMEM, VMEM],
        scratch_shapes=[
            pltpu.VMEM(index.shape, index.dtype),
            pltpu.SemaphoreType.DMA((2,)),
        ],
        compiler_params=LIMIT,
        cost_estimate=pl.CostEstimate(flops=0, bytes_accessed=0, transcendentals=0),
    )(place, *in_hbm(index, blocks))


def add_products(stage, order_ref, blocks, source, total):
    @pl.loop(0, order_ref[stage, order_ref.shape[1] - UNROLL])
    def _(batch):
        made = []
        for part in range(BATCHES[stage]):
            slot, row, target = unpack(order_ref[stage, batch * BATCHES[stage] + part])
            product = jnp.dot(blocks[slot], source[row], preferred_element_type=jnp.float32)
            made.append((target, product))
        for target, product in made:
            total[target] += product


def gather_panels(panels, source):
    for at, panel in enumerate(panels):
        rows = panel.shape[0]
        source[at * rows : (at + 1) * rows] = panel[...]


def early_kernel(order_ref, *refs):
    *panels, blocks, total, source = refs
    gather_panels(panels, source)
    total[...] = jnp.zeros_like(total)
    add_products(0, order_ref, blocks, source, total)


def far_kernel(tiles_dev, order_ref, *refs):
    *panels, blocks, _, far, first, total, source = refs
    others = len(panels) // 2 * tiles_dev
    gather_panels(panels, source)
    first[...] = jnp.zeros_like(first)
    add_products(1, order_ref, blocks, source.at[others:], total)
    add_products(2, order_ref, blocks, source, first)
    far[...] = total[: far.shape[0]].astype(far.dtype)


def first_kernel(order_ref, *refs):
    *panels, blocks, _, first, total, source = refs
    gather_panels(panels, source)
    add_products(3, order_ref, blocks, source, total)
    first[...] = total[: first.shape[0]].astype(first.dtype)


def rest_kernel(order_ref, *refs):
    *panels, blocks, own, later, source, total = refs
    gather_panels(panels, source)
    total[...] = jnp.zeros_like(total)
    add_products(4, order_ref, blocks, source, total)
    tiles_dev = own.shape[0]
    own[...] = total[:tiles_dev]
    later[...] = total[tiles_dev : tiles_dev + later.shape[0]]


def final_kernel(factors, own, *refs):
    *arrived, out_hbm, out, sems = refs
    copies = []
    for tile in range(out.shape[0]):
        value = own[tile]
        for piece in arrived:
            value = value + piece[tile].astype(jnp.float32)
        out[tile] = (value * factors[tile]).astype(out.dtype)
        copies.append(pltpu.make_async_copy(out.at[tile], out_hbm.at[tile], sems.at[tile]))
        copies[-1].start()
    for copy in copies:
        copy.wait()


def cost_of(slots, tile_rows, row_width):
    return pl.CostEstimate(
        flops=2 * slots * tile_rows * tile_rows * row_width,
        bytes_accessed=2 * slots * tile_rows * tile_rows,
        transcendentals=0,
    )


def shards(embed_codes, embed_exps, degrees, adjacency, block_index):
    tile_rows = adjacency.shape[2]
    row_width = embed_codes.shape[2]
    row_count = embed_codes.shape[1]
    capacity = adjacency.shape[1]
    tiles_dev = row_count // tile_rows
    groups = lax.axis_size("grp")
    blks = lax.axis_size("blk")
    part = (tiles_dev, tile_rows, row_width)
    codes = embed_codes.reshape(part)
    source, factors, scales = scale_rows(codes, embed_exps, degrees)

    def across(value, step):
        pairs = [
            (side * blks + at, (1 - side) * blks + (at ^ (2 * step if at & 1 else blks - 2 - 2 * step)))
            for side in range(2)
            for at in range(blks)
        ]
        return lax.ppermute(value, ("side", "blk"), pairs)

    def paired(value, axis, hop):
        return lax.ppermute(value, axis, [(at, at ^ hop) for at in range(lax.axis_size(axis))])

    place = jnp.stack([lax.axis_index("blk"), lax.axis_index("grp")]).astype(jnp.int32)
    early = across(codes, 0)
    middle = [across(source, step) for step in range(1, blks // 2)]
    early_scales = across(scales, 0)
    order, blocks = stage_blocks(block_index[0], place, adjacency[0], blks, groups, tiles_dev)
    *middle, early, early_scales, order = lax.optimization_barrier((*middle, early, early_scales, order))
    early = (early.astype(jnp.float32) * early_scales[:, :, None]).astype(jnp.bfloat16)
    panels = [early] + middle
    others = [paired(panel, "blk", 1) for panel in panels]
    far_tiles = (groups // 2 - 1) * tiles_dev

    def held(count, dtype):
        return pltpu.VMEM((count, tile_rows, row_width), dtype)

    total = pl.pallas_call(
        early_kernel,
        out_shape=jax.ShapeDtypeStruct((far_tiles + 1, tile_rows, row_width), jnp.float32),
        in_specs=[SMEM] + [VMEM] * (len(panels) + 1),
        out_specs=VMEM,
        scratch_shapes=[held(len(panels) * tiles_dev, jnp.bfloat16)],
        compiler_params=LIMIT,
        cost_estimate=cost_of(capacity // 8, tile_rows, row_width),
    )(order, *panels, blocks)
    *others, total = lax.optimization_barrier((*others, total))
    panels += others
    far, first, _ = pl.pallas_call(
        functools.partial(far_kernel, tiles_dev),
        out_shape=[
            jax.ShapeDtypeStruct((far_tiles, tile_rows, row_width), jnp.bfloat16),
            jax.ShapeDtypeStruct((tiles_dev + 1, tile_rows, row_width), jnp.float32),
            jax.ShapeDtypeStruct(total.shape, total.dtype),
        ],
        in_specs=[SMEM] + [VMEM] * (len(panels) + 2),
        out_specs=[VMEM] * 3,
        input_output_aliases={len(panels) + 2: 2},
        scratch_shapes=[held(len(panels) * tiles_dev, jnp.bfloat16)],
        compiler_params=LIMIT,
        cost_estimate=cost_of(capacity // 8, tile_rows, row_width),
    )(order, *panels, blocks, total)
    far, order = lax.optimization_barrier((far, order))
    first, _ = pl.pallas_call(
        first_kernel,
        out_shape=[
            jax.ShapeDtypeStruct(part, jnp.bfloat16),
            jax.ShapeDtypeStruct(first.shape, first.dtype),
        ],
        in_specs=[SMEM] + [VMEM] * (len(panels) + 2),
        out_specs=[VMEM] * 2,
        input_output_aliases={len(panels) + 2: 1},
        scratch_shapes=[held(len(panels) * tiles_dev, jnp.bfloat16)],
        compiler_params=LIMIT,
        cost_estimate=cost_of(capacity // 4, tile_rows, row_width),
    )(order, *panels, blocks, first)
    first, order = lax.optimization_barrier((first, order))
    own, later = pl.pallas_call(
        rest_kernel,
        out_shape=[
            jax.ShapeDtypeStruct(part, jnp.float32),
            jax.ShapeDtypeStruct((far_tiles, tile_rows, row_width), jnp.float32),
        ],
        in_specs=[SMEM] + [VMEM] * (len(panels) + 1),
        out_specs=[VMEM] * 2,
        scratch_shapes=[
            held(len(panels) * tiles_dev, jnp.bfloat16),
            held(groups // 2 * tiles_dev + 1, jnp.float32),
        ],
        compiler_params=LIMIT,
        cost_estimate=cost_of(capacity // 2, tile_rows, row_width),
    )(order, *panels, blocks)

    def turned(value, even_hop, odd_hop):
        hops = (even_hop, odd_hop)
        pairs = [
            (at * blks + blk, (at ^ hops[blk & 1]) * blks + blk)
            for at in range(groups)
            for blk in range(blks)
        ]
        return lax.ppermute(value, ("grp", "blk"), pairs)

    steps = groups // 2 - 1
    even_core = lax.axis_index("blk") % 2 == 0
    pieces = [slice(at * tiles_dev, (at + 1) * tiles_dev) for at in range(steps)]
    handed = [turned(far[pieces[at]], 1, 2 * at + 2).astype(jnp.float32) for at in range(steps)]
    arrived = [turned(first, 1, 2)]
    for at in range(steps):
        value = later[pieces[at]]
        for step, extra in enumerate(handed):
            if step == at == steps - 1:
                value = value + extra
            elif step == at:
                value = value + jnp.where(even_core, extra, 0.0)
            elif at == steps - 1:
                value = value + jnp.where(even_core, 0.0, extra)
        odd_hop = 1 if at == steps - 1 else 2 * at + 4
        arrived.append(turned(value.astype(jnp.bfloat16), 2 * at + 2, odd_hop))
    own = own + arrived[0].astype(jnp.float32)
    own, *sums = lax.optimization_barrier((own, *arrived[1:]))
    out = pl.pallas_call(
        final_kernel,
        out_shape=jax.ShapeDtypeStruct(part, jnp.bfloat16),
        in_specs=[VMEM] * (2 + len(sums)),
        out_specs=HBM,
        scratch_shapes=[
            held(tiles_dev, jnp.bfloat16),
            pltpu.SemaphoreType.DMA((tiles_dev,)),
        ],
        compiler_params=LIMIT,
        cost_estimate=cost_of(0, tile_rows, row_width),
    )(factors, own, *sums)
    return out.reshape(1, row_count, row_width)


def solution(mesh):
    placed = (
        P("side", ("grp", "blk"), None),
        P("side", ("grp", "blk")),
        P("side", ("grp", "blk")),
        P("side", ("grp", "blk"), None, None),
        P("side", None, ("grp", "blk")),
    )
    return jax.shard_map(
        shards,
        mesh=mesh,
        in_specs=placed,
        out_specs=P("side", ("grp", "blk"), None),
        check_vma=False,
    )
```

```python
import functools

import jax
import jax.numpy as jnp
from jax import lax
from jax.experimental import pallas as pl
from jax.experimental.pallas import tpu as pltpu
from jax.sharding import PartitionSpec as P

UNROLL = 8
BATCHES = (4, 4, 4, 8, 8, 8, 8)
STAGES = len(BATCHES)
VMEM = pl.BlockSpec(memory_space=pltpu.VMEM)
SMEM = pl.BlockSpec(memory_space=pltpu.SMEM)
HBM = pl.BlockSpec(memory_space=pltpu.HBM)
LIMIT = pltpu.CompilerParams(vmem_limit_bytes=48 * 1024 * 1024)


def in_hbm(*arrays):
    return [pltpu.with_memory_space_constraint(array, pltpu.HBM) for array in arrays]


def split(value, size):
    if size & (size - 1) == 0:
        return value >> (size.bit_length() - 1), value & (size - 1)
    return value // size, value % size


def scale_kernel(
    exps_hbm, degrees_hbm, codes_hbm, rows, factors, scales, exps_ref, degrees, codes, sems
):
    pairs = [(exps_hbm, exps_ref), (degrees_hbm, degrees), (codes_hbm, codes)]
    fetches = [
        pltpu.make_async_copy(held, wanted, sems.at[at])
        for at, (held, wanted) in enumerate(pairs)
    ]
    for fetch in fetches:
        fetch.start()
    fetches[0].wait()
    fetches[1].wait()
    tiles_dev, tile_rows, row_width = rows.shape
    inverse = lax.rsqrt(degrees[...].astype(jnp.float32))
    for tile in range(tiles_dev):
        lanes = inverse[:, tile * tile_rows : (tile + 1) * tile_rows]
        factors[tile] = jnp.broadcast_to(lanes, (row_width, tile_rows)).T
        scale = jnp.exp2(jnp.full((1, 1), exps_ref[0, tile], jnp.int32).astype(jnp.float32))
        scales[tile : tile + 1, :] = lanes * scale
    fetches[2].wait()
    for tile in range(tiles_dev):
        scale = jnp.exp2(jnp.full((1, 1), exps_ref[0, tile], jnp.int32).astype(jnp.float32))
        scaled = codes[tile].astype(jnp.float32) * scale * factors[tile]
        rows[tile] = scaled.astype(rows.dtype)


def scale_rows(codes, exps, degrees):
    return pl.pallas_call(
        scale_kernel,
        out_shape=[
            jax.ShapeDtypeStruct(codes.shape, jnp.bfloat16),
            jax.ShapeDtypeStruct(codes.shape, jnp.float32),
            jax.ShapeDtypeStruct(codes.shape[:2], jnp.float32),
        ],
        in_specs=[HBM] * 3,
        out_specs=[VMEM] * 3,
        scratch_shapes=[
            pltpu.SMEM(exps.shape, exps.dtype),
            pltpu.VMEM(degrees.shape, degrees.dtype),
            pltpu.VMEM(codes.shape, codes.dtype),
            pltpu.SemaphoreType.DMA((3,)),
        ],
        compiler_params=LIMIT,
        cost_estimate=pl.CostEstimate(
            flops=codes.size, bytes_accessed=4 * codes.size, transcendentals=0
        ),
    )(*in_hbm(exps, degrees, codes))


def count_up(shape, axis):
    return lax.broadcasted_iota(jnp.int32, shape, axis)


def stage_kernel(
    blks, groups, tiles_dev, place_ref, index_hbm, blocks_hbm, order_ref, blocks, index_ref, sems
):
    fetch = pltpu.make_async_copy(index_hbm, index_ref, sems.at[0])
    fetch.start()
    copy = pltpu.make_async_copy(blocks_hbm, blocks, sems.at[1])
    copy.start()
    fetch.wait()
    my_blk = place_ref[0]
    my_grp = place_ref[1]
    capacity = index_ref.shape[1]
    width = order_ref.shape[1]
    source_tiles = blks * tiles_dev
    half = blks // 2
    role = my_blk & 1

    target = index_ref[0:1, :]
    origin = index_ref[1:2, :]
    hop, row = split(origin, tiles_dev)
    chunk, tile = split(target, tiles_dev)
    hop = hop ^ my_blk
    chunk = chunk ^ my_grp
    odd = hop & 1
    rank = jnp.where(odd == role, half - 1 - (hop >> 1), hop >> 1)
    far = (chunk >= 2) & ((chunk & 1) == 1)
    kept = jnp.where(chunk == 1, 1 + role * (groups // 2 - 1), (chunk >> 1) + 1 - role)
    kept = jnp.where(chunk == 0, 0, jnp.where(far, (chunk >> 1) - 1, kept))
    near = jnp.where(kept == 0, 6, jnp.where(kept == 1, 4 - role, 5))
    stage = jnp.where(far, jnp.where(odd == 1, 2, jnp.minimum(rank, 1)), near)
    kept = jnp.where(stage == 5, kept - 2, jnp.where(far, kept, 0))
    stage = jnp.where(origin < source_tiles, stage, STAGES)
    panel = jnp.where(stage == 1, rank - 1, jnp.where(stage == 2, rank, rank + odd * half))
    slot = count_up((1, capacity), 1)

    stages = (count_up((8, capacity), 0) == stage).astype(jnp.float32)
    earlier = count_up((capacity, capacity), 0) < count_up((capacity, capacity), 1)
    before = jnp.dot(
        stages.astype(jnp.bfloat16), earlier.astype(jnp.bfloat16), preferred_element_type=jnp.float32
    )
    position = jnp.sum(stages * before, axis=0, keepdims=True).astype(jnp.int32)
    parts = (slot & 127, slot >> 7, panel * tiles_dev + row, kept * tiles_dev + tile)
    values = sum(
        jnp.where(count_up((8, capacity), 0) == at, part, 0) for at, part in enumerate(parts)
    ).astype(jnp.bfloat16)
    far_tiles = (groups // 2 - 1) * tiles_dev
    tops = [far_tiles] * 3 + [tiles_dev] * 2 + [far_tiles, tiles_dev]
    lanes = count_up((1, width), 1)
    for at, top in enumerate(tops):
        where = jnp.where(stage == at, position, -1)
        chosen = (count_up((width, capacity), 0) == where).astype(jnp.bfloat16)
        listed = lax.dot_general(
            values, chosen, (((1,), (1,)), ((), ())), preferred_element_type=jnp.float32
        ).astype(jnp.int32)
        word = pack(listed[0:1] + (listed[1:2] << 7), listed[2:3], listed[3:4])
        count = jnp.sum((stage == at).astype(jnp.int32), axis=1, keepdims=True)
        word = jnp.where(lanes < count, word, pack(0, 0, top))
        batches = split(count + (BATCHES[at] - 1), BATCHES[at])[0]
        order_ref[at : at + 1, :] = jnp.where(lanes == width - UNROLL, batches, word)
    copy.wait()


def pack(slot, row, target):
    return (slot << 16) | (row << 8) | target


def unpack(word):
    return word >> 16, (word >> 8) & 255, word & 255


def stage_blocks(index, place, blocks, blks, groups, tiles_dev):
    capacity = blocks.shape[0]
    assert blks * tiles_dev < 256 and groups * tiles_dev < 256 and capacity < 2**15
    width = -(-(capacity + 2 * UNROLL) // 128) * 128
    return pl.pallas_call(
        functools.partial(stage_kernel, blks, groups, tiles_dev),
        out_shape=[
            jax.ShapeDtypeStruct((8, width), jnp.int32),
            jax.ShapeDtypeStruct(blocks.shape, blocks.dtype),
        ],
        in_specs=[SMEM, HBM, HBM],
        out_specs=[VMEM, VMEM],
        scratch_shapes=[
            pltpu.VMEM(index.shape, index.dtype),
            pltpu.SemaphoreType.DMA((2,)),
        ],
        compiler_params=LIMIT,
        cost_estimate=pl.CostEstimate(flops=0, bytes_accessed=0, transcendentals=0),
    )(place, *in_hbm(index, blocks))


def add_products(stage, order_ref, blocks, source, total):
    @pl.loop(0, order_ref[stage, order_ref.shape[1] - UNROLL])
    def _(batch):
        made = []
        for part in range(BATCHES[stage]):
            slot, row, target = unpack(order_ref[stage, batch * BATCHES[stage] + part])
            product = jnp.dot(blocks[slot], source[row], preferred_element_type=jnp.float32)
            made.append((target, product))
        for target, product in made:
            total[target] += product


def gather_panels(panels, source):
    for at, panel in enumerate(panels):
        rows = panel.shape[0]
        source[at * rows : (at + 1) * rows] = panel[...]


def early_kernel(order_ref, panel, blocks, total):
    total[...] = jnp.zeros_like(total)
    add_products(0, order_ref, blocks, panel, total)


def middle_kernel(order_ref, *refs):
    *panels, blocks, _, total, source = refs
    gather_panels(panels, source)
    add_products(1, order_ref, blocks, source, total)


def far_kernel(tiles_dev, order_ref, *refs):
    *panels, blocks, _, far, first, total, source = refs
    others = len(panels) // 2 * tiles_dev
    gather_panels(panels, source)
    first[...] = jnp.zeros_like(first)
    add_products(2, order_ref, blocks, source.at[others:], total)
    add_products(3, order_ref, blocks, source, first)
    far[...] = total[: far.shape[0]].astype(far.dtype)


def first_kernel(order_ref, *refs):
    *panels, blocks, _, first, total, source = refs
    gather_panels(panels, source)
    add_products(4, order_ref, blocks, source, total)
    first[...] = total[: first.shape[0]].astype(first.dtype)


def later_kernel(stage, order_ref, *refs):
    *panels, blocks, later, source, total = refs
    gather_panels(panels, source)
    total[...] = jnp.zeros_like(total)
    add_products(stage, order_ref, blocks, source, total)
    later[...] = total[: later.shape[0]]


def final_kernel(factors, own, *refs):
    *arrived, out_hbm, out, sems = refs
    copies = []
    for tile in range(out.shape[0]):
        value = own[tile]
        for piece in arrived:
            value = value + piece[tile].astype(jnp.float32)
        out[tile] = (value * factors[tile]).astype(out.dtype)
        copies.append(pltpu.make_async_copy(out.at[tile], out_hbm.at[tile], sems.at[tile]))
        copies[-1].start()
    for copy in copies:
        copy.wait()


def cost_of(slots, tile_rows, row_width):
    return pl.CostEstimate(
        flops=2 * slots * tile_rows * tile_rows * row_width,
        bytes_accessed=2 * slots * tile_rows * tile_rows,
        transcendentals=0,
    )


def shards(embed_codes, embed_exps, degrees, adjacency, block_index):
    tile_rows = adjacency.shape[2]
    row_width = embed_codes.shape[2]
    row_count = embed_codes.shape[1]
    capacity = adjacency.shape[1]
    tiles_dev = row_count // tile_rows
    groups = lax.axis_size("grp")
    blks = lax.axis_size("blk")
    part = (tiles_dev, tile_rows, row_width)
    codes = embed_codes.reshape(part)
    source, factors, scales = scale_rows(codes, embed_exps, degrees)

    def across(value, step):
        pairs = [
            (side * blks + at, (1 - side) * blks + (at ^ (2 * step if at & 1 else blks - 2 - 2 * step)))
            for side in range(2)
            for at in range(blks)
        ]
        return lax.ppermute(value, ("side", "blk"), pairs)

    def paired(value, axis, hop):
        return lax.ppermute(value, axis, [(at, at ^ hop) for at in range(lax.axis_size(axis))])

    place = jnp.stack([lax.axis_index("blk"), lax.axis_index("grp")]).astype(jnp.int32)
    early = across(codes, 0)
    middle = [across(source, step) for step in range(1, blks // 2)]
    early_scales = across(scales, 0)
    order, blocks = stage_blocks(block_index[0], place, adjacency[0], blks, groups, tiles_dev)
    early, early_scales, order = lax.optimization_barrier((early, early_scales, order))
    early = (early.astype(jnp.float32) * early_scales[:, :, None]).astype(jnp.bfloat16)
    other = paired(early, "blk", 1)
    far_tiles = (groups // 2 - 1) * tiles_dev

    def held(count, dtype):
        return pltpu.VMEM((count, tile_rows, row_width), dtype)

    total = pl.pallas_call(
        early_kernel,
        out_shape=jax.ShapeDtypeStruct((far_tiles + 1, tile_rows, row_width), jnp.float32),
        in_specs=[SMEM] + [VMEM] * 2,
        out_specs=VMEM,
        compiler_params=LIMIT,
        cost_estimate=cost_of(capacity // 8, tile_rows, row_width),
    )(order, early, blocks)
    *middle, total = lax.optimization_barrier((*middle, total))
    others = [other] + [paired(panel, "blk", 1) for panel in middle]
    total = pl.pallas_call(
        middle_kernel,
        out_shape=jax.ShapeDtypeStruct(total.shape, total.dtype),
        in_specs=[SMEM] + [VMEM] * (len(middle) + 2),
        out_specs=VMEM,
        input_output_aliases={len(middle) + 2: 0},
        scratch_shapes=[held(len(middle) * tiles_dev, jnp.bfloat16)],
        compiler_params=LIMIT,
        cost_estimate=cost_of(capacity // 8, tile_rows, row_width),
    )(order, *middle, blocks, total)
    *others, total = lax.optimization_barrier((*others, total))
    panels = [early] + middle + others
    far, first, _ = pl.pallas_call(
        functools.partial(far_kernel, tiles_dev),
        out_shape=[
            jax.ShapeDtypeStruct((far_tiles, tile_rows, row_width), jnp.bfloat16),
            jax.ShapeDtypeStruct((tiles_dev + 1, tile_rows, row_width), jnp.float32),
            jax.ShapeDtypeStruct(total.shape, total.dtype),
        ],
        in_specs=[SMEM] + [VMEM] * (len(panels) + 2),
        out_specs=[VMEM] * 3,
        input_output_aliases={len(panels) + 2: 2},
        scratch_shapes=[held(len(panels) * tiles_dev, jnp.bfloat16)],
        compiler_params=LIMIT,
        cost_estimate=cost_of(capacity // 8, tile_rows, row_width),
    )(order, *panels, blocks, total)
    far, order = lax.optimization_barrier((far, order))
    first, _ = pl.pallas_call(
        first_kernel,
        out_shape=[
            jax.ShapeDtypeStruct(part, jnp.bfloat16),
            jax.ShapeDtypeStruct(first.shape, first.dtype),
        ],
        in_specs=[SMEM] + [VMEM] * (len(panels) + 2),
        out_specs=[VMEM] * 2,
        input_output_aliases={len(panels) + 2: 1},
        scratch_shapes=[held(len(panels) * tiles_dev, jnp.bfloat16)],
        compiler_params=LIMIT,
        cost_estimate=cost_of(capacity // 4, tile_rows, row_width),
    )(order, *panels, blocks, first)
    first, order = lax.optimization_barrier((first, order))
    def multiplied(stage, count, ready):
        return pl.pallas_call(
            functools.partial(later_kernel, stage),
            out_shape=jax.ShapeDtypeStruct((count, tile_rows, row_width), jnp.float32),
            in_specs=[SMEM] + [VMEM] * (len(panels) + 1),
            out_specs=VMEM,
            scratch_shapes=[
                held(len(panels) * tiles_dev, jnp.bfloat16),
                held(count + 1, jnp.float32),
            ],
            compiler_params=LIMIT,
            cost_estimate=cost_of(capacity // 4, tile_rows, row_width),
        )(ready, *panels, blocks)

    later = multiplied(5, far_tiles, order)

    def turned(value, even_hop, odd_hop):
        hops = (even_hop, odd_hop)
        pairs = [
            (at * blks + blk, (at ^ hops[blk & 1]) * blks + blk)
            for at in range(groups)
            for blk in range(blks)
        ]
        return lax.ppermute(value, ("grp", "blk"), pairs)

    steps = groups // 2 - 1
    even_core = lax.axis_index("blk") % 2 == 0
    pieces = [slice(at * tiles_dev, (at + 1) * tiles_dev) for at in range(steps)]
    handed = [turned(far[pieces[at]], 1, 2 * at + 2).astype(jnp.float32) for at in range(steps)]
    arrived = [turned(first, 1, 2)]
    for at in range(steps):
        value = later[pieces[at]]
        for step, extra in enumerate(handed):
            if step == at == steps - 1:
                value = value + extra
            elif step == at:
                value = value + jnp.where(even_core, extra, 0.0)
            elif at == steps - 1:
                value = value + jnp.where(even_core, 0.0, extra)
        odd_hop = 1 if at == steps - 1 else 2 * at + 4
        value, order = lax.optimization_barrier((value.astype(jnp.bfloat16), order))
        arrived.append(turned(value, 2 * at + 2, odd_hop))
    own = multiplied(6, tiles_dev, order) + arrived[0].astype(jnp.float32)
    own, *sums = lax.optimization_barrier((own, *arrived[1:]))
    out = pl.pallas_call(
        final_kernel,
        out_shape=jax.ShapeDtypeStruct(part, jnp.bfloat16),
        in_specs=[VMEM] * (2 + len(sums)),
        out_specs=HBM,
        scratch_shapes=[
            held(tiles_dev, jnp.bfloat16),
            pltpu.SemaphoreType.DMA((tiles_dev,)),
        ],
        compiler_params=LIMIT,
        cost_estimate=cost_of(0, tile_rows, row_width),
    )(factors, own, *sums)
    return out.reshape(1, row_count, row_width)


def solution(mesh):
    placed = (
        P("side", ("grp", "blk"), None),
        P("side", ("grp", "blk")),
        P("side", ("grp", "blk")),
        P("side", ("grp", "blk"), None, None),
        P("side", None, ("grp", "blk")),
    )
    return jax.shard_map(
        shards,
        mesh=mesh,
        in_specs=placed,
        out_specs=P("side", ("grp", "blk"), None),
        check_vma=False,
    )
```

```python
import functools

import jax
import jax.numpy as jnp
from jax import lax
from jax.experimental import pallas as pl
from jax.experimental.pallas import tpu as pltpu
from jax.sharding import PartitionSpec as P

UNROLL = 8
BATCHES = (4, 4, 4, 8, 8, 8, 8)
STAGES = len(BATCHES)
VMEM = pl.BlockSpec(memory_space=pltpu.VMEM)
SMEM = pl.BlockSpec(memory_space=pltpu.SMEM)
HBM = pl.BlockSpec(memory_space=pltpu.HBM)
LIMIT = pltpu.CompilerParams(vmem_limit_bytes=48 * 1024 * 1024)


def in_hbm(*arrays):
    return [pltpu.with_memory_space_constraint(array, pltpu.HBM) for array in arrays]


def split(value, size):
    if size & (size - 1) == 0:
        return value >> (size.bit_length() - 1), value & (size - 1)
    return value // size, value % size


def scale_kernel(
    exps_hbm, degrees_hbm, codes_hbm, rows, factors, scales, exps_ref, degrees, codes, sems
):
    pairs = [(exps_hbm, exps_ref), (degrees_hbm, degrees), (codes_hbm, codes)]
    fetches = [
        pltpu.make_async_copy(held, wanted, sems.at[at])
        for at, (held, wanted) in enumerate(pairs)
    ]
    for fetch in fetches:
        fetch.start()
    fetches[0].wait()
    fetches[1].wait()
    tiles_dev, tile_rows, row_width = rows.shape
    inverse = lax.rsqrt(degrees[...].astype(jnp.float32))
    for tile in range(tiles_dev):
        lanes = inverse[:, tile * tile_rows : (tile + 1) * tile_rows]
        factors[tile] = jnp.broadcast_to(lanes, (row_width, tile_rows)).T
        scale = jnp.exp2(jnp.full((1, 1), exps_ref[0, tile], jnp.int32).astype(jnp.float32))
        scales[tile : tile + 1, :] = lanes * scale
    fetches[2].wait()
    for tile in range(tiles_dev):
        scale = jnp.exp2(jnp.full((1, 1), exps_ref[0, tile], jnp.int32).astype(jnp.float32))
        scaled = codes[tile].astype(jnp.float32) * scale * factors[tile]
        rows[tile] = scaled.astype(rows.dtype)


def scale_rows(codes, exps, degrees):
    return pl.pallas_call(
        scale_kernel,
        out_shape=[
            jax.ShapeDtypeStruct(codes.shape, jnp.bfloat16),
            jax.ShapeDtypeStruct(codes.shape, jnp.float32),
            jax.ShapeDtypeStruct(codes.shape[:2], jnp.float32),
        ],
        in_specs=[HBM] * 3,
        out_specs=[VMEM] * 3,
        scratch_shapes=[
            pltpu.SMEM(exps.shape, exps.dtype),
            pltpu.VMEM(degrees.shape, degrees.dtype),
            pltpu.VMEM(codes.shape, codes.dtype),
            pltpu.SemaphoreType.DMA((3,)),
        ],
        compiler_params=LIMIT,
        cost_estimate=pl.CostEstimate(
            flops=codes.size, bytes_accessed=4 * codes.size, transcendentals=0
        ),
    )(*in_hbm(exps, degrees, codes))


def count_up(shape, axis):
    return lax.broadcasted_iota(jnp.int32, shape, axis)


def stage_kernel(
    blks, groups, tiles_dev, place_ref, index_hbm, blocks_hbm, order_ref, blocks, index_ref, sems
):
    fetch = pltpu.make_async_copy(index_hbm, index_ref, sems.at[0])
    fetch.start()
    copy = pltpu.make_async_copy(blocks_hbm, blocks, sems.at[1])
    copy.start()
    fetch.wait()
    my_blk = place_ref[0]
    my_grp = place_ref[1]
    capacity = index_ref.shape[1]
    width = order_ref.shape[1]
    source_tiles = blks * tiles_dev
    half = blks // 2
    role = my_blk & 1

    target = index_ref[0:1, :]
    origin = index_ref[1:2, :]
    hop, row = split(origin, tiles_dev)
    chunk, tile = split(target, tiles_dev)
    hop = hop ^ my_blk
    chunk = chunk ^ my_grp
    odd = hop & 1
    rank = jnp.where(odd == role, half - 1 - (hop >> 1), hop >> 1)
    far = (chunk >= 2) & ((chunk & 1) == 1)
    kept = jnp.where(chunk == 1, 1 + role * (groups // 2 - 1), (chunk >> 1) + 1 - role)
    kept = jnp.where(chunk == 0, 0, jnp.where(far, (chunk >> 1) - 1, kept))
    near = jnp.where(kept == 0, 6, jnp.where(kept == 1, 4 - role, 5))
    stage = jnp.where(far, jnp.where(odd == 1, 2, jnp.minimum(rank, 1)), near)
    kept = jnp.where(stage == 5, kept - 2, jnp.where(far, kept, 0))
    stage = jnp.where(origin < source_tiles, stage, STAGES)
    panel = jnp.where(stage == 1, rank - 1, jnp.where(stage == 2, rank, rank + odd * half))
    slot = count_up((1, capacity), 1)

    stages = (count_up((8, capacity), 0) == stage).astype(jnp.float32)
    earlier = count_up((capacity, capacity), 0) < count_up((capacity, capacity), 1)
    before = jnp.dot(
        stages.astype(jnp.bfloat16), earlier.astype(jnp.bfloat16), preferred_element_type=jnp.float32
    )
    position = jnp.sum(stages * before, axis=0, keepdims=True).astype(jnp.int32)
    parts = (slot & 127, slot >> 7, panel * tiles_dev + row, kept * tiles_dev + tile)
    values = sum(
        jnp.where(count_up((8, capacity), 0) == at, part, 0) for at, part in enumerate(parts)
    ).astype(jnp.bfloat16)
    far_tiles = (groups // 2 - 1) * tiles_dev
    tops = [far_tiles] * 3 + [tiles_dev] * 2 + [far_tiles, tiles_dev]
    lanes = count_up((1, width), 1)
    for at, top in enumerate(tops):
        where = jnp.where(stage == at, position, -1)
        chosen = (count_up((width, capacity), 0) == where).astype(jnp.bfloat16)
        listed = lax.dot_general(
            values, chosen, (((1,), (1,)), ((), ())), preferred_element_type=jnp.float32
        ).astype(jnp.int32)
        word = pack(listed[0:1] + (listed[1:2] << 7), listed[2:3], listed[3:4])
        count = jnp.sum((stage == at).astype(jnp.int32), axis=1, keepdims=True)
        word = jnp.where(lanes < count, word, pack(0, 0, top))
        batches = split(count + (BATCHES[at] - 1), BATCHES[at])[0]
        order_ref[at : at + 1, :] = jnp.where(lanes == width - UNROLL, batches, word)
    copy.wait()


def pack(slot, row, target):
    return (slot << 16) | (row << 8) | target


def unpack(word):
    return word >> 16, (word >> 8) & 255, word & 255


def stage_blocks(index, place, blocks, blks, groups, tiles_dev):
    capacity = blocks.shape[0]
    assert blks * tiles_dev < 256 and groups * tiles_dev < 256 and capacity < 2**15
    width = -(-(capacity + 2 * UNROLL) // 128) * 128
    return pl.pallas_call(
        functools.partial(stage_kernel, blks, groups, tiles_dev),
        out_shape=[
            jax.ShapeDtypeStruct((8, width), jnp.int32),
            jax.ShapeDtypeStruct(blocks.shape, blocks.dtype),
        ],
        in_specs=[SMEM, HBM, HBM],
        out_specs=[VMEM, VMEM],
        scratch_shapes=[
            pltpu.VMEM(index.shape, index.dtype),
            pltpu.SemaphoreType.DMA((2,)),
        ],
        compiler_params=LIMIT,
        cost_estimate=pl.CostEstimate(flops=0, bytes_accessed=0, transcendentals=0),
    )(place, *in_hbm(index, blocks))


def add_products(stage, order_ref, blocks, source, total):
    @pl.loop(0, order_ref[stage, order_ref.shape[1] - UNROLL])
    def _(batch):
        made = []
        for part in range(BATCHES[stage]):
            slot, row, target = unpack(order_ref[stage, batch * BATCHES[stage] + part])
            product = jnp.dot(blocks[slot], source[row], preferred_element_type=jnp.float32)
            made.append((target, product))
        for target, product in made:
            total[target] += product


def gather_panels(panels, source):
    for at, panel in enumerate(panels):
        rows = panel.shape[0]
        source[at * rows : (at + 1) * rows] = panel[...]


def early_kernel(order_ref, panel, blocks, total):
    total[...] = jnp.zeros_like(total)
    add_products(0, order_ref, blocks, panel, total)


def middle_kernel(order_ref, *refs):
    *panels, blocks, _, total, source = refs
    gather_panels(panels, source)
    add_products(1, order_ref, blocks, source, total)


def far_kernel(tiles_dev, order_ref, *refs):
    *panels, blocks, _, far, first, total, source = refs
    others = len(panels) // 2 * tiles_dev
    gather_panels(panels, source)
    first[...] = jnp.zeros_like(first)
    add_products(2, order_ref, blocks, source.at[others:], total)
    add_products(3, order_ref, blocks, source, first)
    far[...] = total[: far.shape[0]].astype(far.dtype)


def first_kernel(order_ref, *refs):
    *panels, blocks, _, first, total, source = refs
    gather_panels(panels, source)
    add_products(4, order_ref, blocks, source, total)
    first[...] = total[: first.shape[0]].astype(first.dtype)


def later_kernel(stage, order_ref, *refs):
    *panels, blocks, later, source, total = refs
    gather_panels(panels, source)
    total[...] = jnp.zeros_like(total)
    add_products(stage, order_ref, blocks, source, total)
    later[...] = total[: later.shape[0]]


def final_kernel(factors, own, *refs):
    *arrived, out_hbm, out, sems = refs
    copies = []
    for tile in range(out.shape[0]):
        value = own[tile]
        for piece in arrived:
            value = value + piece[tile].astype(jnp.float32)
        out[tile] = (value * factors[tile]).astype(out.dtype)
        copies.append(pltpu.make_async_copy(out.at[tile], out_hbm.at[tile], sems.at[tile]))
        copies[-1].start()
    for copy in copies:
        copy.wait()


def cost_of(slots, tile_rows, row_width):
    return pl.CostEstimate(
        flops=2 * slots * tile_rows * tile_rows * row_width,
        bytes_accessed=2 * slots * tile_rows * tile_rows,
        transcendentals=0,
    )


def shards(embed_codes, embed_exps, degrees, adjacency, block_index):
    tile_rows = adjacency.shape[2]
    row_width = embed_codes.shape[2]
    row_count = embed_codes.shape[1]
    capacity = adjacency.shape[1]
    tiles_dev = row_count // tile_rows
    groups = lax.axis_size("grp")
    blks = lax.axis_size("blk")
    part = (tiles_dev, tile_rows, row_width)
    codes = embed_codes.reshape(part)
    source, factors, scales = scale_rows(codes, embed_exps, degrees)

    def across(value, step):
        pairs = [
            (side * blks + at, (1 - side) * blks + (at ^ (2 * step if at & 1 else blks - 2 - 2 * step)))
            for side in range(2)
            for at in range(blks)
        ]
        return lax.ppermute(value, ("side", "blk"), pairs)

    def paired(value, axis, hop):
        return lax.ppermute(value, axis, [(at, at ^ hop) for at in range(lax.axis_size(axis))])

    place = jnp.stack([lax.axis_index("blk"), lax.axis_index("grp")]).astype(jnp.int32)
    early = across(codes, 0)
    middle = [across(source, step) for step in range(1, blks // 2)]
    early_scales = across(scales, 0)
    order, blocks = stage_blocks(block_index[0], place, adjacency[0], blks, groups, tiles_dev)
    early, early_scales, order = lax.optimization_barrier((early, early_scales, order))
    early = (early.astype(jnp.float32) * early_scales[:, :, None]).astype(jnp.bfloat16)
    other = paired(early, "blk", 1)
    far_tiles = (groups // 2 - 1) * tiles_dev

    def held(count, dtype):
        return pltpu.VMEM((count, tile_rows, row_width), dtype)

    total = pl.pallas_call(
        early_kernel,
        out_shape=jax.ShapeDtypeStruct((far_tiles + 1, tile_rows, row_width), jnp.float32),
        in_specs=[SMEM] + [VMEM] * 2,
        out_specs=VMEM,
        compiler_params=LIMIT,
        cost_estimate=cost_of(capacity // 8, tile_rows, row_width),
    )(order, early, blocks)
    *middle, total = lax.optimization_barrier((*middle, total))
    others = [other] + [paired(panel, "blk", 1) for panel in middle]
    total = pl.pallas_call(
        middle_kernel,
        out_shape=jax.ShapeDtypeStruct(total.shape, total.dtype),
        in_specs=[SMEM] + [VMEM] * (len(middle) + 2),
        out_specs=VMEM,
        input_output_aliases={len(middle) + 2: 0},
        scratch_shapes=[held(len(middle) * tiles_dev, jnp.bfloat16)],
        compiler_params=LIMIT,
        cost_estimate=cost_of(capacity // 8, tile_rows, row_width),
    )(order, *middle, blocks, total)
    *others, total = lax.optimization_barrier((*others, total))
    panels = [early] + middle + others
    far, first, _ = pl.pallas_call(
        functools.partial(far_kernel, tiles_dev),
        out_shape=[
            jax.ShapeDtypeStruct((far_tiles, tile_rows, row_width), jnp.bfloat16),
            jax.ShapeDtypeStruct((tiles_dev + 1, tile_rows, row_width), jnp.float32),
            jax.ShapeDtypeStruct(total.shape, total.dtype),
        ],
        in_specs=[SMEM] + [VMEM] * (len(panels) + 2),
        out_specs=[VMEM] * 3,
        input_output_aliases={len(panels) + 2: 2},
        scratch_shapes=[held(len(panels) * tiles_dev, jnp.bfloat16)],
        compiler_params=LIMIT,
        cost_estimate=cost_of(capacity // 8, tile_rows, row_width),
    )(order, *panels, blocks, total)
    far, order = lax.optimization_barrier((far, order))
    first, _ = pl.pallas_call(
        first_kernel,
        out_shape=[
            jax.ShapeDtypeStruct(part, jnp.bfloat16),
            jax.ShapeDtypeStruct(first.shape, first.dtype),
        ],
        in_specs=[SMEM] + [VMEM] * (len(panels) + 2),
        out_specs=[VMEM] * 2,
        input_output_aliases={len(panels) + 2: 1},
        scratch_shapes=[held(len(panels) * tiles_dev, jnp.bfloat16)],
        compiler_params=LIMIT,
        cost_estimate=cost_of(capacity // 4, tile_rows, row_width),
    )(order, *panels, blocks, first)
    first, order = lax.optimization_barrier((first, order))
    def multiplied(stage, count, ready):
        return pl.pallas_call(
            functools.partial(later_kernel, stage),
            out_shape=jax.ShapeDtypeStruct((count, tile_rows, row_width), jnp.float32),
            in_specs=[SMEM] + [VMEM] * (len(panels) + 1),
            out_specs=VMEM,
            scratch_shapes=[
                held(len(panels) * tiles_dev, jnp.bfloat16),
                held(count + 1, jnp.float32),
            ],
            compiler_params=LIMIT,
            cost_estimate=cost_of(capacity // 4, tile_rows, row_width),
        )(ready, *panels, blocks)

    later = multiplied(5, far_tiles, order)
    later, first = lax.optimization_barrier((later, first))

    def turned(value, even_hop, odd_hop):
        hops = (even_hop, odd_hop)
        pairs = [
            (at * blks + blk, (at ^ hops[blk & 1]) * blks + blk)
            for at in range(groups)
            for blk in range(blks)
        ]
        return lax.ppermute(value, ("grp", "blk"), pairs)

    steps = groups // 2 - 1
    even_core = lax.axis_index("blk") % 2 == 0
    pieces = [slice(at * tiles_dev, (at + 1) * tiles_dev) for at in range(steps)]
    handed = [turned(far[pieces[at]], 1, 2 * at + 2).astype(jnp.float32) for at in range(steps)]
    arrived = [turned(first, 1, 2)]
    for at in range(steps):
        value = later[pieces[at]]
        for step, extra in enumerate(handed):
            if step == at == steps - 1:
                value = value + extra
            elif step == at:
                value = value + jnp.where(even_core, extra, 0.0)
            elif at == steps - 1:
                value = value + jnp.where(even_core, 0.0, extra)
        odd_hop = 1 if at == steps - 1 else 2 * at + 4
        value, order = lax.optimization_barrier((value.astype(jnp.bfloat16), order))
        arrived.append(turned(value, 2 * at + 2, odd_hop))
    own = multiplied(6, tiles_dev, order) + arrived[0].astype(jnp.float32)
    own, *sums = lax.optimization_barrier((own, *arrived[1:]))
    out = pl.pallas_call(
        final_kernel,
        out_shape=jax.ShapeDtypeStruct(part, jnp.bfloat16),
        in_specs=[VMEM] * (2 + len(sums)),
        out_specs=HBM,
        scratch_shapes=[
            held(tiles_dev, jnp.bfloat16),
            pltpu.SemaphoreType.DMA((tiles_dev,)),
        ],
        compiler_params=LIMIT,
        cost_estimate=cost_of(0, tile_rows, row_width),
    )(factors, own, *sums)
    return out.reshape(1, row_count, row_width)


def solution(mesh):
    placed = (
        P("side", ("grp", "blk"), None),
        P("side", ("grp", "blk")),
        P("side", ("grp", "blk")),
        P("side", ("grp", "blk"), None, None),
        P("side", None, ("grp", "blk")),
    )
    return jax.shard_map(
        shards,
        mesh=mesh,
        in_specs=placed,
        out_specs=P("side", ("grp", "blk"), None),
        check_vma=False,
    )
```

```python
import functools

import jax
import jax.numpy as jnp
from jax import lax
from jax.experimental import pallas as pl
from jax.experimental.pallas import tpu as pltpu
from jax.sharding import PartitionSpec as P

UNROLL = 8
BATCHES = (4, 4, 4, 8, 8, 8)
STAGES = len(BATCHES)
VMEM = pl.BlockSpec(memory_space=pltpu.VMEM)
SMEM = pl.BlockSpec(memory_space=pltpu.SMEM)
HBM = pl.BlockSpec(memory_space=pltpu.HBM)
LIMIT = pltpu.CompilerParams(vmem_limit_bytes=48 * 1024 * 1024)


def in_hbm(*arrays):
    return [pltpu.with_memory_space_constraint(array, pltpu.HBM) for array in arrays]


def split(value, size):
    if size & (size - 1) == 0:
        return value >> (size.bit_length() - 1), value & (size - 1)
    return value // size, value % size


def scale_kernel(
    exps_hbm, degrees_hbm, codes_hbm, rows, factors, scales, exps_ref, degrees, codes, sems
):
    pairs = [(exps_hbm, exps_ref), (degrees_hbm, degrees), (codes_hbm, codes)]
    fetches = [
        pltpu.make_async_copy(held, wanted, sems.at[at])
        for at, (held, wanted) in enumerate(pairs)
    ]
    for fetch in fetches:
        fetch.start()
    fetches[0].wait()
    fetches[1].wait()
    tiles_dev, tile_rows, row_width = rows.shape
    inverse = lax.rsqrt(degrees[...].astype(jnp.float32))
    for tile in range(tiles_dev):
        lanes = inverse[:, tile * tile_rows : (tile + 1) * tile_rows]
        factors[tile] = jnp.broadcast_to(lanes, (row_width, tile_rows)).T
        scale = jnp.exp2(jnp.full((1, 1), exps_ref[0, tile], jnp.int32).astype(jnp.float32))
        scales[tile : tile + 1, :] = lanes * scale
    fetches[2].wait()
    for tile in range(tiles_dev):
        scale = jnp.exp2(jnp.full((1, 1), exps_ref[0, tile], jnp.int32).astype(jnp.float32))
        scaled = codes[tile].astype(jnp.float32) * scale * factors[tile]
        rows[tile] = scaled.astype(rows.dtype)


def scale_rows(codes, exps, degrees):
    return pl.pallas_call(
        scale_kernel,
        out_shape=[
            jax.ShapeDtypeStruct(codes.shape, jnp.bfloat16),
            jax.ShapeDtypeStruct(codes.shape, jnp.float32),
            jax.ShapeDtypeStruct(codes.shape[:2], jnp.float32),
        ],
        in_specs=[HBM] * 3,
        out_specs=[VMEM] * 3,
        scratch_shapes=[
            pltpu.SMEM(exps.shape, exps.dtype),
            pltpu.VMEM(degrees.shape, degrees.dtype),
            pltpu.VMEM(codes.shape, codes.dtype),
            pltpu.SemaphoreType.DMA((3,)),
        ],
        compiler_params=LIMIT,
        cost_estimate=pl.CostEstimate(
            flops=codes.size, bytes_accessed=4 * codes.size, transcendentals=0
        ),
    )(*in_hbm(exps, degrees, codes))


def count_up(shape, axis):
    return lax.broadcasted_iota(jnp.int32, shape, axis)


def stage_kernel(
    blks, groups, tiles_dev, place_ref, index_hbm, blocks_hbm, order_ref, blocks, index_ref, sems
):
    fetch = pltpu.make_async_copy(index_hbm, index_ref, sems.at[0])
    fetch.start()
    copy = pltpu.make_async_copy(blocks_hbm, blocks, sems.at[1])
    copy.start()
    fetch.wait()
    my_blk = place_ref[0]
    my_grp = place_ref[1]
    capacity = index_ref.shape[1]
    width = order_ref.shape[1]
    source_tiles = blks * tiles_dev
    half = blks // 2
    role = my_blk & 1

    target = index_ref[0:1, :]
    origin = index_ref[1:2, :]
    hop, row = split(origin, tiles_dev)
    chunk, tile = split(target, tiles_dev)
    hop = hop ^ my_blk
    chunk = chunk ^ my_grp
    odd = hop & 1
    rank = jnp.where(odd == role, hop >> 1, half - 1 - (hop >> 1))
    far = (chunk >= 2) & ((chunk & 1) == 1)
    kept = jnp.where(chunk == 1, 1 + role * (groups // 2 - 1), (chunk >> 1) + 1 - role)
    kept = jnp.where(chunk == 0, 0, jnp.where(far, (chunk >> 1) - 1, kept))
    stage = jnp.where(far, jnp.where(odd == 1, 2, jnp.minimum(rank, 1)), 5)
    stage = jnp.where(far | (kept != 1), stage, 4 - role)
    kept = jnp.where(far | (kept == 0), kept, kept - 1)
    stage = jnp.where(origin < source_tiles, stage, STAGES)
    panel = jnp.where(stage == 1, rank - 1, jnp.where(stage == 2, rank, rank + odd * half))
    slot = count_up((1, capacity), 1)

    stages = (count_up((8, capacity), 0) == stage).astype(jnp.float32)
    earlier = count_up((capacity, capacity), 0) < count_up((capacity, capacity), 1)
    before = jnp.dot(
        stages.astype(jnp.bfloat16), earlier.astype(jnp.bfloat16), preferred_element_type=jnp.float32
    )
    position = jnp.sum(stages * before, axis=0, keepdims=True).astype(jnp.int32)
    parts = (slot & 127, slot >> 7, panel * tiles_dev + row, kept * tiles_dev + tile)
    values = sum(
        jnp.where(count_up((8, capacity), 0) == at, part, 0) for at, part in enumerate(parts)
    ).astype(jnp.bfloat16)
    far_tiles = (groups // 2 - 1) * tiles_dev
    tops = [far_tiles] * 3 + [tiles_dev] * 2 + [groups // 2 * tiles_dev]
    lanes = count_up((1, width), 1)
    for at, top in enumerate(tops):
        where = jnp.where(stage == at, position, -1)
        chosen = (count_up((width, capacity), 0) == where).astype(jnp.bfloat16)
        listed = lax.dot_general(
            values, chosen, (((1,), (1,)), ((), ())), preferred_element_type=jnp.float32
        ).astype(jnp.int32)
        word = pack(listed[0:1] + (listed[1:2] << 7), listed[2:3], listed[3:4])
        count = jnp.sum((stage == at).astype(jnp.int32), axis=1, keepdims=True)
        word = jnp.where(lanes < count, word, pack(0, 0, top))
        batches = split(count + (BATCHES[at] - 1), BATCHES[at])[0]
        order_ref[at : at + 1, :] = jnp.where(lanes == width - UNROLL, batches, word)
    copy.wait()


def pack(slot, row, target):
    return (slot << 16) | (row << 8) | target


def unpack(word):
    return word >> 16, (word >> 8) & 255, word & 255


def stage_blocks(index, place, blocks, blks, groups, tiles_dev):
    capacity = blocks.shape[0]
    assert blks * tiles_dev < 256 and groups * tiles_dev < 256 and capacity < 2**15
    width = -(-(capacity + 2 * UNROLL) // 128) * 128
    return pl.pallas_call(
        functools.partial(stage_kernel, blks, groups, tiles_dev),
        out_shape=[
            jax.ShapeDtypeStruct((8, width), jnp.int32),
            jax.ShapeDtypeStruct(blocks.shape, blocks.dtype),
        ],
        in_specs=[SMEM, HBM, HBM],
        out_specs=[VMEM, VMEM],
        scratch_shapes=[
            pltpu.VMEM(index.shape, index.dtype),
            pltpu.SemaphoreType.DMA((2,)),
        ],
        compiler_params=LIMIT,
        cost_estimate=pl.CostEstimate(flops=0, bytes_accessed=0, transcendentals=0),
    )(place, *in_hbm(index, blocks))


def add_products(stage, order_ref, blocks, source, total):
    @pl.loop(0, order_ref[stage, order_ref.shape[1] - UNROLL])
    def _(batch):
        made = []
        for part in range(BATCHES[stage]):
            slot, row, target = unpack(order_ref[stage, batch * BATCHES[stage] + part])
            product = jnp.dot(blocks[slot], source[row], preferred_element_type=jnp.float32)
            made.append((target, product))
        for target, product in made:
            total[target] += product


def gather_panels(panels, source):
    for at, panel in enumerate(panels):
        rows = panel.shape[0]
        source[at * rows : (at + 1) * rows] = panel[...]


def early_kernel(order_ref, panel, blocks, total):
    total[...] = jnp.zeros_like(total)
    add_products(0, order_ref, blocks, panel, total)


def middle_kernel(order_ref, *refs):
    *panels, blocks, _, total, source = refs
    gather_panels(panels, source)
    add_products(1, order_ref, blocks, source, total)


def far_kernel(tiles_dev, order_ref, *refs):
    *panels, blocks, _, far, first, total, source = refs
    others = len(panels) // 2 * tiles_dev
    gather_panels(panels, source)
    first[...] = jnp.zeros_like(first)
    add_products(2, order_ref, blocks, source.at[others:], total)
    add_products(3, order_ref, blocks, source, first)
    far[...] = total[: far.shape[0]].astype(far.dtype)


def first_kernel(order_ref, *refs):
    *panels, blocks, _, first, total, source = refs
    gather_panels(panels, source)
    add_products(4, order_ref, blocks, source, total)
    first[...] = total[: first.shape[0]].astype(first.dtype)


def rest_kernel(order_ref, *refs):
    *panels, blocks, own, later, source, total = refs
    gather_panels(panels, source)
    total[...] = jnp.zeros_like(total)
    add_products(5, order_ref, blocks, source, total)
    tiles_dev = own.shape[0]
    own[...] = total[:tiles_dev]
    later[...] = total[tiles_dev : tiles_dev + later.shape[0]]


def final_kernel(factors, own, *refs):
    *arrived, out_hbm, out, sems = refs
    copies = []
    for tile in range(out.shape[0]):
        value = own[tile]
        for piece in arrived:
            value = value + piece[tile].astype(jnp.float32)
        out[tile] = (value * factors[tile]).astype(out.dtype)
        copies.append(pltpu.make_async_copy(out.at[tile], out_hbm.at[tile], sems.at[tile]))
        copies[-1].start()
    for copy in copies:
        copy.wait()


def cost_of(slots, tile_rows, row_width):
    return pl.CostEstimate(
        flops=2 * slots * tile_rows * tile_rows * row_width,
        bytes_accessed=2 * slots * tile_rows * tile_rows,
        transcendentals=0,
    )


def shards(embed_codes, embed_exps, degrees, adjacency, block_index):
    tile_rows = adjacency.shape[2]
    row_width = embed_codes.shape[2]
    row_count = embed_codes.shape[1]
    capacity = adjacency.shape[1]
    tiles_dev = row_count // tile_rows
    groups = lax.axis_size("grp")
    blks = lax.axis_size("blk")
    part = (tiles_dev, tile_rows, row_width)
    codes = embed_codes.reshape(part)
    source, factors, scales = scale_rows(codes, embed_exps, degrees)

    def across(value, step):
        pairs = [
            (side * blks + at, (1 - side) * blks + (at ^ (blks - 2 - 2 * step if at & 1 else 2 * step)))
            for side in range(2)
            for at in range(blks)
        ]
        return lax.ppermute(value, ("side", "blk"), pairs)

    def paired(value, axis, hop):
        return lax.ppermute(value, axis, [(at, at ^ hop) for at in range(lax.axis_size(axis))])

    place = jnp.stack([lax.axis_index("blk"), lax.axis_index("grp")]).astype(jnp.int32)
    early = across(codes, 0)
    middle = [across(source, step) for step in range(1, blks // 2)]
    early_scales = across(scales, 0)
    order, blocks = stage_blocks(block_index[0], place, adjacency[0], blks, groups, tiles_dev)
    early, early_scales, order = lax.optimization_barrier((early, early_scales, order))
    early = (early.astype(jnp.float32) * early_scales[:, :, None]).astype(jnp.bfloat16)
    other = paired(early, "blk", 1)
    far_tiles = (groups // 2 - 1) * tiles_dev

    def held(count, dtype):
        return pltpu.VMEM((count, tile_rows, row_width), dtype)

    total = pl.pallas_call(
        early_kernel,
        out_shape=jax.ShapeDtypeStruct((far_tiles + 1, tile_rows, row_width), jnp.float32),
        in_specs=[SMEM] + [VMEM] * 2,
        out_specs=VMEM,
        compiler_params=LIMIT,
        cost_estimate=cost_of(capacity // 8, tile_rows, row_width),
    )(order, early, blocks)
    *middle, total = lax.optimization_barrier((*middle, total))
    others = [other] + [paired(panel, "blk", 1) for panel in middle]
    total = pl.pallas_call(
        middle_kernel,
        out_shape=jax.ShapeDtypeStruct(total.shape, total.dtype),
        in_specs=[SMEM] + [VMEM] * (len(middle) + 2),
        out_specs=VMEM,
        input_output_aliases={len(middle) + 2: 0},
        scratch_shapes=[held(len(middle) * tiles_dev, jnp.bfloat16)],
        compiler_params=LIMIT,
        cost_estimate=cost_of(capacity // 8, tile_rows, row_width),
    )(order, *middle, blocks, total)
    *others, total = lax.optimization_barrier((*others, total))
    panels = [early] + middle + others
    far, first, _ = pl.pallas_call(
        functools.partial(far_kernel, tiles_dev),
        out_shape=[
            jax.ShapeDtypeStruct((far_tiles, tile_rows, row_width), jnp.bfloat16),
            jax.ShapeDtypeStruct((tiles_dev + 1, tile_rows, row_width), jnp.float32),
            jax.ShapeDtypeStruct(total.shape, total.dtype),
        ],
        in_specs=[SMEM] + [VMEM] * (len(panels) + 2),
        out_specs=[VMEM] * 3,
        input_output_aliases={len(panels) + 2: 2},
        scratch_shapes=[held(len(panels) * tiles_dev, jnp.bfloat16)],
        compiler_params=LIMIT,
        cost_estimate=cost_of(capacity // 8, tile_rows, row_width),
    )(order, *panels, blocks, total)
    far, order = lax.optimization_barrier((far, order))
    first, _ = pl.pallas_call(
        first_kernel,
        out_shape=[
            jax.ShapeDtypeStruct(part, jnp.bfloat16),
            jax.ShapeDtypeStruct(first.shape, first.dtype),
        ],
        in_specs=[SMEM] + [VMEM] * (len(panels) + 2),
        out_specs=[VMEM] * 2,
        input_output_aliases={len(panels) + 2: 1},
        scratch_shapes=[held(len(panels) * tiles_dev, jnp.bfloat16)],
        compiler_params=LIMIT,
        cost_estimate=cost_of(capacity // 4, tile_rows, row_width),
    )(order, *panels, blocks, first)
    first, order = lax.optimization_barrier((first, order))
    own, later = pl.pallas_call(
        rest_kernel,
        out_shape=[
            jax.ShapeDtypeStruct(part, jnp.float32),
            jax.ShapeDtypeStruct((far_tiles, tile_rows, row_width), jnp.float32),
        ],
        in_specs=[SMEM] + [VMEM] * (len(panels) + 1),
        out_specs=[VMEM] * 2,
        scratch_shapes=[
            held(len(panels) * tiles_dev, jnp.bfloat16),
            held(groups // 2 * tiles_dev + 1, jnp.float32),
        ],
        compiler_params=LIMIT,
        cost_estimate=cost_of(capacity // 2, tile_rows, row_width),
    )(order, *panels, blocks)

    def turned(value, even_hop, odd_hop):
        hops = (even_hop, odd_hop)
        pairs = [
            (at * blks + blk, (at ^ hops[blk & 1]) * blks + blk)
            for at in range(groups)
            for blk in range(blks)
        ]
        return lax.ppermute(value, ("grp", "blk"), pairs)

    steps = groups // 2 - 1
    even_core = lax.axis_index("blk") % 2 == 0
    pieces = [slice(at * tiles_dev, (at + 1) * tiles_dev) for at in range(steps)]
    handed = [turned(far[pieces[at]], 1, 2 * at + 2).astype(jnp.float32) for at in range(steps)]
    arrived = [turned(first, 1, 2)]
    for at in range(steps):
        value = later[pieces[at]]
        for step, extra in enumerate(handed):
            if step == at == steps - 1:
                value = value + extra
            elif step == at:
                value = value + jnp.where(even_core, extra, 0.0)
            elif at == steps - 1:
                value = value + jnp.where(even_core, 0.0, extra)
        odd_hop = 1 if at == steps - 1 else 2 * at + 4
        arrived.append(turned(value.astype(jnp.bfloat16), 2 * at + 2, odd_hop))
    own = own + arrived[0].astype(jnp.float32)
    own, *sums = lax.optimization_barrier((own, *arrived[1:]))
    out = pl.pallas_call(
        final_kernel,
        out_shape=jax.ShapeDtypeStruct(part, jnp.bfloat16),
        in_specs=[VMEM] * (2 + len(sums)),
        out_specs=HBM,
        scratch_shapes=[
            held(tiles_dev, jnp.bfloat16),
            pltpu.SemaphoreType.DMA((tiles_dev,)),
        ],
        compiler_params=LIMIT,
        cost_estimate=cost_of(0, tile_rows, row_width),
    )(factors, own, *sums)
    return out.reshape(1, row_count, row_width)


def solution(mesh):
    placed = (
        P("side", ("grp", "blk"), None),
        P("side", ("grp", "blk")),
        P("side", ("grp", "blk")),
        P("side", ("grp", "blk"), None, None),
        P("side", None, ("grp", "blk")),
    )
    return jax.shard_map(
        shards,
        mesh=mesh,
        in_specs=placed,
        out_specs=P("side", ("grp", "blk"), None),
        check_vma=False,
    )
```

```python
import functools

import jax
import jax.numpy as jnp
from jax import lax
from jax.experimental import pallas as pl
from jax.experimental.pallas import tpu as pltpu
from jax.sharding import PartitionSpec as P

UNROLL = 8
BATCHES = (4, 4, 4, 8, 8, 8)
STAGES = len(BATCHES)
VMEM = pl.BlockSpec(memory_space=pltpu.VMEM)
SMEM = pl.BlockSpec(memory_space=pltpu.SMEM)
HBM = pl.BlockSpec(memory_space=pltpu.HBM)
LIMIT = pltpu.CompilerParams(vmem_limit_bytes=48 * 1024 * 1024)


def in_hbm(*arrays):
    return [pltpu.with_memory_space_constraint(array, pltpu.HBM) for array in arrays]


def split(value, size):
    if size & (size - 1) == 0:
        return value >> (size.bit_length() - 1), value & (size - 1)
    return value // size, value % size


def scale_kernel(
    exps_hbm, degrees_hbm, codes_hbm, rows, factors, scales, exps_ref, degrees, codes, sems
):
    pairs = [(exps_hbm, exps_ref), (degrees_hbm, degrees), (codes_hbm, codes)]
    fetches = [
        pltpu.make_async_copy(held, wanted, sems.at[at])
        for at, (held, wanted) in enumerate(pairs)
    ]
    for fetch in fetches:
        fetch.start()
    fetches[0].wait()
    fetches[1].wait()
    tiles_dev, tile_rows, row_width = rows.shape
    inverse = lax.rsqrt(degrees[...].astype(jnp.float32))
    for tile in range(tiles_dev):
        lanes = inverse[:, tile * tile_rows : (tile + 1) * tile_rows]
        factors[tile] = jnp.broadcast_to(lanes, (row_width, tile_rows)).T
        scale = jnp.exp2(jnp.full((1, 1), exps_ref[0, tile], jnp.int32).astype(jnp.float32))
        scales[tile : tile + 1, :] = lanes * scale
    fetches[2].wait()
    for tile in range(tiles_dev):
        scale = jnp.exp2(jnp.full((1, 1), exps_ref[0, tile], jnp.int32).astype(jnp.float32))
        scaled = codes[tile].astype(jnp.float32) * scale * factors[tile]
        rows[tile] = scaled.astype(rows.dtype)


def scale_rows(codes, exps, degrees):
    return pl.pallas_call(
        scale_kernel,
        out_shape=[
            jax.ShapeDtypeStruct(codes.shape, jnp.bfloat16),
            jax.ShapeDtypeStruct(codes.shape, jnp.float32),
            jax.ShapeDtypeStruct(codes.shape[:2], jnp.float32),
        ],
        in_specs=[HBM] * 3,
        out_specs=[VMEM] * 3,
        scratch_shapes=[
            pltpu.SMEM(exps.shape, exps.dtype),
            pltpu.VMEM(degrees.shape, degrees.dtype),
            pltpu.VMEM(codes.shape, codes.dtype),
            pltpu.SemaphoreType.DMA((3,)),
        ],
        compiler_params=LIMIT,
        cost_estimate=pl.CostEstimate(
            flops=codes.size, bytes_accessed=4 * codes.size, transcendentals=0
        ),
    )(*in_hbm(exps, degrees, codes))


def count_up(shape, axis):
    return lax.broadcasted_iota(jnp.int32, shape, axis)


def stage_kernel(
    blks, groups, tiles_dev, place_ref, index_hbm, blocks_hbm, order_ref, blocks, index_ref, sems
):
    fetch = pltpu.make_async_copy(index_hbm, index_ref, sems.at[0])
    fetch.start()
    copy = pltpu.make_async_copy(blocks_hbm, blocks, sems.at[1])
    copy.start()
    fetch.wait()
    my_blk = place_ref[0]
    my_grp = place_ref[1]
    capacity = index_ref.shape[1]
    width = order_ref.shape[1]
    source_tiles = blks * tiles_dev
    half = blks // 2
    role = my_blk & 1

    target = index_ref[0:1, :]
    origin = index_ref[1:2, :]
    hop, row = split(origin, tiles_dev)
    chunk, tile = split(target, tiles_dev)
    hop = hop ^ my_blk
    chunk = chunk ^ my_grp
    odd = hop & 1
    rank = jnp.where(odd == role, half - 1 - (hop >> 1), hop >> 1)
    far = (chunk >= 2) & ((chunk & 1) == 1)
    kept = jnp.where(chunk == 1, 1 + role * (groups // 2 - 1), (chunk >> 1) + 1 - role)
    kept = jnp.where(chunk == 0, 0, jnp.where(far, (chunk >> 1) - 1, kept))
    stage = jnp.where(far, jnp.where(odd == 1, 2, jnp.minimum(rank, 1)), 5)
    stage = jnp.where(far | (kept != 1), stage, 4 - role)
    kept = jnp.where(far | (kept == 0), kept, kept - 1)
    stage = jnp.where(origin < source_tiles, stage, STAGES)
    panel = jnp.where(stage == 1, rank - 1, jnp.where(stage == 2, rank, rank + odd * half))
    slot = count_up((1, capacity), 1)

    stages = (count_up((8, capacity), 0) == stage).astype(jnp.float32)
    earlier = count_up((capacity, capacity), 0) < count_up((capacity, capacity), 1)
    before = jnp.dot(
        stages.astype(jnp.bfloat16), earlier.astype(jnp.bfloat16), preferred_element_type=jnp.float32
    )
    position = jnp.sum(stages * before, axis=0, keepdims=True).astype(jnp.int32)
    parts = (slot & 127, slot >> 7, panel * tiles_dev + row, kept * tiles_dev + tile)
    values = sum(
        jnp.where(count_up((8, capacity), 0) == at, part, 0) for at, part in enumerate(parts)
    ).astype(jnp.bfloat16)
    far_tiles = (groups // 2 - 1) * tiles_dev
    tops = [far_tiles] * 3 + [tiles_dev] * 2 + [groups // 2 * tiles_dev]
    lanes = count_up((1, width), 1)
    for at, top in enumerate(tops):
        where = jnp.where(stage == at, position, -1)
        chosen = (count_up((width, capacity), 0) == where).astype(jnp.bfloat16)
        listed = lax.dot_general(
            values, chosen, (((1,), (1,)), ((), ())), preferred_element_type=jnp.float32
        ).astype(jnp.int32)
        word = pack(listed[0:1] + (listed[1:2] << 7), listed[2:3], listed[3:4])
        count = jnp.sum((stage == at).astype(jnp.int32), axis=1, keepdims=True)
        word = jnp.where(lanes < count, word, pack(0, 0, top))
        batches = split(count + (BATCHES[at] - 1), BATCHES[at])[0]
        order_ref[at : at + 1, :] = jnp.where(lanes == width - UNROLL, batches, word)
    copy.wait()


def pack(slot, row, target):
    return (slot << 16) | (row << 8) | target


def unpack(word):
    return word >> 16, (word >> 8) & 255, word & 255


def stage_blocks(index, place, blocks, blks, groups, tiles_dev):
    capacity = blocks.shape[0]
    assert blks * tiles_dev < 256 and groups * tiles_dev < 256 and capacity < 2**15
    width = -(-(capacity + 2 * UNROLL) // 128) * 128
    return pl.pallas_call(
        functools.partial(stage_kernel, blks, groups, tiles_dev),
        out_shape=[
            jax.ShapeDtypeStruct((8, width), jnp.int32),
            jax.ShapeDtypeStruct(blocks.shape, blocks.dtype),
        ],
        in_specs=[SMEM, HBM, HBM],
        out_specs=[VMEM, VMEM],
        scratch_shapes=[
            pltpu.VMEM(index.shape, index.dtype),
            pltpu.SemaphoreType.DMA((2,)),
        ],
        compiler_params=LIMIT,
        cost_estimate=pl.CostEstimate(flops=0, bytes_accessed=0, transcendentals=0),
    )(place, *in_hbm(index, blocks))


def batches_of(stage, order_ref):
    return order_ref[stage, order_ref.shape[1] - UNROLL]


def add_products(stage, order_ref, blocks, source, total):
    @pl.loop(0, batches_of(stage, order_ref))
    def _(batch):
        made = []
        for part in range(BATCHES[stage]):
            slot, row, target = unpack(order_ref[stage, batch * BATCHES[stage] + part])
            product = jnp.dot(blocks[slot], source[row], preferred_element_type=jnp.float32)
            made.append((target, product))
        for target, product in made:
            total[target] += product


def gather_panels(panels, source):
    for at, panel in enumerate(panels):
        rows = panel.shape[0]
        source[at * rows : (at + 1) * rows] = panel[...]


def early_kernel(order_ref, panel, blocks, total):
    total[...] = jnp.zeros_like(total)
    add_products(0, order_ref, blocks, panel, total)


def middle_kernel(order_ref, *refs):
    *panels, blocks, _, total, source = refs
    gather_panels(panels, source)
    add_products(1, order_ref, blocks, source, total)


def far_kernel(tiles_dev, order_ref, *refs):
    *panels, blocks, _, far, first, total, source = refs
    half = len(panels) // 2
    others = source.at[half * tiles_dev :]
    gather_panels(panels[half:], others)
    add_products(2, order_ref, blocks, others, total)
    far[...] = total[: far.shape[0]].astype(far.dtype)

    @pl.when(batches_of(3, order_ref) > 0)
    def _():
        gather_panels(panels[:half], source)
        first[...] = jnp.zeros_like(first)
        add_products(3, order_ref, blocks, source, first)


def first_kernel(order_ref, *refs):
    *panels, blocks, _, first, total, source = refs

    @pl.when(batches_of(3, order_ref) == 0)
    def _():
        gather_panels(panels, source)
        total[...] = jnp.zeros_like(total)
        add_products(4, order_ref, blocks, source, total)

    first[...] = total[: first.shape[0]].astype(first.dtype)


def rest_kernel(order_ref, *refs):
    *panels, blocks, own, later, source, total = refs
    gather_panels(panels, source)
    total[...] = jnp.zeros_like(total)
    add_products(5, order_ref, blocks, source, total)
    tiles_dev = own.shape[0]
    own[...] = total[:tiles_dev]
    later[...] = total[tiles_dev : tiles_dev + later.shape[0]]


def final_kernel(factors, own, *refs):
    *arrived, out_hbm, out, sems = refs
    copies = []
    for tile in range(out.shape[0]):
        value = own[tile]
        for piece in arrived:
            value = value + piece[tile].astype(jnp.float32)
        out[tile] = (value * factors[tile]).astype(out.dtype)
        copies.append(pltpu.make_async_copy(out.at[tile], out_hbm.at[tile], sems.at[tile]))
        copies[-1].start()
    for copy in copies:
        copy.wait()


def cost_of(slots, tile_rows, row_width):
    return pl.CostEstimate(
        flops=2 * slots * tile_rows * tile_rows * row_width,
        bytes_accessed=2 * slots * tile_rows * tile_rows,
        transcendentals=0,
    )


def shards(embed_codes, embed_exps, degrees, adjacency, block_index):
    tile_rows = adjacency.shape[2]
    row_width = embed_codes.shape[2]
    row_count = embed_codes.shape[1]
    capacity = adjacency.shape[1]
    tiles_dev = row_count // tile_rows
    groups = lax.axis_size("grp")
    blks = lax.axis_size("blk")
    part = (tiles_dev, tile_rows, row_width)
    codes = embed_codes.reshape(part)
    source, factors, scales = scale_rows(codes, embed_exps, degrees)

    def across(value, step):
        pairs = [
            (side * blks + at, (1 - side) * blks + (at ^ (2 * step if at & 1 else blks - 2 - 2 * step)))
            for side in range(2)
            for at in range(blks)
        ]
        return lax.ppermute(value, ("side", "blk"), pairs)

    def paired(value, axis, hop):
        return lax.ppermute(value, axis, [(at, at ^ hop) for at in range(lax.axis_size(axis))])

    place = jnp.stack([lax.axis_index("blk"), lax.axis_index("grp")]).astype(jnp.int32)
    early = across(codes, 0)
    middle = [across(source, step) for step in range(1, blks // 2)]
    early_scales = across(scales, 0)
    order, blocks = stage_blocks(block_index[0], place, adjacency[0], blks, groups, tiles_dev)
    early, early_scales, order = lax.optimization_barrier((early, early_scales, order))
    early = (early.astype(jnp.float32) * early_scales[:, :, None]).astype(jnp.bfloat16)
    other = paired(early, "blk", 1)
    far_tiles = (groups // 2 - 1) * tiles_dev

    def held(count, dtype):
        return pltpu.VMEM((count, tile_rows, row_width), dtype)

    total = pl.pallas_call(
        early_kernel,
        out_shape=jax.ShapeDtypeStruct((far_tiles + 1, tile_rows, row_width), jnp.float32),
        in_specs=[SMEM] + [VMEM] * 2,
        out_specs=VMEM,
        compiler_params=LIMIT,
        cost_estimate=cost_of(capacity // 8, tile_rows, row_width),
    )(order, early, blocks)
    *middle, total = lax.optimization_barrier((*middle, total))
    others = [other] + [paired(panel, "blk", 1) for panel in middle]
    total = pl.pallas_call(
        middle_kernel,
        out_shape=jax.ShapeDtypeStruct(total.shape, total.dtype),
        in_specs=[SMEM] + [VMEM] * (len(middle) + 2),
        out_specs=VMEM,
        input_output_aliases={len(middle) + 2: 0},
        scratch_shapes=[held(len(middle) * tiles_dev, jnp.bfloat16)],
        compiler_params=LIMIT,
        cost_estimate=cost_of(capacity // 8, tile_rows, row_width),
    )(order, *middle, blocks, total)
    *others, total = lax.optimization_barrier((*others, total))
    panels = [early] + middle + others
    far, first, _ = pl.pallas_call(
        functools.partial(far_kernel, tiles_dev),
        out_shape=[
            jax.ShapeDtypeStruct((far_tiles, tile_rows, row_width), jnp.bfloat16),
            jax.ShapeDtypeStruct((tiles_dev + 1, tile_rows, row_width), jnp.float32),
            jax.ShapeDtypeStruct(total.shape, total.dtype),
        ],
        in_specs=[SMEM] + [VMEM] * (len(panels) + 2),
        out_specs=[VMEM] * 3,
        input_output_aliases={len(panels) + 2: 2},
        scratch_shapes=[held(len(panels) * tiles_dev, jnp.bfloat16)],
        compiler_params=LIMIT,
        cost_estimate=cost_of(capacity // 8, tile_rows, row_width),
    )(order, *panels, blocks, total)
    far, order = lax.optimization_barrier((far, order))
    first, _ = pl.pallas_call(
        first_kernel,
        out_shape=[
            jax.ShapeDtypeStruct(part, jnp.bfloat16),
            jax.ShapeDtypeStruct(first.shape, first.dtype),
        ],
        in_specs=[SMEM] + [VMEM] * (len(panels) + 2),
        out_specs=[VMEM] * 2,
        input_output_aliases={len(panels) + 2: 1},
        scratch_shapes=[held(len(panels) * tiles_dev, jnp.bfloat16)],
        compiler_params=LIMIT,
        cost_estimate=cost_of(capacity // 4, tile_rows, row_width),
    )(order, *panels, blocks, first)
    first, order = lax.optimization_barrier((first, order))
    own, later = pl.pallas_call(
        rest_kernel,
        out_shape=[
            jax.ShapeDtypeStruct(part, jnp.float32),
            jax.ShapeDtypeStruct((far_tiles, tile_rows, row_width), jnp.float32),
        ],
        in_specs=[SMEM] + [VMEM] * (len(panels) + 1),
        out_specs=[VMEM] * 2,
        scratch_shapes=[
            held(len(panels) * tiles_dev, jnp.bfloat16),
            held(groups // 2 * tiles_dev + 1, jnp.float32),
        ],
        compiler_params=LIMIT,
        cost_estimate=cost_of(capacity // 2, tile_rows, row_width),
    )(order, *panels, blocks)

    def turned(value, even_hop, odd_hop):
        hops = (even_hop, odd_hop)
        pairs = [
            (at * blks + blk, (at ^ hops[blk & 1]) * blks + blk)
            for at in range(groups)
            for blk in range(blks)
        ]
        return lax.ppermute(value, ("grp", "blk"), pairs)

    steps = groups // 2 - 1
    even_core = lax.axis_index("blk") % 2 == 0
    pieces = [slice(at * tiles_dev, (at + 1) * tiles_dev) for at in range(steps)]
    handed = [turned(far[pieces[at]], 1, 2 * at + 2).astype(jnp.float32) for at in range(steps)]
    arrived = [turned(first, 1, 2)]
    for at in range(steps):
        value = later[pieces[at]]
        for step, extra in enumerate(handed):
            if step == at == steps - 1:
                value = value + extra
            elif step == at:
                value = value + jnp.where(even_core, extra, 0.0)
            elif at == steps - 1:
                value = value + jnp.where(even_core, 0.0, extra)
        odd_hop = 1 if at == steps - 1 else 2 * at + 4
        arrived.append(turned(value.astype(jnp.bfloat16), 2 * at + 2, odd_hop))
    own = own + arrived[0].astype(jnp.float32)
    own, *sums = lax.optimization_barrier((own, *arrived[1:]))
    out = pl.pallas_call(
        final_kernel,
        out_shape=jax.ShapeDtypeStruct(part, jnp.bfloat16),
        in_specs=[VMEM] * (2 + len(sums)),
        out_specs=HBM,
        scratch_shapes=[
            held(tiles_dev, jnp.bfloat16),
            pltpu.SemaphoreType.DMA((tiles_dev,)),
        ],
        compiler_params=LIMIT,
        cost_estimate=cost_of(0, tile_rows, row_width),
    )(factors, own, *sums)
    return out.reshape(1, row_count, row_width)


def solution(mesh):
    placed = (
        P("side", ("grp", "blk"), None),
        P("side", ("grp", "blk")),
        P("side", ("grp", "blk")),
        P("side", ("grp", "blk"), None, None),
        P("side", None, ("grp", "blk")),
    )
    return jax.shard_map(
        shards,
        mesh=mesh,
        in_specs=placed,
        out_specs=P("side", ("grp", "blk"), None),
        check_vma=False,
    )
```

```python
import functools

import jax
import jax.numpy as jnp
from jax import lax
from jax.experimental import pallas as pl
from jax.experimental.pallas import tpu as pltpu
from jax.sharding import PartitionSpec as P

UNROLL = 8
STAGES = 5
VMEM = pl.BlockSpec(memory_space=pltpu.VMEM)
SMEM = pl.BlockSpec(memory_space=pltpu.SMEM)
HBM = pl.BlockSpec(memory_space=pltpu.HBM)
LIMIT = pltpu.CompilerParams(vmem_limit_bytes=48 * 1024 * 1024)


def in_hbm(*arrays):
    return [pltpu.with_memory_space_constraint(array, pltpu.HBM) for array in arrays]


def split(value, size):
    if size & (size - 1) == 0:
        return value >> (size.bit_length() - 1), value & (size - 1)
    return value // size, value % size


def scale_kernel(
    exps_hbm, degrees_hbm, codes_hbm, rows, factors, scales, exps_ref, degrees, codes, sems
):
    pairs = [(exps_hbm, exps_ref), (degrees_hbm, degrees), (codes_hbm, codes)]
    fetches = [
        pltpu.make_async_copy(held, wanted, sems.at[at])
        for at, (held, wanted) in enumerate(pairs)
    ]
    for fetch in fetches:
        fetch.start()
    fetches[0].wait()
    fetches[1].wait()
    tiles_dev, tile_rows, row_width = rows.shape
    inverse = lax.rsqrt(degrees[...].astype(jnp.float32))
    for tile in range(tiles_dev):
        lanes = inverse[:, tile * tile_rows : (tile + 1) * tile_rows]
        factors[tile] = jnp.broadcast_to(lanes, (row_width, tile_rows)).T
        scale = jnp.exp2(jnp.full((1, 1), exps_ref[0, tile], jnp.int32).astype(jnp.float32))
        scales[tile : tile + 1, :] = lanes * scale
    fetches[2].wait()
    for tile in range(tiles_dev):
        scale = jnp.exp2(jnp.full((1, 1), exps_ref[0, tile], jnp.int32).astype(jnp.float32))
        scaled = codes[tile].astype(jnp.float32) * scale * factors[tile]
        rows[tile] = scaled.astype(rows.dtype)


def scale_rows(codes, exps, degrees):
    return pl.pallas_call(
        scale_kernel,
        out_shape=[
            jax.ShapeDtypeStruct(codes.shape, jnp.bfloat16),
            jax.ShapeDtypeStruct(codes.shape, jnp.float32),
            jax.ShapeDtypeStruct(codes.shape[:2], jnp.float32),
        ],
        in_specs=[HBM] * 3,
        out_specs=[VMEM] * 3,
        scratch_shapes=[
            pltpu.SMEM(exps.shape, exps.dtype),
            pltpu.VMEM(degrees.shape, degrees.dtype),
            pltpu.VMEM(codes.shape, codes.dtype),
            pltpu.SemaphoreType.DMA((3,)),
        ],
        compiler_params=LIMIT,
        cost_estimate=pl.CostEstimate(
            flops=codes.size, bytes_accessed=4 * codes.size, transcendentals=0
        ),
    )(*in_hbm(exps, degrees, codes))


def count_up(shape, axis):
    return lax.broadcasted_iota(jnp.int32, shape, axis)


def stage_kernel(
    blks, groups, tiles_dev, place_ref, index_hbm, blocks_hbm, order_ref, blocks, index_ref, sems
):
    fetch = pltpu.make_async_copy(index_hbm, index_ref, sems.at[0])
    fetch.start()
    copy = pltpu.make_async_copy(blocks_hbm, blocks, sems.at[1])
    copy.start()
    fetch.wait()
    my_blk = place_ref[0]
    my_grp = place_ref[1]
    capacity = index_ref.shape[1]
    width = order_ref.shape[1]
    source_tiles = blks * tiles_dev
    half = blks // 2
    role = my_blk & 1

    target = index_ref[0:1, :]
    origin = index_ref[1:2, :]
    hop, row = split(origin, tiles_dev)
    chunk, tile = split(target, tiles_dev)
    hop = hop ^ my_blk
    chunk = chunk ^ my_grp
    odd = hop & 1
    rank = jnp.where(odd == role, half - 1 - (hop >> 1), hop >> 1)
    far = (chunk >= 2) & ((chunk & 1) == 1)
    kept = jnp.where(chunk == 1, 1 + role * (groups // 2 - 1), (chunk >> 1) + 1 - role)
    kept = jnp.where(chunk == 0, 0, jnp.where(far, (chunk >> 1) - 1, kept))
    stage = jnp.where(far, jnp.where(odd == 1, 2, jnp.minimum(rank, 1)), 4)
    stage = jnp.where(far | (kept != 1), stage, 3)
    kept = jnp.where(far, kept, jnp.where(stage == 3, 0, kept - (kept > 1).astype(jnp.int32)))
    stage = jnp.where(origin < source_tiles, stage, STAGES)
    panel = jnp.where(stage == 1, rank - 1, jnp.where(stage == 2, rank, rank + odd * half))
    slot = count_up((1, capacity), 1)

    stages = (count_up((8, capacity), 0) == stage).astype(jnp.float32)
    earlier = count_up((capacity, capacity), 0) < count_up((capacity, capacity), 1)
    before = jnp.dot(
        stages.astype(jnp.bfloat16), earlier.astype(jnp.bfloat16), preferred_element_type=jnp.float32
    )
    position = jnp.sum(stages * before, axis=0, keepdims=True).astype(jnp.int32)
    parts = (slot & 127, slot >> 7, panel * tiles_dev + row, kept * tiles_dev + tile)
    values = sum(
        jnp.where(count_up((8, capacity), 0) == at, part, 0) for at, part in enumerate(parts)
    ).astype(jnp.bfloat16)
    far_tiles = (groups // 2 - 1) * tiles_dev
    tops = [far_tiles] * 3 + [tiles_dev, groups // 2 * tiles_dev]
    lanes = count_up((1, width), 1)
    for at, top in enumerate(tops):
        where = jnp.where(stage == at, position, -1)
        chosen = (count_up((width, capacity), 0) == where).astype(jnp.bfloat16)
        listed = lax.dot_general(
            values, chosen, (((1,), (1,)), ((), ())), preferred_element_type=jnp.float32
        ).astype(jnp.int32)
        word = pack(listed[0:1] + (listed[1:2] << 7), listed[2:3], listed[3:4])
        count = jnp.sum((stage == at).astype(jnp.int32), axis=1, keepdims=True)
        word = jnp.where(lanes < count, word, pack(0, 0, top))
        batches = split(count + (UNROLL - 1), UNROLL)[0]
        order_ref[at : at + 1, :] = jnp.where(lanes == width - UNROLL, batches, word)
    copy.wait()


def pack(slot, row, target):
    return (slot << 16) | (row << 8) | target


def unpack(word):
    return word >> 16, (word >> 8) & 255, word & 255


def stage_blocks(index, place, blocks, blks, groups, tiles_dev):
    capacity = blocks.shape[0]
    assert blks * tiles_dev < 256 and groups * tiles_dev < 256 and capacity < 2**15
    width = -(-(capacity + 2 * UNROLL) // 128) * 128
    return pl.pallas_call(
        functools.partial(stage_kernel, blks, groups, tiles_dev),
        out_shape=[
            jax.ShapeDtypeStruct((8, width), jnp.int32),
            jax.ShapeDtypeStruct(blocks.shape, blocks.dtype),
        ],
        in_specs=[SMEM, HBM, HBM],
        out_specs=[VMEM, VMEM],
        scratch_shapes=[
            pltpu.VMEM(index.shape, index.dtype),
            pltpu.SemaphoreType.DMA((2,)),
        ],
        compiler_params=LIMIT,
        cost_estimate=pl.CostEstimate(flops=0, bytes_accessed=0, transcendentals=0),
    )(place, *in_hbm(index, blocks))


def add_products(stage, order_ref, blocks, source, total):
    @pl.loop(0, order_ref[stage, order_ref.shape[1] - UNROLL])
    def _(batch):
        made = []
        for part in range(UNROLL):
            slot, row, target = unpack(order_ref[stage, batch * UNROLL + part])
            product = jnp.dot(blocks[slot], source[row], preferred_element_type=jnp.float32)
            made.append((target, product))
        for target, product in made:
            total[target] += product


def gather_panels(panels, source):
    for at, panel in enumerate(panels):
        rows = panel.shape[0]
        source[at * rows : (at + 1) * rows] = panel[...]


def early_kernel(order_ref, panel, blocks, total):
    total[...] = jnp.zeros_like(total)
    add_products(0, order_ref, blocks, panel, total)


def middle_kernel(order_ref, *refs):
    *panels, blocks, _, total, source = refs
    gather_panels(panels, source)
    add_products(1, order_ref, blocks, source, total)


def far_kernel(order_ref, *refs):
    *panels, blocks, _, far, total, source = refs
    gather_panels(panels, source)
    add_products(2, order_ref, blocks, source, total)
    far[...] = total[: far.shape[0]].astype(far.dtype)


def first_kernel(order_ref, *refs):
    *panels, blocks, first, source, total = refs
    gather_panels(panels, source)
    total[...] = jnp.zeros_like(total)
    add_products(3, order_ref, blocks, source, total)
    first[...] = total[: first.shape[0]].astype(first.dtype)


def rest_kernel(order_ref, *refs):
    *panels, blocks, own, later, source, total = refs
    gather_panels(panels, source)
    total[...] = jnp.zeros_like(total)
    add_products(4, order_ref, blocks, source, total)
    tiles_dev = own.shape[0]
    own[...] = total[:tiles_dev]
    later[...] = total[tiles_dev : tiles_dev + later.shape[0]]


def final_kernel(factors, own, *refs):
    *arrived, out_hbm, out, sems = refs
    copies = []
    for tile in range(out.shape[0]):
        value = own[tile]
        for piece in arrived:
            value = value + piece[tile].astype(jnp.float32)
        out[tile] = (value * factors[tile]).astype(out.dtype)
        copies.append(pltpu.make_async_copy(out.at[tile], out_hbm.at[tile], sems.at[tile]))
        copies[-1].start()
    for copy in copies:
        copy.wait()


def cost_of(slots, tile_rows, row_width):
    return pl.CostEstimate(
        flops=2 * slots * tile_rows * tile_rows * row_width,
        bytes_accessed=2 * slots * tile_rows * tile_rows,
        transcendentals=0,
    )


def shards(embed_codes, embed_exps, degrees, adjacency, block_index):
    tile_rows = adjacency.shape[2]
    row_width = embed_codes.shape[2]
    row_count = embed_codes.shape[1]
    capacity = adjacency.shape[1]
    tiles_dev = row_count // tile_rows
    groups = lax.axis_size("grp")
    blks = lax.axis_size("blk")
    part = (tiles_dev, tile_rows, row_width)
    codes = embed_codes.reshape(part)
    source, factors, scales = scale_rows(codes, embed_exps, degrees)

    def across(value, step):
        pairs = [
            (side * blks + at, (1 - side) * blks + (at ^ (2 * step if at & 1 else blks - 2 - 2 * step)))
            for side in range(2)
            for at in range(blks)
        ]
        return lax.ppermute(value, ("side", "blk"), pairs)

    def paired(value, axis, hop):
        return lax.ppermute(value, axis, [(at, at ^ hop) for at in range(lax.axis_size(axis))])

    place = jnp.stack([lax.axis_index("blk"), lax.axis_index("grp")]).astype(jnp.int32)
    early = across(codes, 0)
    middle = [across(source, step) for step in range(1, blks // 2)]
    early_scales = across(scales, 0)
    order, blocks = stage_blocks(block_index[0], place, adjacency[0], blks, groups, tiles_dev)
    early, early_scales, order = lax.optimization_barrier((early, early_scales, order))
    early = (early.astype(jnp.float32) * early_scales[:, :, None]).astype(jnp.bfloat16)
    other = paired(early, "blk", 1)
    far_tiles = (groups // 2 - 1) * tiles_dev

    def held(count, dtype):
        return pltpu.VMEM((count, tile_rows, row_width), dtype)

    total = pl.pallas_call(
        early_kernel,
        out_shape=jax.ShapeDtypeStruct((far_tiles + 1, tile_rows, row_width), jnp.float32),
        in_specs=[SMEM] + [VMEM] * 2,
        out_specs=VMEM,
        compiler_params=LIMIT,
        cost_estimate=cost_of(capacity // 8, tile_rows, row_width),
    )(order, early, blocks)
    *middle, total = lax.optimization_barrier((*middle, total))
    others = [other] + [paired(panel, "blk", 1) for panel in middle]
    total = pl.pallas_call(
        middle_kernel,
        out_shape=jax.ShapeDtypeStruct(total.shape, total.dtype),
        in_specs=[SMEM] + [VMEM] * (len(middle) + 2),
        out_specs=VMEM,
        input_output_aliases={len(middle) + 2: 0},
        scratch_shapes=[held(len(middle) * tiles_dev, jnp.bfloat16)],
        compiler_params=LIMIT,
        cost_estimate=cost_of(capacity // 8, tile_rows, row_width),
    )(order, *middle, blocks, total)
    *others, total = lax.optimization_barrier((*others, total))
    far, _ = pl.pallas_call(
        far_kernel,
        out_shape=[
            jax.ShapeDtypeStruct((far_tiles, tile_rows, row_width), jnp.bfloat16),
            jax.ShapeDtypeStruct(total.shape, total.dtype),
        ],
        in_specs=[SMEM] + [VMEM] * (len(others) + 2),
        out_specs=[VMEM] * 2,
        input_output_aliases={len(others) + 2: 1},
        scratch_shapes=[held(len(others) * tiles_dev, jnp.bfloat16)],
        compiler_params=LIMIT,
        cost_estimate=cost_of(capacity // 8, tile_rows, row_width),
    )(order, *others, blocks, total)
    far, order = lax.optimization_barrier((far, order))
    panels = [early] + middle + others
    first = pl.pallas_call(
        first_kernel,
        out_shape=jax.ShapeDtypeStruct(part, jnp.bfloat16),
        in_specs=[SMEM] + [VMEM] * (len(panels) + 1),
        out_specs=VMEM,
        scratch_shapes=[
            held(len(panels) * tiles_dev, jnp.bfloat16),
            held(tiles_dev + 1, jnp.float32),
        ],
        compiler_params=LIMIT,
        cost_estimate=cost_of(capacity // 4, tile_rows, row_width),
    )(order, *panels, blocks)
    first, order = lax.optimization_barrier((first, order))
    own, later = pl.pallas_call(
        rest_kernel,
        out_shape=[
            jax.ShapeDtypeStruct(part, jnp.float32),
            jax.ShapeDtypeStruct((far_tiles, tile_rows, row_width), jnp.float32),
        ],
        in_specs=[SMEM] + [VMEM] * (len(panels) + 1),
        out_specs=[VMEM] * 2,
        scratch_shapes=[
            held(len(panels) * tiles_dev, jnp.bfloat16),
            held(groups // 2 * tiles_dev + 1, jnp.float32),
        ],
        compiler_params=LIMIT,
        cost_estimate=cost_of(capacity // 2, tile_rows, row_width),
    )(order, *panels, blocks)

    def turned(value, even_hop, odd_hop):
        hops = (even_hop, odd_hop)
        pairs = [
            (at * blks + blk, (at ^ hops[blk & 1]) * blks + blk)
            for at in range(groups)
            for blk in range(blks)
        ]
        return lax.ppermute(value, ("grp", "blk"), pairs)

    steps = groups // 2 - 1
    even_core = lax.axis_index("blk") % 2 == 0
    pieces = [slice(at * tiles_dev, (at + 1) * tiles_dev) for at in range(steps)]
    handed = [turned(far[pieces[at]], 1, 2 * at + 2).astype(jnp.float32) for at in range(steps)]
    arrived = [turned(first, 1, 2)]
    for at in range(steps):
        value = later[pieces[at]]
        for step, extra in enumerate(handed):
            if step == at == steps - 1:
                value = value + extra
            elif step == at:
                value = value + jnp.where(even_core, extra, 0.0)
            elif at == steps - 1:
                value = value + jnp.where(even_core, 0.0, extra)
        odd_hop = 1 if at == steps - 1 else 2 * at + 4
        arrived.append(turned(value.astype(jnp.bfloat16), 2 * at + 2, odd_hop))
    own = own + arrived[0].astype(jnp.float32)
    own, *sums = lax.optimization_barrier((own, *arrived[1:]))
    out = pl.pallas_call(
        final_kernel,
        out_shape=jax.ShapeDtypeStruct(part, jnp.bfloat16),
        in_specs=[VMEM] * (2 + len(sums)),
        out_specs=HBM,
        scratch_shapes=[
            held(tiles_dev, jnp.bfloat16),
            pltpu.SemaphoreType.DMA((tiles_dev,)),
        ],
        compiler_params=LIMIT,
        cost_estimate=cost_of(0, tile_rows, row_width),
    )(factors, own, *sums)
    return out.reshape(1, row_count, row_width)


def solution(mesh):
    placed = (
        P("side", ("grp", "blk"), None),
        P("side", ("grp", "blk")),
        P("side", ("grp", "blk")),
        P("side", ("grp", "blk"), None, None),
        P("side", None, ("grp", "blk")),
    )
    return jax.shard_map(
        shards,
        mesh=mesh,
        in_specs=placed,
        out_specs=P("side", ("grp", "blk"), None),
        check_vma=False,
    )
```

```python
import functools

import jax
import jax.numpy as jnp
from jax import lax
from jax.experimental import pallas as pl
from jax.experimental.pallas import tpu as pltpu
from jax.sharding import PartitionSpec as P

UNROLL = 8
STAGES = 5
VMEM = pl.BlockSpec(memory_space=pltpu.VMEM)
SMEM = pl.BlockSpec(memory_space=pltpu.SMEM)
HBM = pl.BlockSpec(memory_space=pltpu.HBM)
LIMIT = pltpu.CompilerParams(vmem_limit_bytes=48 * 1024 * 1024)


def in_hbm(*arrays):
    return [pltpu.with_memory_space_constraint(array, pltpu.HBM) for array in arrays]


def split(value, size):
    if size & (size - 1) == 0:
        return value >> (size.bit_length() - 1), value & (size - 1)
    return value // size, value % size


def scale_kernel(
    exps_hbm, degrees_hbm, codes_hbm, rows, factors, scales, exps_ref, degrees, codes, sems
):
    pairs = [(exps_hbm, exps_ref), (degrees_hbm, degrees), (codes_hbm, codes)]
    fetches = [
        pltpu.make_async_copy(held, wanted, sems.at[at])
        for at, (held, wanted) in enumerate(pairs)
    ]
    for fetch in fetches:
        fetch.start()
    fetches[0].wait()
    fetches[1].wait()
    tiles_dev, tile_rows, row_width = rows.shape
    inverse = lax.rsqrt(degrees[...].astype(jnp.float32))
    for tile in range(tiles_dev):
        lanes = inverse[:, tile * tile_rows : (tile + 1) * tile_rows]
        factors[tile] = jnp.broadcast_to(lanes, (row_width, tile_rows)).T
        scale = jnp.exp2(jnp.full((1, 1), exps_ref[0, tile], jnp.int32).astype(jnp.float32))
        scales[tile : tile + 1, :] = lanes * scale
    fetches[2].wait()
    for tile in range(tiles_dev):
        scale = jnp.exp2(jnp.full((1, 1), exps_ref[0, tile], jnp.int32).astype(jnp.float32))
        scaled = codes[tile].astype(jnp.float32) * scale * factors[tile]
        rows[tile] = scaled.astype(rows.dtype)


def scale_rows(codes, exps, degrees):
    return pl.pallas_call(
        scale_kernel,
        out_shape=[
            jax.ShapeDtypeStruct(codes.shape, jnp.bfloat16),
            jax.ShapeDtypeStruct(codes.shape, jnp.float32),
            jax.ShapeDtypeStruct(codes.shape[:2], jnp.float32),
        ],
        in_specs=[HBM] * 3,
        out_specs=[VMEM] * 3,
        scratch_shapes=[
            pltpu.SMEM(exps.shape, exps.dtype),
            pltpu.VMEM(degrees.shape, degrees.dtype),
            pltpu.VMEM(codes.shape, codes.dtype),
            pltpu.SemaphoreType.DMA((3,)),
        ],
        compiler_params=LIMIT,
        cost_estimate=pl.CostEstimate(
            flops=codes.size, bytes_accessed=4 * codes.size, transcendentals=0
        ),
    )(*in_hbm(exps, degrees, codes))


def count_up(shape, axis):
    return lax.broadcasted_iota(jnp.int32, shape, axis)


def stage_kernel(
    blks, groups, tiles_dev, place_ref, index_hbm, blocks_hbm, order_ref, blocks, index_ref, sems
):
    fetch = pltpu.make_async_copy(index_hbm, index_ref, sems.at[0])
    fetch.start()
    copy = pltpu.make_async_copy(blocks_hbm, blocks, sems.at[1])
    copy.start()
    fetch.wait()
    my_blk = place_ref[0]
    my_grp = place_ref[1]
    capacity = index_ref.shape[1]
    width = order_ref.shape[1]
    source_tiles = blks * tiles_dev
    half = blks // 2
    role = my_blk & 1

    target = index_ref[0:1, :]
    origin = index_ref[1:2, :]
    hop, row = split(origin, tiles_dev)
    chunk, tile = split(target, tiles_dev)
    hop = hop ^ my_blk
    chunk = chunk ^ my_grp
    odd = hop & 1
    rank = jnp.where(odd == role, half - 1 - (hop >> 1), hop >> 1)
    far = (chunk >= 2) & ((chunk & 1) == 1)
    kept = jnp.where(chunk == 1, 1 + role * (groups // 2 - 1), (chunk >> 1) + 1 - role)
    kept = jnp.where(chunk == 0, 0, jnp.where(far, (chunk >> 1) - 1, kept))
    stage = jnp.where(far, jnp.where(odd == 1, 2, jnp.minimum(rank, 1)), 4)
    drawn = (kept == 0) & (role == 0)
    stage = jnp.where(far | ((kept != 1) & ~drawn), stage, 3)
    near = jnp.where(stage == 3, 1 - kept, kept - (kept > 1).astype(jnp.int32))
    kept = jnp.where(far, kept, near)
    stage = jnp.where(origin < source_tiles, stage, STAGES)
    panel = jnp.where(stage == 1, rank - 1, jnp.where(stage == 2, rank, rank + odd * half))
    slot = count_up((1, capacity), 1)

    stages = (count_up((8, capacity), 0) == stage).astype(jnp.float32)
    earlier = count_up((capacity, capacity), 0) < count_up((capacity, capacity), 1)
    before = jnp.dot(
        stages.astype(jnp.bfloat16), earlier.astype(jnp.bfloat16), preferred_element_type=jnp.float32
    )
    position = jnp.sum(stages * before, axis=0, keepdims=True).astype(jnp.int32)
    parts = (slot & 127, slot >> 7, panel * tiles_dev + row, kept * tiles_dev + tile)
    values = sum(
        jnp.where(count_up((8, capacity), 0) == at, part, 0) for at, part in enumerate(parts)
    ).astype(jnp.bfloat16)
    far_tiles = (groups // 2 - 1) * tiles_dev
    tops = [far_tiles] * 3 + [2 * tiles_dev, groups // 2 * tiles_dev]
    lanes = count_up((1, width), 1)
    for at, top in enumerate(tops):
        where = jnp.where(stage == at, position, -1)
        chosen = (count_up((width, capacity), 0) == where).astype(jnp.bfloat16)
        listed = lax.dot_general(
            values, chosen, (((1,), (1,)), ((), ())), preferred_element_type=jnp.float32
        ).astype(jnp.int32)
        word = pack(listed[0:1] + (listed[1:2] << 7), listed[2:3], listed[3:4])
        count = jnp.sum((stage == at).astype(jnp.int32), axis=1, keepdims=True)
        word = jnp.where(lanes < count, word, pack(0, 0, top))
        batches = split(count + (UNROLL - 1), UNROLL)[0]
        order_ref[at : at + 1, :] = jnp.where(lanes == width - UNROLL, batches, word)
    copy.wait()


def pack(slot, row, target):
    return (slot << 16) | (row << 8) | target


def unpack(word):
    return word >> 16, (word >> 8) & 255, word & 255


def stage_blocks(index, place, blocks, blks, groups, tiles_dev):
    capacity = blocks.shape[0]
    assert blks * tiles_dev < 256 and groups * tiles_dev < 256 and capacity < 2**15
    width = -(-(capacity + 2 * UNROLL) // 128) * 128
    return pl.pallas_call(
        functools.partial(stage_kernel, blks, groups, tiles_dev),
        out_shape=[
            jax.ShapeDtypeStruct((8, width), jnp.int32),
            jax.ShapeDtypeStruct(blocks.shape, blocks.dtype),
        ],
        in_specs=[SMEM, HBM, HBM],
        out_specs=[VMEM, VMEM],
        scratch_shapes=[
            pltpu.VMEM(index.shape, index.dtype),
            pltpu.SemaphoreType.DMA((2,)),
        ],
        compiler_params=LIMIT,
        cost_estimate=pl.CostEstimate(flops=0, bytes_accessed=0, transcendentals=0),
    )(place, *in_hbm(index, blocks))


def add_products(stage, order_ref, blocks, source, total):
    @pl.loop(0, order_ref[stage, order_ref.shape[1] - UNROLL])
    def _(batch):
        made = []
        for part in range(UNROLL):
            slot, row, target = unpack(order_ref[stage, batch * UNROLL + part])
            product = jnp.dot(blocks[slot], source[row], preferred_element_type=jnp.float32)
            made.append((target, product))
        for target, product in made:
            total[target] += product


def gather_panels(panels, source):
    for at, panel in enumerate(panels):
        rows = panel.shape[0]
        source[at * rows : (at + 1) * rows] = panel[...]


def early_kernel(order_ref, panel, blocks, total):
    total[...] = jnp.zeros_like(total)
    add_products(0, order_ref, blocks, panel, total)


def middle_kernel(order_ref, *refs):
    *panels, blocks, _, total, source = refs
    gather_panels(panels, source)
    add_products(1, order_ref, blocks, source, total)


def far_kernel(order_ref, *refs):
    *panels, blocks, _, far, total, source = refs
    gather_panels(panels, source)
    add_products(2, order_ref, blocks, source, total)
    far[...] = total[: far.shape[0]].astype(far.dtype)


def first_kernel(order_ref, *refs):
    *panels, blocks, first, own, source, total = refs
    gather_panels(panels, source)
    total[...] = jnp.zeros_like(total)
    add_products(3, order_ref, blocks, source, total)
    tiles_dev = first.shape[0]
    first[...] = total[:tiles_dev].astype(first.dtype)
    own[...] = total[tiles_dev : 2 * tiles_dev]


def rest_kernel(order_ref, *refs):
    *panels, blocks, own, later, source, total = refs
    gather_panels(panels, source)
    total[...] = jnp.zeros_like(total)
    add_products(4, order_ref, blocks, source, total)
    tiles_dev = own.shape[0]
    own[...] = total[:tiles_dev]
    later[...] = total[tiles_dev : tiles_dev + later.shape[0]]


def final_kernel(factors, own, *refs):
    *arrived, out_hbm, out, sems = refs
    copies = []
    for tile in range(out.shape[0]):
        value = own[tile]
        for piece in arrived:
            value = value + piece[tile].astype(jnp.float32)
        out[tile] = (value * factors[tile]).astype(out.dtype)
        copies.append(pltpu.make_async_copy(out.at[tile], out_hbm.at[tile], sems.at[tile]))
        copies[-1].start()
    for copy in copies:
        copy.wait()


def cost_of(slots, tile_rows, row_width):
    return pl.CostEstimate(
        flops=2 * slots * tile_rows * tile_rows * row_width,
        bytes_accessed=2 * slots * tile_rows * tile_rows,
        transcendentals=0,
    )


def shards(embed_codes, embed_exps, degrees, adjacency, block_index):
    tile_rows = adjacency.shape[2]
    row_width = embed_codes.shape[2]
    row_count = embed_codes.shape[1]
    capacity = adjacency.shape[1]
    tiles_dev = row_count // tile_rows
    groups = lax.axis_size("grp")
    blks = lax.axis_size("blk")
    part = (tiles_dev, tile_rows, row_width)
    codes = embed_codes.reshape(part)
    source, factors, scales = scale_rows(codes, embed_exps, degrees)

    def across(value, step):
        pairs = [
            (side * blks + at, (1 - side) * blks + (at ^ (2 * step if at & 1 else blks - 2 - 2 * step)))
            for side in range(2)
            for at in range(blks)
        ]
        return lax.ppermute(value, ("side", "blk"), pairs)

    def paired(value, axis, hop):
        return lax.ppermute(value, axis, [(at, at ^ hop) for at in range(lax.axis_size(axis))])

    place = jnp.stack([lax.axis_index("blk"), lax.axis_index("grp")]).astype(jnp.int32)
    early = across(codes, 0)
    middle = [across(source, step) for step in range(1, blks // 2)]
    early_scales = across(scales, 0)
    order, blocks = stage_blocks(block_index[0], place, adjacency[0], blks, groups, tiles_dev)
    early, early_scales, order = lax.optimization_barrier((early, early_scales, order))
    early = (early.astype(jnp.float32) * early_scales[:, :, None]).astype(jnp.bfloat16)
    other = paired(early, "blk", 1)
    far_tiles = (groups // 2 - 1) * tiles_dev

    def held(count, dtype):
        return pltpu.VMEM((count, tile_rows, row_width), dtype)

    total = pl.pallas_call(
        early_kernel,
        out_shape=jax.ShapeDtypeStruct((far_tiles + 1, tile_rows, row_width), jnp.float32),
        in_specs=[SMEM] + [VMEM] * 2,
        out_specs=VMEM,
        compiler_params=LIMIT,
        cost_estimate=cost_of(capacity // 8, tile_rows, row_width),
    )(order, early, blocks)
    *middle, total = lax.optimization_barrier((*middle, total))
    others = [other] + [paired(panel, "blk", 1) for panel in middle]
    total = pl.pallas_call(
        middle_kernel,
        out_shape=jax.ShapeDtypeStruct(total.shape, total.dtype),
        in_specs=[SMEM] + [VMEM] * (len(middle) + 2),
        out_specs=VMEM,
        input_output_aliases={len(middle) + 2: 0},
        scratch_shapes=[held(len(middle) * tiles_dev, jnp.bfloat16)],
        compiler_params=LIMIT,
        cost_estimate=cost_of(capacity // 8, tile_rows, row_width),
    )(order, *middle, blocks, total)
    *others, total = lax.optimization_barrier((*others, total))
    far, _ = pl.pallas_call(
        far_kernel,
        out_shape=[
            jax.ShapeDtypeStruct((far_tiles, tile_rows, row_width), jnp.bfloat16),
            jax.ShapeDtypeStruct(total.shape, total.dtype),
        ],
        in_specs=[SMEM] + [VMEM] * (len(others) + 2),
        out_specs=[VMEM] * 2,
        input_output_aliases={len(others) + 2: 1},
        scratch_shapes=[held(len(others) * tiles_dev, jnp.bfloat16)],
        compiler_params=LIMIT,
        cost_estimate=cost_of(capacity // 8, tile_rows, row_width),
    )(order, *others, blocks, total)
    far, order = lax.optimization_barrier((far, order))
    panels = [early] + middle + others
    first, even_own = pl.pallas_call(
        first_kernel,
        out_shape=[
            jax.ShapeDtypeStruct(part, jnp.bfloat16),
            jax.ShapeDtypeStruct(part, jnp.float32),
        ],
        in_specs=[SMEM] + [VMEM] * (len(panels) + 1),
        out_specs=[VMEM] * 2,
        scratch_shapes=[
            held(len(panels) * tiles_dev, jnp.bfloat16),
            held(2 * tiles_dev + 1, jnp.float32),
        ],
        compiler_params=LIMIT,
        cost_estimate=cost_of(capacity // 4, tile_rows, row_width),
    )(order, *panels, blocks)
    first, order = lax.optimization_barrier((first, order))
    own, later = pl.pallas_call(
        rest_kernel,
        out_shape=[
            jax.ShapeDtypeStruct(part, jnp.float32),
            jax.ShapeDtypeStruct((far_tiles, tile_rows, row_width), jnp.float32),
        ],
        in_specs=[SMEM] + [VMEM] * (len(panels) + 1),
        out_specs=[VMEM] * 2,
        scratch_shapes=[
            held(len(panels) * tiles_dev, jnp.bfloat16),
            held(groups // 2 * tiles_dev + 1, jnp.float32),
        ],
        compiler_params=LIMIT,
        cost_estimate=cost_of(capacity // 2, tile_rows, row_width),
    )(order, *panels, blocks)

    def turned(value, even_hop, odd_hop):
        hops = (even_hop, odd_hop)
        pairs = [
            (at * blks + blk, (at ^ hops[blk & 1]) * blks + blk)
            for at in range(groups)
            for blk in range(blks)
        ]
        return lax.ppermute(value, ("grp", "blk"), pairs)

    steps = groups // 2 - 1
    even_core = lax.axis_index("blk") % 2 == 0
    pieces = [slice(at * tiles_dev, (at + 1) * tiles_dev) for at in range(steps)]
    handed = [turned(far[pieces[at]], 1, 2 * at + 2).astype(jnp.float32) for at in range(steps)]
    arrived = [turned(first, 1, 2)]
    for at in range(steps):
        value = later[pieces[at]]
        for step, extra in enumerate(handed):
            if step == at == steps - 1:
                value = value + extra
            elif step == at:
                value = value + jnp.where(even_core, extra, 0.0)
            elif at == steps - 1:
                value = value + jnp.where(even_core, 0.0, extra)
        odd_hop = 1 if at == steps - 1 else 2 * at + 4
        arrived.append(turned(value.astype(jnp.bfloat16), 2 * at + 2, odd_hop))
    own = own + even_own + arrived[0].astype(jnp.float32)
    own, *sums = lax.optimization_barrier((own, *arrived[1:]))
    out = pl.pallas_call(
        final_kernel,
        out_shape=jax.ShapeDtypeStruct(part, jnp.bfloat16),
        in_specs=[VMEM] * (2 + len(sums)),
        out_specs=HBM,
        scratch_shapes=[
            held(tiles_dev, jnp.bfloat16),
            pltpu.SemaphoreType.DMA((tiles_dev,)),
        ],
        compiler_params=LIMIT,
        cost_estimate=cost_of(0, tile_rows, row_width),
    )(factors, own, *sums)
    return out.reshape(1, row_count, row_width)


def solution(mesh):
    placed = (
        P("side", ("grp", "blk"), None),
        P("side", ("grp", "blk")),
        P("side", ("grp", "blk")),
        P("side", ("grp", "blk"), None, None),
        P("side", None, ("grp", "blk")),
    )
    return jax.shard_map(
        shards,
        mesh=mesh,
        in_specs=placed,
        out_specs=P("side", ("grp", "blk"), None),
        check_vma=False,
    )
```

```python
import functools

import jax
import jax.numpy as jnp
from jax import lax
from jax.experimental import pallas as pl
from jax.experimental.pallas import tpu as pltpu
from jax.sharding import PartitionSpec as P

UNROLL = 8
BATCHES = (8, 8, 4, 8, 8)
STAGES = len(BATCHES)
VMEM = pl.BlockSpec(memory_space=pltpu.VMEM)
SMEM = pl.BlockSpec(memory_space=pltpu.SMEM)
HBM = pl.BlockSpec(memory_space=pltpu.HBM)
LIMIT = pltpu.CompilerParams(vmem_limit_bytes=48 * 1024 * 1024)


def in_hbm(*arrays):
    return [pltpu.with_memory_space_constraint(array, pltpu.HBM) for array in arrays]


def split(value, size):
    if size & (size - 1) == 0:
        return value >> (size.bit_length() - 1), value & (size - 1)
    return value // size, value % size


def scale_kernel(
    exps_hbm, degrees_hbm, codes_hbm, rows, factors, scales, exps_ref, degrees, codes, sems
):
    pairs = [(exps_hbm, exps_ref), (degrees_hbm, degrees), (codes_hbm, codes)]
    fetches = [
        pltpu.make_async_copy(held, wanted, sems.at[at])
        for at, (held, wanted) in enumerate(pairs)
    ]
    for fetch in fetches:
        fetch.start()
    fetches[0].wait()
    fetches[1].wait()
    tiles_dev, tile_rows, row_width = rows.shape
    inverse = lax.rsqrt(degrees[...].astype(jnp.float32))
    for tile in range(tiles_dev):
        lanes = inverse[:, tile * tile_rows : (tile + 1) * tile_rows]
        factors[tile] = jnp.broadcast_to(lanes, (row_width, tile_rows)).T
        scale = jnp.exp2(jnp.full((1, 1), exps_ref[0, tile], jnp.int32).astype(jnp.float32))
        scales[tile : tile + 1, :] = lanes * scale
    fetches[2].wait()
    for tile in range(tiles_dev):
        scale = jnp.exp2(jnp.full((1, 1), exps_ref[0, tile], jnp.int32).astype(jnp.float32))
        scaled = codes[tile].astype(jnp.float32) * scale * factors[tile]
        rows[tile] = scaled.astype(rows.dtype)


def scale_rows(codes, exps, degrees):
    return pl.pallas_call(
        scale_kernel,
        out_shape=[
            jax.ShapeDtypeStruct(codes.shape, jnp.bfloat16),
            jax.ShapeDtypeStruct(codes.shape, jnp.float32),
            jax.ShapeDtypeStruct(codes.shape[:2], jnp.float32),
        ],
        in_specs=[HBM] * 3,
        out_specs=[VMEM] * 3,
        scratch_shapes=[
            pltpu.SMEM(exps.shape, exps.dtype),
            pltpu.VMEM(degrees.shape, degrees.dtype),
            pltpu.VMEM(codes.shape, codes.dtype),
            pltpu.SemaphoreType.DMA((3,)),
        ],
        compiler_params=LIMIT,
        cost_estimate=pl.CostEstimate(
            flops=codes.size, bytes_accessed=4 * codes.size, transcendentals=0
        ),
    )(*in_hbm(exps, degrees, codes))


def count_up(shape, axis):
    return lax.broadcasted_iota(jnp.int32, shape, axis)


def stage_kernel(
    blks, groups, tiles_dev, place_ref, index_hbm, blocks_hbm, order_ref, blocks, index_ref, sems
):
    fetch = pltpu.make_async_copy(index_hbm, index_ref, sems.at[0])
    fetch.start()
    copy = pltpu.make_async_copy(blocks_hbm, blocks, sems.at[1])
    copy.start()
    fetch.wait()
    my_blk = place_ref[0]
    my_grp = place_ref[1]
    capacity = index_ref.shape[1]
    width = order_ref.shape[1]
    source_tiles = blks * tiles_dev
    half = blks // 2
    role = my_blk & 1

    target = index_ref[0:1, :]
    origin = index_ref[1:2, :]
    hop, row = split(origin, tiles_dev)
    chunk, tile = split(target, tiles_dev)
    hop = hop ^ my_blk
    chunk = chunk ^ my_grp
    odd = hop & 1
    rank = jnp.where(odd == role, half - 1 - (hop >> 1), hop >> 1)
    far = (chunk >= 2) & ((chunk & 1) == 1)
    kept = jnp.where(chunk == 1, 1 + role * (groups // 2 - 1), (chunk >> 1) + 1 - role)
    kept = jnp.where(chunk == 0, 0, jnp.where(far, (chunk >> 1) - 1, kept))
    stage = jnp.where(far, jnp.where(odd == 1, 2, jnp.minimum(rank, 1)), 4)
    drawn = (kept == 0) & (role == 0)
    stage = jnp.where(far | ((kept != 1) & ~drawn), stage, 3)
    near = jnp.where(stage == 3, 1 - kept, kept - (kept > 1).astype(jnp.int32))
    kept = jnp.where(far, kept, near)
    stage = jnp.where(origin < source_tiles, stage, STAGES)
    panel = jnp.where(stage == 1, rank - 1, jnp.where(stage == 2, rank, rank + odd * half))
    slot = count_up((1, capacity), 1)

    stages = (count_up((8, capacity), 0) == stage).astype(jnp.float32)
    earlier = count_up((capacity, capacity), 0) < count_up((capacity, capacity), 1)
    before = jnp.dot(
        stages.astype(jnp.bfloat16), earlier.astype(jnp.bfloat16), preferred_element_type=jnp.float32
    )
    position = jnp.sum(stages * before, axis=0, keepdims=True).astype(jnp.int32)
    parts = (slot & 127, slot >> 7, panel * tiles_dev + row, kept * tiles_dev + tile)
    values = sum(
        jnp.where(count_up((8, capacity), 0) == at, part, 0) for at, part in enumerate(parts)
    ).astype(jnp.bfloat16)
    far_tiles = (groups // 2 - 1) * tiles_dev
    tops = [far_tiles] * 3 + [2 * tiles_dev, groups // 2 * tiles_dev]
    lanes = count_up((1, width), 1)
    for at, top in enumerate(tops):
        where = jnp.where(stage == at, position, -1)
        chosen = (count_up((width, capacity), 0) == where).astype(jnp.bfloat16)
        listed = lax.dot_general(
            values, chosen, (((1,), (1,)), ((), ())), preferred_element_type=jnp.float32
        ).astype(jnp.int32)
        word = pack(listed[0:1] + (listed[1:2] << 7), listed[2:3], listed[3:4])
        count = jnp.sum((stage == at).astype(jnp.int32), axis=1, keepdims=True)
        word = jnp.where(lanes < count, word, pack(0, 0, top))
        batches = split(count + (BATCHES[at] - 1), BATCHES[at])[0]
        order_ref[at : at + 1, :] = jnp.where(lanes == width - UNROLL, batches, word)
    copy.wait()


def pack(slot, row, target):
    return (slot << 16) | (row << 8) | target


def unpack(word):
    return word >> 16, (word >> 8) & 255, word & 255


def stage_blocks(index, place, blocks, blks, groups, tiles_dev):
    capacity = blocks.shape[0]
    assert blks * tiles_dev < 256 and groups * tiles_dev < 256 and capacity < 2**15
    width = -(-(capacity + 2 * UNROLL) // 128) * 128
    return pl.pallas_call(
        functools.partial(stage_kernel, blks, groups, tiles_dev),
        out_shape=[
            jax.ShapeDtypeStruct((8, width), jnp.int32),
            jax.ShapeDtypeStruct(blocks.shape, blocks.dtype),
        ],
        in_specs=[SMEM, HBM, HBM],
        out_specs=[VMEM, VMEM],
        scratch_shapes=[
            pltpu.VMEM(index.shape, index.dtype),
            pltpu.SemaphoreType.DMA((2,)),
        ],
        compiler_params=LIMIT,
        cost_estimate=pl.CostEstimate(flops=0, bytes_accessed=0, transcendentals=0),
    )(place, *in_hbm(index, blocks))


def add_products(stage, order_ref, blocks, source, total):
    @pl.loop(0, order_ref[stage, order_ref.shape[1] - UNROLL])
    def _(batch):
        made = []
        for part in range(BATCHES[stage]):
            slot, row, target = unpack(order_ref[stage, batch * BATCHES[stage] + part])
            product = jnp.dot(blocks[slot], source[row], preferred_element_type=jnp.float32)
            made.append((target, product))
        for target, product in made:
            total[target] += product


def gather_panels(panels, source):
    for at, panel in enumerate(panels):
        rows = panel.shape[0]
        source[at * rows : (at + 1) * rows] = panel[...]


def early_kernel(order_ref, panel, blocks, total):
    total[...] = jnp.zeros_like(total)
    add_products(0, order_ref, blocks, panel, total)


def middle_kernel(order_ref, *refs):
    *panels, blocks, _, total, source = refs
    gather_panels(panels, source)
    add_products(1, order_ref, blocks, source, total)


def far_kernel(order_ref, *refs):
    *panels, blocks, _, far, total, source = refs
    gather_panels(panels, source)
    add_products(2, order_ref, blocks, source, total)
    far[...] = total[: far.shape[0]].astype(far.dtype)


def first_kernel(order_ref, *refs):
    *panels, blocks, first, own, source, total = refs
    gather_panels(panels, source)
    total[...] = jnp.zeros_like(total)
    add_products(3, order_ref, blocks, source, total)
    tiles_dev = first.shape[0]
    first[...] = total[:tiles_dev].astype(first.dtype)
    own[...] = total[tiles_dev : 2 * tiles_dev]


def rest_kernel(order_ref, *refs):
    *panels, blocks, own, later, source, total = refs
    gather_panels(panels, source)
    total[...] = jnp.zeros_like(total)
    add_products(4, order_ref, blocks, source, total)
    tiles_dev = own.shape[0]
    own[...] = total[:tiles_dev]
    later[...] = total[tiles_dev : tiles_dev + later.shape[0]]


def final_kernel(factors, own, *refs):
    *arrived, out_hbm, out, sems = refs
    copies = []
    for tile in range(out.shape[0]):
        value = own[tile]
        for piece in arrived:
            value = value + piece[tile].astype(jnp.float32)
        out[tile] = (value * factors[tile]).astype(out.dtype)
        copies.append(pltpu.make_async_copy(out.at[tile], out_hbm.at[tile], sems.at[tile]))
        copies[-1].start()
    for copy in copies:
        copy.wait()


def cost_of(slots, tile_rows, row_width):
    return pl.CostEstimate(
        flops=2 * slots * tile_rows * tile_rows * row_width,
        bytes_accessed=2 * slots * tile_rows * tile_rows,
        transcendentals=0,
    )


def shards(embed_codes, embed_exps, degrees, adjacency, block_index):
    tile_rows = adjacency.shape[2]
    row_width = embed_codes.shape[2]
    row_count = embed_codes.shape[1]
    capacity = adjacency.shape[1]
    tiles_dev = row_count // tile_rows
    groups = lax.axis_size("grp")
    blks = lax.axis_size("blk")
    part = (tiles_dev, tile_rows, row_width)
    codes = embed_codes.reshape(part)
    source, factors, scales = scale_rows(codes, embed_exps, degrees)

    def across(value, step):
        pairs = [
            (side * blks + at, (1 - side) * blks + (at ^ (2 * step if at & 1 else blks - 2 - 2 * step)))
            for side in range(2)
            for at in range(blks)
        ]
        return lax.ppermute(value, ("side", "blk"), pairs)

    def paired(value, axis, hop):
        return lax.ppermute(value, axis, [(at, at ^ hop) for at in range(lax.axis_size(axis))])

    place = jnp.stack([lax.axis_index("blk"), lax.axis_index("grp")]).astype(jnp.int32)
    early = across(codes, 0)
    middle = [across(source, step) for step in range(1, blks // 2)]
    early_scales = across(scales, 0)
    order, blocks = stage_blocks(block_index[0], place, adjacency[0], blks, groups, tiles_dev)
    early, early_scales, order = lax.optimization_barrier((early, early_scales, order))
    early = (early.astype(jnp.float32) * early_scales[:, :, None]).astype(jnp.bfloat16)
    other = paired(early, "blk", 1)
    far_tiles = (groups // 2 - 1) * tiles_dev

    def held(count, dtype):
        return pltpu.VMEM((count, tile_rows, row_width), dtype)

    total = pl.pallas_call(
        early_kernel,
        out_shape=jax.ShapeDtypeStruct((far_tiles + 1, tile_rows, row_width), jnp.float32),
        in_specs=[SMEM] + [VMEM] * 2,
        out_specs=VMEM,
        compiler_params=LIMIT,
        cost_estimate=cost_of(capacity // 8, tile_rows, row_width),
    )(order, early, blocks)
    *middle, total = lax.optimization_barrier((*middle, total))
    others = [other] + [paired(panel, "blk", 1) for panel in middle]
    total = pl.pallas_call(
        middle_kernel,
        out_shape=jax.ShapeDtypeStruct(total.shape, total.dtype),
        in_specs=[SMEM] + [VMEM] * (len(middle) + 2),
        out_specs=VMEM,
        input_output_aliases={len(middle) + 2: 0},
        scratch_shapes=[held(len(middle) * tiles_dev, jnp.bfloat16)],
        compiler_params=LIMIT,
        cost_estimate=cost_of(capacity // 8, tile_rows, row_width),
    )(order, *middle, blocks, total)
    *others, total = lax.optimization_barrier((*others, total))
    far, _ = pl.pallas_call(
        far_kernel,
        out_shape=[
            jax.ShapeDtypeStruct((far_tiles, tile_rows, row_width), jnp.bfloat16),
            jax.ShapeDtypeStruct(total.shape, total.dtype),
        ],
        in_specs=[SMEM] + [VMEM] * (len(others) + 2),
        out_specs=[VMEM] * 2,
        input_output_aliases={len(others) + 2: 1},
        scratch_shapes=[held(len(others) * tiles_dev, jnp.bfloat16)],
        compiler_params=LIMIT,
        cost_estimate=cost_of(capacity // 8, tile_rows, row_width),
    )(order, *others, blocks, total)
    far, order = lax.optimization_barrier((far, order))
    panels = [early] + middle + others
    first, even_own = pl.pallas_call(
        first_kernel,
        out_shape=[
            jax.ShapeDtypeStruct(part, jnp.bfloat16),
            jax.ShapeDtypeStruct(part, jnp.float32),
        ],
        in_specs=[SMEM] + [VMEM] * (len(panels) + 1),
        out_specs=[VMEM] * 2,
        scratch_shapes=[
            held(len(panels) * tiles_dev, jnp.bfloat16),
            held(2 * tiles_dev + 1, jnp.float32),
        ],
        compiler_params=LIMIT,
        cost_estimate=cost_of(capacity // 4, tile_rows, row_width),
    )(order, *panels, blocks)
    first, order = lax.optimization_barrier((first, order))
    own, later = pl.pallas_call(
        rest_kernel,
        out_shape=[
            jax.ShapeDtypeStruct(part, jnp.float32),
            jax.ShapeDtypeStruct((far_tiles, tile_rows, row_width), jnp.float32),
        ],
        in_specs=[SMEM] + [VMEM] * (len(panels) + 1),
        out_specs=[VMEM] * 2,
        scratch_shapes=[
            held(len(panels) * tiles_dev, jnp.bfloat16),
            held(groups // 2 * tiles_dev + 1, jnp.float32),
        ],
        compiler_params=LIMIT,
        cost_estimate=cost_of(capacity // 2, tile_rows, row_width),
    )(order, *panels, blocks)

    def turned(value, even_hop, odd_hop):
        hops = (even_hop, odd_hop)
        pairs = [
            (at * blks + blk, (at ^ hops[blk & 1]) * blks + blk)
            for at in range(groups)
            for blk in range(blks)
        ]
        return lax.ppermute(value, ("grp", "blk"), pairs)

    steps = groups // 2 - 1
    even_core = lax.axis_index("blk") % 2 == 0
    pieces = [slice(at * tiles_dev, (at + 1) * tiles_dev) for at in range(steps)]
    handed = [turned(far[pieces[at]], 1, 2 * at + 2).astype(jnp.float32) for at in range(steps)]
    arrived = [turned(first, 1, 2)]
    for at in range(steps):
        value = later[pieces[at]]
        for step, extra in enumerate(handed):
            if step == at == steps - 1:
                value = value + extra
            elif step == at:
                value = value + jnp.where(even_core, extra, 0.0)
            elif at == steps - 1:
                value = value + jnp.where(even_core, 0.0, extra)
        odd_hop = 1 if at == steps - 1 else 2 * at + 4
        arrived.append(turned(value.astype(jnp.bfloat16), 2 * at + 2, odd_hop))
    own = own + even_own + arrived[0].astype(jnp.float32)
    own, *sums = lax.optimization_barrier((own, *arrived[1:]))
    out = pl.pallas_call(
        final_kernel,
        out_shape=jax.ShapeDtypeStruct(part, jnp.bfloat16),
        in_specs=[VMEM] * (2 + len(sums)),
        out_specs=HBM,
        scratch_shapes=[
            held(tiles_dev, jnp.bfloat16),
            pltpu.SemaphoreType.DMA((tiles_dev,)),
        ],
        compiler_params=LIMIT,
        cost_estimate=cost_of(0, tile_rows, row_width),
    )(factors, own, *sums)
    return out.reshape(1, row_count, row_width)


def solution(mesh):
    placed = (
        P("side", ("grp", "blk"), None),
        P("side", ("grp", "blk")),
        P("side", ("grp", "blk")),
        P("side", ("grp", "blk"), None, None),
        P("side", None, ("grp", "blk")),
    )
    return jax.shard_map(
        shards,
        mesh=mesh,
        in_specs=placed,
        out_specs=P("side", ("grp", "blk"), None),
        check_vma=False,
    )
```

```python
import functools

import jax
import jax.numpy as jnp
from jax import lax
from jax.experimental import pallas as pl
from jax.experimental.pallas import tpu as pltpu
from jax.sharding import PartitionSpec as P

UNROLL = 8
STAGES = 5
VMEM = pl.BlockSpec(memory_space=pltpu.VMEM)
SMEM = pl.BlockSpec(memory_space=pltpu.SMEM)
HBM = pl.BlockSpec(memory_space=pltpu.HBM)
LIMIT = pltpu.CompilerParams(vmem_limit_bytes=48 * 1024 * 1024)


def in_hbm(*arrays):
    return [pltpu.with_memory_space_constraint(array, pltpu.HBM) for array in arrays]


def split(value, size):
    if size & (size - 1) == 0:
        return value >> (size.bit_length() - 1), value & (size - 1)
    return value // size, value % size


def scale_kernel(
    exps_hbm, degrees_hbm, codes_hbm, rows, factors, scales, exps_ref, degrees, codes, sems
):
    pairs = [(exps_hbm, exps_ref), (degrees_hbm, degrees), (codes_hbm, codes)]
    fetches = [
        pltpu.make_async_copy(held, wanted, sems.at[at])
        for at, (held, wanted) in enumerate(pairs)
    ]
    for fetch in fetches:
        fetch.start()
    fetches[0].wait()
    fetches[1].wait()
    tiles_dev, tile_rows, row_width = rows.shape
    inverse = lax.rsqrt(degrees[...].astype(jnp.float32))
    for tile in range(tiles_dev):
        lanes = inverse[:, tile * tile_rows : (tile + 1) * tile_rows]
        factors[tile] = jnp.broadcast_to(lanes, (row_width, tile_rows)).T
        scale = jnp.exp2(jnp.full((1, 1), exps_ref[0, tile], jnp.int32).astype(jnp.float32))
        scales[tile : tile + 1, :] = lanes * scale
    fetches[2].wait()
    for tile in range(tiles_dev):
        scale = jnp.exp2(jnp.full((1, 1), exps_ref[0, tile], jnp.int32).astype(jnp.float32))
        scaled = codes[tile].astype(jnp.float32) * scale * factors[tile]
        rows[tile] = scaled.astype(rows.dtype)


def scale_rows(codes, exps, degrees):
    return pl.pallas_call(
        scale_kernel,
        out_shape=[
            jax.ShapeDtypeStruct(codes.shape, jnp.bfloat16),
            jax.ShapeDtypeStruct(codes.shape, jnp.float32),
            jax.ShapeDtypeStruct(codes.shape[:2], jnp.float32),
        ],
        in_specs=[HBM] * 3,
        out_specs=[VMEM] * 3,
        scratch_shapes=[
            pltpu.SMEM(exps.shape, exps.dtype),
            pltpu.VMEM(degrees.shape, degrees.dtype),
            pltpu.VMEM(codes.shape, codes.dtype),
            pltpu.SemaphoreType.DMA((3,)),
        ],
        compiler_params=LIMIT,
        cost_estimate=pl.CostEstimate(
            flops=codes.size, bytes_accessed=4 * codes.size, transcendentals=0
        ),
    )(*in_hbm(exps, degrees, codes))


def count_up(shape, axis):
    return lax.broadcasted_iota(jnp.int32, shape, axis)


def stage_kernel(
    blks, groups, tiles_dev, index_hbm, blocks_hbm, order_ref, blocks, index_ref, sems
):
    fetch = pltpu.make_async_copy(index_hbm, index_ref, sems.at[0])
    fetch.start()
    copy = pltpu.make_async_copy(blocks_hbm, blocks, sems.at[1])
    copy.start()
    fetch.wait()
    my_blk = lax.axis_index("blk")
    my_grp = lax.axis_index("grp")
    capacity = index_ref.shape[1]
    width = order_ref.shape[1]
    source_tiles = blks * tiles_dev
    half = blks // 2
    role = my_blk & 1

    target = index_ref[0:1, :]
    origin = index_ref[1:2, :]
    hop, row = split(origin, tiles_dev)
    chunk, tile = split(target, tiles_dev)
    hop = hop ^ my_blk
    chunk = chunk ^ my_grp
    odd = hop & 1
    rank = jnp.where(odd == role, half - 1 - (hop >> 1), hop >> 1)
    far = (chunk >= 2) & ((chunk & 1) == 1)
    kept = jnp.where(chunk == 1, 1 + role * (groups // 2 - 1), (chunk >> 1) + 1 - role)
    kept = jnp.where(chunk == 0, 0, jnp.where(far, (chunk >> 1) - 1, kept))
    stage = jnp.where(far, jnp.where(odd == 1, 2, jnp.minimum(rank, 1)), 4)
    drawn = (kept == 0) & (role == 0)
    stage = jnp.where(far | ((kept != 1) & ~drawn), stage, 3)
    near = jnp.where(stage == 3, 1 - kept, kept - (kept > 1).astype(jnp.int32))
    kept = jnp.where(far, kept, near)
    stage = jnp.where(origin < source_tiles, stage, STAGES)
    panel = jnp.where(stage == 1, rank - 1, jnp.where(stage == 2, rank, rank + odd * half))
    slot = count_up((1, capacity), 1)

    stages = (count_up((8, capacity), 0) == stage).astype(jnp.float32)
    earlier = count_up((capacity, capacity), 0) < count_up((capacity, capacity), 1)
    before = jnp.dot(
        stages.astype(jnp.bfloat16), earlier.astype(jnp.bfloat16), preferred_element_type=jnp.float32
    )
    position = jnp.sum(stages * before, axis=0, keepdims=True).astype(jnp.int32)
    parts = (slot & 127, slot >> 7, panel * tiles_dev + row, kept * tiles_dev + tile)
    values = sum(
        jnp.where(count_up((8, capacity), 0) == at, part, 0) for at, part in enumerate(parts)
    ).astype(jnp.bfloat16)
    far_tiles = (groups // 2 - 1) * tiles_dev
    tops = [far_tiles] * 3 + [2 * tiles_dev, groups // 2 * tiles_dev]
    lanes = count_up((1, width), 1)
    for at, top in enumerate(tops):
        where = jnp.where(stage == at, position, -1)
        chosen = (count_up((width, capacity), 0) == where).astype(jnp.bfloat16)
        listed = lax.dot_general(
            values, chosen, (((1,), (1,)), ((), ())), preferred_element_type=jnp.float32
        ).astype(jnp.int32)
        word = pack(listed[0:1] + (listed[1:2] << 7), listed[2:3], listed[3:4])
        count = jnp.sum((stage == at).astype(jnp.int32), axis=1, keepdims=True)
        word = jnp.where(lanes < count, word, pack(0, 0, top))
        batches = split(count + (UNROLL - 1), UNROLL)[0]
        order_ref[at : at + 1, :] = jnp.where(lanes == width - UNROLL, batches, word)
    copy.wait()


def pack(slot, row, target):
    return (slot << 16) | (row << 8) | target


def unpack(word):
    return word >> 16, (word >> 8) & 255, word & 255


def stage_blocks(index, blocks, blks, groups, tiles_dev):
    capacity = blocks.shape[0]
    assert blks * tiles_dev < 256 and groups * tiles_dev < 256 and capacity < 2**15
    width = -(-(capacity + 2 * UNROLL) // 128) * 128
    return pl.pallas_call(
        functools.partial(stage_kernel, blks, groups, tiles_dev),
        out_shape=[
            jax.ShapeDtypeStruct((8, width), jnp.int32),
            jax.ShapeDtypeStruct(blocks.shape, blocks.dtype),
        ],
        in_specs=[HBM, HBM],
        out_specs=[VMEM, VMEM],
        scratch_shapes=[
            pltpu.VMEM(index.shape, index.dtype),
            pltpu.SemaphoreType.DMA((2,)),
        ],
        compiler_params=LIMIT,
        cost_estimate=pl.CostEstimate(flops=0, bytes_accessed=0, transcendentals=0),
    )(*in_hbm(index, blocks))


def add_products(stage, order_ref, blocks, source, total):
    @pl.loop(0, order_ref[stage, order_ref.shape[1] - UNROLL])
    def _(batch):
        made = []
        for part in range(UNROLL):
            slot, row, target = unpack(order_ref[stage, batch * UNROLL + part])
            product = jnp.dot(blocks[slot], source[row], preferred_element_type=jnp.float32)
            made.append((target, product))
        for target, product in made:
            total[target] += product


def gather_panels(panels, source):
    for at, panel in enumerate(panels):
        rows = panel.shape[0]
        source[at * rows : (at + 1) * rows] = panel[...]


def early_kernel(order_ref, panel, blocks, total):
    total[...] = jnp.zeros_like(total)
    add_products(0, order_ref, blocks, panel, total)


def middle_kernel(order_ref, *refs):
    *panels, blocks, _, total, source = refs
    gather_panels(panels, source)
    add_products(1, order_ref, blocks, source, total)


def far_kernel(order_ref, *refs):
    *panels, blocks, _, far, total, source = refs
    gather_panels(panels, source)
    add_products(2, order_ref, blocks, source, total)
    far[...] = total[: far.shape[0]].astype(far.dtype)


def first_kernel(order_ref, *refs):
    *panels, blocks, first, own, source, total = refs
    gather_panels(panels, source)
    total[...] = jnp.zeros_like(total)
    add_products(3, order_ref, blocks, source, total)
    tiles_dev = first.shape[0]
    first[...] = total[:tiles_dev].astype(first.dtype)
    own[...] = total[tiles_dev : 2 * tiles_dev]


def rest_kernel(order_ref, *refs):
    *panels, blocks, own, later, source, total = refs
    gather_panels(panels, source)
    total[...] = jnp.zeros_like(total)
    add_products(4, order_ref, blocks, source, total)
    tiles_dev = own.shape[0]
    own[...] = total[:tiles_dev]
    later[...] = total[tiles_dev : tiles_dev + later.shape[0]]


def final_kernel(factors, own, *refs):
    *arrived, out_hbm, out, sems = refs
    copies = []
    for tile in range(out.shape[0]):
        value = own[tile]
        for piece in arrived:
            value = value + piece[tile].astype(jnp.float32)
        out[tile] = (value * factors[tile]).astype(out.dtype)
        copies.append(pltpu.make_async_copy(out.at[tile], out_hbm.at[tile], sems.at[tile]))
        copies[-1].start()
    for copy in copies:
        copy.wait()


def cost_of(slots, tile_rows, row_width):
    return pl.CostEstimate(
        flops=2 * slots * tile_rows * tile_rows * row_width,
        bytes_accessed=2 * slots * tile_rows * tile_rows,
        transcendentals=0,
    )


def shards(embed_codes, embed_exps, degrees, adjacency, block_index):
    tile_rows = adjacency.shape[2]
    row_width = embed_codes.shape[2]
    row_count = embed_codes.shape[1]
    capacity = adjacency.shape[1]
    tiles_dev = row_count // tile_rows
    groups = lax.axis_size("grp")
    blks = lax.axis_size("blk")
    part = (tiles_dev, tile_rows, row_width)
    codes = embed_codes.reshape(part)
    source, factors, scales = scale_rows(codes, embed_exps, degrees)

    def across(value, step):
        pairs = [
            (side * blks + at, (1 - side) * blks + (at ^ (2 * step if at & 1 else blks - 2 - 2 * step)))
            for side in range(2)
            for at in range(blks)
        ]
        return lax.ppermute(value, ("side", "blk"), pairs)

    def paired(value, axis, hop):
        return lax.ppermute(value, axis, [(at, at ^ hop) for at in range(lax.axis_size(axis))])

    early = across(codes, 0)
    middle = [across(source, step) for step in range(1, blks // 2)]
    early_scales = across(scales, 0)
    order, blocks = stage_blocks(block_index[0], adjacency[0], blks, groups, tiles_dev)
    early, early_scales, order = lax.optimization_barrier((early, early_scales, order))
    early = (early.astype(jnp.float32) * early_scales[:, :, None]).astype(jnp.bfloat16)
    other = paired(early, "blk", 1)
    far_tiles = (groups // 2 - 1) * tiles_dev

    def held(count, dtype):
        return pltpu.VMEM((count, tile_rows, row_width), dtype)

    total = pl.pallas_call(
        early_kernel,
        out_shape=jax.ShapeDtypeStruct((far_tiles + 1, tile_rows, row_width), jnp.float32),
        in_specs=[SMEM] + [VMEM] * 2,
        out_specs=VMEM,
        compiler_params=LIMIT,
        cost_estimate=cost_of(capacity // 8, tile_rows, row_width),
    )(order, early, blocks)
    *middle, total = lax.optimization_barrier((*middle, total))
    others = [other] + [paired(panel, "blk", 1) for panel in middle]
    total = pl.pallas_call(
        middle_kernel,
        out_shape=jax.ShapeDtypeStruct(total.shape, total.dtype),
        in_specs=[SMEM] + [VMEM] * (len(middle) + 2),
        out_specs=VMEM,
        input_output_aliases={len(middle) + 2: 0},
        scratch_shapes=[held(len(middle) * tiles_dev, jnp.bfloat16)],
        compiler_params=LIMIT,
        cost_estimate=cost_of(capacity // 8, tile_rows, row_width),
    )(order, *middle, blocks, total)
    *others, total = lax.optimization_barrier((*others, total))
    far, _ = pl.pallas_call(
        far_kernel,
        out_shape=[
            jax.ShapeDtypeStruct((far_tiles, tile_rows, row_width), jnp.bfloat16),
            jax.ShapeDtypeStruct(total.shape, total.dtype),
        ],
        in_specs=[SMEM] + [VMEM] * (len(others) + 2),
        out_specs=[VMEM] * 2,
        input_output_aliases={len(others) + 2: 1},
        scratch_shapes=[held(len(others) * tiles_dev, jnp.bfloat16)],
        compiler_params=LIMIT,
        cost_estimate=cost_of(capacity // 8, tile_rows, row_width),
    )(order, *others, blocks, total)
    far, order = lax.optimization_barrier((far, order))
    panels = [early] + middle + others
    first, even_own = pl.pallas_call(
        first_kernel,
        out_shape=[
            jax.ShapeDtypeStruct(part, jnp.bfloat16),
            jax.ShapeDtypeStruct(part, jnp.float32),
        ],
        in_specs=[SMEM] + [VMEM] * (len(panels) + 1),
        out_specs=[VMEM] * 2,
        scratch_shapes=[
            held(len(panels) * tiles_dev, jnp.bfloat16),
            held(2 * tiles_dev + 1, jnp.float32),
        ],
        compiler_params=LIMIT,
        cost_estimate=cost_of(capacity // 4, tile_rows, row_width),
    )(order, *panels, blocks)
    first, order = lax.optimization_barrier((first, order))
    own, later = pl.pallas_call(
        rest_kernel,
        out_shape=[
            jax.ShapeDtypeStruct(part, jnp.float32),
            jax.ShapeDtypeStruct((far_tiles, tile_rows, row_width), jnp.float32),
        ],
        in_specs=[SMEM] + [VMEM] * (len(panels) + 1),
        out_specs=[VMEM] * 2,
        scratch_shapes=[
            held(len(panels) * tiles_dev, jnp.bfloat16),
            held(groups // 2 * tiles_dev + 1, jnp.float32),
        ],
        compiler_params=LIMIT,
        cost_estimate=cost_of(capacity // 2, tile_rows, row_width),
    )(order, *panels, blocks)

    def turned(value, even_hop, odd_hop):
        hops = (even_hop, odd_hop)
        pairs = [
            (at * blks + blk, (at ^ hops[blk & 1]) * blks + blk)
            for at in range(groups)
            for blk in range(blks)
        ]
        return lax.ppermute(value, ("grp", "blk"), pairs)

    steps = groups // 2 - 1
    even_core = lax.axis_index("blk") % 2 == 0
    pieces = [slice(at * tiles_dev, (at + 1) * tiles_dev) for at in range(steps)]
    handed = [turned(far[pieces[at]], 1, 2 * at + 2).astype(jnp.float32) for at in range(steps)]
    arrived = [turned(first, 1, 2)]
    for at in range(steps):
        value = later[pieces[at]]
        for step, extra in enumerate(handed):
            if step == at == steps - 1:
                value = value + extra
            elif step == at:
                value = value + jnp.where(even_core, extra, 0.0)
            elif at == steps - 1:
                value = value + jnp.where(even_core, 0.0, extra)
        odd_hop = 1 if at == steps - 1 else 2 * at + 4
        arrived.append(turned(value.astype(jnp.bfloat16), 2 * at + 2, odd_hop))
    own = own + even_own + arrived[0].astype(jnp.float32)
    own, *sums = lax.optimization_barrier((own, *arrived[1:]))
    out = pl.pallas_call(
        final_kernel,
        out_shape=jax.ShapeDtypeStruct(part, jnp.bfloat16),
        in_specs=[VMEM] * (2 + len(sums)),
        out_specs=HBM,
        scratch_shapes=[
            held(tiles_dev, jnp.bfloat16),
            pltpu.SemaphoreType.DMA((tiles_dev,)),
        ],
        compiler_params=LIMIT,
        cost_estimate=cost_of(0, tile_rows, row_width),
    )(factors, own, *sums)
    return out.reshape(1, row_count, row_width)


def solution(mesh):
    placed = (
        P("side", ("grp", "blk"), None),
        P("side", ("grp", "blk")),
        P("side", ("grp", "blk")),
        P("side", ("grp", "blk"), None, None),
        P("side", None, ("grp", "blk")),
    )
    return jax.shard_map(
        shards,
        mesh=mesh,
        in_specs=placed,
        out_specs=P("side", ("grp", "blk"), None),
        check_vma=False,
    )
```
